32 devices in a mesh: lat: 8 (over z, y), lon: 4 (over x, core).
Axes of the slice: x: 2, y: 2, z: 4, core: 2. Of those that a mesh axis runs over, the one named last changes fastest.
Arguments:
- state: float32 [5, 24, 8, 8, 2880], P(None, 'lat', None, None, 'lon'), may hold values from -6 to 6
- courant_x: float32 [24, 8, 8, 2880], P('lat', None, None, 'lon'), may hold values from -4 to 4
- courant_y: float32 [24, 8, 8, 2880], P('lat', None, None, 'lon'), may hold values from -4 to 4
- block_of_slot: int32 [24], P('lat'), may hold values from 0 to 23, as said below
- face_source: int32 [24, 2], P('lat'), may hold values from -1 to 23, as said below
- cutoff: int32 [192], replicated, may hold values from 0 to 256, as said below
Outputs:
- new_state: float32 [5, 24, 8, 8, 2880], P(None, 'lat', None, None, 'lon')
The draws below stay inside these ranges and needn't reach their ends.
Inputs may be any that keep to these rules, and one draw needn't show every extreme that they name: `block_of_slot`: each block number appears once. The polar blocks are the first and the last 4 block numbers; the 3 slots of one index of lat hold at most 2 polar blocks, and some index holds 2. `face_source`: entry 0 of slot s is the slot holding block block_of_slot[s] - 1 and entry 1 the slot holding block block_of_slot[s] + 1; -1 where that block does not exist. Rows of polar blocks have a cutoff of 1 or more; all other rows have 0.
All inputs are finite; a program needn't handle non-finite values.
Results may differ from the reference program's by a relative error of at most 0.00005.
Values sent between devices are 32-bit elements; how exact they have to be, the bound alone decides.
No kernel may reach another device: no remote copies, remote signals or barrier semaphores. Data moves between devices by JAX's collectives and lax.ppermute only.
A program may use at most 64 MiB of HBM per device.

```python
import math
import jax
import jax.numpy as jnp
from jax import lax

NLON = 2880
KCUT = 256
FIELDS = 5
LEV = 8
BLK_DEV = 3
BR = 8
NBLK = 24


def layout_tables(key):
    base_key = jax.random.fold_in(key, 7)
    key_rank, key_pos, key_perm = jax.random.split(base_key, 3)
    devices = NBLK // BLK_DEV
    rank = jax.random.permutation(key_rank, devices)
    counts = jnp.where(rank < devices // 4, 2, jnp.where(rank < 3 * devices // 4, 1, 0))
    scores = jax.random.randint(key_pos, (devices, BLK_DEV), 0, 1024) * BLK_DEV + jnp.arange(BLK_DEV, dtype=jnp.int32)[None, :]
    inner = jnp.argsort(jnp.argsort(scores, axis=1), axis=1)
    polar_flag = (inner < counts[:, None]).reshape(-1)
    shuffle = jax.random.permutation(key_perm, NBLK)
    order = jnp.argsort(jnp.where(polar_flag, 0, NBLK) + shuffle).astype(jnp.int32)
    polar_count = NBLK // 6
    position = jnp.arange(NBLK, dtype=jnp.int32)
    sorted_blocks = jnp.where(position < polar_count, position, jnp.where(position < 2 * polar_count, NBLK - 2 * polar_count + position, position - polar_count))
    block_table = jnp.zeros((NBLK,), jnp.int32).at[order].set(sorted_blocks.astype(jnp.int32))
    slot_table = jnp.zeros((NBLK,), jnp.int32).at[block_table].set(position)
    north_slot = jnp.where(block_table > 0, slot_table[jnp.maximum(block_table - 1, 0)], -1)
    south_slot = jnp.where(block_table < NBLK - 1, slot_table[jnp.minimum(block_table + 1, NBLK - 1)], -1)
    return (block_table, jnp.stack([north_slot, south_slot], axis=1).astype(jnp.int32))


def draw_block_of_slot(key, part):
    return layout_tables(key)[0]


def draw_face_source(key, part):
    return layout_tables(key)[1]


def draw_cutoff(key, part):
    total_rows = NBLK * BR
    polar_rows = NBLK // 6 * BR
    row_index = jnp.arange(total_rows, dtype=jnp.int32)
    distance = jnp.minimum(row_index, total_rows - 1 - row_index)
    ramp = KCUT * (distance + 1) // polar_rows
    jitter = jax.random.randint(jax.random.fold_in(key, 11), (total_rows,), 0, 4)
    value = jnp.maximum(ramp - jitter, 1)
    value = jnp.where(distance == polar_rows - 1, KCUT, value)
    return jnp.where(distance < polar_rows, value, 0).astype(jnp.int32)


def block_scale(key, dims, shards, least, largest):
    def one(dim, parts):
        draws = jax.random.uniform(jax.random.fold_in(jax.random.fold_in(key, 6), dim), (parts,), jnp.float32, least / len(shards), largest / len(shards))
        return jnp.repeat(jnp.exp(draws), dims[dim] // parts).reshape((-1,) + (1,) * (len(dims) - dim - 1))

    gain = one(*shards[0])
    for cut in shards[1:]:
        gain = gain * one(*cut)
    return gain


def bell_draw(rng, extent, deviation, reach, shards=(), held_as=jnp.bfloat16):
    loudness = block_scale(rng, extent, shards, -0.22, 0.18) if shards else 1.0
    array = jax.random.normal(rng, extent, jnp.float32) * deviation * loudness
    return jnp.minimum(jnp.maximum(array, -reach), reach).astype(held_as)


def setup_inputs(seed: int = 0) -> dict:
    keys = jax.random.split(jax.random.key(seed), 7)
    state = bell_draw(keys[0], (FIELDS, NBLK, BR, LEV, NLON), 1.0, 6.0, ((1, 8), (4, 4)), jnp.float32)
    courant_x = bell_draw(keys[1], (NBLK, BR, LEV, NLON), 0.3, 4.0, ((0, 8), (3, 4)), jnp.float32)
    courant_y = bell_draw(keys[2], (NBLK, BR, LEV, NLON), 0.3, 4.0, ((0, 8), (3, 4)), jnp.float32)
    block_of_slot = draw_block_of_slot(jax.random.fold_in(keys[6], 71), 0)
    face_source = draw_face_source(jax.random.fold_in(keys[6], 71), 0)
    cutoff = draw_cutoff(jax.random.fold_in(keys[6], 71), 0)
    return dict(state=state, courant_x=courant_x, courant_y=courant_y, block_of_slot=block_of_slot, face_source=face_source, cutoff=cutoff)


def fourier_basis(columns):
    wavenumber = jnp.arange(KCUT, dtype=jnp.int32)
    phase = ((columns[:, None] * wavenumber[None, :]) % NLON).astype(jnp.float32) * (2.0 * math.pi / NLON)
    return jnp.concatenate([jnp.cos(phase), jnp.sin(phase)], axis=1)


def spectral_weights(cut_rows):
    wavenumber = jnp.arange(KCUT, dtype=jnp.int32)
    scaling = jnp.where(wavenumber == 0, 1.0 / NLON, 2.0 / NLON).astype(jnp.float32)
    kept = jnp.where(wavenumber[None, :] < cut_rows[:, None], scaling[None, :], 0.0).astype(jnp.float32)
    return jnp.concatenate([kept, kept], axis=1)


def reference(state, courant_x, courant_y, block_of_slot, face_source, cutoff):
    north_slot = face_source[:, 0]
    south_slot = face_source[:, 1]
    has_north = north_slot >= 0
    has_south = south_slot >= 0
    north_safe = jnp.maximum(north_slot, 0).astype(jnp.int32)
    south_safe = jnp.maximum(south_slot, 0).astype(jnp.int32)
    north_rows = jnp.where(has_north[None, :, None, None], state[:, north_safe, BR - 1], 0.0)
    south_rows = jnp.where(has_south[None, :, None, None], state[:, south_safe, 0], 0.0)
    north_wind = jnp.where(has_north[:, None, None], courant_y[north_safe, BR - 1], 0.0)
    extended = jnp.concatenate([north_rows[:, :, None], state, south_rows[:, :, None]], axis=2)
    wind_ext = jnp.concatenate([north_wind[:, None], courant_y], axis=1)
    face_keep = jnp.concatenate([jnp.ones((NBLK, BR), jnp.float32), has_south[:, None].astype(jnp.float32)], axis=1)
    merid_flux = wind_ext[None] * (extended[:, :, :-1] + extended[:, :, 1:]) * 0.5 * face_keep[None, :, :, None, None]
    merid_div = merid_flux[:, :, 1:] - merid_flux[:, :, :-1]
    zonal_flux = courant_x[None] * (state + jnp.roll(state, -1, axis=4)) * 0.5
    zonal_div = zonal_flux - jnp.roll(zonal_flux, 1, axis=4)
    tendency = -(zonal_div + merid_div)
    global_rows = block_of_slot[:, None] * BR + jnp.arange(BR, dtype=jnp.int32)[None, :]
    row_cut = cutoff[global_rows]
    cut_rows = jnp.broadcast_to(row_cut[:, :, None], (NBLK, BR, LEV)).reshape(-1)
    basis = fourier_basis(jnp.arange(NLON, dtype=jnp.int32))
    weights = spectral_weights(cut_rows)

    def filter_field(field_tend):
        row_matrix = field_tend.reshape(-1, NLON)
        spectrum = jnp.dot(row_matrix, basis, precision=lax.Precision.HIGHEST, preferred_element_type=jnp.float32)
        smoothed = jnp.dot(spectrum * weights, basis.T, precision=lax.Precision.HIGHEST, preferred_element_type=jnp.float32)
        return jnp.where(cut_rows[:, None] > 0, smoothed, row_matrix).reshape(field_tend.shape)

    filtered = lax.map(filter_field, tendency)
    return state + filtered
```

```python
import math

import jax
import jax.numpy as jnp
import numpy as np
from jax import lax
from jax.sharding import PartitionSpec as P

NLON = 2880
KCUT = 256
HIGH = lax.Precision.HIGH


def basis_table(width):
    column = np.arange(width, dtype=np.int64)
    wavenumber = np.arange(KCUT, dtype=np.int64)
    phase = (column[:, None] * wavenumber[None, :] % NLON).astype(np.float64) * (
        2.0 * math.pi / NLON
    )
    return np.concatenate([np.cos(phase), np.sin(phase)], axis=1).astype(np.float32)


def rotation(lon_index, width):
    wavenumber = jnp.arange(KCUT, dtype=jnp.int32)
    phase = (lon_index * width * wavenumber % NLON).astype(jnp.float32) * (2.0 * math.pi / NLON)
    return jnp.cos(phase), jnp.sin(phase)


def to_pieces(units, parts):
    count, levels, width = units.shape
    groups = math.gcd(parts, levels)
    chunks = parts // groups
    span = -(-width // chunks)
    units = jnp.pad(units, ((0, 0), (0, 0), (0, span * chunks - width)))
    units = units.reshape(count, groups, levels // groups, chunks, span)
    return units.transpose(1, 3, 0, 2, 4).reshape(parts, count, levels // groups * span)


def from_pieces(pieces, levels, width):
    parts, count, _ = pieces.shape
    groups = math.gcd(parts, levels)
    chunks = parts // groups
    span = -(-width // chunks)
    pieces = pieces.reshape(groups, chunks, count, levels // groups, span)
    return pieces.transpose(2, 0, 3, 1, 4).reshape(count, levels, chunks * span)[:, :, :width]


def swap(array, axis, bit):
    size = lax.axis_size(axis)
    return lax.ppermute(array, axis, [(i, i ^ bit) for i in range(size)])


def lon_sum(partial):
    size = lax.axis_size("lon")
    core = lax.axis_index("lon") % 2
    half = partial.shape[0] // 2
    lower, upper = partial[:half], partial[half:]
    mine = jnp.where(core == 0, lower, upper)
    other = jnp.where(core == 0, upper, lower)
    total = mine + swap(other, "lon", 1)
    bit = 2
    while bit < size:
        total = total + swap(total, "lon", bit)
        bit *= 2
    away = swap(total, "lon", 1)
    return jnp.where(
        core == 0, jnp.concatenate([total, away], 0), jnp.concatenate([away, total], 0)
    )


def shards(state, courant_x, courant_y, block_of_slot, face_source, cutoff):
    fields, slots, rows, levels, width = state.shape
    lat = lax.axis_size("lat")
    lon = lax.axis_size("lon")
    lon_index = lax.axis_index("lon")
    first = state[:, :, 0].transpose(1, 0, 2, 3)
    last = state[:, :, rows - 1].transpose(1, 0, 2, 3)
    wind = courant_y[:, rows - 1][:, None] * 0.5
    units = jnp.concatenate([first, last * wind, wind], axis=1)
    count = 2 * fields + 1
    sent = to_pieces(units.reshape(slots * count, levels, width), lat)
    span = sent.shape[2]
    table = jnp.pad(
        face_source.astype(jnp.float32).reshape(1, slots * 2), ((0, 0), (0, span - slots * 2))
    )
    sent = jnp.concatenate([sent, jnp.broadcast_to(table[None], (lat, 1, span))], axis=1)
    got = lax.all_to_all(sent, "lat", 0, 0, tiled=True)

    edge = jnp.concatenate([state, courant_x[None]], axis=0)
    west = lax.ppermute(edge[..., width - 1], "lon", [(i, (i + 1) % lon) for i in range(lon)])
    east = lax.ppermute(edge[:fields, ..., 0], "lon", [((i + 1) % lon, i) for i in range(lon)])
    shifted = jnp.concatenate([state[..., 1:], east[..., None]], axis=4)
    flux = courant_x[None] * (state + shifted) * 0.5
    flux_west = west[fields][None] * (west[:fields] + state[..., 0]) * 0.5
    flux_before = jnp.concatenate([flux_west[..., None], flux[..., :-1]], axis=4)
    inner = courant_y[None, :, : rows - 1] * (state[:, :, :-1] + state[:, :, 1:]) * 0.5
    zero = jnp.zeros_like(inner[:, :, :1])
    merid = jnp.concatenate([inner, zero], axis=2) - jnp.concatenate([zero, inner], axis=2)
    local = -((flux - flux_before) + merid)

    global_rows = block_of_slot[:, None] * rows + jnp.arange(rows, dtype=jnp.int32)[None, :]
    latitudes = jnp.arange(cutoff.shape[0], dtype=jnp.int32)
    row_cut = jnp.sum(
        jnp.where(global_rows[:, :, None] == latitudes[None, None, :], cutoff[None, None, :], 0),
        axis=2,
    )
    polar = row_cut[:, 0] > 0
    order = jnp.argsort(jnp.where(polar, 0, 1), stable=True)
    chosen = order[: slots - 1]
    cut = row_cut[chosen]

    basis = jnp.asarray(basis_table(width))
    turn_cos, turn_sin = rotation(lon_index, width)

    def turned(spec, sign):
        real, imag = spec[..., :KCUT], spec[..., KCUT:]
        return jnp.concatenate(
            [
                real * turn_cos - sign * imag * turn_sin,
                imag * turn_cos + sign * real * turn_sin,
            ],
            axis=-1,
        )

    scale = jnp.where(jnp.arange(KCUT) == 0, 1.0 / NLON, 2.0 / NLON).astype(jnp.float32)

    def weights(cut_rows):
        kept = jnp.where(jnp.arange(KCUT) < cut_rows[..., None], scale, 0.0)
        return jnp.concatenate([kept, kept], axis=-1)

    def smooth(tend, cuts):
        shape = tend.shape
        spec = jnp.dot(
            tend.reshape(-1, width), basis, precision=HIGH, preferred_element_type=jnp.float32
        )
        total = turned(lon_sum(turned(spec, 1.0)), -1.0)
        total = total.reshape(shape[:-1] + (2 * KCUT,)) * weights(cuts)[None, :, :, None]
        back = jnp.dot(
            total.reshape(-1, 2 * KCUT),
            basis.T,
            precision=HIGH,
            preferred_element_type=jnp.float32,
        ).reshape(shape)
        return jnp.where(cuts[None, :, :, None, None] > 0, back, tend)

    body = local[:, :, 1 : rows - 1][:, chosen]
    body_out = smooth(body, cut[:, 1 : rows - 1])

    indices = got[:, slots * count, : slots * 2].reshape(lat * slots, 2).astype(jnp.int32)
    data = got[:, : slots * count].reshape(lat * slots, count, span)
    north_all, south_all = indices[:, 0], indices[:, 1]
    face = data[:, fields : 2 * fields] + data[:, 2 * fields :] * data[
        jnp.maximum(south_all, 0), :fields
    ]
    face = jnp.where((south_all >= 0)[:, None, None], face, 0.0)
    face_north = jnp.where(
        (north_all >= 0)[:, None, None], face[jnp.maximum(north_all, 0)], 0.0
    )
    back = jnp.concatenate([face_north, face], axis=1).reshape(lat, slots * 2 * fields, span)
    back = lax.all_to_all(back, "lat", 0, 0, tiled=True)
    faces = from_pieces(back, levels, width).reshape(slots, 2, fields, levels, width)
    top = local[:, :, 0] + faces[:, 0].transpose(1, 0, 2, 3)
    bottom = local[:, :, rows - 1] - faces[:, 1].transpose(1, 0, 2, 3)
    rim = jnp.stack([top, bottom], axis=2)
    rim_cut = jnp.stack([cut[:, 0], cut[:, rows - 1]], axis=1)
    rim_out = smooth(rim[:, chosen], rim_cut)

    done = jnp.concatenate([rim_out[:, :, :1], body_out, rim_out[:, :, 1:]], axis=2)
    plain = jnp.concatenate([rim[:, :, :1], local[:, :, 1 : rows - 1], rim[:, :, 1:]], axis=2)
    place = jnp.argsort(order)
    filtered = jnp.concatenate([done, plain[:, order[slots - 1 :]]], axis=1)[:, place]
    return state + filtered


def solution(mesh):
    placed = (
        P(None, "lat", None, None, "lon"),
        P("lat", None, None, "lon"),
        P("lat", None, None, "lon"),
        P("lat"),
        P("lat", None),
        P(),
    )
    return jax.shard_map(
        shards,
        mesh=mesh,
        in_specs=placed,
        out_specs=P(None, "lat", None, None, "lon"),
        check_vma=False,
    )
```

```python
import functools
import math

import jax
import jax.numpy as jnp
import numpy as np
from jax import lax
from jax.experimental import pallas as pl
from jax.experimental.pallas import tpu as pltpu
from jax.sharding import PartitionSpec as P

NLON = 2880
KCUT = 256
LANES = 128
VMEM_LIMIT = 50 * 1024 * 1024
BF16 = jnp.bfloat16
F32 = jnp.float32


def phases(columns):
    wavenumber = np.arange(KCUT, dtype=np.int64)
    return (columns[:, None] * wavenumber[None, :] % NLON).astype(np.float64) * (
        2.0 * math.pi / NLON
    )


def basis_tables(width):
    phase = phases(np.arange(width, dtype=np.int64))
    table = np.concatenate([np.cos(phase), np.sin(phase)], axis=1).astype(np.float32)
    high = table.astype(jnp.bfloat16)
    low = (table - high.astype(np.float32)).astype(jnp.bfloat16)
    forward = (jnp.asarray(high), jnp.asarray(low))
    inverse = (
        jnp.asarray(np.ascontiguousarray(high.T)),
        jnp.asarray(np.ascontiguousarray(low.T)),
    )
    return forward, inverse


def turn_table(lon, width):
    phase = phases(np.arange(lon, dtype=np.int64) * width)
    table = np.concatenate([np.cos(phase), np.sin(phase)], axis=1).astype(np.float32)
    return jnp.asarray(table[:, None, :])


def split_dot(rows, high, low):
    rows_high = rows.astype(BF16)
    rows_low = (rows - rows_high.astype(F32)).astype(BF16)
    dot = functools.partial(jnp.dot, preferred_element_type=F32)
    return dot(rows_high, high) + (dot(rows_low, high) + dot(rows_high, low))


def turned(spec, turn, sign):
    real, imag = spec[:, :KCUT], spec[:, KCUT:]
    cos, sin = turn[:, :KCUT], turn[:, KCUT:] * sign
    return jnp.concatenate([real * cos - imag * sin, imag * cos + real * sin], axis=1)


def row_weights(cut):
    column = lax.broadcasted_iota(jnp.int32, (1, 2 * KCUT), 1)
    wavenumber = jnp.where(column >= KCUT, column - KCUT, column)
    scale = jnp.where(wavenumber == 0, 1.0 / NLON, 2.0 / NLON).astype(F32)
    return jnp.where(wavenumber < cut, scale, 0.0)


def pick_slots(block_ref, cutoff_ref, rows):
    polar1 = cutoff_ref[block_ref[1] * rows] > 0
    polar2 = cutoff_ref[block_ref[2] * rows] > 0
    rest = jnp.where(polar2, jnp.where(polar1, 0, 1), 2)
    return jnp.where(rest == 0, 1, 0), jnp.where(rest == 2, 1, 2), rest


def mine_first(pair, core):
    a, b = pair
    return jnp.where(core == 0, a, b), jnp.where(core == 0, b, a)


def edge_kernel(lane_last, head_ref, tail_ref, wind_ref, west_ref, east_ref):
    fields, slots, rows = head_ref.shape[:3]
    lane = lax.broadcasted_iota(jnp.int32, (8, LANES), 1)
    for s in range(slots):
        west = jnp.zeros((8, LANES), F32)
        east = jnp.zeros((8, LANES), F32)
        for r in range(rows):
            for f in range(fields):
                here = lane == f * rows + r
                west = jnp.where(here, tail_ref[f, s, r, :, lane_last : lane_last + 1], west)
                east = jnp.where(here, head_ref[f, s, r, :, 0:1], east)
            here = lane == fields * rows + r
            west = jnp.where(here, wind_ref[s, r, :, lane_last : lane_last + 1], west)
        west_ref[s] = west
        east_ref[s] = east


def edges(state, courant_x):
    fields, slots, rows, levels, width = state.shape
    last = (width - 1) // LANES
    out = jax.ShapeDtypeStruct((slots, levels, LANES), F32)
    return pl.pallas_call(
        functools.partial(edge_kernel, (width - 1) % LANES),
        grid=(1,),
        in_specs=[
            pl.BlockSpec((fields, slots, rows, levels, LANES), lambda i: (0, 0, 0, 0, 0)),
            pl.BlockSpec((fields, slots, rows, levels, LANES), lambda i: (0, 0, 0, 0, last)),
            pl.BlockSpec((slots, rows, levels, LANES), lambda i: (0, 0, 0, last)),
        ],
        out_specs=[pl.BlockSpec((slots, levels, LANES), lambda i: (0, 0, 0))] * 2,
        out_shape=[out, out],
        cost_estimate=pl.CostEstimate(flops=10**5, bytes_accessed=1200000, transcendentals=0),
        name="edges",
    )(state, state, courant_x)


PIECE = 200
BACK = 192


def tile_of(slab, t, width):
    part = slab[:, t * LANES : min((t + 1) * LANES, width)]
    if part.shape[1] < LANES:
        part = jnp.concatenate([part, jnp.zeros((8, LANES - part.shape[1]), F32)], axis=1)
    return part


def pack_kernel(width, first_ref, last_ref, wind_ref, source_ref, out_ref):
    fields, slots = first_ref.shape[:2]
    tiles = -(-width // LANES)

    def put(row, tile):
        out_ref[pl.ds(row, 8, stride=PIECE), :] = tile

    for j in range(slots):
        half = wind_ref[j, 0] * 0.5
        for t in range(tiles):
            row = {0: 192 + 2 * j, 1: 193 + 2 * j, 2: 64 * j + 62, 3: 64 * j + 63}.get(
                t, 64 * j + 26 + t
            )
            put(row, tile_of(half, t, width))
        for f in range(fields):
            north = last_ref[f, j, 0] * half
            south = first_ref[f, j, 0]
            for t in range(tiles):
                put(64 * j + f * tiles + t, tile_of(north, t, width))
                put(64 * j + 32 + f * tiles + t, tile_of(south, t, width))
    lane = lax.broadcasted_iota(jnp.int32, (8, LANES), 1)
    table = jnp.zeros((8, LANES), F32)
    for j in range(slots):
        for side in range(2):
            table = jnp.where(lane == 2 * j + side, source_ref[j, side].astype(F32), table)
    put(198, table)
    put(199, table)


def pack(state, courant_y, face_source):
    fields, slots, rows, levels, width = state.shape
    return pl.pallas_call(
        functools.partial(pack_kernel, width),
        grid=(1,),
        in_specs=[
            pl.BlockSpec((fields, slots, 1, levels, width), lambda i: (0, 0, 0, 0, 0)),
            pl.BlockSpec((fields, slots, 1, levels, width), lambda i: (0, 0, rows - 1, 0, 0)),
            pl.BlockSpec((slots, 1, levels, width), lambda i: (0, rows - 1, 0, 0)),
            pl.BlockSpec(memory_space=pltpu.SMEM),
        ],
        out_specs=pl.BlockSpec((levels * PIECE, LANES), lambda i: (0, 0)),
        out_shape=jax.ShapeDtypeStruct((levels * PIECE, LANES), F32),
        cost_estimate=pl.CostEstimate(flops=10**5, bytes_accessed=1700000, transcendentals=0),
        name="pack",
    )(state, state, courant_y, face_source)


def face_kernel(got_ref, out_ref, face_ref, table_ref, sem):
    parts = got_ref.shape[0]
    slots = out_ref.shape[1]
    copy = pltpu.make_async_copy(got_ref.at[:, 192:200, :], table_ref, sem)
    copy.start()
    copy.wait()
    for s in range(parts * slots):
        src, j = divmod(s, slots)
        south = table_ref[src, 6, 2 * j + 1].astype(jnp.int32)
        safe = jnp.maximum(south, 0)
        from_src = lax.div(safe, slots)
        from_slot = safe - from_src * slots
        half = jnp.concatenate(
            [
                got_ref[src, 192 + 2 * j : 194 + 2 * j, :],
                got_ref[src, 64 * j + 62 : 64 * j + 64, :],
                got_ref[src, 64 * j + 30 : 64 * j + 32, :],
            ],
            axis=0,
        )
        half = jnp.concatenate([half] * 5 + [half[:2]], axis=0)
        other = got_ref[from_src, pl.ds(pl.multiple_of(64 * from_slot + 32, 32), 32), :]
        face = got_ref[src, 64 * j : 64 * j + 32, :] + half * other
        face = jnp.where(south >= 0, face, 0.0)
        face_ref[s] = face
        out_ref[src, j, 1] = face
    for s in range(parts * slots):
        src, j = divmod(s, slots)
        north = table_ref[src, 6, 2 * j].astype(jnp.int32)
        out_ref[src, j, 0] = jnp.where(north >= 0, face_ref[jnp.maximum(north, 0)], 0.0)


def faces_of_pieces(got, slots):
    parts = got.shape[0]
    return pl.pallas_call(
        face_kernel,
        in_specs=[pl.BlockSpec(memory_space=pltpu.VMEM)],
        out_specs=pl.BlockSpec(memory_space=pltpu.VMEM),
        out_shape=jax.ShapeDtypeStruct((parts, slots, 2, 32, LANES), F32),
        scratch_shapes=[
            pltpu.VMEM((parts * slots, 32, LANES), F32),
            pltpu.SMEM((parts, 8, LANES), F32),
            pltpu.SemaphoreType.DMA(()),
        ],
        cost_estimate=pl.CostEstimate(flops=10**5, bytes_accessed=1600000, transcendentals=0),
        name="faces",
    )(got)


def to_pieces(units, parts):
    count, levels, width = units.shape
    groups = math.gcd(parts, levels)
    chunks = parts // groups
    span = -(-width // chunks)
    units = jnp.pad(units, ((0, 0), (0, 0), (0, span * chunks - width)))
    units = units.reshape(count, groups, levels // groups, chunks, span)
    return units.transpose(1, 3, 0, 2, 4).reshape(parts, count, levels // groups * span)


def from_pieces(pieces, levels, width):
    parts, count, _ = pieces.shape
    groups = math.gcd(parts, levels)
    chunks = parts // groups
    span = -(-width // chunks)
    pieces = pieces.reshape(groups, chunks, count, levels // groups, span)
    return pieces.transpose(2, 0, 3, 1, 4).reshape(count, levels, chunks * span)[:, :, :width]


def exchange_faces(state, courant_y, face_source):
    fields, slots, rows, levels, width = state.shape
    lat = lax.axis_size("lat")
    count = 2 * fields + 1
    first = state[:, :, 0].transpose(1, 0, 2, 3)
    last = state[:, :, rows - 1].transpose(1, 0, 2, 3)
    half = courant_y[:, rows - 1][:, None] * 0.5
    units = jnp.concatenate([first, last * half, half], axis=1)
    sent = to_pieces(units.reshape(slots * count, levels, width), lat)
    span = sent.shape[2]
    table = jnp.pad(
        face_source.astype(F32).reshape(1, slots * 2), ((0, 0), (0, span - slots * 2))
    )
    sent = jnp.concatenate([sent, jnp.broadcast_to(table[None], (lat, 1, span))], axis=1)
    got = lax.all_to_all(sent, "lat", 0, 0, tiled=True)
    indices = got[:, slots * count, : slots * 2].reshape(lat * slots, 2).astype(jnp.int32)
    data = got[:, : slots * count].reshape(lat * slots, count, span)
    north, south = indices[:, 0], indices[:, 1]
    face = data[:, fields : 2 * fields] + data[:, 2 * fields :] * data[
        jnp.maximum(south, 0), :fields
    ]
    face = jnp.where((south >= 0)[:, None, None], face, 0.0)
    face_north = jnp.where((north >= 0)[:, None, None], face[jnp.maximum(north, 0)], 0.0)
    back = jnp.concatenate([face_north, face], axis=1).reshape(lat, slots * 2 * fields, span)
    back = lax.all_to_all(back, "lat", 0, 0, tiled=True)
    return from_pieces(back, levels, width).reshape(slots, 2, fields, levels, width)


def tendency_kernel(
    state_ref,
    cx_ref,
    cy_ref,
    west_ref,
    east_ref,
    high_ref,
    low_ref,
    turn_ref,
    place_ref,
    block_ref,
    cutoff_ref,
    tend_ref,
    mine_ref,
    other_ref,
):
    fields, slots, rows, levels, width = state_ref.shape

    def one_slot(s, carry):
        west, east = west_ref[s], east_ref[s]
        for f in range(fields):
            above = None
            now = state_ref[f, s, 0]
            for r in range(rows):
                column = f * rows + r
                right = jnp.concatenate([now[:, 1:], east[:, column : column + 1]], axis=1)
                flux = cx_ref[s, r] * (now + right) * 0.5
                wind = west[:, fields * rows + r : fields * rows + r + 1]
                first = wind * (west[:, column : column + 1] + now[:, 0:1]) * 0.5
                change = flux - jnp.concatenate([first, flux[:, :-1]], axis=1)
                if above is not None:
                    change = change - above
                if r + 1 < rows:
                    later = state_ref[f, s, r + 1]
                    above = cy_ref[s, r] * (now + later) * 0.5
                    change = change + above
                    now = later
                tend_ref[f, s, r] = -change
        return carry

    lax.fori_loop(0, slots, one_slot, 0)
    turn = turn_ref[place_ref[0]]
    first, second, _ = pick_slots(block_ref, cutoff_ref, rows)
    mine, other = mine_first((first, second), place_ref[1])
    for slot, out_ref in ((other, other_ref), (mine, mine_ref)):
        spec = split_dot(
            tend_ref[:, slot].reshape(fields * rows * levels, width), high_ref[...], low_ref[...]
        )
        out_ref[...] = turned(spec, turn, 1.0)


def vmem(count):
    return [pl.BlockSpec(memory_space=pltpu.VMEM)] * count


def smem(count):
    return [pl.BlockSpec(memory_space=pltpu.SMEM)] * count


def local_tendency(state, courant_x, courant_y, west, east, forward, turn, place, block, cutoff):
    fields, slots, rows, levels, width = state.shape
    count = fields * rows * levels
    spec = jax.ShapeDtypeStruct((count, 2 * KCUT), F32)
    return pl.pallas_call(
        tendency_kernel,
        in_specs=vmem(8) + smem(3),
        out_specs=vmem(3),
        out_shape=[jax.ShapeDtypeStruct(state.shape, F32), spec, spec],
        compiler_params=pltpu.CompilerParams(vmem_limit_bytes=VMEM_LIMIT),
        cost_estimate=pl.CostEstimate(
            flops=6 * count * 2 * KCUT * width * 2, bytes_accessed=9 * 10**6, transcendentals=0
        ),
        name="tendency",
    )(state, courant_x, courant_y, west, east, *forward, turn, place, block, cutoff)


def main_kernel(
    state_ref,
    tend_ref,
    mine_ref,
    away_ref,
    high_ref,
    low_ref,
    turn_ref,
    place_ref,
    block_ref,
    cutoff_ref,
    out_ref,
):
    fields, slots, rows, levels, width = state_ref.shape
    turn = turn_ref[place_ref[0]]
    first, second, rest = pick_slots(block_ref, cutoff_ref, rows)
    mine, other = mine_first((first, second), place_ref[1])
    out_ref[:, rest] = state_ref[:, rest] + tend_ref[:, rest]
    for slot, spec_ref in ((mine, mine_ref), (other, away_ref)):
        spec = turned(spec_ref[...], turn, -1.0).reshape(fields, rows, levels, 2 * KCUT)
        cuts = [cutoff_ref[block_ref[slot] * rows + r] for r in range(rows)]
        spec = jnp.concatenate(
            [spec[:, r : r + 1] * row_weights(cuts[r]) for r in range(rows)], axis=1
        )
        smooth = split_dot(
            spec.reshape(fields * rows * levels, 2 * KCUT), high_ref[...], low_ref[...]
        ).reshape(fields, rows, levels, width)
        for r in range(rows):
            out_ref[:, slot, r] = state_ref[:, slot, r] + jnp.where(
                cuts[r] > 0, smooth[:, r], tend_ref[:, slot, r]
            )


def main_part(state, tend, mine, away, inverse, turn, place, block, cutoff):
    width = state.shape[-1]
    return pl.pallas_call(
        main_kernel,
        in_specs=vmem(7) + smem(3),
        out_specs=vmem(1)[0],
        out_shape=jax.ShapeDtypeStruct(state.shape, F32),
        compiler_params=pltpu.CompilerParams(vmem_limit_bytes=VMEM_LIMIT),
        cost_estimate=pl.CostEstimate(
            flops=12 * mine.shape[0] * 2 * KCUT * width, bytes_accessed=10**7, transcendentals=0
        ),
        name="main",
    )(state, tend, mine, away, *inverse, turn, place, block, cutoff)


def rim_kernel(
    packed, got_ref, high_ref, low_ref, turn_ref, place_ref, block_ref, cutoff_ref, *out_refs
):
    faces_ref, mine_ref, other_ref = out_refs
    slots, _, fields, levels, width = faces_ref.shape
    tiles = -(-width // LANES)
    if packed:
        for j in range(slots):
            for side in range(2):
                for f in range(fields):
                    for t in range(tiles):
                        row = 64 * j + 32 * side + f * tiles + t
                        tile = got_ref[pl.ds(row, 8, stride=BACK), :]
                        stop = min((t + 1) * LANES, width)
                        faces_ref[j, side, f, :, t * LANES : stop] = tile[:, : stop - t * LANES]
    else:
        faces_ref[...] = got_ref[...]
    rows = 8
    turn = turn_ref[place_ref[0]]
    first, second, _ = pick_slots(block_ref, cutoff_ref, rows)
    mine, other = mine_first((first, second), place_ref[1])
    both = jnp.concatenate(
        [
            part
            for slot in (mine, other)
            for part in (faces_ref[slot, 0], -faces_ref[slot, 1])
        ],
        axis=0,
    ).reshape(4 * fields * levels, width)
    spec = turned(split_dot(both, high_ref[...], low_ref[...]), turn, 1.0)
    mine_ref[...] = spec[: 2 * fields * levels]
    other_ref[...] = spec[2 * fields * levels :]


def rim_spectra(got, shape, forward, turn, place, block, cutoff):
    slots, _, fields, levels, width = shape
    spec = jax.ShapeDtypeStruct((2 * fields * levels, 2 * KCUT), F32)
    return pl.pallas_call(
        functools.partial(rim_kernel, got.ndim == 2),
        in_specs=vmem(4) + smem(3),
        out_specs=vmem(3),
        out_shape=[jax.ShapeDtypeStruct(shape, F32), spec, spec],
        compiler_params=pltpu.CompilerParams(vmem_limit_bytes=VMEM_LIMIT),
        cost_estimate=pl.CostEstimate(
            flops=24 * fields * levels * 2 * KCUT * width,
            bytes_accessed=3 * 10**6,
            transcendentals=0,
        ),
        name="rim_spectra",
    )(got, *forward, turn, place, block, cutoff)


def final_kernel(
    main_ref,
    faces_ref,
    mine_ref,
    away_ref,
    high_ref,
    low_ref,
    turn_ref,
    place_ref,
    block_ref,
    cutoff_ref,
    out_ref,
):
    fields, slots, _, levels, width = main_ref.shape
    rows = 8
    side = pl.program_id(0)
    row = side * (rows - 1)
    turn = turn_ref[place_ref[0]]
    first, second, rest = pick_slots(block_ref, cutoff_ref, rows)
    mine, other = mine_first((first, second), place_ref[1])
    count = fields * levels
    part = pl.ds(pl.multiple_of(side * count, 8), count)
    sign = jnp.where(side == 0, 1.0, -1.0).astype(F32)
    out_ref[:, rest, 0] = main_ref[:, rest, 0] + faces_ref[rest, side] * sign
    cuts = [cutoff_ref[block_ref[slot] * rows + row] for slot in (mine, other)]
    spec = jnp.concatenate(
        [
            turned(ref[part, :], turn, -1.0) * row_weights(cut)
            for ref, cut in ((mine_ref, cuts[0]), (away_ref, cuts[1]))
        ],
        axis=0,
    )
    smooth = split_dot(spec, high_ref[...], low_ref[...]).reshape(2, fields, levels, width)
    for i, slot in enumerate((mine, other)):
        out_ref[:, slot, 0] = main_ref[:, slot, 0] + jnp.where(
            cuts[i] > 0, smooth[i], faces_ref[slot, side] * sign
        )


def final_part(main, faces, mine, away, inverse, turn, place, block, cutoff):
    fields, slots, rows, levels, width = main.shape
    block_spec = pl.BlockSpec(
        (fields, slots, 1, levels, width), lambda i: (0, 0, i * (rows - 1), 0, 0)
    )
    return pl.pallas_call(
        final_kernel,
        grid=(2,),
        in_specs=[block_spec] + vmem(6) + smem(3),
        out_specs=block_spec,
        out_shape=jax.ShapeDtypeStruct(main.shape, F32),
        input_output_aliases={0: 0},
        compiler_params=pltpu.CompilerParams(vmem_limit_bytes=VMEM_LIMIT),
        cost_estimate=pl.CostEstimate(
            flops=12 * mine.shape[0] * 2 * KCUT * width,
            bytes_accessed=4 * 10**6,
            transcendentals=0,
        ),
        name="final",
    )(main, faces, mine, away, *inverse, turn, place, block, cutoff)


def swap(array, bit):
    size = lax.axis_size("lon")
    return lax.ppermute(array, "lon", [(i, i ^ bit) for i in range(size)])


def lon_sum(mine, other):
    total = mine + swap(other, 1)
    bit = 2
    while bit < lax.axis_size("lon"):
        total = total + swap(total, bit)
        bit *= 2
    return total, swap(total, 1)


def shards(state, courant_x, courant_y, block_of_slot, face_source, cutoff):
    fields, slots, rows, levels, width = state.shape
    lat, lon = lax.axis_size("lat"), lax.axis_size("lon")
    lon_index = lax.axis_index("lon")
    place = jnp.stack([lon_index, lon_index % 2]).astype(jnp.int32)
    forward, inverse = basis_tables(width)
    turn = turn_table(lon, width)
    tables = (turn, place, block_of_slot, cutoff)

    packed = lat == levels == 8 and -(-width // LANES) * fields == 30
    if packed:
        sent = pack(state, courant_y, face_source).reshape(lat, PIECE, LANES)
        got = lax.all_to_all(sent, "lat", 0, 0, tiled=True)

    west, east = edges(state, courant_x)
    west = lax.ppermute(west, "lon", [(i, (i + 1) % lon) for i in range(lon)])
    east = lax.ppermute(east, "lon", [((i + 1) % lon, i) for i in range(lon)])
    tend, mine, other = local_tendency(
        state, courant_x, courant_y, west, east, forward, *tables
    )
    total, away = lon_sum(mine, other)
    main = main_part(state, tend, total, away, inverse, *tables)

    if packed:
        back = faces_of_pieces(got, slots).reshape(lat, BACK, LANES)
        back = lax.all_to_all(back, "lat", 0, 0, tiled=True).reshape(lat * BACK, LANES)
    else:
        back = exchange_faces(state, courant_y, face_source)
    shape = (slots, 2, fields, levels, width)
    faces, rim_mine, rim_other = rim_spectra(back, shape, forward, *tables)
    rim_total, rim_away = lon_sum(rim_mine, rim_other)
    return final_part(main, faces, rim_total, rim_away, inverse, *tables)


def solution(mesh):
    placed = (
        P(None, "lat", None, None, "lon"),
        P("lat", None, None, "lon"),
        P("lat", None, None, "lon"),
        P("lat"),
        P("lat", None),
        P(),
    )
    return jax.shard_map(
        shards,
        mesh=mesh,
        in_specs=placed,
        out_specs=P(None, "lat", None, None, "lon"),
        check_vma=False,
    )
```

```python
import functools
import math

import jax
import jax.numpy as jnp
import numpy as np
from jax import lax
from jax.experimental import pallas as pl
from jax.experimental.pallas import tpu as pltpu
from jax.sharding import PartitionSpec as P

NLON = 2880
KCUT = 256
LANES = 128
VMEM_LIMIT = 50 * 1024 * 1024
BF16 = jnp.bfloat16
F32 = jnp.float32


def phases(columns):
    wavenumber = np.arange(KCUT, dtype=np.int64)
    return (columns[:, None] * wavenumber[None, :] % NLON).astype(np.float64) * (
        2.0 * math.pi / NLON
    )


def basis_tables(width):
    phase = phases(np.arange(width, dtype=np.int64))
    table = np.concatenate([np.cos(phase), np.sin(phase)], axis=1).astype(np.float32)
    high = table.astype(jnp.bfloat16)
    low = (table - high.astype(np.float32)).astype(jnp.bfloat16)
    forward = (jnp.asarray(high), jnp.asarray(low))
    inverse = (
        jnp.asarray(np.ascontiguousarray(high.T)),
        jnp.asarray(np.ascontiguousarray(low.T)),
    )
    return forward, inverse


def turn_table(lon, width):
    phase = phases(np.arange(lon, dtype=np.int64) * width)
    table = np.concatenate([np.cos(phase), np.sin(phase)], axis=1).astype(np.float32)
    return jnp.asarray(table[:, None, :])


def split_dot(rows, high, low):
    rows_high = rows.astype(BF16)
    rows_low = (rows - rows_high.astype(F32)).astype(BF16)
    dot = functools.partial(jnp.dot, preferred_element_type=F32)
    return dot(rows_high, high) + (dot(rows_low, high) + dot(rows_high, low))


def turned(spec, turn, sign):
    real, imag = spec[:, :KCUT], spec[:, KCUT:]
    cos, sin = turn[:, :KCUT], turn[:, KCUT:] * sign
    return jnp.concatenate([real * cos - imag * sin, imag * cos + real * sin], axis=1)


def row_weights(cut):
    column = lax.broadcasted_iota(jnp.int32, (1, 2 * KCUT), 1)
    wavenumber = jnp.where(column >= KCUT, column - KCUT, column)
    scale = jnp.where(wavenumber == 0, 1.0 / NLON, 2.0 / NLON).astype(F32)
    return jnp.where(wavenumber < cut, scale, 0.0)


def pick_slots(block_ref, cutoff_ref, rows):
    polar1 = cutoff_ref[block_ref[1] * rows] > 0
    polar2 = cutoff_ref[block_ref[2] * rows] > 0
    rest = jnp.where(polar2, jnp.where(polar1, 0, 1), 2)
    return jnp.where(rest == 0, 1, 0), jnp.where(rest == 2, 1, 2), rest


def mine_first(pair, core):
    a, b = pair
    return jnp.where(core == 0, a, b), jnp.where(core == 0, b, a)


def vmem(count):
    return [pl.BlockSpec(memory_space=pltpu.VMEM)] * count


def smem(count):
    return [pl.BlockSpec(memory_space=pltpu.SMEM)] * count


def edge_kernel(lane_last, head_ref, tail_ref, wind_ref, west_ref, east_ref):
    fields, slots, rows = head_ref.shape[:3]
    lane = lax.broadcasted_iota(jnp.int32, (8, LANES), 1)
    for s in range(slots):
        west = jnp.zeros((8, LANES), F32)
        east = jnp.zeros((8, LANES), F32)
        for r in range(rows):
            for f in range(fields):
                here = lane == f * rows + r
                west = jnp.where(here, tail_ref[f, s, r, :, lane_last : lane_last + 1], west)
                east = jnp.where(here, head_ref[f, s, r, :, 0:1], east)
            here = lane == fields * rows + r
            west = jnp.where(here, wind_ref[s, r, :, lane_last : lane_last + 1], west)
        west_ref[s] = west
        east_ref[s] = east


def edges(state, courant_x):
    fields, slots, rows, levels, width = state.shape
    last = (width - 1) // LANES
    out = jax.ShapeDtypeStruct((slots, levels, LANES), F32)
    return pl.pallas_call(
        functools.partial(edge_kernel, (width - 1) % LANES),
        grid=(1,),
        in_specs=[
            pl.BlockSpec((fields, slots, rows, levels, LANES), lambda i: (0, 0, 0, 0, 0)),
            pl.BlockSpec((fields, slots, rows, levels, LANES), lambda i: (0, 0, 0, 0, last)),
            pl.BlockSpec((slots, rows, levels, LANES), lambda i: (0, 0, 0, last)),
        ],
        out_specs=[pl.BlockSpec((slots, levels, LANES), lambda i: (0, 0, 0))] * 2,
        out_shape=[out, out],
        cost_estimate=pl.CostEstimate(flops=10**5, bytes_accessed=1200000, transcendentals=0),
        name="edges",
    )(state, state, courant_x)


PIECE = 200


def tile_of(slab, t, width):
    part = slab[:, t * LANES : min((t + 1) * LANES, width)]
    if part.shape[1] < LANES:
        part = jnp.concatenate([part, jnp.zeros((8, LANES - part.shape[1]), F32)], axis=1)
    return part


def pack_kernel(width, first_ref, last_ref, wind_ref, block_ref, out_ref):
    fields, slots = first_ref.shape[:2]
    tiles = -(-width // LANES)

    def put(row, tile):
        out_ref[pl.ds(row, 8, stride=PIECE), :] = tile

    for j in range(slots):
        half = wind_ref[j, 0] * 0.5
        for t in range(tiles):
            row = {0: 192 + 2 * j, 1: 193 + 2 * j, 2: 64 * j + 62, 3: 64 * j + 63}.get(
                t, 64 * j + 26 + t
            )
            put(row, tile_of(half, t, width))
        for f in range(fields):
            north = last_ref[f, j, 0] * half
            south = first_ref[f, j, 0]
            for t in range(tiles):
                put(64 * j + f * tiles + t, tile_of(north, t, width))
                put(64 * j + 32 + f * tiles + t, tile_of(south, t, width))
    lane = lax.broadcasted_iota(jnp.int32, (8, LANES), 1)
    table = jnp.zeros((8, LANES), F32)
    for j in range(slots):
        table = jnp.where(lane == j, block_ref[j].astype(F32), table)
    put(198, table)
    put(199, table)


def pack(state, courant_y, block):
    fields, slots, rows, levels, width = state.shape
    return pl.pallas_call(
        functools.partial(pack_kernel, width),
        grid=(1,),
        in_specs=[
            pl.BlockSpec((fields, slots, 1, levels, width), lambda i: (0, 0, 0, 0, 0)),
            pl.BlockSpec((fields, slots, 1, levels, width), lambda i: (0, 0, rows - 1, 0, 0)),
            pl.BlockSpec((slots, 1, levels, width), lambda i: (0, rows - 1, 0, 0)),
            pl.BlockSpec(memory_space=pltpu.SMEM),
        ],
        out_specs=pl.BlockSpec((levels * PIECE, LANES), lambda i: (0, 0)),
        out_shape=jax.ShapeDtypeStruct((levels * PIECE, LANES), F32),
        cost_estimate=pl.CostEstimate(flops=10**5, bytes_accessed=1700000, transcendentals=0),
        name="pack",
    )(state, state, courant_y, block)


def face_kernel(got_ref, cutoff_ref, pair_ref, rest_ref, face_ref, table_ref, slot_ref, sem):
    parts = got_ref.shape[0]
    slots = face_ref.shape[0] // parts
    count = parts * slots
    copy = pltpu.make_async_copy(got_ref.at[:, 192:200, :], table_ref, sem)
    copy.start()
    copy.wait()
    blocks = [table_ref[s // slots, 6, s % slots].astype(jnp.int32) for s in range(count)]
    slot_ref[0] = -1
    slot_ref[count + 1] = -1
    for s in range(count):
        slot_ref[blocks[s] + 1] = s
    for s in range(count):
        src, j = divmod(s, slots)
        south = slot_ref[blocks[s] + 2]
        safe = jnp.maximum(south, 0)
        from_src = lax.div(safe, slots)
        from_slot = safe - from_src * slots
        half = jnp.concatenate(
            [
                got_ref[src, 192 + 2 * j : 194 + 2 * j, :],
                got_ref[src, 64 * j + 62 : 64 * j + 64, :],
                got_ref[src, 64 * j + 30 : 64 * j + 32, :],
            ],
            axis=0,
        )
        half = jnp.concatenate([half] * 5 + [half[:2]], axis=0)
        other = got_ref[from_src, pl.ds(pl.multiple_of(64 * from_slot + 32, 32), 32), :]
        face = got_ref[src, 64 * j : 64 * j + 32, :] + half * other
        face_ref[s] = jnp.where(south >= 0, face, 0.0)
    for d in range(parts):
        first, second, rest = pick_slots(blocks[slots * d : slots * d + slots], cutoff_ref, 8)
        for slot, out in (
            (first, pair_ref.at[d, 0]),
            (second, pair_ref.at[d, 1]),
            (rest, rest_ref.at[d]),
        ):
            block = jnp.where(
                slot == 0,
                blocks[slots * d],
                jnp.where(slot == 1, blocks[slots * d + 1], blocks[slots * d + 2]),
            )
            north = slot_ref[block]
            out[0] = jnp.where(north >= 0, face_ref[jnp.maximum(north, 0)], 0.0)
            out[1] = face_ref[slots * d + slot]


def faces_of_pieces(got, slots, cutoff):
    parts = got.shape[0]
    return pl.pallas_call(
        face_kernel,
        in_specs=vmem(1) + smem(1),
        out_specs=vmem(2),
        out_shape=[
            jax.ShapeDtypeStruct((parts, 2, 2, 32, LANES), F32),
            jax.ShapeDtypeStruct((parts, 2, 32, LANES), F32),
        ],
        scratch_shapes=[
            pltpu.VMEM((parts * slots, 32, LANES), F32),
            pltpu.SMEM((parts, 8, LANES), F32),
            pltpu.SMEM((parts * slots + 2,), jnp.int32),
            pltpu.SemaphoreType.DMA(()),
        ],
        cost_estimate=pl.CostEstimate(flops=10**5, bytes_accessed=1600000, transcendentals=0),
        name="faces",
    )(got, cutoff)


def to_pieces(units, parts):
    count, levels, width = units.shape
    groups = math.gcd(parts, levels)
    chunks = parts // groups
    span = -(-width // chunks)
    units = jnp.pad(units, ((0, 0), (0, 0), (0, span * chunks - width)))
    units = units.reshape(count, groups, levels // groups, chunks, span)
    return units.transpose(1, 3, 0, 2, 4).reshape(parts, count, levels // groups * span)


def from_pieces(pieces, levels, width):
    parts, count, _ = pieces.shape
    groups = math.gcd(parts, levels)
    chunks = parts // groups
    span = -(-width // chunks)
    pieces = pieces.reshape(groups, chunks, count, levels // groups, span)
    return pieces.transpose(2, 0, 3, 1, 4).reshape(count, levels, chunks * span)[:, :, :width]


def exchange_faces(state, courant_y, face_source):
    fields, slots, rows, levels, width = state.shape
    lat = lax.axis_size("lat")
    count = 2 * fields + 1
    first = state[:, :, 0].transpose(1, 0, 2, 3)
    last = state[:, :, rows - 1].transpose(1, 0, 2, 3)
    half = courant_y[:, rows - 1][:, None] * 0.5
    units = jnp.concatenate([first, last * half, half], axis=1)
    sent = to_pieces(units.reshape(slots * count, levels, width), lat)
    span = sent.shape[2]
    table = jnp.pad(
        face_source.astype(F32).reshape(1, slots * 2), ((0, 0), (0, span - slots * 2))
    )
    sent = jnp.concatenate([sent, jnp.broadcast_to(table[None], (lat, 1, span))], axis=1)
    got = lax.all_to_all(sent, "lat", 0, 0, tiled=True)
    indices = got[:, slots * count, : slots * 2].reshape(lat * slots, 2).astype(jnp.int32)
    data = got[:, : slots * count].reshape(lat * slots, count, span)
    north, south = indices[:, 0], indices[:, 1]
    face = data[:, fields : 2 * fields] + data[:, 2 * fields :] * data[
        jnp.maximum(south, 0), :fields
    ]
    face = jnp.where((south >= 0)[:, None, None], face, 0.0)
    face_north = jnp.where((north >= 0)[:, None, None], face[jnp.maximum(north, 0)], 0.0)
    back = jnp.concatenate([face_north, face], axis=1).reshape(lat, slots * 2 * fields, span)
    back = lax.all_to_all(back, "lat", 0, 0, tiled=True)
    return from_pieces(back, levels, width).reshape(slots, 2, fields, levels, width)


def tendency_kernel(
    state_ref,
    cx_ref,
    cy_ref,
    west_ref,
    east_ref,
    high_ref,
    low_ref,
    turn_ref,
    place_ref,
    block_ref,
    cutoff_ref,
    tend_ref,
    mine_ref,
    other_ref,
):
    fields, slots, rows, levels, width = state_ref.shape

    tiles = -(-width // LANES)
    lane = lax.broadcasted_iota(jnp.int32, (levels, LANES), 1)
    head, tail, last = lane == 0, lane == LANES - 1, lane == (width - 1) % LANES

    def load(ref, *index):
        out = []
        for t in range(tiles):
            part = ref[index + (slice(None), slice(t * LANES, min((t + 1) * LANES, width)))]
            if part.shape[1] < LANES:
                pad = jnp.zeros((levels, LANES - part.shape[1]), F32)
                part = jnp.concatenate([part, pad], axis=1)
            out.append(part)
        return out

    def one_slot(s, carry):
        west, east = west_ref[s], east_ref[s]
        for f in range(fields):
            above = None
            now = load(state_ref, f, s, 0)
            for r in range(rows):
                column = f * rows + r
                left = [pltpu.roll(x, LANES - 1, 1) for x in now]
                left = [
                    jnp.where(tail, left[t + 1], left[t])
                    if t + 1 < tiles
                    else jnp.where(last, east[:, column : column + 1], left[t])
                    for t in range(tiles)
                ]
                half = [x * 0.5 for x in load(cx_ref, s, r)]
                flux = [h * (x + y) for h, x, y in zip(half, now, left)]
                wind = west[:, fields * rows + r : fields * rows + r + 1] * 0.5
                first = wind * (west[:, column : column + 1] + now[0])
                right = [pltpu.roll(x, 1, 1) for x in flux]
                right = [jnp.where(head, y, x) for x, y in zip(right, [first] + right[:-1])]
                change = [x - y for x, y in zip(right, flux)]
                if above is not None:
                    change = [x + y for x, y in zip(change, above)]
                if r + 1 < rows:
                    later = load(state_ref, f, s, r + 1)
                    half = load(cy_ref, s, r)
                    above = [h * 0.5 * (x + y) for h, x, y in zip(half, now, later)]
                    change = [x - y for x, y in zip(change, above)]
                    now = later
                for t in range(tiles):
                    stop = min((t + 1) * LANES, width)
                    tend_ref[f, s, r, :, t * LANES : stop] = change[t][:, : stop - t * LANES]
        return carry

    lax.fori_loop(0, slots, one_slot, 0)
    turn = turn_ref[place_ref[0]]
    first, second, _ = pick_slots(block_ref, cutoff_ref, rows)
    mine, other = mine_first((first, second), place_ref[1])
    for slot, out_ref in ((other, other_ref), (mine, mine_ref)):
        spec = split_dot(
            tend_ref[:, slot].reshape(fields * rows * levels, width), high_ref[...], low_ref[...]
        )
        out_ref[...] = turned(spec, turn, 1.0)


def local_tendency(state, courant_x, courant_y, west, east, forward, turn, place, block, cutoff):
    fields, slots, rows, levels, width = state.shape
    count = fields * rows * levels
    spec = jax.ShapeDtypeStruct((count, 2 * KCUT), F32)
    return pl.pallas_call(
        tendency_kernel,
        in_specs=vmem(8) + smem(3),
        out_specs=vmem(3),
        out_shape=[jax.ShapeDtypeStruct(state.shape, F32), spec, spec],
        compiler_params=pltpu.CompilerParams(vmem_limit_bytes=VMEM_LIMIT),
        cost_estimate=pl.CostEstimate(
            flops=6 * count * 2 * KCUT * width * 2, bytes_accessed=9 * 10**6, transcendentals=0
        ),
        name="tendency",
    )(state, courant_x, courant_y, west, east, *forward, turn, place, block, cutoff)


def main_kernel(
    state_ref,
    tend_ref,
    mine_ref,
    away_ref,
    high_ref,
    low_ref,
    turn_ref,
    place_ref,
    block_ref,
    cutoff_ref,
    out_ref,
    token_ref,
):
    fields, slots, rows, levels, width = state_ref.shape
    token_ref[...] = jnp.zeros_like(token_ref)
    turn = turn_ref[place_ref[0]]
    first, second, rest = pick_slots(block_ref, cutoff_ref, rows)
    mine, other = mine_first((first, second), place_ref[1])
    out_ref[:, rest] = state_ref[:, rest] + tend_ref[:, rest]
    for slot, spec_ref in ((mine, mine_ref), (other, away_ref)):
        spec = turned(spec_ref[...], turn, -1.0).reshape(fields, rows, levels, 2 * KCUT)
        cuts = [cutoff_ref[block_ref[slot] * rows + r] for r in range(rows)]
        spec = jnp.concatenate(
            [spec[:, r : r + 1] * row_weights(cuts[r]) for r in range(rows)], axis=1
        )
        smooth = split_dot(
            spec.reshape(fields * rows * levels, 2 * KCUT), high_ref[...], low_ref[...]
        ).reshape(fields, rows, levels, width)
        for r in range(rows):
            out_ref[:, slot, r] = state_ref[:, slot, r] + jnp.where(
                cuts[r] > 0, smooth[:, r], tend_ref[:, slot, r]
            )


def main_part(state, tend, mine, away, inverse, turn, place, block, cutoff):
    width = state.shape[-1]
    return pl.pallas_call(
        main_kernel,
        in_specs=vmem(7) + smem(3),
        out_specs=vmem(2),
        out_shape=[
            jax.ShapeDtypeStruct(state.shape, F32),
            jax.ShapeDtypeStruct((8, LANES), F32),
        ],
        compiler_params=pltpu.CompilerParams(vmem_limit_bytes=VMEM_LIMIT),
        cost_estimate=pl.CostEstimate(
            flops=12 * mine.shape[0] * 2 * KCUT * width, bytes_accessed=10**7, transcendentals=0
        ),
        name="main",
    )(state, tend, mine, away, *inverse, turn, place, block, cutoff)


def unpack(ref, base, stride, put, fields, width):
    tiles = -(-width // LANES)
    for f in range(fields):
        for t in range(tiles):
            tile = ref[pl.ds(base + f * tiles + t, 8, stride=stride), :]
            stop = min((t + 1) * LANES, width)
            put(f, t * LANES, stop, tile[:, : stop - t * LANES])


def rim_kernel(
    packed,
    token_ref,
    got_ref,
    high_ref,
    low_ref,
    turn_ref,
    place_ref,
    faces_ref,
    mine_ref,
    other_ref,
):
    _, _, fields, levels, width = faces_ref.shape
    if packed:
        for i in range(2):
            for side in range(2):

                def put(f, start, stop, tile, i=i, side=side):
                    faces_ref[i, side, f, :, start:stop] = tile

                unpack(got_ref, 64 * i + 32 * side, 128, put, fields, width)
    else:
        faces_ref[...] = got_ref[...]
    turn = turn_ref[place_ref[0]]
    core = place_ref[1]
    both = jnp.concatenate(
        [part for i in (core, 1 - core) for part in (faces_ref[i, 0], -faces_ref[i, 1])], axis=0
    ).reshape(4 * fields * levels, width)
    spec = turned(split_dot(both, high_ref[...], low_ref[...]), turn, 1.0)
    mine_ref[...] = spec[: 2 * fields * levels]
    other_ref[...] = spec[2 * fields * levels :]


def rim_spectra(token, got, shape, forward, turn, place):
    _, _, fields, levels, width = shape
    spec = jax.ShapeDtypeStruct((2 * fields * levels, 2 * KCUT), F32)
    return pl.pallas_call(
        functools.partial(rim_kernel, got.ndim == 2),
        in_specs=vmem(5) + smem(1),
        out_specs=vmem(3),
        out_shape=[jax.ShapeDtypeStruct(shape, F32), spec, spec],
        compiler_params=pltpu.CompilerParams(vmem_limit_bytes=VMEM_LIMIT),
        cost_estimate=pl.CostEstimate(
            flops=24 * fields * levels * 2 * KCUT * width,
            bytes_accessed=3 * 10**6,
            transcendentals=0,
        ),
        name="rim_spectra",
    )(token, got, *forward, turn, place)


def final_kernel(
    packed,
    main_ref,
    pair_ref,
    back_ref,
    mine_ref,
    away_ref,
    high_ref,
    low_ref,
    turn_ref,
    place_ref,
    block_ref,
    cutoff_ref,
    out_ref,
):
    fields, slots, _, levels, width = main_ref.shape
    rows = 8
    side = pl.program_id(0)
    row = side * (rows - 1)
    turn = turn_ref[place_ref[0]]
    core = place_ref[1]
    first, second, rest = pick_slots(block_ref, cutoff_ref, rows)
    mine, other = mine_first((first, second), core)
    count = fields * levels
    part = pl.ds(pl.multiple_of(side * count, 8), count)
    sign = jnp.where(side == 0, 1.0, -1.0).astype(F32)
    if packed:

        def put(f, start, stop, tile):
            old = main_ref[f, rest, 0, :, start:stop]
            out_ref[f, rest, 0, :, start:stop] = old + tile * sign

        unpack(back_ref, 32 * side, 64, put, fields, width)
    else:
        out_ref[:, rest, 0] = main_ref[:, rest, 0] + back_ref[side] * sign
    cuts = [cutoff_ref[block_ref[slot] * rows + row] for slot in (mine, other)]
    spec = jnp.concatenate(
        [
            turned(ref[part, :], turn, -1.0) * row_weights(cut)
            for ref, cut in ((mine_ref, cuts[0]), (away_ref, cuts[1]))
        ],
        axis=0,
    )
    smooth = split_dot(spec, high_ref[...], low_ref[...]).reshape(2, fields, levels, width)
    for i, (slot, order) in enumerate(((mine, core), (other, 1 - core))):
        out_ref[:, slot, 0] = main_ref[:, slot, 0] + jnp.where(
            cuts[i] > 0, smooth[i], pair_ref[order, side] * sign
        )


def final_part(main, pair, back, mine, away, inverse, turn, place, block, cutoff):
    fields, slots, rows, levels, width = main.shape
    block_spec = pl.BlockSpec(
        (fields, slots, 1, levels, width), lambda i: (0, 0, i * (rows - 1), 0, 0)
    )
    return pl.pallas_call(
        functools.partial(final_kernel, back.ndim == 2),
        grid=(2,),
        in_specs=[block_spec] + vmem(7) + smem(3),
        out_specs=block_spec,
        out_shape=jax.ShapeDtypeStruct(main.shape, F32),
        input_output_aliases={0: 0},
        compiler_params=pltpu.CompilerParams(vmem_limit_bytes=VMEM_LIMIT),
        cost_estimate=pl.CostEstimate(
            flops=12 * mine.shape[0] * 2 * KCUT * width,
            bytes_accessed=4 * 10**6,
            transcendentals=0,
        ),
        name="final",
    )(main, pair, back, mine, away, *inverse, turn, place, block, cutoff)


def swap(array, bit):
    size = lax.axis_size("lon")
    return lax.ppermute(array, "lon", [(i, i ^ bit) for i in range(size)])


def lon_sum(mine, other):
    total = mine + swap(other, 1)
    bit = 2
    while bit < lax.axis_size("lon"):
        total = total + swap(total, bit)
        bit *= 2
    return total, swap(total, 1)


def shards(state, courant_x, courant_y, block_of_slot, face_source, cutoff):
    fields, slots, rows, levels, width = state.shape
    lat, lon = lax.axis_size("lat"), lax.axis_size("lon")
    lon_index = lax.axis_index("lon")
    place = jnp.stack([lon_index, lon_index % 2]).astype(jnp.int32)
    forward, inverse = basis_tables(width)
    turn = turn_table(lon, width)
    tables = (turn, place, block_of_slot, cutoff)

    packed = lat == levels == 8 and -(-width // LANES) * fields == 30
    if packed:
        sent = pack(state, courant_y, block_of_slot).reshape(lat, PIECE, LANES)
        got = lax.all_to_all(sent, "lat", 0, 0, tiled=True)

    west, east = edges(state, courant_x)
    west = lax.ppermute(west, "lon", [(i, (i + 1) % lon) for i in range(lon)])
    east = lax.ppermute(east, "lon", [((i + 1) % lon, i) for i in range(lon)])
    tend, mine, other = local_tendency(
        state, courant_x, courant_y, west, east, forward, *tables
    )
    total, away = lon_sum(mine, other)
    main, token = main_part(state, tend, total, away, inverse, *tables)

    if packed:
        pair, rest = faces_of_pieces(got, slots, cutoff)
        pair, rest = (
            lax.all_to_all(x.reshape(lat, -1, LANES), "lat", 0, 0, tiled=True).reshape(-1, LANES)
            for x in (pair, rest)
        )
    else:
        faces = exchange_faces(state, courant_y, face_source)
        picked = pick_slots(block_of_slot, cutoff, rows)
        pair, rest = faces[jnp.stack(picked[:2])], faces[picked[2]]
    shape = (2, 2, fields, levels, width)
    pair, rim_mine, rim_other = rim_spectra(token, pair, shape, forward, turn, place)
    rim_total, rim_away = lon_sum(rim_mine, rim_other)
    return final_part(main, pair, rest, rim_total, rim_away, inverse, *tables)


def solution(mesh):
    placed = (
        P(None, "lat", None, None, "lon"),
        P("lat", None, None, "lon"),
        P("lat", None, None, "lon"),
        P("lat"),
        P("lat", None),
        P(),
    )
    return jax.shard_map(
        shards,
        mesh=mesh,
        in_specs=placed,
        out_specs=P(None, "lat", None, None, "lon"),
        check_vma=False,
    )
```

```python
import functools
import math

import jax
import jax.numpy as jnp
import numpy as np
from jax import lax
from jax.experimental import pallas as pl
from jax.experimental.pallas import tpu as pltpu
from jax.sharding import PartitionSpec as P

NLON = 2880
KCUT = 256
LANES = 128
VMEM_LIMIT = 50 * 1024 * 1024
BF16 = jnp.bfloat16
F32 = jnp.float32


def phases(columns):
    wavenumber = np.arange(KCUT, dtype=np.int64)
    return (columns[:, None] * wavenumber[None, :] % NLON).astype(np.float64) * (
        2.0 * math.pi / NLON
    )


def basis_tables(width):
    phase = phases(np.arange(width, dtype=np.int64))
    table = np.concatenate([np.cos(phase), np.sin(phase)], axis=1).astype(np.float32)
    high = table.astype(jnp.bfloat16)
    low = (table - high.astype(np.float32)).astype(jnp.bfloat16)
    forward = (jnp.asarray(high), jnp.asarray(low))
    inverse = (
        jnp.asarray(np.ascontiguousarray(high.T)),
        jnp.asarray(np.ascontiguousarray(low.T)),
    )
    return forward, inverse


def turn_table(lon, width):
    phase = phases(np.arange(lon, dtype=np.int64) * width)
    table = np.concatenate([np.cos(phase), np.sin(phase)], axis=1).astype(np.float32)
    return jnp.asarray(table[:, None, :])


def split_dot(rows, high, low):
    rows_high = rows.astype(BF16)
    rows_low = (rows - rows_high.astype(F32)).astype(BF16)
    dot = functools.partial(jnp.dot, preferred_element_type=F32)
    return dot(rows_high, high) + (dot(rows_low, high) + dot(rows_high, low))


def turned(spec, turn, sign):
    real, imag = spec[:, :KCUT], spec[:, KCUT:]
    cos, sin = turn[:, :KCUT], turn[:, KCUT:] * sign
    return jnp.concatenate([real * cos - imag * sin, imag * cos + real * sin], axis=1)


def row_weights(cut):
    column = lax.broadcasted_iota(jnp.int32, (1, 2 * KCUT), 1)
    wavenumber = jnp.where(column >= KCUT, column - KCUT, column)
    scale = jnp.where(wavenumber == 0, 1.0 / NLON, 2.0 / NLON).astype(F32)
    return jnp.where(wavenumber < cut, scale, 0.0)


def pick_slots(block_ref, cutoff_ref, rows):
    polar1 = cutoff_ref[block_ref[1] * rows] > 0
    polar2 = cutoff_ref[block_ref[2] * rows] > 0
    rest = jnp.where(polar2, jnp.where(polar1, 0, 1), 2)
    return jnp.where(rest == 0, 1, 0), jnp.where(rest == 2, 1, 2), rest


def mine_first(pair, core):
    a, b = pair
    return jnp.where(core == 0, a, b), jnp.where(core == 0, b, a)


def vmem(count):
    return [pl.BlockSpec(memory_space=pltpu.VMEM)] * count


def smem(count):
    return [pl.BlockSpec(memory_space=pltpu.SMEM)] * count


def edge_kernel(lane_last, head_ref, tail_ref, wind_ref, west_ref, east_ref):
    fields, slots, rows = head_ref.shape[:3]
    lane = lax.broadcasted_iota(jnp.int32, (8, LANES), 1)
    for s in range(slots):
        west = jnp.zeros((8, LANES), F32)
        east = jnp.zeros((8, LANES), F32)
        for r in range(rows):
            for f in range(fields):
                here = lane == f * rows + r
                west = jnp.where(here, tail_ref[f, s, r, :, lane_last : lane_last + 1], west)
                east = jnp.where(here, head_ref[f, s, r, :, 0:1], east)
            here = lane == fields * rows + r
            west = jnp.where(here, wind_ref[s, r, :, lane_last : lane_last + 1], west)
        west_ref[s] = west
        east_ref[s] = east


def edges(state, courant_x):
    fields, slots, rows, levels, width = state.shape
    last = (width - 1) // LANES
    out = jax.ShapeDtypeStruct((slots, levels, LANES), F32)
    return pl.pallas_call(
        functools.partial(edge_kernel, (width - 1) % LANES),
        grid=(1,),
        in_specs=[
            pl.BlockSpec((fields, slots, rows, levels, LANES), lambda i: (0, 0, 0, 0, 0)),
            pl.BlockSpec((fields, slots, rows, levels, LANES), lambda i: (0, 0, 0, 0, last)),
            pl.BlockSpec((slots, rows, levels, LANES), lambda i: (0, 0, 0, last)),
        ],
        out_specs=[pl.BlockSpec((slots, levels, LANES), lambda i: (0, 0, 0))] * 2,
        out_shape=[out, out],
        cost_estimate=pl.CostEstimate(flops=10**5, bytes_accessed=1200000, transcendentals=0),
        name="edges",
    )(state, state, courant_x)


PIECE = 200


def tile_of(slab, t, width):
    part = slab[:, t * LANES : min((t + 1) * LANES, width)]
    if part.shape[1] < LANES:
        part = jnp.concatenate([part, jnp.zeros((8, LANES - part.shape[1]), F32)], axis=1)
    return part


def pack_kernel(width, first_ref, last_ref, wind_ref, block_ref, me_ref, *refs):
    out_refs, sent_ref = refs[:-1], refs[-1]
    fields, slots = first_ref.shape[:2]
    back = (8 - me_ref[0]) & 7
    tiles = -(-width // LANES)

    def put(row, tile):
        sent_ref[pl.ds(row, 8, stride=PIECE), :] = pltpu.roll(tile, back, 0)

    for j in range(slots):
        half = wind_ref[j, 0] * 0.5
        for t in range(tiles):
            row = {0: 192 + 2 * j, 1: 193 + 2 * j, 2: 64 * j + 62, 3: 64 * j + 63}.get(
                t, 64 * j + 26 + t
            )
            put(row, tile_of(half, t, width))
        for f in range(fields):
            north = last_ref[f, j, 0] * half
            south = first_ref[f, j, 0]
            for t in range(tiles):
                put(64 * j + f * tiles + t, tile_of(north, t, width))
                put(64 * j + 32 + f * tiles + t, tile_of(south, t, width))
    lane = lax.broadcasted_iota(jnp.int32, (8, LANES), 1)
    table = jnp.zeros((8, LANES), F32)
    for j in range(slots):
        table = jnp.where(lane == j, block_ref[j].astype(F32), table)
    put(198, table)
    put(199, table)
    for k, out_ref in enumerate(out_refs):
        out_ref[...] = sent_ref[k * PIECE : (k + 1) * PIECE, :]


def pack(state, courant_y, block, me):
    fields, slots, rows, levels, width = state.shape
    return pl.pallas_call(
        functools.partial(pack_kernel, width),
        grid=(1,),
        in_specs=[
            pl.BlockSpec((fields, slots, 1, levels, width), lambda i: (0, 0, 0, 0, 0)),
            pl.BlockSpec((fields, slots, 1, levels, width), lambda i: (0, 0, rows - 1, 0, 0)),
            pl.BlockSpec((slots, 1, levels, width), lambda i: (0, rows - 1, 0, 0)),
        ]
        + smem(2),
        out_specs=[pl.BlockSpec((PIECE, LANES), lambda i: (0, 0))] * levels,
        out_shape=[jax.ShapeDtypeStruct((PIECE, LANES), F32)] * levels,
        scratch_shapes=[pltpu.VMEM((levels * PIECE, LANES), F32)],
        cost_estimate=pl.CostEstimate(flops=10**5, bytes_accessed=1700000, transcendentals=0),
        name="pack",
    )(state, state, courant_y, block, me)


def rotate(pieces):
    size = len(pieces)
    return [pieces[0]] + [
        lax.ppermute(pieces[k], "lat", [(i, (i + k) % size) for i in range(size)])
        for k in range(1, size)
    ]


def face_kernel(parts, *refs):
    piece_refs, (cutoff_ref, me_ref), refs = refs[:parts], refs[parts : parts + 2], refs[parts + 2 :]
    pair_refs, rest_refs, refs = refs[:parts], refs[parts : 2 * parts], refs[2 * parts :]
    got_ref, face_ref, table_ref, slot_ref, held_ref, sem = refs
    me = me_ref[0]
    slots = face_ref.shape[0] // parts
    count = parts * slots
    for k in range(parts):
        got_ref[(me + parts - k) & (parts - 1), 192:200] = piece_refs[k][192:200]
    copy = pltpu.make_async_copy(got_ref.at[:, 192:200, :], table_ref, sem)
    copy.start()
    for k in range(parts):
        got_ref[(me + parts - k) & (parts - 1), :192] = piece_refs[k][:192]
    copy.wait()
    blocks = [table_ref[s // slots, 6, s % slots].astype(jnp.int32) for s in range(count)]
    slot_ref[0] = -1
    slot_ref[count + 1] = -1
    for s in range(count):
        slot_ref[blocks[s] + 1] = s
        held_ref[s] = blocks[s]
    for s in range(count):
        src, j = divmod(s, slots)
        south = slot_ref[blocks[s] + 2]
        safe = jnp.maximum(south, 0)
        from_src = lax.div(safe, slots)
        from_slot = safe - from_src * slots
        half = jnp.concatenate(
            [
                got_ref[src, 192 + 2 * j : 194 + 2 * j, :],
                got_ref[src, 64 * j + 62 : 64 * j + 64, :],
                got_ref[src, 64 * j + 30 : 64 * j + 32, :],
            ],
            axis=0,
        )
        half = jnp.concatenate([half] * 5 + [half[:2]], axis=0)
        other = got_ref[from_src, pl.ds(pl.multiple_of(64 * from_slot + 32, 32), 32), :]
        face = got_ref[src, 64 * j : 64 * j + 32, :] + half * other
        face_ref[s] = jnp.where(south >= 0, face, 0.0)
    for k in range(parts):
        base = ((me + k) & (parts - 1)) * slots
        own = [held_ref[base + j] for j in range(slots)]
        first, second, rest = pick_slots(own, cutoff_ref, 8)
        for slot, out in (
            (first, pair_refs[k].at[pl.ds(0, 64)]),
            (second, pair_refs[k].at[pl.ds(64, 64)]),
            (rest, rest_refs[k]),
        ):
            north = slot_ref[held_ref[base + slot]]
            out[:32] = jnp.where(north >= 0, face_ref[jnp.maximum(north, 0)], 0.0)
            out[32:] = face_ref[base + slot]


def faces_of_pieces(pieces, slots, cutoff, me):
    parts = len(pieces)
    out = pl.pallas_call(
        functools.partial(face_kernel, parts),
        in_specs=vmem(parts) + smem(2),
        out_specs=vmem(2 * parts),
        out_shape=[jax.ShapeDtypeStruct((128, LANES), F32)] * parts
        + [jax.ShapeDtypeStruct((64, LANES), F32)] * parts,
        scratch_shapes=[
            pltpu.VMEM((parts, PIECE, LANES), F32),
            pltpu.VMEM((parts * slots, 32, LANES), F32),
            pltpu.SMEM((parts, 8, LANES), F32),
            pltpu.SMEM((parts * slots + 2,), jnp.int32),
            pltpu.SMEM((parts * slots,), jnp.int32),
            pltpu.SemaphoreType.DMA(()),
        ],
        cost_estimate=pl.CostEstimate(flops=10**5, bytes_accessed=1600000, transcendentals=0),
        name="faces",
    )(*pieces, cutoff, me)
    return out[:parts], out[parts:]


def to_pieces(units, parts):
    count, levels, width = units.shape
    groups = math.gcd(parts, levels)
    chunks = parts // groups
    span = -(-width // chunks)
    units = jnp.pad(units, ((0, 0), (0, 0), (0, span * chunks - width)))
    units = units.reshape(count, groups, levels // groups, chunks, span)
    return units.transpose(1, 3, 0, 2, 4).reshape(parts, count, levels // groups * span)


def from_pieces(pieces, levels, width):
    parts, count, _ = pieces.shape
    groups = math.gcd(parts, levels)
    chunks = parts // groups
    span = -(-width // chunks)
    pieces = pieces.reshape(groups, chunks, count, levels // groups, span)
    return pieces.transpose(2, 0, 3, 1, 4).reshape(count, levels, chunks * span)[:, :, :width]


def exchange_faces(state, courant_y, face_source):
    fields, slots, rows, levels, width = state.shape
    lat = lax.axis_size("lat")
    count = 2 * fields + 1
    first = state[:, :, 0].transpose(1, 0, 2, 3)
    last = state[:, :, rows - 1].transpose(1, 0, 2, 3)
    half = courant_y[:, rows - 1][:, None] * 0.5
    units = jnp.concatenate([first, last * half, half], axis=1)
    sent = to_pieces(units.reshape(slots * count, levels, width), lat)
    span = sent.shape[2]
    table = jnp.pad(
        face_source.astype(F32).reshape(1, slots * 2), ((0, 0), (0, span - slots * 2))
    )
    sent = jnp.concatenate([sent, jnp.broadcast_to(table[None], (lat, 1, span))], axis=1)
    got = lax.all_to_all(sent, "lat", 0, 0, tiled=True)
    indices = got[:, slots * count, : slots * 2].reshape(lat * slots, 2).astype(jnp.int32)
    data = got[:, : slots * count].reshape(lat * slots, count, span)
    north, south = indices[:, 0], indices[:, 1]
    face = data[:, fields : 2 * fields] + data[:, 2 * fields :] * data[
        jnp.maximum(south, 0), :fields
    ]
    face = jnp.where((south >= 0)[:, None, None], face, 0.0)
    face_north = jnp.where((north >= 0)[:, None, None], face[jnp.maximum(north, 0)], 0.0)
    back = jnp.concatenate([face_north, face], axis=1).reshape(lat, slots * 2 * fields, span)
    back = lax.all_to_all(back, "lat", 0, 0, tiled=True)
    return from_pieces(back, levels, width).reshape(slots, 2, fields, levels, width)


def tendency_kernel(
    state_ref,
    cx_ref,
    cy_ref,
    west_ref,
    east_ref,
    high_ref,
    low_ref,
    turn_ref,
    place_ref,
    block_ref,
    cutoff_ref,
    out_ref,
    mine_ref,
    other_ref,
    tend_ref,
    base_ref,
    sem,
):
    fields, slots, rows, levels, width = state_ref.shape

    def streamed(s):
        return pltpu.make_async_copy(base_ref.at[:, s], out_ref.at[:, s], sem.at[s])


    tiles = -(-width // LANES)
    lane = lax.broadcasted_iota(jnp.int32, (levels, LANES), 1)
    head, tail, last = lane == 0, lane == LANES - 1, lane == (width - 1) % LANES

    def load(ref, *index):
        out = []
        for t in range(tiles):
            part = ref[index + (slice(None), slice(t * LANES, min((t + 1) * LANES, width)))]
            if part.shape[1] < LANES:
                pad = jnp.zeros((levels, LANES - part.shape[1]), F32)
                part = jnp.concatenate([part, pad], axis=1)
            out.append(part)
        return out

    def one_slot(s, carry):
        west, east = west_ref[s], east_ref[s]
        for f in range(fields):
            above = None
            now = load(state_ref, f, s, 0)
            for r in range(rows):
                column = f * rows + r
                left = [pltpu.roll(x, LANES - 1, 1) for x in now]
                left = [
                    jnp.where(tail, left[t + 1], left[t])
                    if t + 1 < tiles
                    else jnp.where(last, east[:, column : column + 1], left[t])
                    for t in range(tiles)
                ]
                half = [x * 0.5 for x in load(cx_ref, s, r)]
                flux = [h * (x + y) for h, x, y in zip(half, now, left)]
                wind = west[:, fields * rows + r : fields * rows + r + 1] * 0.5
                first = wind * (west[:, column : column + 1] + now[0])
                right = [pltpu.roll(x, 1, 1) for x in flux]
                right = [jnp.where(head, y, x) for x, y in zip(right, [first] + right[:-1])]
                change = [x - y for x, y in zip(right, flux)]
                if above is not None:
                    change = [x + y for x, y in zip(change, above)]
                if r + 1 < rows:
                    later = load(state_ref, f, s, r + 1)
                    half = load(cy_ref, s, r)
                    above = [h * 0.5 * (x + y) for h, x, y in zip(half, now, later)]
                    change = [x - y for x, y in zip(change, above)]
                for t in range(tiles):
                    stop = min((t + 1) * LANES, width)
                    base = now[t] + change[t]
                    tend_ref[f, s, r, :, t * LANES : stop] = change[t][:, : stop - t * LANES]
                    base_ref[f, s, r, :, t * LANES : stop] = base[:, : stop - t * LANES]
                now = later
        streamed(s).start()
        return carry

    lax.fori_loop(0, slots, one_slot, 0)
    turn = turn_ref[place_ref[0]]
    first, second, _ = pick_slots(block_ref, cutoff_ref, rows)
    mine, other = mine_first((first, second), place_ref[1])
    for slot, spec_ref in ((other, other_ref), (mine, mine_ref)):
        spec = split_dot(
            tend_ref[:, slot].reshape(fields * rows * levels, width), high_ref[...], low_ref[...]
        )
        spec_ref[...] = turned(spec, turn, 1.0)
    for s in range(slots):
        streamed(s).wait()


def local_tendency(state, courant_x, courant_y, west, east, forward, turn, place, block, cutoff):
    fields, slots, rows, levels, width = state.shape
    count = fields * rows * levels
    spec = jax.ShapeDtypeStruct((count, 2 * KCUT), F32)
    return pl.pallas_call(
        tendency_kernel,
        in_specs=vmem(8) + smem(3),
        out_specs=[pl.BlockSpec(memory_space=pl.ANY)] + vmem(2),
        out_shape=[jax.ShapeDtypeStruct(state.shape, F32), spec, spec],
        scratch_shapes=[
            pltpu.VMEM(state.shape, F32),
            pltpu.VMEM(state.shape, F32),
            pltpu.SemaphoreType.DMA((slots,)),
        ],
        compiler_params=pltpu.CompilerParams(vmem_limit_bytes=VMEM_LIMIT),
        cost_estimate=pl.CostEstimate(
            flops=6 * count * 2 * KCUT * width * 2, bytes_accessed=9 * 10**6, transcendentals=0
        ),
        name="tendency",
    )(state, courant_x, courant_y, west, east, *forward, turn, place, block, cutoff)


def chosen_slot(i, place_ref, block_ref, cutoff_ref, rows):
    first, second, _ = pick_slots(block_ref, cutoff_ref, rows)
    return jnp.where(i == place_ref[1], first, second)


def main_kernel(
    place_ref,
    block_ref,
    cutoff_ref,
    state_ref,
    base_ref,
    mine_ref,
    away_ref,
    high_ref,
    low_ref,
    turn_ref,
    out_ref,
    token_ref,
):
    fields, _, rows, levels, width = state_ref.shape
    token_ref[...] = jnp.zeros_like(token_ref)
    i = pl.program_id(0)
    turn = turn_ref[place_ref[0]]
    slot = chosen_slot(i, place_ref, block_ref, cutoff_ref, rows)
    spec = turned(jnp.where(i == 0, mine_ref[...], away_ref[...]), turn, -1.0)
    spec = spec.reshape(fields, rows, levels, 2 * KCUT)
    cuts = [cutoff_ref[block_ref[slot] * rows + r] for r in range(rows)]
    spec = jnp.concatenate(
        [spec[:, r : r + 1] * row_weights(cuts[r]) for r in range(rows)], axis=1
    )
    smooth = split_dot(
        spec.reshape(fields * rows * levels, 2 * KCUT), high_ref[...], low_ref[...]
    ).reshape(fields, rows, levels, width)
    for r in range(rows):
        out_ref[:, 0, r] = jnp.where(
            cuts[r] > 0, state_ref[:, 0, r] + smooth[:, r], base_ref[:, 0, r]
        )


def main_part(state, base, mine, away, inverse, turn, place, block, cutoff):
    fields, slots, rows, levels, width = state.shape
    slot_block = pl.BlockSpec(
        (fields, 1, rows, levels, width),
        lambda i, *scalars: (0, chosen_slot(i, *scalars, rows), 0, 0, 0),
    )
    return pl.pallas_call(
        main_kernel,
        grid_spec=pltpu.PrefetchScalarGridSpec(
            num_scalar_prefetch=3,
            grid=(2,),
            in_specs=[slot_block, slot_block] + vmem(5),
            out_specs=[slot_block, pl.BlockSpec((8, LANES), lambda i, *scalars: (0, 0))],
        ),
        out_shape=[
            jax.ShapeDtypeStruct(state.shape, F32),
            jax.ShapeDtypeStruct((8, LANES), F32),
        ],
        input_output_aliases={4: 0},
        compiler_params=pltpu.CompilerParams(vmem_limit_bytes=VMEM_LIMIT),
        cost_estimate=pl.CostEstimate(
            flops=12 * mine.shape[0] * 2 * KCUT * width,
            bytes_accessed=6 * 10**6,
            transcendentals=0,
        ),
        name="main",
    )(place, block, cutoff, state, base, mine, away, *inverse, turn)


def unpack(ref, base, stride, put, fields, width):
    tiles = -(-width // LANES)
    for f in range(fields):
        for t in range(tiles):
            tile = ref[pl.ds(base + f * tiles + t, 8, stride=stride), :]
            stop = min((t + 1) * LANES, width)
            put(f, t * LANES, stop, tile[:, : stop - t * LANES])


def gather_pieces(piece_refs, me, out_ref):
    parts, count = len(piece_refs), piece_refs[0].shape[0]
    for k in range(parts):
        start = ((me + parts - k) & (parts - 1)) * count
        out_ref[pl.ds(pl.multiple_of(start, 8), count), :] = piece_refs[k][...]


def rim_kernel(parts, token_ref, high_ref, low_ref, turn_ref, place_ref, *refs):
    piece_refs, refs = refs[:parts], refs[parts:]
    faces_ref, mine_ref, other_ref = refs[:3]
    _, _, fields, levels, width = faces_ref.shape
    if parts > 1:
        got_ref = refs[3]
        gather_pieces(piece_refs, place_ref[2], got_ref)
        for i in range(2):
            for side in range(2):

                def put(f, start, stop, tile, i=i, side=side):
                    faces_ref[i, side, f, :, start:stop] = tile

                unpack(got_ref, 64 * i + 32 * side, 128, put, fields, width)
    else:
        faces_ref[...] = piece_refs[0][...]
    turn = turn_ref[place_ref[0]]
    core = place_ref[1]
    both = jnp.concatenate(
        [part for i in (core, 1 - core) for part in (faces_ref[i, 0], -faces_ref[i, 1])], axis=0
    ).reshape(4 * fields * levels, width)
    spec = turned(split_dot(both, high_ref[...], low_ref[...]), turn, 1.0)
    mine_ref[...] = spec[: 2 * fields * levels]
    other_ref[...] = spec[2 * fields * levels :]


def rim_spectra(token, pieces, shape, forward, turn, place):
    parts = len(pieces)
    _, _, fields, levels, width = shape
    spec = jax.ShapeDtypeStruct((2 * fields * levels, 2 * KCUT), F32)
    return pl.pallas_call(
        functools.partial(rim_kernel, parts),
        in_specs=vmem(4) + smem(1) + vmem(parts),
        out_specs=vmem(3),
        out_shape=[jax.ShapeDtypeStruct(shape, F32), spec, spec],
        scratch_shapes=[pltpu.VMEM((parts * 128, LANES), F32)] if parts > 1 else [],
        compiler_params=pltpu.CompilerParams(vmem_limit_bytes=VMEM_LIMIT),
        cost_estimate=pl.CostEstimate(
            flops=24 * fields * levels * 2 * KCUT * width,
            bytes_accessed=3 * 10**6,
            transcendentals=0,
        ),
        name="rim_spectra",
    )(token, *forward, turn, place, *pieces)


def final_kernel(
    parts,
    main_ref,
    pair_ref,
    mine_ref,
    away_ref,
    high_ref,
    low_ref,
    turn_ref,
    place_ref,
    block_ref,
    cutoff_ref,
    *refs,
):
    piece_refs, out_ref, refs = refs[:parts], refs[parts], refs[parts + 1 :]
    fields, slots, _, levels, width = main_ref.shape
    rows = 8
    side = pl.program_id(0)
    row = side * (rows - 1)
    turn = turn_ref[place_ref[0]]
    core = place_ref[1]
    first, second, rest = pick_slots(block_ref, cutoff_ref, rows)
    mine, other = mine_first((first, second), core)
    count = fields * levels
    part = pl.ds(pl.multiple_of(side * count, 8), count)
    sign = jnp.where(side == 0, 1.0, -1.0).astype(F32)
    if parts > 1:
        back_ref = refs[0]

        @pl.when(side == 0)
        def _():
            gather_pieces(piece_refs, place_ref[2], back_ref)

        def put(f, start, stop, tile):
            old = main_ref[f, rest, 0, :, start:stop]
            out_ref[f, rest, 0, :, start:stop] = old + tile * sign

        unpack(back_ref, 32 * side, 64, put, fields, width)
    else:
        out_ref[:, rest, 0] = main_ref[:, rest, 0] + piece_refs[0][side] * sign
    cuts = [cutoff_ref[block_ref[slot] * rows + row] for slot in (mine, other)]
    spec = jnp.concatenate(
        [
            turned(ref[part, :], turn, -1.0) * row_weights(cut)
            for ref, cut in ((mine_ref, cuts[0]), (away_ref, cuts[1]))
        ],
        axis=0,
    )
    smooth = split_dot(spec, high_ref[...], low_ref[...]).reshape(2, fields, levels, width)
    for i, (slot, order) in enumerate(((mine, core), (other, 1 - core))):
        out_ref[:, slot, 0] = main_ref[:, slot, 0] + jnp.where(
            cuts[i] > 0, smooth[i], pair_ref[order, side] * sign
        )


def final_part(main, pair, pieces, mine, away, inverse, turn, place, block, cutoff):
    fields, slots, rows, levels, width = main.shape
    block_spec = pl.BlockSpec(
        (fields, slots, 1, levels, width), lambda i: (0, 0, i * (rows - 1), 0, 0)
    )
    return pl.pallas_call(
        functools.partial(final_kernel, len(pieces)),
        grid=(2,),
        in_specs=[block_spec] + vmem(6) + smem(3) + vmem(len(pieces)),
        out_specs=block_spec,
        scratch_shapes=[pltpu.VMEM((len(pieces) * 64, LANES), F32)] if len(pieces) > 1 else [],
        out_shape=jax.ShapeDtypeStruct(main.shape, F32),
        input_output_aliases={0: 0},
        compiler_params=pltpu.CompilerParams(vmem_limit_bytes=VMEM_LIMIT),
        cost_estimate=pl.CostEstimate(
            flops=12 * mine.shape[0] * 2 * KCUT * width,
            bytes_accessed=4 * 10**6,
            transcendentals=0,
        ),
        name="final",
    )(main, pair, mine, away, *inverse, turn, place, block, cutoff, *pieces)


def swap(array, bit):
    size = lax.axis_size("lon")
    return lax.ppermute(array, "lon", [(i, i ^ bit) for i in range(size)])


def lon_sum(mine, other):
    total = mine + swap(other, 1)
    bit = 2
    while bit < lax.axis_size("lon"):
        total = total + swap(total, bit)
        bit *= 2
    return total, swap(total, 1)


def shards(state, courant_x, courant_y, block_of_slot, face_source, cutoff):
    fields, slots, rows, levels, width = state.shape
    lat, lon = lax.axis_size("lat"), lax.axis_size("lon")
    lon_index = lax.axis_index("lon")
    me = lax.axis_index("lat").astype(jnp.int32)
    place = jnp.stack([lon_index, lon_index % 2, me]).astype(jnp.int32)
    forward, inverse = basis_tables(width)
    turn = turn_table(lon, width)
    tables = (turn, place, block_of_slot, cutoff)

    packed = lat == levels == 8 and -(-width // LANES) * fields == 30
    if packed:
        me = me.reshape(1)
        got = rotate(pack(state, courant_y, block_of_slot, me))

    west, east = edges(state, courant_x)
    west = lax.ppermute(west, "lon", [(i, (i + 1) % lon) for i in range(lon)])
    east = lax.ppermute(east, "lon", [((i + 1) % lon, i) for i in range(lon)])
    base, mine, other = local_tendency(
        state, courant_x, courant_y, west, east, forward, *tables
    )
    total, away = lon_sum(mine, other)
    main, token = main_part(state, base, total, away, inverse, *tables)

    if packed:
        pair, rest = faces_of_pieces(got, slots, cutoff, me)
        pair, rest = rotate(pair), rotate(rest)
    else:
        faces = exchange_faces(state, courant_y, face_source)
        picked = pick_slots(block_of_slot, cutoff, rows)
        pair, rest = [faces[jnp.stack(picked[:2])]], [faces[picked[2]]]
    shape = (2, 2, fields, levels, width)
    pair, rim_mine, rim_other = rim_spectra(token, pair, shape, forward, turn, place)
    rim_total, rim_away = lon_sum(rim_mine, rim_other)
    return final_part(main, pair, rest, rim_total, rim_away, inverse, *tables)


def solution(mesh):
    placed = (
        P(None, "lat", None, None, "lon"),
        P("lat", None, None, "lon"),
        P("lat", None, None, "lon"),
        P("lat"),
        P("lat", None),
        P(),
    )
    return jax.shard_map(
        shards,
        mesh=mesh,
        in_specs=placed,
        out_specs=P(None, "lat", None, None, "lon"),
        check_vma=False,
    )
```

```python
import functools
import math

import jax
import jax.numpy as jnp
import numpy as np
from jax import lax
from jax.experimental import pallas as pl
from jax.experimental.pallas import tpu as pltpu
from jax.sharding import PartitionSpec as P

NLON = 2880
KCUT = 256
LANES = 128
VMEM_LIMIT = 50 * 1024 * 1024
BF16 = jnp.bfloat16
F32 = jnp.float32


def phases(columns):
    wavenumber = np.arange(KCUT, dtype=np.int64)
    return (columns[:, None] * wavenumber[None, :] % NLON).astype(np.float64) * (
        2.0 * math.pi / NLON
    )


def basis_tables(width):
    phase = phases(np.arange(width, dtype=np.int64))
    table = np.concatenate([np.cos(phase), np.sin(phase)], axis=1).astype(np.float32)
    high = table.astype(jnp.bfloat16)
    low = (table - high.astype(np.float32)).astype(jnp.bfloat16)
    forward = (jnp.asarray(high), jnp.asarray(low))
    inverse = (
        jnp.asarray(np.ascontiguousarray(high.T)),
        jnp.asarray(np.ascontiguousarray(low.T)),
    )
    return forward, inverse


def turn_table(lon, width):
    phase = phases(np.arange(lon, dtype=np.int64) * width)
    table = np.concatenate([np.cos(phase), np.sin(phase)], axis=1).astype(np.float32)
    return jnp.asarray(table[:, None, :])


def split_dot(rows, high, low):
    rows_high = rows.astype(BF16)
    rows_low = (rows - rows_high.astype(F32)).astype(BF16)
    dot = functools.partial(jnp.dot, preferred_element_type=F32)
    return dot(rows_high, high) + (dot(rows_low, high) + dot(rows_high, low))


def turned(spec, turn, sign):
    real, imag = spec[:, :KCUT], spec[:, KCUT:]
    cos, sin = turn[:, :KCUT], turn[:, KCUT:] * sign
    return jnp.concatenate([real * cos - imag * sin, imag * cos + real * sin], axis=1)


def row_weights(cut):
    column = lax.broadcasted_iota(jnp.int32, (1, 2 * KCUT), 1)
    wavenumber = jnp.where(column >= KCUT, column - KCUT, column)
    scale = jnp.where(wavenumber == 0, 1.0 / NLON, 2.0 / NLON).astype(F32)
    return jnp.where(wavenumber < cut, scale, 0.0)


def pick_slots(block_ref, cutoff_ref, rows):
    polar1 = cutoff_ref[block_ref[1] * rows] > 0
    polar2 = cutoff_ref[block_ref[2] * rows] > 0
    rest = jnp.where(polar2, jnp.where(polar1, 0, 1), 2)
    return jnp.where(rest == 0, 1, 0), jnp.where(rest == 2, 1, 2), rest


def mine_first(pair, core):
    a, b = pair
    return jnp.where(core == 0, a, b), jnp.where(core == 0, b, a)


def vmem(count):
    return [pl.BlockSpec(memory_space=pltpu.VMEM)] * count


def smem(count):
    return [pl.BlockSpec(memory_space=pltpu.SMEM)] * count


def edge_kernel(lane_last, head_ref, tail_ref, wind_ref, west_ref, east_ref):
    fields, slots, rows = head_ref.shape[:3]
    lane = lax.broadcasted_iota(jnp.int32, (8, LANES), 1)
    for s in range(slots):
        west = jnp.zeros((8, LANES), F32)
        east = jnp.zeros((8, LANES), F32)
        for r in range(rows):
            for f in range(fields):
                here = lane == f * rows + r
                west = jnp.where(here, tail_ref[f, s, r, :, lane_last : lane_last + 1], west)
                east = jnp.where(here, head_ref[f, s, r, :, 0:1], east)
            here = lane == fields * rows + r
            west = jnp.where(here, wind_ref[s, r, :, lane_last : lane_last + 1], west)
        west_ref[s] = west
        east_ref[s] = east


def edges(state, courant_x):
    fields, slots, rows, levels, width = state.shape
    last = (width - 1) // LANES
    out = jax.ShapeDtypeStruct((slots, levels, LANES), F32)
    return pl.pallas_call(
        functools.partial(edge_kernel, (width - 1) % LANES),
        grid=(1,),
        in_specs=[
            pl.BlockSpec((fields, slots, rows, levels, LANES), lambda i: (0, 0, 0, 0, 0)),
            pl.BlockSpec((fields, slots, rows, levels, LANES), lambda i: (0, 0, 0, 0, last)),
            pl.BlockSpec((slots, rows, levels, LANES), lambda i: (0, 0, 0, last)),
        ],
        out_specs=[pl.BlockSpec((slots, levels, LANES), lambda i: (0, 0, 0))] * 2,
        out_shape=[out, out],
        cost_estimate=pl.CostEstimate(flops=10**5, bytes_accessed=1200000, transcendentals=0),
        name="edges",
    )(state, state, courant_x)


PIECE = 200
BACK = 192


def tile_of(slab, t, width):
    part = slab[:, t * LANES : min((t + 1) * LANES, width)]
    if part.shape[1] < LANES:
        part = jnp.concatenate([part, jnp.zeros((8, LANES - part.shape[1]), F32)], axis=1)
    return part


def pack_kernel(width, first_ref, last_ref, wind_ref, block_ref, out_ref):
    fields, slots = first_ref.shape[:2]
    tiles = -(-width // LANES)

    def put(row, tile):
        out_ref[pl.ds(row, 8, stride=PIECE), :] = tile

    for j in range(slots):
        half = wind_ref[j, 0] * 0.5
        for t in range(tiles):
            row = {0: 192 + 2 * j, 1: 193 + 2 * j, 2: 64 * j + 62, 3: 64 * j + 63}.get(
                t, 64 * j + 26 + t
            )
            put(row, tile_of(half, t, width))
        for f in range(fields):
            north = last_ref[f, j, 0] * half
            south = first_ref[f, j, 0]
            for t in range(tiles):
                put(64 * j + f * tiles + t, tile_of(north, t, width))
                put(64 * j + 32 + f * tiles + t, tile_of(south, t, width))
    lane = lax.broadcasted_iota(jnp.int32, (8, LANES), 1)
    table = jnp.zeros((8, LANES), F32)
    for j in range(slots):
        table = jnp.where(lane == j, block_ref[j].astype(F32), table)
    put(198, table)
    put(199, table)


def pack(state, courant_y, block):
    fields, slots, rows, levels, width = state.shape
    return pl.pallas_call(
        functools.partial(pack_kernel, width),
        grid=(1,),
        in_specs=[
            pl.BlockSpec((fields, slots, 1, levels, width), lambda i: (0, 0, 0, 0, 0)),
            pl.BlockSpec((fields, slots, 1, levels, width), lambda i: (0, 0, rows - 1, 0, 0)),
            pl.BlockSpec((slots, 1, levels, width), lambda i: (0, rows - 1, 0, 0)),
            pl.BlockSpec(memory_space=pltpu.SMEM),
        ],
        out_specs=pl.BlockSpec((levels * PIECE, LANES), lambda i: (0, 0)),
        out_shape=jax.ShapeDtypeStruct((levels * PIECE, LANES), F32),
        cost_estimate=pl.CostEstimate(flops=10**5, bytes_accessed=1700000, transcendentals=0),
        name="pack",
    )(state, state, courant_y, block)


def face_kernel(got_ref, cutoff_ref, out_ref, face_ref, table_ref, slot_ref, sem):
    parts = got_ref.shape[0]
    slots = face_ref.shape[0] // parts
    count = parts * slots
    copy = pltpu.make_async_copy(got_ref.at[:, 192:200, :], table_ref, sem)
    copy.start()
    copy.wait()
    blocks = [table_ref[s // slots, 6, s % slots].astype(jnp.int32) for s in range(count)]
    slot_ref[0] = -1
    slot_ref[count + 1] = -1
    for s in range(count):
        slot_ref[blocks[s] + 1] = s
    for s in range(count):
        src, j = divmod(s, slots)
        south = slot_ref[blocks[s] + 2]
        safe = jnp.maximum(south, 0)
        from_src = lax.div(safe, slots)
        from_slot = safe - from_src * slots
        half = jnp.concatenate(
            [
                got_ref[src, 192 + 2 * j : 194 + 2 * j, :],
                got_ref[src, 64 * j + 62 : 64 * j + 64, :],
                got_ref[src, 64 * j + 30 : 64 * j + 32, :],
            ],
            axis=0,
        )
        half = jnp.concatenate([half] * 5 + [half[:2]], axis=0)
        other = got_ref[from_src, pl.ds(pl.multiple_of(64 * from_slot + 32, 32), 32), :]
        face = got_ref[src, 64 * j : 64 * j + 32, :] + half * other
        face_ref[s] = jnp.where(south >= 0, face, 0.0)
    for d in range(parts):
        first, second, rest = pick_slots(blocks[slots * d : slots * d + slots], cutoff_ref, 8)
        for i, slot in enumerate((first, second, rest)):
            out = out_ref.at[d, i]
            block = jnp.where(
                slot == 0,
                blocks[slots * d],
                jnp.where(slot == 1, blocks[slots * d + 1], blocks[slots * d + 2]),
            )
            north = slot_ref[block]
            out[0] = jnp.where(north >= 0, face_ref[jnp.maximum(north, 0)], 0.0)
            out[1] = face_ref[slots * d + slot]


def faces_of_pieces(got, slots, cutoff):
    parts = got.shape[0]
    return pl.pallas_call(
        face_kernel,
        in_specs=vmem(1) + smem(1),
        out_specs=vmem(1)[0],
        out_shape=jax.ShapeDtypeStruct((parts, slots, 2, 32, LANES), F32),
        scratch_shapes=[
            pltpu.VMEM((parts * slots, 32, LANES), F32),
            pltpu.SMEM((parts, 8, LANES), F32),
            pltpu.SMEM((parts * slots + 2,), jnp.int32),
            pltpu.SemaphoreType.DMA(()),
        ],
        cost_estimate=pl.CostEstimate(flops=10**5, bytes_accessed=1600000, transcendentals=0),
        name="faces",
    )(got, cutoff)


def to_pieces(units, parts):
    count, levels, width = units.shape
    groups = math.gcd(parts, levels)
    chunks = parts // groups
    span = -(-width // chunks)
    units = jnp.pad(units, ((0, 0), (0, 0), (0, span * chunks - width)))
    units = units.reshape(count, groups, levels // groups, chunks, span)
    return units.transpose(1, 3, 0, 2, 4).reshape(parts, count, levels // groups * span)


def from_pieces(pieces, levels, width):
    parts, count, _ = pieces.shape
    groups = math.gcd(parts, levels)
    chunks = parts // groups
    span = -(-width // chunks)
    pieces = pieces.reshape(groups, chunks, count, levels // groups, span)
    return pieces.transpose(2, 0, 3, 1, 4).reshape(count, levels, chunks * span)[:, :, :width]


def exchange_faces(state, courant_y, face_source):
    fields, slots, rows, levels, width = state.shape
    lat = lax.axis_size("lat")
    count = 2 * fields + 1
    first = state[:, :, 0].transpose(1, 0, 2, 3)
    last = state[:, :, rows - 1].transpose(1, 0, 2, 3)
    half = courant_y[:, rows - 1][:, None] * 0.5
    units = jnp.concatenate([first, last * half, half], axis=1)
    sent = to_pieces(units.reshape(slots * count, levels, width), lat)
    span = sent.shape[2]
    table = jnp.pad(
        face_source.astype(F32).reshape(1, slots * 2), ((0, 0), (0, span - slots * 2))
    )
    sent = jnp.concatenate([sent, jnp.broadcast_to(table[None], (lat, 1, span))], axis=1)
    got = lax.all_to_all(sent, "lat", 0, 0, tiled=True)
    indices = got[:, slots * count, : slots * 2].reshape(lat * slots, 2).astype(jnp.int32)
    data = got[:, : slots * count].reshape(lat * slots, count, span)
    north, south = indices[:, 0], indices[:, 1]
    face = data[:, fields : 2 * fields] + data[:, 2 * fields :] * data[
        jnp.maximum(south, 0), :fields
    ]
    face = jnp.where((south >= 0)[:, None, None], face, 0.0)
    face_north = jnp.where((north >= 0)[:, None, None], face[jnp.maximum(north, 0)], 0.0)
    back = jnp.concatenate([face_north, face], axis=1).reshape(lat, slots * 2 * fields, span)
    back = lax.all_to_all(back, "lat", 0, 0, tiled=True)
    return from_pieces(back, levels, width).reshape(slots, 2, fields, levels, width)


def tendency_kernel(
    state_ref,
    cx_ref,
    cy_ref,
    west_ref,
    east_ref,
    high_ref,
    low_ref,
    turn_ref,
    place_ref,
    block_ref,
    cutoff_ref,
    out_ref,
    mine_ref,
    other_ref,
    tend_ref,
    base_ref,
    sem,
):
    fields, slots, rows, levels, width = state_ref.shape

    def streamed(s):
        return pltpu.make_async_copy(base_ref.at[:, s], out_ref.at[:, s], sem.at[s])


    tiles = -(-width // LANES)
    lane = lax.broadcasted_iota(jnp.int32, (levels, LANES), 1)
    head, tail, last = lane == 0, lane == LANES - 1, lane == (width - 1) % LANES

    def load(ref, *index):
        out = []
        for t in range(tiles):
            part = ref[index + (slice(None), slice(t * LANES, min((t + 1) * LANES, width)))]
            if part.shape[1] < LANES:
                pad = jnp.zeros((levels, LANES - part.shape[1]), F32)
                part = jnp.concatenate([part, pad], axis=1)
            out.append(part)
        return out

    def one_slot(s, carry):
        west, east = west_ref[s], east_ref[s]
        for f in range(fields):
            above = None
            now = load(state_ref, f, s, 0)
            for r in range(rows):
                column = f * rows + r
                left = [pltpu.roll(x, LANES - 1, 1) for x in now]
                left = [
                    jnp.where(tail, left[t + 1], left[t])
                    if t + 1 < tiles
                    else jnp.where(last, east[:, column : column + 1], left[t])
                    for t in range(tiles)
                ]
                half = [x * 0.5 for x in load(cx_ref, s, r)]
                flux = [h * (x + y) for h, x, y in zip(half, now, left)]
                wind = west[:, fields * rows + r : fields * rows + r + 1] * 0.5
                first = wind * (west[:, column : column + 1] + now[0])
                right = [pltpu.roll(x, 1, 1) for x in flux]
                right = [jnp.where(head, y, x) for x, y in zip(right, [first] + right[:-1])]
                change = [x - y for x, y in zip(right, flux)]
                if above is not None:
                    change = [x + y for x, y in zip(change, above)]
                if r + 1 < rows:
                    later = load(state_ref, f, s, r + 1)
                    half = load(cy_ref, s, r)
                    above = [h * 0.5 * (x + y) for h, x, y in zip(half, now, later)]
                    change = [x - y for x, y in zip(change, above)]
                for t in range(tiles):
                    stop = min((t + 1) * LANES, width)
                    base = now[t] + change[t]
                    tend_ref[f, s, r, :, t * LANES : stop] = change[t][:, : stop - t * LANES]
                    base_ref[f, s, r, :, t * LANES : stop] = base[:, : stop - t * LANES]
                now = later
        streamed(s).start()
        return carry

    lax.fori_loop(0, slots, one_slot, 0)
    turn = turn_ref[place_ref[0]]
    first, second, _ = pick_slots(block_ref, cutoff_ref, rows)
    mine, other = mine_first((first, second), place_ref[1])
    for slot, spec_ref in ((other, other_ref), (mine, mine_ref)):
        spec = split_dot(
            tend_ref[:, slot].reshape(fields * rows * levels, width), high_ref[...], low_ref[...]
        )
        spec_ref[...] = turned(spec, turn, 1.0)
    for s in range(slots):
        streamed(s).wait()


def local_tendency(state, courant_x, courant_y, west, east, forward, turn, place, block, cutoff):
    fields, slots, rows, levels, width = state.shape
    count = fields * rows * levels
    spec = jax.ShapeDtypeStruct((count, 2 * KCUT), F32)
    return pl.pallas_call(
        tendency_kernel,
        in_specs=vmem(8) + smem(3),
        out_specs=[pl.BlockSpec(memory_space=pl.ANY)] + vmem(2),
        out_shape=[jax.ShapeDtypeStruct(state.shape, F32), spec, spec],
        scratch_shapes=[
            pltpu.VMEM(state.shape, F32),
            pltpu.VMEM(state.shape, F32),
            pltpu.SemaphoreType.DMA((slots,)),
        ],
        compiler_params=pltpu.CompilerParams(vmem_limit_bytes=VMEM_LIMIT),
        cost_estimate=pl.CostEstimate(
            flops=6 * count * 2 * KCUT * width * 2, bytes_accessed=9 * 10**6, transcendentals=0
        ),
        name="tendency",
    )(state, courant_x, courant_y, west, east, *forward, turn, place, block, cutoff)


def chosen_slot(i, place_ref, block_ref, cutoff_ref, rows):
    first, second, _ = pick_slots(block_ref, cutoff_ref, rows)
    return jnp.where(i == place_ref[1], first, second)


def main_kernel(
    place_ref,
    block_ref,
    cutoff_ref,
    state_ref,
    base_ref,
    mine_ref,
    away_ref,
    high_ref,
    low_ref,
    turn_ref,
    out_ref,
    token_ref,
):
    fields, _, rows, levels, width = state_ref.shape
    token_ref[...] = jnp.zeros_like(token_ref)
    i = pl.program_id(0)
    turn = turn_ref[place_ref[0]]
    slot = chosen_slot(i, place_ref, block_ref, cutoff_ref, rows)
    spec = turned(jnp.where(i == 0, mine_ref[...], away_ref[...]), turn, -1.0)
    spec = spec.reshape(fields, rows, levels, 2 * KCUT)
    cuts = [cutoff_ref[block_ref[slot] * rows + r] for r in range(rows)]
    spec = jnp.concatenate(
        [spec[:, r : r + 1] * row_weights(cuts[r]) for r in range(rows)], axis=1
    )
    smooth = split_dot(
        spec.reshape(fields * rows * levels, 2 * KCUT), high_ref[...], low_ref[...]
    ).reshape(fields, rows, levels, width)
    for r in range(rows):
        out_ref[:, 0, r] = jnp.where(
            cuts[r] > 0, state_ref[:, 0, r] + smooth[:, r], base_ref[:, 0, r]
        )


def main_part(state, base, mine, away, inverse, turn, place, block, cutoff):
    fields, slots, rows, levels, width = state.shape
    slot_block = pl.BlockSpec(
        (fields, 1, rows, levels, width),
        lambda i, *scalars: (0, chosen_slot(i, *scalars, rows), 0, 0, 0),
    )
    return pl.pallas_call(
        main_kernel,
        grid_spec=pltpu.PrefetchScalarGridSpec(
            num_scalar_prefetch=3,
            grid=(2,),
            in_specs=[slot_block, slot_block] + vmem(5),
            out_specs=[slot_block, pl.BlockSpec((8, LANES), lambda i, *scalars: (0, 0))],
        ),
        out_shape=[
            jax.ShapeDtypeStruct(state.shape, F32),
            jax.ShapeDtypeStruct((8, LANES), F32),
        ],
        input_output_aliases={4: 0},
        compiler_params=pltpu.CompilerParams(vmem_limit_bytes=VMEM_LIMIT),
        cost_estimate=pl.CostEstimate(
            flops=12 * mine.shape[0] * 2 * KCUT * width,
            bytes_accessed=6 * 10**6,
            transcendentals=0,
        ),
        name="main",
    )(place, block, cutoff, state, base, mine, away, *inverse, turn)


def unpack(ref, base, stride, put, fields, width):
    tiles = -(-width // LANES)
    for f in range(fields):
        for t in range(tiles):
            tile = ref[pl.ds(base + f * tiles + t, 8, stride=stride), :]
            stop = min((t + 1) * LANES, width)
            put(f, t * LANES, stop, tile[:, : stop - t * LANES])


def rim_kernel(
    packed,
    token_ref,
    got_ref,
    high_ref,
    low_ref,
    turn_ref,
    place_ref,
    faces_ref,
    mine_ref,
    other_ref,
):
    _, _, fields, levels, width = faces_ref.shape
    if packed:
        for i in range(2):
            for side in range(2):

                def put(f, start, stop, tile, i=i, side=side):
                    faces_ref[i, side, f, :, start:stop] = tile

                unpack(got_ref, 64 * i + 32 * side, BACK, put, fields, width)
    else:
        faces_ref[...] = got_ref[...]
    turn = turn_ref[place_ref[0]]
    core = place_ref[1]
    both = jnp.concatenate(
        [part for i in (core, 1 - core) for part in (faces_ref[i, 0], -faces_ref[i, 1])], axis=0
    ).reshape(4 * fields * levels, width)
    spec = turned(split_dot(both, high_ref[...], low_ref[...]), turn, 1.0)
    mine_ref[...] = spec[: 2 * fields * levels]
    other_ref[...] = spec[2 * fields * levels :]


def rim_spectra(token, got, shape, forward, turn, place):
    _, _, fields, levels, width = shape
    spec = jax.ShapeDtypeStruct((2 * fields * levels, 2 * KCUT), F32)
    return pl.pallas_call(
        functools.partial(rim_kernel, got.ndim == 2),
        in_specs=vmem(5) + smem(1),
        out_specs=vmem(3),
        out_shape=[jax.ShapeDtypeStruct(shape, F32), spec, spec],
        compiler_params=pltpu.CompilerParams(vmem_limit_bytes=VMEM_LIMIT),
        cost_estimate=pl.CostEstimate(
            flops=24 * fields * levels * 2 * KCUT * width,
            bytes_accessed=3 * 10**6,
            transcendentals=0,
        ),
        name="rim_spectra",
    )(token, got, *forward, turn, place)


def final_kernel(
    packed,
    main_ref,
    pair_ref,
    back_ref,
    mine_ref,
    away_ref,
    high_ref,
    low_ref,
    turn_ref,
    place_ref,
    block_ref,
    cutoff_ref,
    out_ref,
):
    fields, slots, _, levels, width = main_ref.shape
    rows = 8
    side = pl.program_id(0)
    row = side * (rows - 1)
    turn = turn_ref[place_ref[0]]
    core = place_ref[1]
    first, second, rest = pick_slots(block_ref, cutoff_ref, rows)
    mine, other = mine_first((first, second), core)
    count = fields * levels
    part = pl.ds(pl.multiple_of(side * count, 8), count)
    sign = jnp.where(side == 0, 1.0, -1.0).astype(F32)
    if packed:

        def put(f, start, stop, tile):
            old = main_ref[f, rest, 0, :, start:stop]
            out_ref[f, rest, 0, :, start:stop] = old + tile * sign

        unpack(back_ref, 128 + 32 * side, BACK, put, fields, width)
    else:
        out_ref[:, rest, 0] = main_ref[:, rest, 0] + back_ref[side] * sign
    cuts = [cutoff_ref[block_ref[slot] * rows + row] for slot in (mine, other)]
    spec = jnp.concatenate(
        [
            turned(ref[part, :], turn, -1.0) * row_weights(cut)
            for ref, cut in ((mine_ref, cuts[0]), (away_ref, cuts[1]))
        ],
        axis=0,
    )
    smooth = split_dot(spec, high_ref[...], low_ref[...]).reshape(2, fields, levels, width)
    for i, (slot, order) in enumerate(((mine, core), (other, 1 - core))):
        out_ref[:, slot, 0] = main_ref[:, slot, 0] + jnp.where(
            cuts[i] > 0, smooth[i], pair_ref[order, side] * sign
        )


def final_part(main, pair, back, mine, away, inverse, turn, place, block, cutoff):
    fields, slots, rows, levels, width = main.shape
    block_spec = pl.BlockSpec(
        (fields, slots, 1, levels, width), lambda i: (0, 0, i * (rows - 1), 0, 0)
    )
    return pl.pallas_call(
        functools.partial(final_kernel, back.ndim == 2),
        grid=(2,),
        in_specs=[block_spec] + vmem(7) + smem(3),
        out_specs=block_spec,
        out_shape=jax.ShapeDtypeStruct(main.shape, F32),
        input_output_aliases={0: 0},
        compiler_params=pltpu.CompilerParams(vmem_limit_bytes=VMEM_LIMIT),
        cost_estimate=pl.CostEstimate(
            flops=12 * mine.shape[0] * 2 * KCUT * width,
            bytes_accessed=4 * 10**6,
            transcendentals=0,
        ),
        name="final",
    )(main, pair, back, mine, away, *inverse, turn, place, block, cutoff)


def swap(array, bit):
    size = lax.axis_size("lon")
    return lax.ppermute(array, "lon", [(i, i ^ bit) for i in range(size)])


def lon_sum(mine, other):
    total = mine + swap(other, 1)
    bit = 2
    while bit < lax.axis_size("lon"):
        total = total + swap(total, bit)
        bit *= 2
    return total, swap(total, 1)


def shards(state, courant_x, courant_y, block_of_slot, face_source, cutoff):
    fields, slots, rows, levels, width = state.shape
    lat, lon = lax.axis_size("lat"), lax.axis_size("lon")
    lon_index = lax.axis_index("lon")
    place = jnp.stack([lon_index, lon_index % 2]).astype(jnp.int32)
    forward, inverse = basis_tables(width)
    turn = turn_table(lon, width)
    tables = (turn, place, block_of_slot, cutoff)

    packed = lat == levels == 8 and -(-width // LANES) * fields == 30
    if packed:
        sent = pack(state, courant_y, block_of_slot).reshape(lat, PIECE, LANES)
        got = lax.all_to_all(sent, "lat", 0, 0, tiled=True)

    west, east = edges(state, courant_x)
    west = lax.ppermute(west, "lon", [(i, (i + 1) % lon) for i in range(lon)])
    east = lax.ppermute(east, "lon", [((i + 1) % lon, i) for i in range(lon)])
    base, mine, other = local_tendency(
        state, courant_x, courant_y, west, east, forward, *tables
    )
    total, away = lon_sum(mine, other)
    main, token = main_part(state, base, total, away, inverse, *tables)

    if packed:
        back = faces_of_pieces(got, slots, cutoff).reshape(lat, BACK, LANES)
        back = lax.all_to_all(back, "lat", 0, 0, tiled=True).reshape(lat * BACK, LANES)
        pair = rest = back
    else:
        faces = exchange_faces(state, courant_y, face_source)
        picked = pick_slots(block_of_slot, cutoff, rows)
        pair, rest = faces[jnp.stack(picked[:2])], faces[picked[2]]
    shape = (2, 2, fields, levels, width)
    pair, rim_mine, rim_other = rim_spectra(token, pair, shape, forward, turn, place)
    rim_total, rim_away = lon_sum(rim_mine, rim_other)
    return final_part(main, pair, rest, rim_total, rim_away, inverse, *tables)


def solution(mesh):
    placed = (
        P(None, "lat", None, None, "lon"),
        P("lat", None, None, "lon"),
        P("lat", None, None, "lon"),
        P("lat"),
        P("lat", None),
        P(),
    )
    return jax.shard_map(
        shards,
        mesh=mesh,
        in_specs=placed,
        out_specs=P(None, "lat", None, None, "lon"),
        check_vma=False,
    )
```

```python
import functools
import math

import jax
import jax.numpy as jnp
import numpy as np
from jax import lax
from jax.experimental import pallas as pl
from jax.experimental.pallas import tpu as pltpu
from jax.sharding import PartitionSpec as P

NLON = 2880
KCUT = 256
LANES = 128
MIB = 1024 * 1024
BF16 = jnp.bfloat16
F32 = jnp.float32


def phases(columns):
    wavenumber = np.arange(KCUT, dtype=np.int64)
    return (columns[:, None] * wavenumber[None, :] % NLON).astype(np.float64) * (
        2.0 * math.pi / NLON
    )


def basis_tables(width):
    phase = phases(np.arange(width, dtype=np.int64))
    table = np.concatenate([np.cos(phase), np.sin(phase)], axis=1).astype(np.float32)
    high = table.astype(jnp.bfloat16)
    low = (table - high.astype(np.float32)).astype(jnp.bfloat16)
    forward = (jnp.asarray(high), jnp.asarray(low))
    inverse = (
        jnp.asarray(np.ascontiguousarray(high.T)),
        jnp.asarray(np.ascontiguousarray(low.T)),
    )
    return forward, inverse


def turn_table(lon, width):
    phase = phases(np.arange(lon, dtype=np.int64) * width)
    table = np.concatenate([np.cos(phase), np.sin(phase)], axis=1).astype(np.float32)
    return jnp.asarray(table[:, None, :])


def split_dot(rows, high, low):
    rows_high = rows.astype(BF16)
    rows_low = (rows - rows_high.astype(F32)).astype(BF16)
    dot = functools.partial(jnp.dot, preferred_element_type=F32)
    return dot(rows_high, high) + (dot(rows_low, high) + dot(rows_high, low))


def turned(spec, turn, sign):
    real, imag = spec[:, :KCUT], spec[:, KCUT:]
    cos, sin = turn[:, :KCUT], turn[:, KCUT:] * sign
    return jnp.concatenate([real * cos - imag * sin, imag * cos + real * sin], axis=1)


def row_weights(cut):
    column = lax.broadcasted_iota(jnp.int32, (1, 2 * KCUT), 1)
    wavenumber = jnp.where(column >= KCUT, column - KCUT, column)
    scale = jnp.where(wavenumber == 0, 1.0 / NLON, 2.0 / NLON).astype(F32)
    return jnp.where(wavenumber < cut, scale, 0.0)


def pick_slots(block_ref, cutoff_ref, rows):
    polar1 = cutoff_ref[block_ref[1] * rows] > 0
    polar2 = cutoff_ref[block_ref[2] * rows] > 0
    rest = jnp.where(polar2, jnp.where(polar1, 0, 1), 2)
    return jnp.where(rest == 0, 1, 0), jnp.where(rest == 2, 1, 2), rest


def mine_first(pair, core):
    a, b = pair
    return jnp.where(core == 0, a, b), jnp.where(core == 0, b, a)


def vmem(count):
    return [pl.BlockSpec(memory_space=pltpu.VMEM)] * count


def smem(count):
    return [pl.BlockSpec(memory_space=pltpu.SMEM)] * count


def edge_kernel(lane_last, head_ref, tail_ref, wind_ref, west_ref, east_ref):
    fields, slots, rows = head_ref.shape[:3]
    lane = lax.broadcasted_iota(jnp.int32, (8, LANES), 1)
    for s in range(slots):
        west = jnp.zeros((8, LANES), F32)
        east = jnp.zeros((8, LANES), F32)
        for r in range(rows):
            for f in range(fields):
                here = lane == f * rows + r
                west = jnp.where(here, tail_ref[f, s, r, :, lane_last : lane_last + 1], west)
                east = jnp.where(here, head_ref[f, s, r, :, 0:1], east)
            here = lane == fields * rows + r
            west = jnp.where(here, wind_ref[s, r, :, lane_last : lane_last + 1], west)
        west_ref[s] = west
        east_ref[s] = east


def edges(state, courant_x):
    fields, slots, rows, levels, width = state.shape
    last = (width - 1) // LANES
    out = jax.ShapeDtypeStruct((slots, levels, LANES), F32)
    return pl.pallas_call(
        functools.partial(edge_kernel, (width - 1) % LANES),
        grid=(1,),
        in_specs=[
            pl.BlockSpec((fields, slots, rows, levels, LANES), lambda i: (0, 0, 0, 0, 0)),
            pl.BlockSpec((fields, slots, rows, levels, LANES), lambda i: (0, 0, 0, 0, last)),
            pl.BlockSpec((slots, rows, levels, LANES), lambda i: (0, 0, 0, last)),
        ],
        out_specs=[pl.BlockSpec((slots, levels, LANES), lambda i: (0, 0, 0))] * 2,
        out_shape=[out, out],
        cost_estimate=pl.CostEstimate(flops=10**5, bytes_accessed=1200000, transcendentals=0),
        name="edges",
    )(state, state, courant_x)


PIECE = 200
BACK = 192


def tile_of(slab, t, width):
    part = slab[:, t * LANES : min((t + 1) * LANES, width)]
    if part.shape[1] < LANES:
        part = jnp.concatenate([part, jnp.zeros((8, LANES - part.shape[1]), F32)], axis=1)
    return part


def pack_kernel(width, first_ref, last_ref, wind_ref, block_ref, out_ref):
    fields, slots = first_ref.shape[:2]
    tiles = -(-width // LANES)

    def put(row, tile):
        out_ref[pl.ds(row, 8, stride=PIECE), :] = tile

    for j in range(slots):
        half = wind_ref[j, 0] * 0.5
        for t in range(tiles):
            row = {0: 192 + 2 * j, 1: 193 + 2 * j, 2: 64 * j + 62, 3: 64 * j + 63}.get(
                t, 64 * j + 26 + t
            )
            put(row, tile_of(half, t, width))
        for f in range(fields):
            north = last_ref[f, j, 0] * half
            south = first_ref[f, j, 0]
            for t in range(tiles):
                put(64 * j + f * tiles + t, tile_of(north, t, width))
                put(64 * j + 32 + f * tiles + t, tile_of(south, t, width))
    lane = lax.broadcasted_iota(jnp.int32, (8, LANES), 1)
    table = jnp.zeros((8, LANES), F32)
    for j in range(slots):
        table = jnp.where(lane == j, block_ref[j].astype(F32), table)
    put(198, table)
    put(199, table)


def pack(state, courant_y, block):
    fields, slots, rows, levels, width = state.shape
    return pl.pallas_call(
        functools.partial(pack_kernel, width),
        grid=(1,),
        in_specs=[
            pl.BlockSpec((fields, slots, 1, levels, width), lambda i: (0, 0, 0, 0, 0)),
            pl.BlockSpec((fields, slots, 1, levels, width), lambda i: (0, 0, rows - 1, 0, 0)),
            pl.BlockSpec((slots, 1, levels, width), lambda i: (0, rows - 1, 0, 0)),
            pl.BlockSpec(memory_space=pltpu.SMEM),
        ],
        out_specs=pl.BlockSpec((levels * PIECE, LANES), lambda i: (0, 0)),
        out_shape=jax.ShapeDtypeStruct((levels * PIECE, LANES), F32),
        cost_estimate=pl.CostEstimate(flops=10**5, bytes_accessed=1700000, transcendentals=0),
        name="pack",
    )(state, state, courant_y, block)


def face_kernel(
    got_ref, cutoff_ref, later_in_ref, out_ref, later_ref, face_ref, table_ref, slot_ref, sem
):
    del later_in_ref, later_ref
    parts = got_ref.shape[0]
    slots = face_ref.shape[0] // parts
    count = parts * slots
    copy = pltpu.make_async_copy(got_ref.at[:, 192:200, :], table_ref, sem)
    copy.start()
    copy.wait()
    blocks = [table_ref[s // slots, 6, s % slots].astype(jnp.int32) for s in range(count)]
    slot_ref[0] = -1
    slot_ref[count + 1] = -1
    for s in range(count):
        slot_ref[blocks[s] + 1] = s
    for s in range(count):
        src, j = divmod(s, slots)
        south = slot_ref[blocks[s] + 2]
        safe = jnp.maximum(south, 0)
        from_src = lax.div(safe, slots)
        from_slot = safe - from_src * slots
        half = jnp.concatenate(
            [
                got_ref[src, 192 + 2 * j : 194 + 2 * j, :],
                got_ref[src, 64 * j + 62 : 64 * j + 64, :],
                got_ref[src, 64 * j + 30 : 64 * j + 32, :],
            ],
            axis=0,
        )
        half = jnp.concatenate([half] * 5 + [half[:2]], axis=0)
        other = got_ref[from_src, pl.ds(pl.multiple_of(64 * from_slot + 32, 32), 32), :]
        face = got_ref[src, 64 * j : 64 * j + 32, :] + half * other
        face_ref[s] = jnp.where(south >= 0, face, 0.0)
    for d in range(parts):
        first, second, rest = pick_slots(blocks[slots * d : slots * d + slots], cutoff_ref, 8)
        for i, slot in enumerate((first, second, rest)):
            out = out_ref.at[d, i]
            block = jnp.where(
                slot == 0,
                blocks[slots * d],
                jnp.where(slot == 1, blocks[slots * d + 1], blocks[slots * d + 2]),
            )
            north = slot_ref[block]
            out[0] = jnp.where(north >= 0, face_ref[jnp.maximum(north, 0)], 0.0)
            out[1] = face_ref[slots * d + slot]


def faces_of_pieces(got, slots, cutoff, later):
    parts = got.shape[0]
    return pl.pallas_call(
        face_kernel,
        in_specs=vmem(1) + smem(1) + [pl.BlockSpec(memory_space=pl.ANY)],
        out_specs=vmem(1) + [pl.BlockSpec(memory_space=pl.ANY)],
        out_shape=[
            jax.ShapeDtypeStruct((parts, slots, 2, 32, LANES), F32),
            jax.ShapeDtypeStruct(later.shape, F32),
        ],
        input_output_aliases={2: 1},
        scratch_shapes=[
            pltpu.VMEM((parts * slots, 32, LANES), F32),
            pltpu.SMEM((parts, 8, LANES), F32),
            pltpu.SMEM((parts * slots + 2,), jnp.int32),
            pltpu.SemaphoreType.DMA(()),
        ],
        cost_estimate=pl.CostEstimate(flops=10**5, bytes_accessed=1600000, transcendentals=0),
        name="faces",
    )(got, cutoff, later)


def to_pieces(units, parts):
    count, levels, width = units.shape
    groups = math.gcd(parts, levels)
    chunks = parts // groups
    span = -(-width // chunks)
    units = jnp.pad(units, ((0, 0), (0, 0), (0, span * chunks - width)))
    units = units.reshape(count, groups, levels // groups, chunks, span)
    return units.transpose(1, 3, 0, 2, 4).reshape(parts, count, levels // groups * span)


def from_pieces(pieces, levels, width):
    parts, count, _ = pieces.shape
    groups = math.gcd(parts, levels)
    chunks = parts // groups
    span = -(-width // chunks)
    pieces = pieces.reshape(groups, chunks, count, levels // groups, span)
    return pieces.transpose(2, 0, 3, 1, 4).reshape(count, levels, chunks * span)[:, :, :width]


def exchange_faces(state, courant_y, face_source):
    fields, slots, rows, levels, width = state.shape
    lat = lax.axis_size("lat")
    count = 2 * fields + 1
    first = state[:, :, 0].transpose(1, 0, 2, 3)
    last = state[:, :, rows - 1].transpose(1, 0, 2, 3)
    half = courant_y[:, rows - 1][:, None] * 0.5
    units = jnp.concatenate([first, last * half, half], axis=1)
    sent = to_pieces(units.reshape(slots * count, levels, width), lat)
    span = sent.shape[2]
    table = jnp.pad(
        face_source.astype(F32).reshape(1, slots * 2), ((0, 0), (0, span - slots * 2))
    )
    sent = jnp.concatenate([sent, jnp.broadcast_to(table[None], (lat, 1, span))], axis=1)
    got = lax.all_to_all(sent, "lat", 0, 0, tiled=True)
    indices = got[:, slots * count, : slots * 2].reshape(lat * slots, 2).astype(jnp.int32)
    data = got[:, : slots * count].reshape(lat * slots, count, span)
    north, south = indices[:, 0], indices[:, 1]
    face = data[:, fields : 2 * fields] + data[:, 2 * fields :] * data[
        jnp.maximum(south, 0), :fields
    ]
    face = jnp.where((south >= 0)[:, None, None], face, 0.0)
    face_north = jnp.where((north >= 0)[:, None, None], face[jnp.maximum(north, 0)], 0.0)
    back = jnp.concatenate([face_north, face], axis=1).reshape(lat, slots * 2 * fields, span)
    back = lax.all_to_all(back, "lat", 0, 0, tiled=True)
    return from_pieces(back, levels, width).reshape(slots, 2, fields, levels, width)


def tendency_kernel(
    state_ref,
    cx_ref,
    cy_ref,
    west_ref,
    east_ref,
    high_ref,
    low_ref,
    turn_ref,
    place_ref,
    block_ref,
    cutoff_ref,
    out_ref,
    mine_ref,
    other_ref,
    tend_ref,
    base_ref,
    sem,
):
    fields, slots, rows, levels, width = state_ref.shape

    def streamed(s):
        return pltpu.make_async_copy(base_ref.at[:, s], out_ref.at[:, s], sem.at[s])


    tiles = -(-width // LANES)
    lane = lax.broadcasted_iota(jnp.int32, (levels, LANES), 1)
    head, tail, last = lane == 0, lane == LANES - 1, lane == (width - 1) % LANES

    def load(ref, *index):
        out = []
        for t in range(tiles):
            part = ref[index + (slice(None), slice(t * LANES, min((t + 1) * LANES, width)))]
            if part.shape[1] < LANES:
                pad = jnp.zeros((levels, LANES - part.shape[1]), F32)
                part = jnp.concatenate([part, pad], axis=1)
            out.append(part)
        return out

    def one_slot(s, carry):
        west, east = west_ref[s], east_ref[s]
        for f in range(fields):
            above = None
            now = load(state_ref, f, s, 0)
            for r in range(rows):
                column = f * rows + r
                left = [pltpu.roll(x, LANES - 1, 1) for x in now]
                left = [
                    jnp.where(tail, left[t + 1], left[t])
                    if t + 1 < tiles
                    else jnp.where(last, east[:, column : column + 1], left[t])
                    for t in range(tiles)
                ]
                half = [x * 0.5 for x in load(cx_ref, s, r)]
                flux = [h * (x + y) for h, x, y in zip(half, now, left)]
                wind = west[:, fields * rows + r : fields * rows + r + 1] * 0.5
                first = wind * (west[:, column : column + 1] + now[0])
                right = [pltpu.roll(x, 1, 1) for x in flux]
                right = [jnp.where(head, y, x) for x, y in zip(right, [first] + right[:-1])]
                change = [x - y for x, y in zip(right, flux)]
                if above is not None:
                    change = [x + y for x, y in zip(change, above)]
                if r + 1 < rows:
                    later = load(state_ref, f, s, r + 1)
                    half = load(cy_ref, s, r)
                    above = [h * 0.5 * (x + y) for h, x, y in zip(half, now, later)]
                    change = [x - y for x, y in zip(change, above)]
                for t in range(tiles):
                    stop = min((t + 1) * LANES, width)
                    base = now[t] + change[t]
                    tend_ref[f, s, r, :, t * LANES : stop] = change[t][:, : stop - t * LANES]
                    base_ref[f, s, r, :, t * LANES : stop] = base[:, : stop - t * LANES]
                now = later
        streamed(s).start()
        return carry

    lax.fori_loop(0, slots, one_slot, 0)
    turn = turn_ref[place_ref[0]]
    first, second, _ = pick_slots(block_ref, cutoff_ref, rows)
    mine, other = mine_first((first, second), place_ref[1])
    for slot, spec_ref in ((other, other_ref), (mine, mine_ref)):
        spec = split_dot(
            tend_ref[:, slot].reshape(fields * rows * levels, width), high_ref[...], low_ref[...]
        )
        spec_ref[...] = turned(spec, turn, 1.0)
    for s in range(slots):
        streamed(s).wait()


def local_tendency(state, courant_x, courant_y, west, east, forward, turn, place, block, cutoff):
    fields, slots, rows, levels, width = state.shape
    count = fields * rows * levels
    spec = jax.ShapeDtypeStruct((count, 2 * KCUT), F32)
    return pl.pallas_call(
        tendency_kernel,
        in_specs=vmem(8) + smem(3),
        out_specs=[pl.BlockSpec(memory_space=pl.ANY)] + vmem(2),
        out_shape=[jax.ShapeDtypeStruct(state.shape, F32), spec, spec],
        scratch_shapes=[
            pltpu.VMEM(state.shape, F32),
            pltpu.VMEM(state.shape, F32),
            pltpu.SemaphoreType.DMA((slots,)),
        ],
        compiler_params=pltpu.CompilerParams(vmem_limit_bytes=28 * MIB),
        cost_estimate=pl.CostEstimate(
            flops=6 * count * 2 * KCUT * width * 2, bytes_accessed=9 * 10**6, transcendentals=0
        ),
        name="tendency",
    )(state, courant_x, courant_y, west, east, *forward, turn, place, block, cutoff)


def chosen_slot(i, place_ref, block_ref, cutoff_ref, rows):
    first, second, _ = pick_slots(block_ref, cutoff_ref, rows)
    return jnp.where(i == place_ref[1], first, second)


def main_kernel(
    place_ref,
    block_ref,
    cutoff_ref,
    state_ref,
    base_ref,
    mine_ref,
    away_ref,
    high_ref,
    low_ref,
    turn_ref,
    after_ref,
    out_ref,
    token_ref,
):
    fields, _, rows, levels, width = state_ref.shape
    del after_ref
    token_ref[...] = jnp.zeros_like(token_ref)
    i = pl.program_id(0)
    turn = turn_ref[place_ref[0]]
    slot = chosen_slot(i, place_ref, block_ref, cutoff_ref, rows)
    spec = turned(jnp.where(i == 0, mine_ref[...], away_ref[...]), turn, -1.0)
    spec = spec.reshape(fields, rows, levels, 2 * KCUT)
    cuts = [cutoff_ref[block_ref[slot] * rows + r] for r in range(rows)]
    spec = jnp.concatenate(
        [spec[:, r : r + 1] * row_weights(cuts[r]) for r in range(rows)], axis=1
    )
    smooth = split_dot(
        spec.reshape(fields * rows * levels, 2 * KCUT), high_ref[...], low_ref[...]
    ).reshape(fields, rows, levels, width)
    for r in range(rows):
        out_ref[:, 0, r] = jnp.where(
            cuts[r] > 0, state_ref[:, 0, r] + smooth[:, r], base_ref[:, 0, r]
        )


def main_part(after, state, base, mine, away, inverse, turn, place, block, cutoff):
    fields, slots, rows, levels, width = state.shape
    slot_block = pl.BlockSpec(
        (fields, 1, rows, levels, width),
        lambda i, *scalars: (0, chosen_slot(i, *scalars, rows), 0, 0, 0),
    )
    return pl.pallas_call(
        main_kernel,
        grid_spec=pltpu.PrefetchScalarGridSpec(
            num_scalar_prefetch=3,
            grid=(2,),
            in_specs=[slot_block, slot_block] + vmem(6),
            out_specs=[slot_block, pl.BlockSpec((1, 2 * KCUT), lambda i, *scalars: (0, 0))],
        ),
        out_shape=[
            jax.ShapeDtypeStruct(state.shape, F32),
            jax.ShapeDtypeStruct((1, 2 * KCUT), F32),
        ],
        input_output_aliases={4: 0},
        compiler_params=pltpu.CompilerParams(vmem_limit_bytes=28 * MIB),
        cost_estimate=pl.CostEstimate(
            flops=12 * mine.shape[0] * 2 * KCUT * width,
            bytes_accessed=6 * 10**6,
            transcendentals=0,
        ),
        name="main",
    )(place, block, cutoff, state, base, mine, away, *inverse, turn, after)


def unpack(ref, base, stride, put, fields, width):
    tiles = -(-width // LANES)
    for f in range(fields):
        for t in range(tiles):
            tile = ref[pl.ds(base + f * tiles + t, 8, stride=stride), :]
            stop = min((t + 1) * LANES, width)
            put(f, t * LANES, stop, tile[:, : stop - t * LANES])


def rim_kernel(
    packed,
    got_ref,
    high_ref,
    low_ref,
    turn_ref,
    place_ref,
    faces_ref,
    mine_ref,
    other_ref,
    token_ref,
):
    _, _, fields, levels, width = faces_ref.shape
    token_ref[...] = jnp.zeros_like(token_ref)
    if packed:
        for i in range(2):
            for side in range(2):

                def put(f, start, stop, tile, i=i, side=side):
                    faces_ref[i, side, f, :, start:stop] = tile

                unpack(got_ref, 64 * i + 32 * side, BACK, put, fields, width)
    else:
        faces_ref[...] = got_ref[...]
    turn = turn_ref[place_ref[0]]
    core = place_ref[1]
    both = jnp.concatenate(
        [part for i in (core, 1 - core) for part in (faces_ref[i, 0], -faces_ref[i, 1])], axis=0
    ).reshape(4 * fields * levels, width)
    spec = turned(split_dot(both, high_ref[...], low_ref[...]), turn, 1.0)
    mine_ref[...] = spec[: 2 * fields * levels]
    other_ref[...] = spec[2 * fields * levels :]


def rim_spectra(got, shape, forward, turn, place):
    _, _, fields, levels, width = shape
    spec = jax.ShapeDtypeStruct((2 * fields * levels, 2 * KCUT), F32)
    return pl.pallas_call(
        functools.partial(rim_kernel, got.ndim == 2),
        in_specs=vmem(4) + smem(1),
        out_specs=vmem(4),
        out_shape=[
            jax.ShapeDtypeStruct(shape, F32),
            spec,
            spec,
            jax.ShapeDtypeStruct((8, LANES), F32),
        ],
        compiler_params=pltpu.CompilerParams(vmem_limit_bytes=16 * MIB),
        cost_estimate=pl.CostEstimate(
            flops=24 * fields * levels * 2 * KCUT * width,
            bytes_accessed=3 * 10**6,
            transcendentals=0,
        ),
        name="rim_spectra",
    )(got, *forward, turn, place)


def final_kernel(
    packed,
    main_ref,
    pair_ref,
    back_ref,
    mine_ref,
    away_ref,
    high_ref,
    low_ref,
    turn_ref,
    place_ref,
    block_ref,
    cutoff_ref,
    out_ref,
):
    fields, slots, _, levels, width = main_ref.shape
    rows = 8
    side = pl.program_id(0)
    row = side * (rows - 1)
    turn = turn_ref[place_ref[0]]
    core = place_ref[1]
    first, second, rest = pick_slots(block_ref, cutoff_ref, rows)
    mine, other = mine_first((first, second), core)
    count = fields * levels
    part = pl.ds(pl.multiple_of(side * count, 8), count)
    sign = jnp.where(side == 0, 1.0, -1.0).astype(F32)
    if packed:

        def put(f, start, stop, tile):
            old = main_ref[f, rest, 0, :, start:stop]
            out_ref[f, rest, 0, :, start:stop] = old + tile * sign

        unpack(back_ref, 128 + 32 * side, BACK, put, fields, width)
    else:
        out_ref[:, rest, 0] = main_ref[:, rest, 0] + back_ref[side] * sign
    cuts = [cutoff_ref[block_ref[slot] * rows + row] for slot in (mine, other)]
    spec = jnp.concatenate(
        [
            turned(ref[part, :], turn, -1.0) * row_weights(cut)
            for ref, cut in ((mine_ref, cuts[0]), (away_ref, cuts[1]))
        ],
        axis=0,
    )
    smooth = split_dot(spec, high_ref[...], low_ref[...]).reshape(2, fields, levels, width)
    for i, (slot, order) in enumerate(((mine, core), (other, 1 - core))):
        out_ref[:, slot, 0] = main_ref[:, slot, 0] + jnp.where(
            cuts[i] > 0, smooth[i], pair_ref[order, side] * sign
        )


def final_part(main, pair, back, mine, away, inverse, turn, place, block, cutoff):
    fields, slots, rows, levels, width = main.shape
    block_spec = pl.BlockSpec(
        (fields, slots, 1, levels, width), lambda i: (0, 0, i * (rows - 1), 0, 0)
    )
    return pl.pallas_call(
        functools.partial(final_kernel, back.ndim == 2),
        grid=(2,),
        in_specs=[block_spec] + vmem(7) + smem(3),
        out_specs=block_spec,
        out_shape=jax.ShapeDtypeStruct(main.shape, F32),
        input_output_aliases={0: 0},
        compiler_params=pltpu.CompilerParams(vmem_limit_bytes=16 * MIB),
        cost_estimate=pl.CostEstimate(
            flops=12 * mine.shape[0] * 2 * KCUT * width,
            bytes_accessed=4 * 10**6,
            transcendentals=0,
        ),
        name="final",
    )(main, pair, back, mine, away, *inverse, turn, place, block, cutoff)


def swap(array, bit):
    size = lax.axis_size("lon")
    return lax.ppermute(array, "lon", [(i, i ^ bit) for i in range(size)])


def lon_sum(mine, other, last=None):
    total = mine + swap(other, 1)
    bit = 2
    while bit < lax.axis_size("lon"):
        total = total + swap(total, bit)
        bit *= 2
    if last is not None:
        total = total + last
    return total, swap(total, 1)


def shards(state, courant_x, courant_y, block_of_slot, face_source, cutoff):
    fields, slots, rows, levels, width = state.shape
    lat, lon = lax.axis_size("lat"), lax.axis_size("lon")
    lon_index = lax.axis_index("lon")
    place = jnp.stack([lon_index, lon_index % 2]).astype(jnp.int32)
    forward, inverse = basis_tables(width)
    turn = turn_table(lon, width)
    tables = (turn, place, block_of_slot, cutoff)

    packed = lat == levels == 8 and -(-width // LANES) * fields == 30
    if packed:
        sent = pack(state, courant_y, block_of_slot).reshape(lat, PIECE, LANES)
        got = lax.all_to_all(sent, "lat", 0, 0, tiled=True)

    west, east = edges(state, courant_x)
    west = lax.ppermute(west, "lon", [(i, (i + 1) % lon) for i in range(lon)])
    east = lax.ppermute(east, "lon", [((i + 1) % lon, i) for i in range(lon)])
    base, mine, other = local_tendency(
        state, courant_x, courant_y, west, east, forward, *tables
    )
    if packed:
        back, other = faces_of_pieces(got, slots, cutoff, other)
        back = lax.all_to_all(back.reshape(lat, BACK, LANES), "lat", 0, 0, tiled=True)
        pair = rest = back.reshape(lat * BACK, LANES)
    else:
        faces = exchange_faces(state, courant_y, face_source)
        picked = pick_slots(block_of_slot, cutoff, rows)
        pair, rest = faces[jnp.stack(picked[:2])], faces[picked[2]]
    total, away = lon_sum(mine, other)
    shape = (2, 2, fields, levels, width)
    pair, rim_mine, rim_other, token = rim_spectra(pair, shape, forward, turn, place)
    main, token = main_part(token, state, base, total, away, inverse, *tables)
    rim_total, rim_away = lon_sum(rim_mine, rim_other, token)
    return final_part(main, pair, rest, rim_total, rim_away, inverse, *tables)


def solution(mesh):
    placed = (
        P(None, "lat", None, None, "lon"),
        P("lat", None, None, "lon"),
        P("lat", None, None, "lon"),
        P("lat"),
        P("lat", None),
        P(),
    )
    return jax.shard_map(
        shards,
        mesh=mesh,
        in_specs=placed,
        out_specs=P(None, "lat", None, None, "lon"),
        check_vma=False,
    )
```

```python
import functools
import math

import jax
import jax.numpy as jnp
import numpy as np
from jax import lax
from jax.experimental import pallas as pl
from jax.experimental.pallas import tpu as pltpu
from jax.sharding import PartitionSpec as P

NLON = 2880
KCUT = 256
LANES = 128
MIB = 1024 * 1024
BF16 = jnp.bfloat16
F32 = jnp.float32


def phases(columns):
    wavenumber = np.arange(KCUT, dtype=np.int64)
    return (columns[:, None] * wavenumber[None, :] % NLON).astype(np.float64) * (
        2.0 * math.pi / NLON
    )


def basis_tables(width):
    phase = phases(np.arange(width, dtype=np.int64))
    table = np.concatenate([np.cos(phase), np.sin(phase)], axis=1).astype(np.float32)
    high = table.astype(jnp.bfloat16)
    low = (table - high.astype(np.float32)).astype(jnp.bfloat16)
    forward = (jnp.asarray(high), jnp.asarray(low))
    inverse = (
        jnp.asarray(np.ascontiguousarray(high.T)),
        jnp.asarray(np.ascontiguousarray(low.T)),
    )
    return forward, inverse


def turn_table(lon, width):
    phase = phases(np.arange(lon, dtype=np.int64) * width)
    table = np.concatenate([np.cos(phase), np.sin(phase)], axis=1).astype(np.float32)
    return jnp.asarray(table[:, None, :])


def split_dot(rows, high, low):
    rows_high = rows.astype(BF16)
    rows_low = (rows - rows_high.astype(F32)).astype(BF16)
    dot = functools.partial(jnp.dot, preferred_element_type=F32)
    return dot(rows_high, high) + (dot(rows_low, high) + dot(rows_high, low))


def turned(spec, turn, sign):
    real, imag = spec[:, :KCUT], spec[:, KCUT:]
    cos, sin = turn[:, :KCUT], turn[:, KCUT:] * sign
    return jnp.concatenate([real * cos - imag * sin, imag * cos + real * sin], axis=1)


def row_weights(cut):
    column = lax.broadcasted_iota(jnp.int32, (1, 2 * KCUT), 1)
    wavenumber = jnp.where(column >= KCUT, column - KCUT, column)
    scale = jnp.where(wavenumber == 0, 1.0 / NLON, 2.0 / NLON).astype(F32)
    return jnp.where(wavenumber < cut, scale, 0.0)


def pick_slots(block_ref, cutoff_ref, rows):
    polar1 = cutoff_ref[block_ref[1] * rows] > 0
    polar2 = cutoff_ref[block_ref[2] * rows] > 0
    rest = jnp.where(polar2, jnp.where(polar1, 0, 1), 2)
    return jnp.where(rest == 0, 1, 0), jnp.where(rest == 2, 1, 2), rest


def mine_first(pair, core):
    a, b = pair
    return jnp.where(core == 0, a, b), jnp.where(core == 0, b, a)


def vmem(count):
    return [pl.BlockSpec(memory_space=pltpu.VMEM)] * count


def smem(count):
    return [pl.BlockSpec(memory_space=pltpu.SMEM)] * count


def edge_kernel(lane_last, head_ref, tail_ref, wind_ref, west_ref, east_ref):
    fields, slots, rows = head_ref.shape[:3]
    lane = lax.broadcasted_iota(jnp.int32, (8, LANES), 1)
    for s in range(slots):
        west = jnp.zeros((8, LANES), F32)
        east = jnp.zeros((8, LANES), F32)
        for r in range(rows):
            for f in range(fields):
                here = lane == f * rows + r
                west = jnp.where(here, tail_ref[f, s, r, :, lane_last : lane_last + 1], west)
                east = jnp.where(here, head_ref[f, s, r, :, 0:1], east)
            here = lane == fields * rows + r
            west = jnp.where(here, wind_ref[s, r, :, lane_last : lane_last + 1], west)
        west_ref[s] = west
        east_ref[s] = east


def edges(state, courant_x):
    fields, slots, rows, levels, width = state.shape
    last = (width - 1) // LANES
    out = jax.ShapeDtypeStruct((slots, levels, LANES), F32)
    return pl.pallas_call(
        functools.partial(edge_kernel, (width - 1) % LANES),
        grid=(1,),
        in_specs=[
            pl.BlockSpec((fields, slots, rows, levels, LANES), lambda i: (0, 0, 0, 0, 0)),
            pl.BlockSpec((fields, slots, rows, levels, LANES), lambda i: (0, 0, 0, 0, last)),
            pl.BlockSpec((slots, rows, levels, LANES), lambda i: (0, 0, 0, last)),
        ],
        out_specs=[pl.BlockSpec((slots, levels, LANES), lambda i: (0, 0, 0))] * 2,
        out_shape=[out, out],
        cost_estimate=pl.CostEstimate(flops=10**5, bytes_accessed=1200000, transcendentals=0),
        name="edges",
    )(state, state, courant_x)


PIECE = 200
BACK = 192


def tile_of(slab, t, width):
    part = slab[:, t * LANES : min((t + 1) * LANES, width)]
    if part.shape[1] < LANES:
        part = jnp.concatenate([part, jnp.zeros((8, LANES - part.shape[1]), F32)], axis=1)
    return part


def pack_kernel(width, first_ref, last_ref, wind_ref, block_ref, out_ref):
    fields, slots = first_ref.shape[:2]
    tiles = -(-width // LANES)

    def put(row, tile):
        out_ref[pl.ds(row, 8, stride=PIECE), :] = tile

    for j in range(slots):
        half = wind_ref[j, 0] * 0.5
        for t in range(tiles):
            row = {0: 192 + 2 * j, 1: 193 + 2 * j, 2: 64 * j + 62, 3: 64 * j + 63}.get(
                t, 64 * j + 26 + t
            )
            put(row, tile_of(half, t, width))
        for f in range(fields):
            north = last_ref[f, j, 0] * half
            south = first_ref[f, j, 0]
            for t in range(tiles):
                put(64 * j + f * tiles + t, tile_of(north, t, width))
                put(64 * j + 32 + f * tiles + t, tile_of(south, t, width))
    lane = lax.broadcasted_iota(jnp.int32, (8, LANES), 1)
    table = jnp.zeros((8, LANES), F32)
    for j in range(slots):
        table = jnp.where(lane == j, block_ref[j].astype(F32), table)
    put(198, table)
    put(199, table)


def pack(state, courant_y, block):
    fields, slots, rows, levels, width = state.shape
    return pl.pallas_call(
        functools.partial(pack_kernel, width),
        grid=(1,),
        in_specs=[
            pl.BlockSpec((fields, slots, 1, levels, width), lambda i: (0, 0, 0, 0, 0)),
            pl.BlockSpec((fields, slots, 1, levels, width), lambda i: (0, 0, rows - 1, 0, 0)),
            pl.BlockSpec((slots, 1, levels, width), lambda i: (0, rows - 1, 0, 0)),
            pl.BlockSpec(memory_space=pltpu.SMEM),
        ],
        out_specs=pl.BlockSpec((levels * PIECE, LANES), lambda i: (0, 0)),
        out_shape=jax.ShapeDtypeStruct((levels * PIECE, LANES), F32),
        cost_estimate=pl.CostEstimate(flops=10**5, bytes_accessed=1700000, transcendentals=0),
        name="pack",
    )(state, state, courant_y, block)


def face_kernel(
    got_ref, cutoff_ref, later_in_ref, out_ref, later_ref, face_ref, table_ref, slot_ref, sem
):
    del later_in_ref, later_ref
    parts = got_ref.shape[0]
    slots = face_ref.shape[0] // parts
    count = parts * slots
    copy = pltpu.make_async_copy(got_ref.at[:, 192:200, :], table_ref, sem)
    copy.start()
    copy.wait()
    blocks = [table_ref[s // slots, 6, s % slots].astype(jnp.int32) for s in range(count)]
    slot_ref[0] = -1
    slot_ref[count + 1] = -1
    for s in range(count):
        slot_ref[blocks[s] + 1] = s
    for s in range(count):
        src, j = divmod(s, slots)
        south = slot_ref[blocks[s] + 2]
        safe = jnp.maximum(south, 0)
        from_src = lax.div(safe, slots)
        from_slot = safe - from_src * slots
        half = jnp.concatenate(
            [
                got_ref[src, 192 + 2 * j : 194 + 2 * j, :],
                got_ref[src, 64 * j + 62 : 64 * j + 64, :],
                got_ref[src, 64 * j + 30 : 64 * j + 32, :],
            ],
            axis=0,
        )
        half = jnp.concatenate([half] * 5 + [half[:2]], axis=0)
        other = got_ref[from_src, pl.ds(pl.multiple_of(64 * from_slot + 32, 32), 32), :]
        face = got_ref[src, 64 * j : 64 * j + 32, :] + half * other
        face_ref[s] = jnp.where(south >= 0, face, 0.0)
    for d in range(parts):
        first, second, rest = pick_slots(blocks[slots * d : slots * d + slots], cutoff_ref, 8)
        for i, slot in enumerate((first, second, rest)):
            out = out_ref.at[d, i]
            block = jnp.where(
                slot == 0,
                blocks[slots * d],
                jnp.where(slot == 1, blocks[slots * d + 1], blocks[slots * d + 2]),
            )
            north = slot_ref[block]
            out[0] = jnp.where(north >= 0, face_ref[jnp.maximum(north, 0)], 0.0)
            out[1] = face_ref[slots * d + slot]


def faces_of_pieces(got, slots, cutoff, later):
    parts = got.shape[0]
    return pl.pallas_call(
        face_kernel,
        in_specs=vmem(1) + smem(1) + [pl.BlockSpec(memory_space=pl.ANY)],
        out_specs=vmem(1) + [pl.BlockSpec(memory_space=pl.ANY)],
        out_shape=[
            jax.ShapeDtypeStruct((parts, slots, 2, 32, LANES), F32),
            jax.ShapeDtypeStruct(later.shape, F32),
        ],
        input_output_aliases={2: 1},
        scratch_shapes=[
            pltpu.VMEM((parts * slots, 32, LANES), F32),
            pltpu.SMEM((parts, 8, LANES), F32),
            pltpu.SMEM((parts * slots + 2,), jnp.int32),
            pltpu.SemaphoreType.DMA(()),
        ],
        cost_estimate=pl.CostEstimate(flops=10**5, bytes_accessed=1600000, transcendentals=0),
        name="faces",
    )(got, cutoff, later)


def to_pieces(units, parts):
    count, levels, width = units.shape
    groups = math.gcd(parts, levels)
    chunks = parts // groups
    span = -(-width // chunks)
    units = jnp.pad(units, ((0, 0), (0, 0), (0, span * chunks - width)))
    units = units.reshape(count, groups, levels // groups, chunks, span)
    return units.transpose(1, 3, 0, 2, 4).reshape(parts, count, levels // groups * span)


def from_pieces(pieces, levels, width):
    parts, count, _ = pieces.shape
    groups = math.gcd(parts, levels)
    chunks = parts // groups
    span = -(-width // chunks)
    pieces = pieces.reshape(groups, chunks, count, levels // groups, span)
    return pieces.transpose(2, 0, 3, 1, 4).reshape(count, levels, chunks * span)[:, :, :width]


def exchange_faces(state, courant_y, face_source):
    fields, slots, rows, levels, width = state.shape
    lat = lax.axis_size("lat")
    count = 2 * fields + 1
    first = state[:, :, 0].transpose(1, 0, 2, 3)
    last = state[:, :, rows - 1].transpose(1, 0, 2, 3)
    half = courant_y[:, rows - 1][:, None] * 0.5
    units = jnp.concatenate([first, last * half, half], axis=1)
    sent = to_pieces(units.reshape(slots * count, levels, width), lat)
    span = sent.shape[2]
    table = jnp.pad(
        face_source.astype(F32).reshape(1, slots * 2), ((0, 0), (0, span - slots * 2))
    )
    sent = jnp.concatenate([sent, jnp.broadcast_to(table[None], (lat, 1, span))], axis=1)
    got = lax.all_to_all(sent, "lat", 0, 0, tiled=True)
    indices = got[:, slots * count, : slots * 2].reshape(lat * slots, 2).astype(jnp.int32)
    data = got[:, : slots * count].reshape(lat * slots, count, span)
    north, south = indices[:, 0], indices[:, 1]
    face = data[:, fields : 2 * fields] + data[:, 2 * fields :] * data[
        jnp.maximum(south, 0), :fields
    ]
    face = jnp.where((south >= 0)[:, None, None], face, 0.0)
    face_north = jnp.where((north >= 0)[:, None, None], face[jnp.maximum(north, 0)], 0.0)
    back = jnp.concatenate([face_north, face], axis=1).reshape(lat, slots * 2 * fields, span)
    back = lax.all_to_all(back, "lat", 0, 0, tiled=True)
    return from_pieces(back, levels, width).reshape(slots, 2, fields, levels, width)


def tendency_kernel(
    state_ref,
    cx_ref,
    cy_ref,
    west_ref,
    east_ref,
    high_ref,
    low_ref,
    turn_ref,
    place_ref,
    block_ref,
    cutoff_ref,
    out_ref,
    mine_ref,
    other_ref,
    tend_ref,
    base_ref,
    sem,
):
    fields, slots, rows, levels, width = state_ref.shape

    def streamed(s):
        return pltpu.make_async_copy(base_ref.at[:, s], out_ref.at[:, s], sem.at[s])


    tiles = -(-width // LANES)
    lane = lax.broadcasted_iota(jnp.int32, (levels, LANES), 1)
    head, tail, last = lane == 0, lane == LANES - 1, lane == (width - 1) % LANES

    def load(ref, *index):
        out = []
        for t in range(tiles):
            part = ref[index + (slice(None), slice(t * LANES, min((t + 1) * LANES, width)))]
            if part.shape[1] < LANES:
                pad = jnp.zeros((levels, LANES - part.shape[1]), F32)
                part = jnp.concatenate([part, pad], axis=1)
            out.append(part)
        return out

    def one_slot(s, carry):
        west, east = west_ref[s], east_ref[s]
        for f in range(fields):
            above = None
            now = load(state_ref, f, s, 0)
            for r in range(rows):
                column = f * rows + r
                left = [pltpu.roll(x, LANES - 1, 1) for x in now]
                left = [
                    jnp.where(tail, left[t + 1], left[t])
                    if t + 1 < tiles
                    else jnp.where(last, east[:, column : column + 1], left[t])
                    for t in range(tiles)
                ]
                half = [x * 0.5 for x in load(cx_ref, s, r)]
                flux = [h * (x + y) for h, x, y in zip(half, now, left)]
                wind = west[:, fields * rows + r : fields * rows + r + 1] * 0.5
                first = wind * (west[:, column : column + 1] + now[0])
                right = [pltpu.roll(x, 1, 1) for x in flux]
                right = [jnp.where(head, y, x) for x, y in zip(right, [first] + right[:-1])]
                change = [x - y for x, y in zip(right, flux)]
                if above is not None:
                    change = [x + y for x, y in zip(change, above)]
                if r + 1 < rows:
                    later = load(state_ref, f, s, r + 1)
                    half = load(cy_ref, s, r)
                    above = [h * 0.5 * (x + y) for h, x, y in zip(half, now, later)]
                    change = [x - y for x, y in zip(change, above)]
                for t in range(tiles):
                    stop = min((t + 1) * LANES, width)
                    base = now[t] + change[t]
                    tend_ref[f, s, r, :, t * LANES : stop] = change[t][:, : stop - t * LANES]
                    base_ref[f, s, r, :, t * LANES : stop] = base[:, : stop - t * LANES]
                now = later
        streamed(s).start()
        return carry

    lax.fori_loop(0, slots, one_slot, 0)
    turn = turn_ref[place_ref[0]]
    first, second, _ = pick_slots(block_ref, cutoff_ref, rows)
    mine, other = mine_first((first, second), place_ref[1])
    for slot, spec_ref in ((other, other_ref), (mine, mine_ref)):
        spec = split_dot(
            tend_ref[:, slot].reshape(fields * rows * levels, width), high_ref[...], low_ref[...]
        )
        spec_ref[...] = turned(spec, turn, 1.0)
    for s in range(slots):
        streamed(s).wait()


def local_tendency(state, courant_x, courant_y, west, east, forward, turn, place, block, cutoff):
    fields, slots, rows, levels, width = state.shape
    count = fields * rows * levels
    spec = jax.ShapeDtypeStruct((count, 2 * KCUT), F32)
    return pl.pallas_call(
        tendency_kernel,
        in_specs=vmem(8) + smem(3),
        out_specs=[pl.BlockSpec(memory_space=pl.ANY)] + vmem(2),
        out_shape=[jax.ShapeDtypeStruct(state.shape, F32), spec, spec],
        scratch_shapes=[
            pltpu.VMEM(state.shape, F32),
            pltpu.VMEM(state.shape, F32),
            pltpu.SemaphoreType.DMA((slots,)),
        ],
        compiler_params=pltpu.CompilerParams(vmem_limit_bytes=58 * MIB),
        cost_estimate=pl.CostEstimate(
            flops=6 * count * 2 * KCUT * width * 2, bytes_accessed=9 * 10**6, transcendentals=0
        ),
        name="tendency",
    )(state, courant_x, courant_y, west, east, *forward, turn, place, block, cutoff)


def chosen_slot(i, place_ref, block_ref, cutoff_ref, rows):
    first, second, _ = pick_slots(block_ref, cutoff_ref, rows)
    return jnp.where(i == place_ref[1], first, second)


def main_kernel(
    place_ref,
    block_ref,
    cutoff_ref,
    state_ref,
    base_ref,
    mine_ref,
    away_ref,
    high_ref,
    low_ref,
    turn_ref,
    after_ref,
    out_ref,
    token_ref,
):
    fields, _, rows, levels, width = state_ref.shape
    del after_ref
    token_ref[...] = jnp.zeros_like(token_ref)
    i = pl.program_id(0)
    turn = turn_ref[place_ref[0]]
    slot = chosen_slot(i, place_ref, block_ref, cutoff_ref, rows)
    spec = turned(jnp.where(i == 0, mine_ref[...], away_ref[...]), turn, -1.0)
    spec = spec.reshape(fields, rows, levels, 2 * KCUT)
    cuts = [cutoff_ref[block_ref[slot] * rows + r] for r in range(rows)]
    spec = jnp.concatenate(
        [spec[:, r : r + 1] * row_weights(cuts[r]) for r in range(rows)], axis=1
    )
    smooth = split_dot(
        spec.reshape(fields * rows * levels, 2 * KCUT), high_ref[...], low_ref[...]
    ).reshape(fields, rows, levels, width)
    for r in range(rows):
        out_ref[:, 0, r] = jnp.where(
            cuts[r] > 0, state_ref[:, 0, r] + smooth[:, r], base_ref[:, 0, r]
        )


def main_part(after, state, base, mine, away, inverse, turn, place, block, cutoff):
    fields, slots, rows, levels, width = state.shape
    slot_block = pl.BlockSpec(
        (fields, 1, rows, levels, width),
        lambda i, *scalars: (0, chosen_slot(i, *scalars, rows), 0, 0, 0),
    )
    return pl.pallas_call(
        main_kernel,
        grid_spec=pltpu.PrefetchScalarGridSpec(
            num_scalar_prefetch=3,
            grid=(2,),
            in_specs=[slot_block, slot_block] + vmem(6),
            out_specs=[slot_block, pl.BlockSpec((1, 2 * KCUT), lambda i, *scalars: (0, 0))],
        ),
        out_shape=[
            jax.ShapeDtypeStruct(state.shape, F32),
            jax.ShapeDtypeStruct((1, 2 * KCUT), F32),
        ],
        input_output_aliases={4: 0},
        compiler_params=pltpu.CompilerParams(vmem_limit_bytes=58 * MIB),
        cost_estimate=pl.CostEstimate(
            flops=12 * mine.shape[0] * 2 * KCUT * width,
            bytes_accessed=6 * 10**6,
            transcendentals=0,
        ),
        name="main",
    )(place, block, cutoff, state, base, mine, away, *inverse, turn, after)


def unpack(ref, base, stride, put, fields, width):
    tiles = -(-width // LANES)
    for f in range(fields):
        for t in range(tiles):
            tile = ref[pl.ds(base + f * tiles + t, 8, stride=stride), :]
            stop = min((t + 1) * LANES, width)
            put(f, t * LANES, stop, tile[:, : stop - t * LANES])


def rim_kernel(
    packed,
    got_ref,
    high_ref,
    low_ref,
    turn_ref,
    place_ref,
    faces_ref,
    mine_ref,
    other_ref,
    token_ref,
):
    _, _, fields, levels, width = faces_ref.shape
    token_ref[...] = jnp.zeros_like(token_ref)
    if packed:
        for i in range(2):
            for side in range(2):

                def put(f, start, stop, tile, i=i, side=side):
                    faces_ref[i, side, f, :, start:stop] = tile

                unpack(got_ref, 64 * i + 32 * side, BACK, put, fields, width)
    else:
        faces_ref[...] = got_ref[...]
    turn = turn_ref[place_ref[0]]
    core = place_ref[1]
    both = jnp.concatenate(
        [part for i in (core, 1 - core) for part in (faces_ref[i, 0], -faces_ref[i, 1])], axis=0
    ).reshape(4 * fields * levels, width)
    spec = turned(split_dot(both, high_ref[...], low_ref[...]), turn, 1.0)
    mine_ref[...] = spec[: 2 * fields * levels]
    other_ref[...] = spec[2 * fields * levels :]


def rim_spectra(got, shape, forward, turn, place):
    _, _, fields, levels, width = shape
    spec = jax.ShapeDtypeStruct((2 * fields * levels, 2 * KCUT), F32)
    return pl.pallas_call(
        functools.partial(rim_kernel, got.ndim == 2),
        in_specs=vmem(4) + smem(1),
        out_specs=vmem(4),
        out_shape=[
            jax.ShapeDtypeStruct(shape, F32),
            spec,
            spec,
            jax.ShapeDtypeStruct((8, LANES), F32),
        ],
        compiler_params=pltpu.CompilerParams(vmem_limit_bytes=58 * MIB),
        cost_estimate=pl.CostEstimate(
            flops=24 * fields * levels * 2 * KCUT * width,
            bytes_accessed=3 * 10**6,
            transcendentals=0,
        ),
        name="rim_spectra",
    )(got, *forward, turn, place)


def final_kernel(
    packed,
    main_ref,
    pair_ref,
    back_ref,
    mine_ref,
    away_ref,
    high_ref,
    low_ref,
    turn_ref,
    place_ref,
    block_ref,
    cutoff_ref,
    out_ref,
):
    fields, slots, _, levels, width = main_ref.shape
    rows = 8
    side = pl.program_id(0)
    row = side * (rows - 1)
    turn = turn_ref[place_ref[0]]
    core = place_ref[1]
    first, second, rest = pick_slots(block_ref, cutoff_ref, rows)
    mine, other = mine_first((first, second), core)
    count = fields * levels
    part = pl.ds(pl.multiple_of(side * count, 8), count)
    sign = jnp.where(side == 0, 1.0, -1.0).astype(F32)
    if packed:

        def put(f, start, stop, tile):
            old = main_ref[f, rest, 0, :, start:stop]
            out_ref[f, rest, 0, :, start:stop] = old + tile * sign

        unpack(back_ref, 128 + 32 * side, BACK, put, fields, width)
    else:
        out_ref[:, rest, 0] = main_ref[:, rest, 0] + back_ref[side] * sign
    cuts = [cutoff_ref[block_ref[slot] * rows + row] for slot in (mine, other)]
    spec = jnp.concatenate(
        [
            turned(ref[part, :], turn, -1.0) * row_weights(cut)
            for ref, cut in ((mine_ref, cuts[0]), (away_ref, cuts[1]))
        ],
        axis=0,
    )
    smooth = split_dot(spec, high_ref[...], low_ref[...]).reshape(2, fields, levels, width)
    for i, (slot, order) in enumerate(((mine, core), (other, 1 - core))):
        out_ref[:, slot, 0] = main_ref[:, slot, 0] + jnp.where(
            cuts[i] > 0, smooth[i], pair_ref[order, side] * sign
        )


def final_part(main, pair, back, mine, away, inverse, turn, place, block, cutoff):
    fields, slots, rows, levels, width = main.shape
    block_spec = pl.BlockSpec(
        (fields, slots, 1, levels, width), lambda i: (0, 0, i * (rows - 1), 0, 0)
    )
    return pl.pallas_call(
        functools.partial(final_kernel, back.ndim == 2),
        grid=(2,),
        in_specs=[block_spec] + vmem(7) + smem(3),
        out_specs=block_spec,
        out_shape=jax.ShapeDtypeStruct(main.shape, F32),
        input_output_aliases={0: 0},
        compiler_params=pltpu.CompilerParams(vmem_limit_bytes=58 * MIB),
        cost_estimate=pl.CostEstimate(
            flops=12 * mine.shape[0] * 2 * KCUT * width,
            bytes_accessed=4 * 10**6,
            transcendentals=0,
        ),
        name="final",
    )(main, pair, back, mine, away, *inverse, turn, place, block, cutoff)


def swap(array, bit):
    size = lax.axis_size("lon")
    return lax.ppermute(array, "lon", [(i, i ^ bit) for i in range(size)])


def lon_sum(mine, other, last=None):
    total = mine + swap(other, 1)
    bit = 2
    while bit < lax.axis_size("lon"):
        total = total + swap(total, bit)
        bit *= 2
    if last is not None:
        total = total + last
    return total, swap(total, 1)


def shards(state, courant_x, courant_y, block_of_slot, face_source, cutoff):
    fields, slots, rows, levels, width = state.shape
    lat, lon = lax.axis_size("lat"), lax.axis_size("lon")
    lon_index = lax.axis_index("lon")
    place = jnp.stack([lon_index, lon_index % 2]).astype(jnp.int32)
    forward, inverse = basis_tables(width)
    turn = turn_table(lon, width)
    tables = (turn, place, block_of_slot, cutoff)

    packed = lat == levels == 8 and -(-width // LANES) * fields == 30
    if packed:
        sent = pack(state, courant_y, block_of_slot).reshape(lat, PIECE, LANES)
        got = lax.all_to_all(sent, "lat", 0, 0, tiled=True)

    west, east = edges(state, courant_x)
    west = lax.ppermute(west, "lon", [(i, (i + 1) % lon) for i in range(lon)])
    east = lax.ppermute(east, "lon", [((i + 1) % lon, i) for i in range(lon)])
    base, mine, other = local_tendency(
        state, courant_x, courant_y, west, east, forward, *tables
    )
    if packed:
        back, other = faces_of_pieces(got, slots, cutoff, other)
        back = lax.all_to_all(back.reshape(lat, BACK, LANES), "lat", 0, 0, tiled=True)
        pair = rest = back.reshape(lat * BACK, LANES)
    else:
        faces = exchange_faces(state, courant_y, face_source)
        picked = pick_slots(block_of_slot, cutoff, rows)
        pair, rest = faces[jnp.stack(picked[:2])], faces[picked[2]]
    total, away = lon_sum(mine, other)
    shape = (2, 2, fields, levels, width)
    pair, rim_mine, rim_other, token = rim_spectra(pair, shape, forward, turn, place)
    main, token = main_part(token, state, base, total, away, inverse, *tables)
    rim_total, rim_away = lon_sum(rim_mine, rim_other, token)
    return final_part(main, pair, rest, rim_total, rim_away, inverse, *tables)


def solution(mesh):
    placed = (
        P(None, "lat", None, None, "lon"),
        P("lat", None, None, "lon"),
        P("lat", None, None, "lon"),
        P("lat"),
        P("lat", None),
        P(),
    )
    return jax.shard_map(
        shards,
        mesh=mesh,
        in_specs=placed,
        out_specs=P(None, "lat", None, None, "lon"),
        check_vma=False,
    )
```

```python
import functools
import math

import jax
import jax.numpy as jnp
import numpy as np
from jax import lax
from jax.experimental import pallas as pl
from jax.experimental.pallas import tpu as pltpu
from jax.sharding import PartitionSpec as P

NLON = 2880
KCUT = 256
LANES = 128
VMEM_LIMIT = 50 * 1024 * 1024
BF16 = jnp.bfloat16
F32 = jnp.float32


def phases(columns):
    wavenumber = np.arange(KCUT, dtype=np.int64)
    return (columns[:, None] * wavenumber[None, :] % NLON).astype(np.float64) * (
        2.0 * math.pi / NLON
    )


def basis_tables(width):
    phase = phases(np.arange(width, dtype=np.int64))
    table = np.concatenate([np.cos(phase), np.sin(phase)], axis=1).astype(np.float32)
    high = table.astype(jnp.bfloat16)
    low = (table - high.astype(np.float32)).astype(jnp.bfloat16)
    forward = (jnp.asarray(high), jnp.asarray(low))
    inverse = (
        jnp.asarray(np.ascontiguousarray(high.T)),
        jnp.asarray(np.ascontiguousarray(low.T)),
    )
    return forward, inverse


def turn_table(lon, width):
    phase = phases(np.arange(lon, dtype=np.int64) * width)
    table = np.concatenate([np.cos(phase), np.sin(phase)], axis=1).astype(np.float32)
    return jnp.asarray(table[:, None, :])


def split_dot(rows, high, low):
    rows_high = rows.astype(BF16)
    rows_low = (rows - rows_high.astype(F32)).astype(BF16)
    dot = functools.partial(jnp.dot, preferred_element_type=F32)
    return dot(rows_high, high) + (dot(rows_low, high) + dot(rows_high, low))


def turned(spec, turn, sign):
    real, imag = spec[:, :KCUT], spec[:, KCUT:]
    cos, sin = turn[:, :KCUT], turn[:, KCUT:] * sign
    return jnp.concatenate([real * cos - imag * sin, imag * cos + real * sin], axis=1)


def row_weights(cut):
    column = lax.broadcasted_iota(jnp.int32, (1, 2 * KCUT), 1)
    wavenumber = jnp.where(column >= KCUT, column - KCUT, column)
    scale = jnp.where(wavenumber == 0, 1.0 / NLON, 2.0 / NLON).astype(F32)
    return jnp.where(wavenumber < cut, scale, 0.0)


def pick_slots(block_ref, cutoff_ref, rows):
    polar1 = cutoff_ref[block_ref[1] * rows] > 0
    polar2 = cutoff_ref[block_ref[2] * rows] > 0
    rest = jnp.where(polar2, jnp.where(polar1, 0, 1), 2)
    return jnp.where(rest == 0, 1, 0), jnp.where(rest == 2, 1, 2), rest


def mine_first(pair, core):
    a, b = pair
    return jnp.where(core == 0, a, b), jnp.where(core == 0, b, a)


def vmem(count):
    return [pl.BlockSpec(memory_space=pltpu.VMEM)] * count


def smem(count):
    return [pl.BlockSpec(memory_space=pltpu.SMEM)] * count


def edge_kernel(lane_last, head_ref, tail_ref, wind_ref, west_ref, east_ref):
    fields, slots, rows = head_ref.shape[:3]
    lane = lax.broadcasted_iota(jnp.int32, (8, LANES), 1)
    for s in range(slots):
        west = jnp.zeros((8, LANES), F32)
        east = jnp.zeros((8, LANES), F32)
        for r in range(rows):
            for f in range(fields):
                here = lane == f * rows + r
                west = jnp.where(here, tail_ref[f, s, r, :, lane_last : lane_last + 1], west)
                east = jnp.where(here, head_ref[f, s, r, :, 0:1], east)
            here = lane == fields * rows + r
            west = jnp.where(here, wind_ref[s, r, :, lane_last : lane_last + 1], west)
        west_ref[s] = west
        east_ref[s] = east


def edges(state, courant_x):
    fields, slots, rows, levels, width = state.shape
    last = (width - 1) // LANES
    out = jax.ShapeDtypeStruct((slots, levels, LANES), F32)
    return pl.pallas_call(
        functools.partial(edge_kernel, (width - 1) % LANES),
        grid=(1,),
        in_specs=[
            pl.BlockSpec((fields, slots, rows, levels, LANES), lambda i: (0, 0, 0, 0, 0)),
            pl.BlockSpec((fields, slots, rows, levels, LANES), lambda i: (0, 0, 0, 0, last)),
            pl.BlockSpec((slots, rows, levels, LANES), lambda i: (0, 0, 0, last)),
        ],
        out_specs=[pl.BlockSpec((slots, levels, LANES), lambda i: (0, 0, 0))] * 2,
        out_shape=[out, out],
        cost_estimate=pl.CostEstimate(flops=10**5, bytes_accessed=1200000, transcendentals=0),
        name="edges",
    )(state, state, courant_x)


PIECE = 200
BACK = 192


def tile_of(slab, t, width):
    part = slab[:, t * LANES : min((t + 1) * LANES, width)]
    if part.shape[1] < LANES:
        part = jnp.concatenate([part, jnp.zeros((8, LANES - part.shape[1]), F32)], axis=1)
    return part


def pack_kernel(width, first_ref, last_ref, wind_ref, block_ref, out_ref):
    fields, slots = first_ref.shape[:2]
    tiles = -(-width // LANES)

    def put(row, tile):
        out_ref[pl.ds(row, 8, stride=PIECE), :] = tile

    for j in range(slots):
        half = wind_ref[j, 0] * 0.5
        for t in range(tiles):
            row = {0: 192 + 2 * j, 1: 193 + 2 * j, 2: 64 * j + 62, 3: 64 * j + 63}.get(
                t, 64 * j + 26 + t
            )
            put(row, tile_of(half, t, width))
        for f in range(fields):
            north = last_ref[f, j, 0] * half
            south = first_ref[f, j, 0]
            for t in range(tiles):
                put(64 * j + f * tiles + t, tile_of(north, t, width))
                put(64 * j + 32 + f * tiles + t, tile_of(south, t, width))
    lane = lax.broadcasted_iota(jnp.int32, (8, LANES), 1)
    table = jnp.zeros((8, LANES), F32)
    for j in range(slots):
        table = jnp.where(lane == j, block_ref[j].astype(F32), table)
    put(198, table)
    put(199, table)


def pack(state, courant_y, block):
    fields, slots, rows, levels, width = state.shape
    return pl.pallas_call(
        functools.partial(pack_kernel, width),
        grid=(1,),
        in_specs=[
            pl.BlockSpec((fields, slots, 1, levels, width), lambda i: (0, 0, 0, 0, 0)),
            pl.BlockSpec((fields, slots, 1, levels, width), lambda i: (0, 0, rows - 1, 0, 0)),
            pl.BlockSpec((slots, 1, levels, width), lambda i: (0, rows - 1, 0, 0)),
            pl.BlockSpec(memory_space=pltpu.SMEM),
        ],
        out_specs=pl.BlockSpec((levels * PIECE, LANES), lambda i: (0, 0)),
        out_shape=jax.ShapeDtypeStruct((levels * PIECE, LANES), F32),
        cost_estimate=pl.CostEstimate(flops=10**5, bytes_accessed=1700000, transcendentals=0),
        name="pack",
    )(state, state, courant_y, block)


def face_kernel(
    got_ref,
    cutoff_ref,
    place_ref,
    high_ref,
    low_ref,
    turn_ref,
    out_ref,
    own_ref,
    one_ref,
    two_ref,
    three_ref,
    pick_ref,
    face_ref,
    dense_ref,
    spec_ref,
    table_ref,
    slot_ref,
    sem,
):
    width = high_ref.shape[0]
    parts = got_ref.shape[0]
    slots = face_ref.shape[0] // parts
    count = parts * slots
    copy = pltpu.make_async_copy(got_ref.at[:, 192:200, :], table_ref, sem)
    copy.start()
    copy.wait()
    blocks = [table_ref[s // slots, 6, s % slots].astype(jnp.int32) for s in range(count)]
    slot_ref[0] = -1
    slot_ref[count + 1] = -1
    for s in range(count):
        slot_ref[blocks[s] + 1] = s
    for s in range(count):
        src, j = divmod(s, slots)
        south = slot_ref[blocks[s] + 2]
        safe = jnp.maximum(south, 0)
        from_src = lax.div(safe, slots)
        from_slot = safe - from_src * slots
        half = jnp.concatenate(
            [
                got_ref[src, 192 + 2 * j : 194 + 2 * j, :],
                got_ref[src, 64 * j + 62 : 64 * j + 64, :],
                got_ref[src, 64 * j + 30 : 64 * j + 32, :],
            ],
            axis=0,
        )
        half = jnp.concatenate([half] * 5 + [half[:2]], axis=0)
        other = got_ref[from_src, pl.ds(pl.multiple_of(64 * from_slot + 32, 32), 32), :]
        face = got_ref[src, 64 * j : 64 * j + 32, :] + half * other
        face = jnp.where(south >= 0, face, 0.0)
        face_ref[s] = face
        dense_ref[30 * s : 30 * s + 30] = face[:30]
    for d in range(parts):
        first, second, rest = pick_slots(blocks[slots * d : slots * d + slots], cutoff_ref, 8)
        for i, slot in enumerate((first, second, rest)):
            out = out_ref.at[d, i]
            own = slots * d + slot
            block = jnp.where(
                slot == 0,
                blocks[slots * d],
                jnp.where(slot == 1, blocks[slots * d + 1], blocks[slots * d + 2]),
            )
            north = slot_ref[block]
            out[0] = jnp.where(north >= 0, face_ref[jnp.maximum(north, 0)], 0.0)
            out[1] = face_ref[own]
            if i < 2:
                pick_ref[4 * d + 2 * i] = north
                pick_ref[4 * d + 2 * i + 1] = own
    rows = count * 5
    tiles = [dense_ref[pl.ds(t, rows, stride=6), :] for t in range(6)]
    spec = split_dot(jnp.concatenate(tiles, axis=1)[:, :width], high_ref[...], low_ref[...])
    spec = turned(spec, turn_ref[place_ref[0]], 1.0)
    for q in range(4):
        spec_ref[q] = spec[:, q * LANES : (q + 1) * LANES]
    for k, ref in enumerate((own_ref, one_ref, two_ref, three_ref)):
        ref[...] = spec_ref[place_ref[0] ^ k]


def faces_of_pieces(got, slots, cutoff, place, forward, turn):
    parts = got.shape[0]
    rows = parts * slots * 5
    return pl.pallas_call(
        face_kernel,
        in_specs=vmem(1) + smem(2) + vmem(3),
        out_specs=vmem(5) + smem(1),
        out_shape=[jax.ShapeDtypeStruct((parts, slots, 2, 32, LANES), F32)]
        + [jax.ShapeDtypeStruct((rows, LANES), F32)] * 4
        + [jax.ShapeDtypeStruct((parts * 4,), jnp.int32)],
        scratch_shapes=[
            pltpu.VMEM((parts * slots, 32, LANES), F32),
            pltpu.VMEM((parts * slots * 30, LANES), F32),
            pltpu.VMEM((4, rows, LANES), F32),
            pltpu.SMEM((parts, 8, LANES), F32),
            pltpu.SMEM((parts * slots + 2,), jnp.int32),
            pltpu.SemaphoreType.DMA(()),
        ],
        compiler_params=pltpu.CompilerParams(vmem_limit_bytes=VMEM_LIMIT),
        cost_estimate=pl.CostEstimate(
            flops=12 * rows * KCUT * 720, bytes_accessed=3 * 10**6, transcendentals=0
        ),
        name="faces",
    )(got, cutoff, place, *forward, turn)


def select_kernel(own_ref, one_ref, two_ref, three_ref, pick_ref, out_ref, held_ref):
    parts = out_ref.shape[0]
    total = (own_ref[...] + one_ref[...]) + (two_ref[...] + three_ref[...])
    for s in range(held_ref.shape[0]):
        held_ref[s, :5] = total[5 * s : 5 * s + 5]
    for d in range(parts):
        for i in range(4):
            face = pick_ref[4 * d + i]
            rows = held_ref[jnp.maximum(face, 0), :5]
            out_ref[d, 5 * i : 5 * i + 5] = jnp.where(face >= 0, rows, 0.0)
        out_ref[d, 20:24] = jnp.zeros((4, LANES), F32)


def select_spectra(quarters, pick, parts):
    count = quarters[0].shape[0] // 5
    return pl.pallas_call(
        select_kernel,
        in_specs=vmem(4) + smem(1),
        out_specs=vmem(1)[0],
        out_shape=jax.ShapeDtypeStruct((parts, 24, LANES), F32),
        scratch_shapes=[pltpu.VMEM((count, 8, LANES), F32)],
        cost_estimate=pl.CostEstimate(flops=10**5, bytes_accessed=400000, transcendentals=0),
        name="select",
    )(*quarters, pick)


def to_pieces(units, parts):
    count, levels, width = units.shape
    groups = math.gcd(parts, levels)
    chunks = parts // groups
    span = -(-width // chunks)
    units = jnp.pad(units, ((0, 0), (0, 0), (0, span * chunks - width)))
    units = units.reshape(count, groups, levels // groups, chunks, span)
    return units.transpose(1, 3, 0, 2, 4).reshape(parts, count, levels // groups * span)


def from_pieces(pieces, levels, width):
    parts, count, _ = pieces.shape
    groups = math.gcd(parts, levels)
    chunks = parts // groups
    span = -(-width // chunks)
    pieces = pieces.reshape(groups, chunks, count, levels // groups, span)
    return pieces.transpose(2, 0, 3, 1, 4).reshape(count, levels, chunks * span)[:, :, :width]


def exchange_faces(state, courant_y, face_source):
    fields, slots, rows, levels, width = state.shape
    lat = lax.axis_size("lat")
    count = 2 * fields + 1
    first = state[:, :, 0].transpose(1, 0, 2, 3)
    last = state[:, :, rows - 1].transpose(1, 0, 2, 3)
    half = courant_y[:, rows - 1][:, None] * 0.5
    units = jnp.concatenate([first, last * half, half], axis=1)
    sent = to_pieces(units.reshape(slots * count, levels, width), lat)
    span = sent.shape[2]
    table = jnp.pad(
        face_source.astype(F32).reshape(1, slots * 2), ((0, 0), (0, span - slots * 2))
    )
    sent = jnp.concatenate([sent, jnp.broadcast_to(table[None], (lat, 1, span))], axis=1)
    got = lax.all_to_all(sent, "lat", 0, 0, tiled=True)
    indices = got[:, slots * count, : slots * 2].reshape(lat * slots, 2).astype(jnp.int32)
    data = got[:, : slots * count].reshape(lat * slots, count, span)
    north, south = indices[:, 0], indices[:, 1]
    face = data[:, fields : 2 * fields] + data[:, 2 * fields :] * data[
        jnp.maximum(south, 0), :fields
    ]
    face = jnp.where((south >= 0)[:, None, None], face, 0.0)
    face_north = jnp.where((north >= 0)[:, None, None], face[jnp.maximum(north, 0)], 0.0)
    back = jnp.concatenate([face_north, face], axis=1).reshape(lat, slots * 2 * fields, span)
    back = lax.all_to_all(back, "lat", 0, 0, tiled=True)
    return from_pieces(back, levels, width).reshape(slots, 2, fields, levels, width)


def tendency_kernel(
    state_ref,
    cx_ref,
    cy_ref,
    west_ref,
    east_ref,
    high_ref,
    low_ref,
    turn_ref,
    place_ref,
    block_ref,
    cutoff_ref,
    out_ref,
    mine_ref,
    other_ref,
    tend_ref,
    base_ref,
    sem,
):
    fields, slots, rows, levels, width = state_ref.shape

    def streamed(s):
        return pltpu.make_async_copy(base_ref.at[:, s], out_ref.at[:, s], sem.at[s])


    tiles = -(-width // LANES)
    lane = lax.broadcasted_iota(jnp.int32, (levels, LANES), 1)
    head, tail, last = lane == 0, lane == LANES - 1, lane == (width - 1) % LANES

    def load(ref, *index):
        out = []
        for t in range(tiles):
            part = ref[index + (slice(None), slice(t * LANES, min((t + 1) * LANES, width)))]
            if part.shape[1] < LANES:
                pad = jnp.zeros((levels, LANES - part.shape[1]), F32)
                part = jnp.concatenate([part, pad], axis=1)
            out.append(part)
        return out

    def one_slot(s, carry):
        west, east = west_ref[s], east_ref[s]
        for f in range(fields):
            above = None
            now = load(state_ref, f, s, 0)
            for r in range(rows):
                column = f * rows + r
                left = [pltpu.roll(x, LANES - 1, 1) for x in now]
                left = [
                    jnp.where(tail, left[t + 1], left[t])
                    if t + 1 < tiles
                    else jnp.where(last, east[:, column : column + 1], left[t])
                    for t in range(tiles)
                ]
                half = [x * 0.5 for x in load(cx_ref, s, r)]
                flux = [h * (x + y) for h, x, y in zip(half, now, left)]
                wind = west[:, fields * rows + r : fields * rows + r + 1] * 0.5
                first = wind * (west[:, column : column + 1] + now[0])
                right = [pltpu.roll(x, 1, 1) for x in flux]
                right = [jnp.where(head, y, x) for x, y in zip(right, [first] + right[:-1])]
                change = [x - y for x, y in zip(right, flux)]
                if above is not None:
                    change = [x + y for x, y in zip(change, above)]
                if r + 1 < rows:
                    later = load(state_ref, f, s, r + 1)
                    half = load(cy_ref, s, r)
                    above = [h * 0.5 * (x + y) for h, x, y in zip(half, now, later)]
                    change = [x - y for x, y in zip(change, above)]
                for t in range(tiles):
                    stop = min((t + 1) * LANES, width)
                    base = now[t] + change[t]
                    tend_ref[f, s, r, :, t * LANES : stop] = change[t][:, : stop - t * LANES]
                    base_ref[f, s, r, :, t * LANES : stop] = base[:, : stop - t * LANES]
                now = later
        streamed(s).start()
        return carry

    lax.fori_loop(0, slots, one_slot, 0)
    turn = turn_ref[place_ref[0]]
    first, second, _ = pick_slots(block_ref, cutoff_ref, rows)
    mine, other = mine_first((first, second), place_ref[1])
    for slot, spec_ref in ((other, other_ref), (mine, mine_ref)):
        spec = split_dot(
            tend_ref[:, slot].reshape(fields * rows * levels, width), high_ref[...], low_ref[...]
        )
        spec_ref[...] = turned(spec, turn, 1.0)
    for s in range(slots):
        streamed(s).wait()


def local_tendency(state, courant_x, courant_y, west, east, forward, turn, place, block, cutoff):
    fields, slots, rows, levels, width = state.shape
    count = fields * rows * levels
    spec = jax.ShapeDtypeStruct((count, 2 * KCUT), F32)
    return pl.pallas_call(
        tendency_kernel,
        in_specs=vmem(8) + smem(3),
        out_specs=[pl.BlockSpec(memory_space=pl.ANY)] + vmem(2),
        out_shape=[jax.ShapeDtypeStruct(state.shape, F32), spec, spec],
        scratch_shapes=[
            pltpu.VMEM(state.shape, F32),
            pltpu.VMEM(state.shape, F32),
            pltpu.SemaphoreType.DMA((slots,)),
        ],
        compiler_params=pltpu.CompilerParams(vmem_limit_bytes=VMEM_LIMIT),
        cost_estimate=pl.CostEstimate(
            flops=6 * count * 2 * KCUT * width * 2, bytes_accessed=9 * 10**6, transcendentals=0
        ),
        name="tendency",
    )(state, courant_x, courant_y, west, east, *forward, turn, place, block, cutoff)


def chosen_slot(i, place_ref, block_ref, cutoff_ref, rows):
    first, second, _ = pick_slots(block_ref, cutoff_ref, rows)
    return jnp.where(i == place_ref[1], first, second)


def main_kernel(
    place_ref,
    block_ref,
    cutoff_ref,
    state_ref,
    base_ref,
    mine_ref,
    away_ref,
    high_ref,
    low_ref,
    turn_ref,
    out_ref,
):
    fields, _, rows, levels, width = state_ref.shape
    i = pl.program_id(0)
    turn = turn_ref[place_ref[0]]
    slot = chosen_slot(i, place_ref, block_ref, cutoff_ref, rows)
    spec = turned(jnp.where(i == 0, mine_ref[...], away_ref[...]), turn, -1.0)
    spec = spec.reshape(fields, rows, levels, 2 * KCUT)
    cuts = [cutoff_ref[block_ref[slot] * rows + r] for r in range(rows)]
    spec = jnp.concatenate(
        [spec[:, r : r + 1] * row_weights(cuts[r]) for r in range(rows)], axis=1
    )
    smooth = split_dot(
        spec.reshape(fields * rows * levels, 2 * KCUT), high_ref[...], low_ref[...]
    ).reshape(fields, rows, levels, width)
    for r in range(rows):
        out_ref[:, 0, r] = jnp.where(
            cuts[r] > 0, state_ref[:, 0, r] + smooth[:, r], base_ref[:, 0, r]
        )


def main_part(state, base, mine, away, inverse, turn, place, block, cutoff):
    fields, slots, rows, levels, width = state.shape
    slot_block = pl.BlockSpec(
        (fields, 1, rows, levels, width),
        lambda i, *scalars: (0, chosen_slot(i, *scalars, rows), 0, 0, 0),
    )
    return pl.pallas_call(
        main_kernel,
        grid_spec=pltpu.PrefetchScalarGridSpec(
            num_scalar_prefetch=3,
            grid=(2,),
            in_specs=[slot_block, slot_block] + vmem(5),
            out_specs=slot_block,
        ),
        out_shape=jax.ShapeDtypeStruct(state.shape, F32),
        input_output_aliases={4: 0},
        compiler_params=pltpu.CompilerParams(vmem_limit_bytes=VMEM_LIMIT),
        cost_estimate=pl.CostEstimate(
            flops=12 * mine.shape[0] * 2 * KCUT * width,
            bytes_accessed=6 * 10**6,
            transcendentals=0,
        ),
        name="main",
    )(place, block, cutoff, state, base, mine, away, *inverse, turn)


def unpack(ref, base, stride, put, fields, width):
    tiles = -(-width // LANES)
    for f in range(fields):
        for t in range(tiles):
            tile = ref[pl.ds(base + f * tiles + t, 8, stride=stride), :]
            stop = min((t + 1) * LANES, width)
            put(f, t * LANES, stop, tile[:, : stop - t * LANES])


def final_kernel(
    main_ref,
    back_ref,
    own_ref,
    one_ref,
    two_ref,
    three_ref,
    high_ref,
    low_ref,
    turn_ref,
    place_ref,
    block_ref,
    cutoff_ref,
    out_ref,
    faces_ref,
    spec_ref,
):
    fields, slots, _, levels, width = main_ref.shape
    rows = 8
    side = pl.program_id(0)
    row = side * (rows - 1)
    turn = turn_ref[place_ref[0]]
    first, second, rest = pick_slots(block_ref, cutoff_ref, rows)
    sign = jnp.where(side == 0, 1.0, -1.0).astype(F32)
    for i in range(slots):

        def put(f, start, stop, tile, i=i):
            faces_ref[i, f, :, start:stop] = tile * sign

        unpack(back_ref, 64 * i + 32 * side, BACK, put, fields, width)
    for k, ref in enumerate((own_ref, one_ref, two_ref, three_ref)):
        quarter = place_ref[0] ^ k
        for i in range(2):
            for f in range(fields):
                start = (i * fields + f) * levels
                spec_ref[quarter, start : start + levels] = ref[
                    pl.ds((2 * i + side) * fields + f, levels, stride=24), :
                ]
    cuts = [cutoff_ref[block_ref[slot] * rows + row] for slot in (first, second)]
    spec = turned(jnp.concatenate([spec_ref[q] for q in range(4)], axis=1), turn, -1.0)
    half = fields * levels
    spec = jnp.concatenate(
        [spec[i * half : (i + 1) * half] * (row_weights(cuts[i]) * sign) for i in range(2)], axis=0
    )
    smooth = split_dot(spec, high_ref[...], low_ref[...]).reshape(2, fields, levels, width)
    for i, slot in enumerate((first, second)):
        out_ref[:, slot, 0] = main_ref[:, slot, 0] + jnp.where(
            cuts[i] > 0, smooth[i], faces_ref[i]
        )
    out_ref[:, rest, 0] = main_ref[:, rest, 0] + faces_ref[2]


def final_part(main, back, quarters, inverse, turn, place, block, cutoff):
    fields, slots, rows, levels, width = main.shape
    block_spec = pl.BlockSpec(
        (fields, slots, 1, levels, width), lambda i: (0, 0, i * (rows - 1), 0, 0)
    )
    return pl.pallas_call(
        final_kernel,
        grid=(2,),
        in_specs=[block_spec] + vmem(8) + smem(3),
        out_specs=block_spec,
        out_shape=jax.ShapeDtypeStruct(main.shape, F32),
        input_output_aliases={0: 0},
        scratch_shapes=[
            pltpu.VMEM((slots, fields, levels, width), F32),
            pltpu.VMEM((4, 2 * fields * levels, LANES), F32),
        ],
        compiler_params=pltpu.CompilerParams(vmem_limit_bytes=VMEM_LIMIT),
        cost_estimate=pl.CostEstimate(
            flops=48 * fields * levels * 2 * KCUT * width,
            bytes_accessed=4 * 10**6,
            transcendentals=0,
        ),
        name="final",
    )(main, back, *quarters, *inverse, turn, place, block, cutoff)


def final_plain(main, faces, forward, turn, lon_index, block, cutoff):
    fields, slots, rows, levels, width = main.shape
    picked = pick_slots(block, cutoff, rows)
    faces = faces[jnp.stack(picked)] * jnp.array([1.0, -1.0], F32)[None, :, None, None, None]
    basis = forward[0].astype(F32) + forward[1].astype(F32)
    dot = functools.partial(jnp.dot, precision=lax.Precision.HIGH, preferred_element_type=F32)
    spec = turned(dot(faces[:2].reshape(-1, width), basis), turn[lon_index], 1.0)
    spec = turned(lax.psum(spec, "lon"), turn[lon_index], -1.0)
    cuts = [[cutoff[block[slot] * rows + row] for row in (0, rows - 1)] for slot in picked[:2]]
    weights = jnp.stack([row_weights(cut)[0] for pair in cuts for cut in pair])
    spec = spec.reshape(4, fields * levels, 2 * KCUT) * weights[:, None]
    smooth = dot(spec.reshape(-1, 2 * KCUT), basis.T).reshape((2,) + faces.shape[1:])
    for i, slot in enumerate(picked):
        for j, row in enumerate((0, rows - 1)):
            part = jnp.where(cuts[i][j] > 0, smooth[i, j], faces[i, j]) if i < 2 else faces[i, j]
            main = main.at[:, slot, row].add(part)
    return main


def swap(array, bit):
    size = lax.axis_size("lon")
    return lax.ppermute(array, "lon", [(i, i ^ bit) for i in range(size)])


def lon_sum(mine, other):
    total = mine + swap(other, 1)
    bit = 2
    while bit < lax.axis_size("lon"):
        total = total + swap(total, bit)
        bit *= 2
    return total, swap(total, 1)


def shards(state, courant_x, courant_y, block_of_slot, face_source, cutoff):
    fields, slots, rows, levels, width = state.shape
    lat, lon = lax.axis_size("lat"), lax.axis_size("lon")
    lon_index = lax.axis_index("lon")
    place = jnp.stack([lon_index, lon_index % 2]).astype(jnp.int32)
    forward, inverse = basis_tables(width)
    turn = turn_table(lon, width)
    tables = (turn, place, block_of_slot, cutoff)

    packed = lat == levels == 8 and lon == 4 and -(-width // LANES) == 6 and fields == 5
    if packed:
        sent = pack(state, courant_y, block_of_slot).reshape(lat, PIECE, LANES)
        got = lax.all_to_all(sent, "lat", 0, 0, tiled=True)

    west, east = edges(state, courant_x)
    west = lax.ppermute(west, "lon", [(i, (i + 1) % lon) for i in range(lon)])
    east = lax.ppermute(east, "lon", [((i + 1) % lon, i) for i in range(lon)])
    base, mine, other = local_tendency(
        state, courant_x, courant_y, west, east, forward, *tables
    )
    total, away = lon_sum(mine, other)
    main = main_part(state, base, total, away, inverse, *tables)

    if not packed:
        faces = exchange_faces(state, courant_y, face_source)
        return final_plain(main, faces, forward, turn, lon_index, block_of_slot, cutoff)
    back, *quarters, pick = faces_of_pieces(got, slots, cutoff, place, forward, turn)
    quarters = [quarters[0]] + [swap(quarters[k], k) for k in range(1, 4)]
    back = lax.all_to_all(back.reshape(lat, BACK, LANES), "lat", 0, 0, tiled=True)
    chosen = select_spectra(quarters, pick, lat)
    chosen = lax.all_to_all(chosen, "lat", 0, 0, tiled=True).reshape(lat * 24, LANES)
    quarters = [chosen] + [swap(chosen, k) for k in range(1, 4)]
    return final_part(main, back.reshape(lat * BACK, LANES), quarters, inverse, *tables)


def solution(mesh):
    placed = (
        P(None, "lat", None, None, "lon"),
        P("lat", None, None, "lon"),
        P("lat", None, None, "lon"),
        P("lat"),
        P("lat", None),
        P(),
    )
    return jax.shard_map(
        shards,
        mesh=mesh,
        in_specs=placed,
        out_specs=P(None, "lat", None, None, "lon"),
        check_vma=False,
    )
```

```python
import functools
import math

import jax
import jax.numpy as jnp
import numpy as np
from jax import lax
from jax.experimental import pallas as pl
from jax.experimental.pallas import tpu as pltpu
from jax.sharding import PartitionSpec as P

NLON = 2880
KCUT = 256
LANES = 128
MIB = 1024 * 1024
BF16 = jnp.bfloat16
F32 = jnp.float32


def phases(columns):
    wavenumber = np.arange(KCUT, dtype=np.int64)
    return (columns[:, None] * wavenumber[None, :] % NLON).astype(np.float64) * (
        2.0 * math.pi / NLON
    )


def basis_tables(width):
    phase = phases(np.arange(width, dtype=np.int64))
    table = np.concatenate([np.cos(phase), np.sin(phase)], axis=1).astype(np.float32)
    high = table.astype(jnp.bfloat16)
    low = (table - high.astype(np.float32)).astype(jnp.bfloat16)
    forward = (jnp.asarray(high), jnp.asarray(low))
    inverse = (
        jnp.asarray(np.ascontiguousarray(high.T)),
        jnp.asarray(np.ascontiguousarray(low.T)),
    )
    return forward, inverse


def turn_table(lon, width):
    phase = phases(np.arange(lon, dtype=np.int64) * width)
    table = np.concatenate([np.cos(phase), np.sin(phase)], axis=1).astype(np.float32)
    return jnp.asarray(table[:, None, :])


def split_dot(rows, high, low):
    rows_high = rows.astype(BF16)
    rows_low = (rows - rows_high.astype(F32)).astype(BF16)
    dot = functools.partial(jnp.dot, preferred_element_type=F32)
    return dot(rows_high, high) + (dot(rows_low, high) + dot(rows_high, low))


def turned(spec, turn, sign):
    real, imag = spec[:, :KCUT], spec[:, KCUT:]
    cos, sin = turn[:, :KCUT], turn[:, KCUT:] * sign
    return jnp.concatenate([real * cos - imag * sin, imag * cos + real * sin], axis=1)


def row_weights(cut):
    column = lax.broadcasted_iota(jnp.int32, (1, 2 * KCUT), 1)
    wavenumber = jnp.where(column >= KCUT, column - KCUT, column)
    scale = jnp.where(wavenumber == 0, 1.0 / NLON, 2.0 / NLON).astype(F32)
    return jnp.where(wavenumber < cut, scale, 0.0)


def pick_slots(block_ref, cutoff_ref, rows):
    polar1 = cutoff_ref[block_ref[1] * rows] > 0
    polar2 = cutoff_ref[block_ref[2] * rows] > 0
    rest = jnp.where(polar2, jnp.where(polar1, 0, 1), 2)
    return jnp.where(rest == 0, 1, 0), jnp.where(rest == 2, 1, 2), rest


def mine_first(pair, core):
    a, b = pair
    return jnp.where(core == 0, a, b), jnp.where(core == 0, b, a)


def vmem(count):
    return [pl.BlockSpec(memory_space=pltpu.VMEM)] * count


def smem(count):
    return [pl.BlockSpec(memory_space=pltpu.SMEM)] * count


def edge_kernel(lane_last, head_ref, tail_ref, wind_ref, west_ref, east_ref):
    fields, slots, rows = head_ref.shape[:3]
    lane = lax.broadcasted_iota(jnp.int32, (8, LANES), 1)
    for s in range(slots):
        west = jnp.zeros((8, LANES), F32)
        east = jnp.zeros((8, LANES), F32)
        for r in range(rows):
            for f in range(fields):
                here = lane == f * rows + r
                west = jnp.where(here, tail_ref[f, s, r, :, lane_last : lane_last + 1], west)
                east = jnp.where(here, head_ref[f, s, r, :, 0:1], east)
            here = lane == fields * rows + r
            west = jnp.where(here, wind_ref[s, r, :, lane_last : lane_last + 1], west)
        west_ref[s] = west
        east_ref[s] = east


def edges(state, courant_x):
    fields, slots, rows, levels, width = state.shape
    last = (width - 1) // LANES
    out = jax.ShapeDtypeStruct((slots, levels, LANES), F32)
    return pl.pallas_call(
        functools.partial(edge_kernel, (width - 1) % LANES),
        grid=(1,),
        in_specs=[
            pl.BlockSpec((fields, slots, rows, levels, LANES), lambda i: (0, 0, 0, 0, 0)),
            pl.BlockSpec((fields, slots, rows, levels, LANES), lambda i: (0, 0, 0, 0, last)),
            pl.BlockSpec((slots, rows, levels, LANES), lambda i: (0, 0, 0, last)),
        ],
        out_specs=[pl.BlockSpec((slots, levels, LANES), lambda i: (0, 0, 0))] * 2,
        out_shape=[out, out],
        cost_estimate=pl.CostEstimate(flops=10**5, bytes_accessed=1200000, transcendentals=0),
        name="edges",
    )(state, state, courant_x)


PIECE = 200
BACK = 184


def tile_of(slab, t, width):
    part = slab[:, t * LANES : min((t + 1) * LANES, width)]
    if part.shape[1] < LANES:
        part = jnp.concatenate([part, jnp.zeros((8, LANES - part.shape[1]), F32)], axis=1)
    return part


def pack_kernel(width, first_ref, last_ref, wind_ref, block_ref, out_ref):
    fields, slots = first_ref.shape[:2]
    tiles = -(-width // LANES)

    def put(row, tile):
        out_ref[pl.ds(row, 8, stride=PIECE), :] = tile

    for j in range(slots):
        half = wind_ref[j, 0] * 0.5
        for t in range(tiles):
            row = {0: 192 + 2 * j, 1: 193 + 2 * j, 2: 64 * j + 62, 3: 64 * j + 63}.get(
                t, 64 * j + 26 + t
            )
            put(row, tile_of(half, t, width))
        for f in range(fields):
            north = last_ref[f, j, 0] * half
            south = first_ref[f, j, 0]
            for t in range(tiles):
                put(64 * j + f * tiles + t, tile_of(north, t, width))
                put(64 * j + 32 + f * tiles + t, tile_of(south, t, width))
    lane = lax.broadcasted_iota(jnp.int32, (8, LANES), 1)
    table = jnp.zeros((8, LANES), F32)
    for j in range(slots):
        table = jnp.where(lane == j, block_ref[j].astype(F32), table)
    put(198, table)
    put(199, table)


def pack(state, courant_y, block):
    fields, slots, rows, levels, width = state.shape
    return pl.pallas_call(
        functools.partial(pack_kernel, width),
        grid=(1,),
        in_specs=[
            pl.BlockSpec((fields, slots, 1, levels, width), lambda i: (0, 0, 0, 0, 0)),
            pl.BlockSpec((fields, slots, 1, levels, width), lambda i: (0, 0, rows - 1, 0, 0)),
            pl.BlockSpec((slots, 1, levels, width), lambda i: (0, rows - 1, 0, 0)),
            pl.BlockSpec(memory_space=pltpu.SMEM),
        ],
        out_specs=pl.BlockSpec((levels * PIECE, LANES), lambda i: (0, 0)),
        out_shape=jax.ShapeDtypeStruct((levels * PIECE, LANES), F32),
        cost_estimate=pl.CostEstimate(flops=10**5, bytes_accessed=1700000, transcendentals=0),
        name="pack",
    )(state, state, courant_y, block)


def face_kernel(
    got_ref, cutoff_ref, later_in_ref, out_ref, later_ref, face_ref, table_ref, slot_ref, sem
):
    del later_in_ref, later_ref
    parts = got_ref.shape[0]
    slots = face_ref.shape[0] // parts
    count = parts * slots
    copy = pltpu.make_async_copy(got_ref.at[:, 192:200, :], table_ref, sem)
    copy.start()
    copy.wait()
    blocks = [table_ref[s // slots, 6, s % slots].astype(jnp.int32) for s in range(count)]
    slot_ref[0] = -1
    slot_ref[count + 1] = -1
    for s in range(count):
        slot_ref[blocks[s] + 1] = s
    for s in range(count):
        src, j = divmod(s, slots)
        south = slot_ref[blocks[s] + 2]
        safe = jnp.maximum(south, 0)
        from_src = lax.div(safe, slots)
        from_slot = safe - from_src * slots
        half = jnp.concatenate(
            [
                got_ref[src, 192 + 2 * j : 194 + 2 * j, :],
                got_ref[src, 64 * j + 62 : 64 * j + 64, :],
                got_ref[src, 64 * j + 30 : 64 * j + 32, :],
            ],
            axis=0,
        )
        half = jnp.concatenate([half] * 5 + [half[:2]], axis=0)
        other = got_ref[from_src, pl.ds(pl.multiple_of(64 * from_slot + 32, 32), 32), :]
        face = got_ref[src, 64 * j : 64 * j + 32, :] + half * other
        face_ref[s] = jnp.where(south >= 0, face, 0.0)
    for d in range(parts):
        first, second, rest = pick_slots(blocks[slots * d : slots * d + slots], cutoff_ref, 8)
        for i, slot in enumerate((first, second, rest)):
            row = 60 * i
            block = jnp.where(
                slot == 0,
                blocks[slots * d],
                jnp.where(slot == 1, blocks[slots * d + 1], blocks[slots * d + 2]),
            )
            north = slot_ref[block]
            out_ref[d, row : row + 30] = jnp.where(
                north >= 0, face_ref[jnp.maximum(north, 0), :30], 0.0
            )
            out_ref[d, row + 30 : row + 60] = face_ref[slots * d + slot, :30]
        out_ref[d, 180:184] = jnp.zeros((4, LANES), F32)


def faces_of_pieces(got, slots, cutoff, later):
    parts = got.shape[0]
    return pl.pallas_call(
        face_kernel,
        in_specs=vmem(1) + smem(1) + [pl.BlockSpec(memory_space=pl.ANY)],
        out_specs=vmem(1) + [pl.BlockSpec(memory_space=pl.ANY)],
        out_shape=[
            jax.ShapeDtypeStruct((parts, BACK, LANES), F32),
            jax.ShapeDtypeStruct(later.shape, F32),
        ],
        input_output_aliases={2: 1},
        scratch_shapes=[
            pltpu.VMEM((parts * slots, 32, LANES), F32),
            pltpu.SMEM((parts, 8, LANES), F32),
            pltpu.SMEM((parts * slots + 2,), jnp.int32),
            pltpu.SemaphoreType.DMA(()),
        ],
        cost_estimate=pl.CostEstimate(flops=10**5, bytes_accessed=1600000, transcendentals=0),
        name="faces",
    )(got, cutoff, later)


def to_pieces(units, parts):
    count, levels, width = units.shape
    groups = math.gcd(parts, levels)
    chunks = parts // groups
    span = -(-width // chunks)
    units = jnp.pad(units, ((0, 0), (0, 0), (0, span * chunks - width)))
    units = units.reshape(count, groups, levels // groups, chunks, span)
    return units.transpose(1, 3, 0, 2, 4).reshape(parts, count, levels // groups * span)


def from_pieces(pieces, levels, width):
    parts, count, _ = pieces.shape
    groups = math.gcd(parts, levels)
    chunks = parts // groups
    span = -(-width // chunks)
    pieces = pieces.reshape(groups, chunks, count, levels // groups, span)
    return pieces.transpose(2, 0, 3, 1, 4).reshape(count, levels, chunks * span)[:, :, :width]


def exchange_faces(state, courant_y, face_source):
    fields, slots, rows, levels, width = state.shape
    lat = lax.axis_size("lat")
    count = 2 * fields + 1
    first = state[:, :, 0].transpose(1, 0, 2, 3)
    last = state[:, :, rows - 1].transpose(1, 0, 2, 3)
    half = courant_y[:, rows - 1][:, None] * 0.5
    units = jnp.concatenate([first, last * half, half], axis=1)
    sent = to_pieces(units.reshape(slots * count, levels, width), lat)
    span = sent.shape[2]
    table = jnp.pad(
        face_source.astype(F32).reshape(1, slots * 2), ((0, 0), (0, span - slots * 2))
    )
    sent = jnp.concatenate([sent, jnp.broadcast_to(table[None], (lat, 1, span))], axis=1)
    got = lax.all_to_all(sent, "lat", 0, 0, tiled=True)
    indices = got[:, slots * count, : slots * 2].reshape(lat * slots, 2).astype(jnp.int32)
    data = got[:, : slots * count].reshape(lat * slots, count, span)
    north, south = indices[:, 0], indices[:, 1]
    face = data[:, fields : 2 * fields] + data[:, 2 * fields :] * data[
        jnp.maximum(south, 0), :fields
    ]
    face = jnp.where((south >= 0)[:, None, None], face, 0.0)
    face_north = jnp.where((north >= 0)[:, None, None], face[jnp.maximum(north, 0)], 0.0)
    back = jnp.concatenate([face_north, face], axis=1).reshape(lat, slots * 2 * fields, span)
    back = lax.all_to_all(back, "lat", 0, 0, tiled=True)
    return from_pieces(back, levels, width).reshape(slots, 2, fields, levels, width)


def tendency_kernel(
    state_ref,
    cx_ref,
    cy_ref,
    west_ref,
    east_ref,
    high_ref,
    low_ref,
    turn_ref,
    place_ref,
    block_ref,
    cutoff_ref,
    out_ref,
    mine_ref,
    other_ref,
    tend_ref,
    base_ref,
    sem,
):
    fields, slots, rows, levels, width = state_ref.shape

    def streamed(s):
        return pltpu.make_async_copy(base_ref.at[:, s], out_ref.at[:, s], sem.at[s])


    tiles = -(-width // LANES)
    lane = lax.broadcasted_iota(jnp.int32, (levels, LANES), 1)
    head, tail, last = lane == 0, lane == LANES - 1, lane == (width - 1) % LANES

    def load(ref, *index):
        out = []
        for t in range(tiles):
            part = ref[index + (slice(None), slice(t * LANES, min((t + 1) * LANES, width)))]
            if part.shape[1] < LANES:
                pad = jnp.zeros((levels, LANES - part.shape[1]), F32)
                part = jnp.concatenate([part, pad], axis=1)
            out.append(part)
        return out

    def one_slot(s, carry):
        west, east = west_ref[s], east_ref[s]
        for f in range(fields):
            above = None
            now = load(state_ref, f, s, 0)
            for r in range(rows):
                column = f * rows + r
                left = [pltpu.roll(x, LANES - 1, 1) for x in now]
                left = [
                    jnp.where(tail, left[t + 1], left[t])
                    if t + 1 < tiles
                    else jnp.where(last, east[:, column : column + 1], left[t])
                    for t in range(tiles)
                ]
                half = [x * 0.5 for x in load(cx_ref, s, r)]
                flux = [h * (x + y) for h, x, y in zip(half, now, left)]
                wind = west[:, fields * rows + r : fields * rows + r + 1] * 0.5
                first = wind * (west[:, column : column + 1] + now[0])
                right = [pltpu.roll(x, 1, 1) for x in flux]
                right = [jnp.where(head, y, x) for x, y in zip(right, [first] + right[:-1])]
                change = [x - y for x, y in zip(right, flux)]
                if above is not None:
                    change = [x + y for x, y in zip(change, above)]
                if r + 1 < rows:
                    later = load(state_ref, f, s, r + 1)
                    half = load(cy_ref, s, r)
                    above = [h * 0.5 * (x + y) for h, x, y in zip(half, now, later)]
                    change = [x - y for x, y in zip(change, above)]
                for t in range(tiles):
                    stop = min((t + 1) * LANES, width)
                    base = now[t] + change[t]
                    tend_ref[f, s, r, :, t * LANES : stop] = change[t][:, : stop - t * LANES]
                    base_ref[f, s, r, :, t * LANES : stop] = base[:, : stop - t * LANES]
                now = later
        streamed(s).start()
        return carry

    lax.fori_loop(0, slots, one_slot, 0)
    turn = turn_ref[place_ref[0]]
    first, second, _ = pick_slots(block_ref, cutoff_ref, rows)
    mine, other = mine_first((first, second), place_ref[1])
    for slot, spec_ref in ((other, other_ref), (mine, mine_ref)):
        spec = split_dot(
            tend_ref[:, slot].reshape(fields * rows * levels, width), high_ref[...], low_ref[...]
        )
        spec_ref[...] = turned(spec, turn, 1.0)
    for s in range(slots):
        streamed(s).wait()


def local_tendency(state, courant_x, courant_y, west, east, forward, turn, place, block, cutoff):
    fields, slots, rows, levels, width = state.shape
    count = fields * rows * levels
    spec = jax.ShapeDtypeStruct((count, 2 * KCUT), F32)
    return pl.pallas_call(
        tendency_kernel,
        in_specs=vmem(8) + smem(3),
        out_specs=[pl.BlockSpec(memory_space=pl.ANY)] + vmem(2),
        out_shape=[jax.ShapeDtypeStruct(state.shape, F32), spec, spec],
        scratch_shapes=[
            pltpu.VMEM(state.shape, F32),
            pltpu.VMEM(state.shape, F32),
            pltpu.SemaphoreType.DMA((slots,)),
        ],
        compiler_params=pltpu.CompilerParams(vmem_limit_bytes=50 * MIB),
        cost_estimate=pl.CostEstimate(
            flops=6 * count * 2 * KCUT * width * 2, bytes_accessed=9 * 10**6, transcendentals=0
        ),
        name="tendency",
    )(state, courant_x, courant_y, west, east, *forward, turn, place, block, cutoff)


def chosen_slot(i, place_ref, block_ref, cutoff_ref, rows):
    first, second, _ = pick_slots(block_ref, cutoff_ref, rows)
    return jnp.where(i == place_ref[1], first, second)


def main_kernel(
    place_ref,
    block_ref,
    cutoff_ref,
    state_ref,
    base_ref,
    mine_ref,
    away_ref,
    high_ref,
    low_ref,
    turn_ref,
    after_ref,
    out_ref,
    token_ref,
):
    fields, _, rows, levels, width = state_ref.shape
    del after_ref
    token_ref[...] = jnp.zeros_like(token_ref)
    i = pl.program_id(0)
    turn = turn_ref[place_ref[0]]
    slot = chosen_slot(i, place_ref, block_ref, cutoff_ref, rows)
    spec = turned(jnp.where(i == 0, mine_ref[...], away_ref[...]), turn, -1.0)
    spec = spec.reshape(fields, rows, levels, 2 * KCUT)
    cuts = [cutoff_ref[block_ref[slot] * rows + r] for r in range(rows)]
    spec = jnp.concatenate(
        [spec[:, r : r + 1] * row_weights(cuts[r]) for r in range(rows)], axis=1
    )
    smooth = split_dot(
        spec.reshape(fields * rows * levels, 2 * KCUT), high_ref[...], low_ref[...]
    ).reshape(fields, rows, levels, width)
    for r in range(rows):
        out_ref[:, 0, r] = jnp.where(
            cuts[r] > 0, state_ref[:, 0, r] + smooth[:, r], base_ref[:, 0, r]
        )


def main_part(after, state, base, mine, away, inverse, turn, place, block, cutoff):
    fields, slots, rows, levels, width = state.shape
    slot_block = pl.BlockSpec(
        (fields, 1, rows, levels, width),
        lambda i, *scalars: (0, chosen_slot(i, *scalars, rows), 0, 0, 0),
    )
    return pl.pallas_call(
        main_kernel,
        grid_spec=pltpu.PrefetchScalarGridSpec(
            num_scalar_prefetch=3,
            grid=(2,),
            in_specs=[slot_block, slot_block] + vmem(6),
            out_specs=[slot_block, pl.BlockSpec((1, 2 * KCUT), lambda i, *scalars: (0, 0))],
        ),
        out_shape=[
            jax.ShapeDtypeStruct(state.shape, F32),
            jax.ShapeDtypeStruct((1, 2 * KCUT), F32),
        ],
        input_output_aliases={4: 0},
        compiler_params=pltpu.CompilerParams(vmem_limit_bytes=50 * MIB),
        cost_estimate=pl.CostEstimate(
            flops=12 * mine.shape[0] * 2 * KCUT * width,
            bytes_accessed=6 * 10**6,
            transcendentals=0,
        ),
        name="main",
    )(place, block, cutoff, state, base, mine, away, *inverse, turn, after)


def unpack(ref, base, stride, put, fields, width):
    tiles = -(-width // LANES)
    for f in range(fields):
        for t in range(tiles):
            tile = ref[pl.ds(base + f * tiles + t, 8, stride=stride), :]
            stop = min((t + 1) * LANES, width)
            put(f, t * LANES, stop, tile[:, : stop - t * LANES])


def rim_kernel(
    packed,
    got_ref,
    high_ref,
    low_ref,
    turn_ref,
    place_ref,
    faces_ref,
    mine_ref,
    other_ref,
    token_ref,
):
    _, _, fields, levels, width = faces_ref.shape
    token_ref[...] = jnp.zeros_like(token_ref)
    if packed:
        for i in range(2):
            for side in range(2):

                def put(f, start, stop, tile, i=i, side=side):
                    faces_ref[i, side, f, :, start:stop] = tile

                unpack(got_ref, 60 * i + 30 * side, BACK, put, fields, width)
    else:
        faces_ref[...] = got_ref[...]
    turn = turn_ref[place_ref[0]]
    core = place_ref[1]
    both = jnp.concatenate(
        [part for i in (core, 1 - core) for part in (faces_ref[i, 0], -faces_ref[i, 1])], axis=0
    ).reshape(4 * fields * levels, width)
    spec = turned(split_dot(both, high_ref[...], low_ref[...]), turn, 1.0)
    mine_ref[...] = spec[: 2 * fields * levels]
    other_ref[...] = spec[2 * fields * levels :]


def rim_spectra(got, shape, forward, turn, place):
    _, _, fields, levels, width = shape
    spec = jax.ShapeDtypeStruct((2 * fields * levels, 2 * KCUT), F32)
    return pl.pallas_call(
        functools.partial(rim_kernel, got.ndim == 2),
        in_specs=vmem(4) + smem(1),
        out_specs=vmem(4),
        out_shape=[
            jax.ShapeDtypeStruct(shape, F32),
            spec,
            spec,
            jax.ShapeDtypeStruct((8, LANES), F32),
        ],
        compiler_params=pltpu.CompilerParams(vmem_limit_bytes=50 * MIB),
        cost_estimate=pl.CostEstimate(
            flops=24 * fields * levels * 2 * KCUT * width,
            bytes_accessed=3 * 10**6,
            transcendentals=0,
        ),
        name="rim_spectra",
    )(got, *forward, turn, place)


def final_kernel(
    packed,
    main_ref,
    pair_ref,
    back_ref,
    mine_ref,
    away_ref,
    high_ref,
    low_ref,
    turn_ref,
    place_ref,
    block_ref,
    cutoff_ref,
    out_ref,
):
    fields, slots, _, levels, width = main_ref.shape
    rows = 8
    side = pl.program_id(0)
    row = side * (rows - 1)
    turn = turn_ref[place_ref[0]]
    core = place_ref[1]
    first, second, rest = pick_slots(block_ref, cutoff_ref, rows)
    mine, other = mine_first((first, second), core)
    count = fields * levels
    part = pl.ds(pl.multiple_of(side * count, 8), count)
    sign = jnp.where(side == 0, 1.0, -1.0).astype(F32)
    if packed:

        def put(f, start, stop, tile):
            old = main_ref[f, rest, 0, :, start:stop]
            out_ref[f, rest, 0, :, start:stop] = old + tile * sign

        unpack(back_ref, 120 + 30 * side, BACK, put, fields, width)
    else:
        out_ref[:, rest, 0] = main_ref[:, rest, 0] + back_ref[side] * sign
    cuts = [cutoff_ref[block_ref[slot] * rows + row] for slot in (mine, other)]
    spec = jnp.concatenate(
        [
            turned(ref[part, :], turn, -1.0) * row_weights(cut)
            for ref, cut in ((mine_ref, cuts[0]), (away_ref, cuts[1]))
        ],
        axis=0,
    )
    smooth = split_dot(spec, high_ref[...], low_ref[...]).reshape(2, fields, levels, width)
    for i, (slot, order) in enumerate(((mine, core), (other, 1 - core))):
        out_ref[:, slot, 0] = main_ref[:, slot, 0] + jnp.where(
            cuts[i] > 0, smooth[i], pair_ref[order, side] * sign
        )


def final_part(main, pair, back, mine, away, inverse, turn, place, block, cutoff):
    fields, slots, rows, levels, width = main.shape
    block_spec = pl.BlockSpec(
        (fields, slots, 1, levels, width), lambda i: (0, 0, i * (rows - 1), 0, 0)
    )
    return pl.pallas_call(
        functools.partial(final_kernel, back.ndim == 2),
        grid=(2,),
        in_specs=[block_spec] + vmem(7) + smem(3),
        out_specs=block_spec,
        out_shape=jax.ShapeDtypeStruct(main.shape, F32),
        input_output_aliases={0: 0},
        compiler_params=pltpu.CompilerParams(vmem_limit_bytes=50 * MIB),
        cost_estimate=pl.CostEstimate(
            flops=12 * mine.shape[0] * 2 * KCUT * width,
            bytes_accessed=4 * 10**6,
            transcendentals=0,
        ),
        name="final",
    )(main, pair, back, mine, away, *inverse, turn, place, block, cutoff)


def swap(array, bit):
    size = lax.axis_size("lon")
    return lax.ppermute(array, "lon", [(i, i ^ bit) for i in range(size)])


def lon_sum(mine, other, last=None):
    total = mine + swap(other, 1)
    bit = 2
    while bit < lax.axis_size("lon"):
        total = total + swap(total, bit)
        bit *= 2
    if last is not None:
        total = total + last
    return total, swap(total, 1)


def shards(state, courant_x, courant_y, block_of_slot, face_source, cutoff):
    fields, slots, rows, levels, width = state.shape
    lat, lon = lax.axis_size("lat"), lax.axis_size("lon")
    lon_index = lax.axis_index("lon")
    place = jnp.stack([lon_index, lon_index % 2]).astype(jnp.int32)
    forward, inverse = basis_tables(width)
    turn = turn_table(lon, width)
    tables = (turn, place, block_of_slot, cutoff)

    packed = lat == levels == 8 and -(-width // LANES) * fields == 30
    if packed:
        sent = pack(state, courant_y, block_of_slot).reshape(lat, PIECE, LANES)
        got = lax.all_to_all(sent, "lat", 0, 0, tiled=True)

    west, east = edges(state, courant_x)
    west = lax.ppermute(west, "lon", [(i, (i + 1) % lon) for i in range(lon)])
    east = lax.ppermute(east, "lon", [((i + 1) % lon, i) for i in range(lon)])
    base, mine, other = local_tendency(
        state, courant_x, courant_y, west, east, forward, *tables
    )
    if packed:
        back, other = faces_of_pieces(got, slots, cutoff, other)
        back = lax.all_to_all(back, "lat", 0, 0, tiled=True)
        pair = rest = back.reshape(lat * BACK, LANES)
    else:
        faces = exchange_faces(state, courant_y, face_source)
        picked = pick_slots(block_of_slot, cutoff, rows)
        pair, rest = faces[jnp.stack(picked[:2])], faces[picked[2]]
    total, away = lon_sum(mine, other)
    shape = (2, 2, fields, levels, width)
    pair, rim_mine, rim_other, token = rim_spectra(pair, shape, forward, turn, place)
    main, token = main_part(token, state, base, total, away, inverse, *tables)
    rim_total, rim_away = lon_sum(rim_mine, rim_other, token)
    return final_part(main, pair, rest, rim_total, rim_away, inverse, *tables)


def solution(mesh):
    placed = (
        P(None, "lat", None, None, "lon"),
        P("lat", None, None, "lon"),
        P("lat", None, None, "lon"),
        P("lat"),
        P("lat", None),
        P(),
    )
    return jax.shard_map(
        shards,
        mesh=mesh,
        in_specs=placed,
        out_specs=P(None, "lat", None, None, "lon"),
        check_vma=False,
    )
```

```python
import functools
import math

import jax
import jax.numpy as jnp
import numpy as np
from jax import lax
from jax.experimental import pallas as pl
from jax.experimental.pallas import tpu as pltpu
from jax.sharding import PartitionSpec as P

NLON = 2880
KCUT = 256
LANES = 128
MIB = 1024 * 1024
BF16 = jnp.bfloat16
F32 = jnp.float32


def phases(columns):
    wavenumber = np.arange(KCUT, dtype=np.int64)
    return (columns[:, None] * wavenumber[None, :] % NLON).astype(np.float64) * (
        2.0 * math.pi / NLON
    )


def basis_tables(width):
    phase = phases(np.arange(width, dtype=np.int64))
    table = np.concatenate([np.cos(phase), np.sin(phase)], axis=1).astype(np.float32)
    high = table.astype(jnp.bfloat16)
    low = (table - high.astype(np.float32)).astype(jnp.bfloat16)
    forward = (jnp.asarray(high), jnp.asarray(low))
    inverse = (
        jnp.asarray(np.ascontiguousarray(high.T)),
        jnp.asarray(np.ascontiguousarray(low.T)),
    )
    return forward, inverse


def turn_table(lon, width):
    phase = phases(np.arange(lon, dtype=np.int64) * width)
    table = np.concatenate([np.cos(phase), np.sin(phase)], axis=1).astype(np.float32)
    return jnp.asarray(table[:, None, :])


def split_dot(rows, high, low, axis=0):
    rows_high = rows.astype(BF16)
    rows_low = (rows - rows_high.astype(F32)).astype(BF16)
    dot = functools.partial(
        lax.dot_general,
        dimension_numbers=(((1,), (axis,)), ((), ())),
        preferred_element_type=F32,
    )
    return dot(rows_high, high) + (dot(rows_low, high) + dot(rows_high, low))


def turned(spec, turn, sign):
    real, imag = spec[:, :KCUT], spec[:, KCUT:]
    cos, sin = turn[:, :KCUT], turn[:, KCUT:] * sign
    return jnp.concatenate([real * cos - imag * sin, imag * cos + real * sin], axis=1)


def row_weights(cut):
    column = lax.broadcasted_iota(jnp.int32, (1, 2 * KCUT), 1)
    wavenumber = jnp.where(column >= KCUT, column - KCUT, column)
    scale = jnp.where(wavenumber == 0, 1.0 / NLON, 2.0 / NLON).astype(F32)
    return jnp.where(wavenumber < cut, scale, 0.0)


def pick_slots(block_ref, cutoff_ref, rows):
    polar1 = cutoff_ref[block_ref[1] * rows] > 0
    polar2 = cutoff_ref[block_ref[2] * rows] > 0
    rest = jnp.where(polar2, jnp.where(polar1, 0, 1), 2)
    return jnp.where(rest == 0, 1, 0), jnp.where(rest == 2, 1, 2), rest


def mine_first(pair, core):
    a, b = pair
    return jnp.where(core == 0, a, b), jnp.where(core == 0, b, a)


def vmem(count):
    return [pl.BlockSpec(memory_space=pltpu.VMEM)] * count


def smem(count):
    return [pl.BlockSpec(memory_space=pltpu.SMEM)] * count


def edge_kernel(lane_last, head_ref, tail_ref, wind_ref, west_ref, east_ref):
    fields, slots, rows = head_ref.shape[:3]
    lane = lax.broadcasted_iota(jnp.int32, (8, LANES), 1)
    for s in range(slots):
        west = jnp.zeros((8, LANES), F32)
        east = jnp.zeros((8, LANES), F32)
        for r in range(rows):
            for f in range(fields):
                here = lane == f * rows + r
                west = jnp.where(here, tail_ref[f, s, r, :, lane_last : lane_last + 1], west)
                east = jnp.where(here, head_ref[f, s, r, :, 0:1], east)
            here = lane == fields * rows + r
            west = jnp.where(here, wind_ref[s, r, :, lane_last : lane_last + 1], west)
        west_ref[s] = west
        east_ref[s] = east


def edges(state, courant_x):
    fields, slots, rows, levels, width = state.shape
    last = (width - 1) // LANES
    out = jax.ShapeDtypeStruct((slots, levels, LANES), F32)
    return pl.pallas_call(
        functools.partial(edge_kernel, (width - 1) % LANES),
        grid=(1,),
        in_specs=[
            pl.BlockSpec((fields, slots, rows, levels, LANES), lambda i: (0, 0, 0, 0, 0)),
            pl.BlockSpec((fields, slots, rows, levels, LANES), lambda i: (0, 0, 0, 0, last)),
            pl.BlockSpec((slots, rows, levels, LANES), lambda i: (0, 0, 0, last)),
        ],
        out_specs=[pl.BlockSpec((slots, levels, LANES), lambda i: (0, 0, 0))] * 2,
        out_shape=[out, out],
        cost_estimate=pl.CostEstimate(flops=10**5, bytes_accessed=1200000, transcendentals=0),
        name="edges",
    )(state, state, courant_x)


PIECE = 200
BACK = 184


def tile_of(slab, t, width):
    part = slab[:, t * LANES : min((t + 1) * LANES, width)]
    if part.shape[1] < LANES:
        part = jnp.concatenate([part, jnp.zeros((8, LANES - part.shape[1]), F32)], axis=1)
    return part


def pack_kernel(width, first_ref, last_ref, wind_ref, block_ref, out_ref):
    fields, slots = first_ref.shape[:2]
    tiles = -(-width // LANES)

    def put(row, tile):
        out_ref[pl.ds(row, 8, stride=PIECE), :] = tile

    for j in range(slots):
        half = wind_ref[j, 0] * 0.5
        for t in range(tiles):
            row = {0: 192 + 2 * j, 1: 193 + 2 * j, 2: 64 * j + 62, 3: 64 * j + 63}.get(
                t, 64 * j + 26 + t
            )
            put(row, tile_of(half, t, width))
        for f in range(fields):
            north = last_ref[f, j, 0] * half
            south = first_ref[f, j, 0]
            for t in range(tiles):
                put(64 * j + f * tiles + t, tile_of(north, t, width))
                put(64 * j + 32 + f * tiles + t, tile_of(south, t, width))
    lane = lax.broadcasted_iota(jnp.int32, (8, LANES), 1)
    table = jnp.zeros((8, LANES), F32)
    for j in range(slots):
        table = jnp.where(lane == j, block_ref[j].astype(F32), table)
    put(198, table)
    put(199, table)


def pack(state, courant_y, block):
    fields, slots, rows, levels, width = state.shape
    return pl.pallas_call(
        functools.partial(pack_kernel, width),
        grid=(1,),
        in_specs=[
            pl.BlockSpec((fields, slots, 1, levels, width), lambda i: (0, 0, 0, 0, 0)),
            pl.BlockSpec((fields, slots, 1, levels, width), lambda i: (0, 0, rows - 1, 0, 0)),
            pl.BlockSpec((slots, 1, levels, width), lambda i: (0, rows - 1, 0, 0)),
            pl.BlockSpec(memory_space=pltpu.SMEM),
        ],
        out_specs=pl.BlockSpec((levels * PIECE, LANES), lambda i: (0, 0)),
        out_shape=jax.ShapeDtypeStruct((levels * PIECE, LANES), F32),
        cost_estimate=pl.CostEstimate(flops=10**5, bytes_accessed=1700000, transcendentals=0),
        name="pack",
    )(state, state, courant_y, block)


def face_kernel(
    got_ref, cutoff_ref, later_in_ref, out_ref, later_ref, face_ref, table_ref, slot_ref, sem
):
    del later_in_ref, later_ref
    parts = got_ref.shape[0]
    slots = face_ref.shape[0] // parts
    count = parts * slots
    copy = pltpu.make_async_copy(got_ref.at[:, 192:200, :], table_ref, sem)
    copy.start()
    copy.wait()
    blocks = [table_ref[s // slots, 6, s % slots].astype(jnp.int32) for s in range(count)]
    slot_ref[0] = -1
    slot_ref[count + 1] = -1
    for s in range(count):
        slot_ref[blocks[s] + 1] = s
    for s in range(count):
        src, j = divmod(s, slots)
        south = slot_ref[blocks[s] + 2]
        safe = jnp.maximum(south, 0)
        from_src = lax.div(safe, slots)
        from_slot = safe - from_src * slots
        half = jnp.concatenate(
            [
                got_ref[src, 192 + 2 * j : 194 + 2 * j, :],
                got_ref[src, 64 * j + 62 : 64 * j + 64, :],
                got_ref[src, 64 * j + 30 : 64 * j + 32, :],
            ],
            axis=0,
        )
        half = jnp.concatenate([half] * 5 + [half[:2]], axis=0)
        other = got_ref[from_src, pl.ds(pl.multiple_of(64 * from_slot + 32, 32), 32), :]
        face = got_ref[src, 64 * j : 64 * j + 32, :] + half * other
        face_ref[s] = jnp.where(south >= 0, face, 0.0)
    for d in range(parts):
        first, second, rest = pick_slots(blocks[slots * d : slots * d + slots], cutoff_ref, 8)
        for i, slot in enumerate((first, second, rest)):
            row = 60 * i
            block = jnp.where(
                slot == 0,
                blocks[slots * d],
                jnp.where(slot == 1, blocks[slots * d + 1], blocks[slots * d + 2]),
            )
            north = slot_ref[block]
            out_ref[d, row : row + 30] = jnp.where(
                north >= 0, face_ref[jnp.maximum(north, 0), :30], 0.0
            )
            out_ref[d, row + 30 : row + 60] = face_ref[slots * d + slot, :30]
        out_ref[d, 180:184] = jnp.zeros((4, LANES), F32)


def faces_of_pieces(got, slots, cutoff, later):
    parts = got.shape[0]
    return pl.pallas_call(
        face_kernel,
        in_specs=vmem(1) + smem(1) + [pl.BlockSpec(memory_space=pl.ANY)],
        out_specs=vmem(1) + [pl.BlockSpec(memory_space=pl.ANY)],
        out_shape=[
            jax.ShapeDtypeStruct((parts, BACK, LANES), F32),
            jax.ShapeDtypeStruct(later.shape, F32),
        ],
        input_output_aliases={2: 1},
        scratch_shapes=[
            pltpu.VMEM((parts * slots, 32, LANES), F32),
            pltpu.SMEM((parts, 8, LANES), F32),
            pltpu.SMEM((parts * slots + 2,), jnp.int32),
            pltpu.SemaphoreType.DMA(()),
        ],
        cost_estimate=pl.CostEstimate(flops=10**5, bytes_accessed=1600000, transcendentals=0),
        name="faces",
    )(got, cutoff, later)


def to_pieces(units, parts):
    count, levels, width = units.shape
    groups = math.gcd(parts, levels)
    chunks = parts // groups
    span = -(-width // chunks)
    units = jnp.pad(units, ((0, 0), (0, 0), (0, span * chunks - width)))
    units = units.reshape(count, groups, levels // groups, chunks, span)
    return units.transpose(1, 3, 0, 2, 4).reshape(parts, count, levels // groups * span)


def from_pieces(pieces, levels, width):
    parts, count, _ = pieces.shape
    groups = math.gcd(parts, levels)
    chunks = parts // groups
    span = -(-width // chunks)
    pieces = pieces.reshape(groups, chunks, count, levels // groups, span)
    return pieces.transpose(2, 0, 3, 1, 4).reshape(count, levels, chunks * span)[:, :, :width]


def exchange_faces(state, courant_y, face_source):
    fields, slots, rows, levels, width = state.shape
    lat = lax.axis_size("lat")
    count = 2 * fields + 1
    first = state[:, :, 0].transpose(1, 0, 2, 3)
    last = state[:, :, rows - 1].transpose(1, 0, 2, 3)
    half = courant_y[:, rows - 1][:, None] * 0.5
    units = jnp.concatenate([first, last * half, half], axis=1)
    sent = to_pieces(units.reshape(slots * count, levels, width), lat)
    span = sent.shape[2]
    table = jnp.pad(
        face_source.astype(F32).reshape(1, slots * 2), ((0, 0), (0, span - slots * 2))
    )
    sent = jnp.concatenate([sent, jnp.broadcast_to(table[None], (lat, 1, span))], axis=1)
    got = lax.all_to_all(sent, "lat", 0, 0, tiled=True)
    indices = got[:, slots * count, : slots * 2].reshape(lat * slots, 2).astype(jnp.int32)
    data = got[:, : slots * count].reshape(lat * slots, count, span)
    north, south = indices[:, 0], indices[:, 1]
    face = data[:, fields : 2 * fields] + data[:, 2 * fields :] * data[
        jnp.maximum(south, 0), :fields
    ]
    face = jnp.where((south >= 0)[:, None, None], face, 0.0)
    face_north = jnp.where((north >= 0)[:, None, None], face[jnp.maximum(north, 0)], 0.0)
    back = jnp.concatenate([face_north, face], axis=1).reshape(lat, slots * 2 * fields, span)
    back = lax.all_to_all(back, "lat", 0, 0, tiled=True)
    return from_pieces(back, levels, width).reshape(slots, 2, fields, levels, width)


def tendency_kernel(
    state_ref,
    cx_ref,
    cy_ref,
    west_ref,
    east_ref,
    high_ref,
    low_ref,
    turn_ref,
    place_ref,
    block_ref,
    cutoff_ref,
    out_ref,
    mine_ref,
    other_ref,
    tend_ref,
    base_ref,
    sem,
):
    fields, slots, rows, levels, width = state_ref.shape

    def streamed(s):
        return pltpu.make_async_copy(base_ref.at[:, s], out_ref.at[:, s], sem.at[s])


    tiles = -(-width // LANES)
    lane = lax.broadcasted_iota(jnp.int32, (levels, LANES), 1)
    head, tail, last = lane == 0, lane == LANES - 1, lane == (width - 1) % LANES

    def load(ref, *index):
        out = []
        for t in range(tiles):
            part = ref[index + (slice(None), slice(t * LANES, min((t + 1) * LANES, width)))]
            if part.shape[1] < LANES:
                pad = jnp.zeros((levels, LANES - part.shape[1]), F32)
                part = jnp.concatenate([part, pad], axis=1)
            out.append(part)
        return out

    def one_slot(s, carry):
        west, east = west_ref[s], east_ref[s]
        for f in range(fields):
            above = None
            now = load(state_ref, f, s, 0)
            for r in range(rows):
                column = f * rows + r
                left = [pltpu.roll(x, LANES - 1, 1) for x in now]
                left = [
                    jnp.where(tail, left[t + 1], left[t])
                    if t + 1 < tiles
                    else jnp.where(last, east[:, column : column + 1], left[t])
                    for t in range(tiles)
                ]
                half = [x * 0.5 for x in load(cx_ref, s, r)]
                flux = [h * (x + y) for h, x, y in zip(half, now, left)]
                wind = west[:, fields * rows + r : fields * rows + r + 1] * 0.5
                first = wind * (west[:, column : column + 1] + now[0])
                right = [pltpu.roll(x, 1, 1) for x in flux]
                right = [jnp.where(head, y, x) for x, y in zip(right, [first] + right[:-1])]
                change = [x - y for x, y in zip(right, flux)]
                if above is not None:
                    change = [x + y for x, y in zip(change, above)]
                if r + 1 < rows:
                    later = load(state_ref, f, s, r + 1)
                    half = load(cy_ref, s, r)
                    above = [h * 0.5 * (x + y) for h, x, y in zip(half, now, later)]
                    change = [x - y for x, y in zip(change, above)]
                for t in range(tiles):
                    stop = min((t + 1) * LANES, width)
                    base = now[t] + change[t]
                    tend_ref[f, s, r, :, t * LANES : stop] = change[t][:, : stop - t * LANES]
                    base_ref[f, s, r, :, t * LANES : stop] = base[:, : stop - t * LANES]
                now = later
        streamed(s).start()
        return carry

    lax.fori_loop(0, slots, one_slot, 0)
    turn = turn_ref[place_ref[0]]
    first, second, _ = pick_slots(block_ref, cutoff_ref, rows)
    mine, other = mine_first((first, second), place_ref[1])
    for slot, spec_ref in ((other, other_ref), (mine, mine_ref)):
        spec = split_dot(
            tend_ref[:, slot].reshape(fields * rows * levels, width), high_ref[...], low_ref[...]
        )
        spec_ref[...] = turned(spec, turn, 1.0)
    for s in range(slots):
        streamed(s).wait()


def local_tendency(state, courant_x, courant_y, west, east, forward, turn, place, block, cutoff):
    fields, slots, rows, levels, width = state.shape
    count = fields * rows * levels
    spec = jax.ShapeDtypeStruct((count, 2 * KCUT), F32)
    return pl.pallas_call(
        tendency_kernel,
        in_specs=vmem(8) + smem(3),
        out_specs=[pl.BlockSpec(memory_space=pl.ANY)] + vmem(2),
        out_shape=[jax.ShapeDtypeStruct(state.shape, F32), spec, spec],
        scratch_shapes=[
            pltpu.VMEM(state.shape, F32),
            pltpu.VMEM(state.shape, F32),
            pltpu.SemaphoreType.DMA((slots,)),
        ],
        compiler_params=pltpu.CompilerParams(vmem_limit_bytes=50 * MIB),
        cost_estimate=pl.CostEstimate(
            flops=6 * count * 2 * KCUT * width * 2, bytes_accessed=9 * 10**6, transcendentals=0
        ),
        name="tendency",
    )(state, courant_x, courant_y, west, east, *forward, turn, place, block, cutoff)


def chosen_slot(i, place_ref, block_ref, cutoff_ref, rows):
    first, second, _ = pick_slots(block_ref, cutoff_ref, rows)
    return jnp.where(i == place_ref[1], first, second)


def main_kernel(
    place_ref,
    block_ref,
    cutoff_ref,
    state_ref,
    base_ref,
    mine_ref,
    away_ref,
    high_ref,
    low_ref,
    turn_ref,
    after_ref,
    out_ref,
    token_ref,
):
    fields, _, rows, levels, width = state_ref.shape
    del after_ref
    token_ref[...] = jnp.zeros_like(token_ref)
    i = pl.program_id(0)
    turn = turn_ref[place_ref[0]]
    slot = chosen_slot(i, place_ref, block_ref, cutoff_ref, rows)
    spec = turned(jnp.where(i == 0, mine_ref[...], away_ref[...]), turn, -1.0)
    spec = spec.reshape(fields, rows, levels, 2 * KCUT)
    cuts = [cutoff_ref[block_ref[slot] * rows + r] for r in range(rows)]
    spec = jnp.concatenate(
        [spec[:, r : r + 1] * row_weights(cuts[r]) for r in range(rows)], axis=1
    )
    smooth = split_dot(
        spec.reshape(fields * rows * levels, 2 * KCUT), high_ref[...], low_ref[...]
    ).reshape(fields, rows, levels, width)
    for r in range(rows):
        out_ref[:, 0, r] = jnp.where(
            cuts[r] > 0, state_ref[:, 0, r] + smooth[:, r], base_ref[:, 0, r]
        )


def main_part(after, state, base, mine, away, inverse, turn, place, block, cutoff):
    fields, slots, rows, levels, width = state.shape
    slot_block = pl.BlockSpec(
        (fields, 1, rows, levels, width),
        lambda i, *scalars: (0, chosen_slot(i, *scalars, rows), 0, 0, 0),
    )
    return pl.pallas_call(
        main_kernel,
        grid_spec=pltpu.PrefetchScalarGridSpec(
            num_scalar_prefetch=3,
            grid=(2,),
            in_specs=[slot_block, slot_block] + vmem(6),
            out_specs=[slot_block, pl.BlockSpec((1, 2 * KCUT), lambda i, *scalars: (0, 0))],
        ),
        out_shape=[
            jax.ShapeDtypeStruct(state.shape, F32),
            jax.ShapeDtypeStruct((1, 2 * KCUT), F32),
        ],
        input_output_aliases={4: 0},
        compiler_params=pltpu.CompilerParams(vmem_limit_bytes=50 * MIB),
        cost_estimate=pl.CostEstimate(
            flops=12 * mine.shape[0] * 2 * KCUT * width,
            bytes_accessed=6 * 10**6,
            transcendentals=0,
        ),
        name="main",
    )(place, block, cutoff, state, base, mine, away, *inverse, turn, after)


def unpack(ref, base, stride, put, fields, width):
    tiles = -(-width // LANES)
    for f in range(fields):
        for t in range(tiles):
            tile = ref[pl.ds(base + f * tiles + t, 8, stride=stride), :]
            stop = min((t + 1) * LANES, width)
            put(f, t * LANES, stop, tile[:, : stop - t * LANES])


def rim_kernel(
    packed,
    got_ref,
    high_ref,
    low_ref,
    turn_ref,
    place_ref,
    faces_ref,
    mine_ref,
    other_ref,
    token_ref,
):
    _, _, fields, levels, width = faces_ref.shape
    token_ref[...] = jnp.zeros_like(token_ref)
    if packed:
        for i in range(2):
            for side in range(2):

                def put(f, start, stop, tile, i=i, side=side):
                    faces_ref[i, side, f, :, start:stop] = tile

                unpack(got_ref, 60 * i + 30 * side, BACK, put, fields, width)
    else:
        faces_ref[...] = got_ref[...]
    turn = turn_ref[place_ref[0]]
    core = place_ref[1]
    both = jnp.concatenate(
        [part for i in (core, 1 - core) for part in (faces_ref[i, 0], -faces_ref[i, 1])], axis=0
    ).reshape(4 * fields * levels, width)
    spec = turned(split_dot(both, high_ref[...], low_ref[...], axis=1), turn, 1.0)
    mine_ref[...] = spec[: 2 * fields * levels]
    other_ref[...] = spec[2 * fields * levels :]


def rim_spectra(got, shape, inverse, turn, place):
    _, _, fields, levels, width = shape
    spec = jax.ShapeDtypeStruct((2 * fields * levels, 2 * KCUT), F32)
    return pl.pallas_call(
        functools.partial(rim_kernel, got.ndim == 2),
        in_specs=vmem(4) + smem(1),
        out_specs=vmem(4),
        out_shape=[
            jax.ShapeDtypeStruct(shape, F32),
            spec,
            spec,
            jax.ShapeDtypeStruct((8, LANES), F32),
        ],
        compiler_params=pltpu.CompilerParams(vmem_limit_bytes=50 * MIB),
        cost_estimate=pl.CostEstimate(
            flops=24 * fields * levels * 2 * KCUT * width,
            bytes_accessed=3 * 10**6,
            transcendentals=0,
        ),
        name="rim_spectra",
    )(got, *inverse, turn, place)


def final_kernel(
    packed,
    main_ref,
    pair_ref,
    back_ref,
    mine_ref,
    away_ref,
    high_ref,
    low_ref,
    turn_ref,
    place_ref,
    block_ref,
    cutoff_ref,
    out_ref,
    smooth_ref,
):
    fields, slots, _, levels, width = main_ref.shape
    rows = 8
    side = pl.program_id(0)
    row = side * (rows - 1)
    turn = turn_ref[place_ref[0]]
    core = place_ref[1]
    first, second, rest = pick_slots(block_ref, cutoff_ref, rows)
    mine, other = mine_first((first, second), core)
    count = fields * levels

    @pl.when(side == 0)
    def _():
        spec = [
            turned(ref[j * count : (j + 1) * count], turn, -1.0)
            * row_weights(cutoff_ref[block_ref[slot] * rows + j * (rows - 1)])
            for slot, ref in ((mine, mine_ref), (other, away_ref))
            for j in range(2)
        ]
        smooth = split_dot(jnp.concatenate(spec, axis=0), high_ref[...], low_ref[...])
        smooth_ref[...] = smooth.reshape(2, 2, fields, levels, width)

    sign = jnp.where(side == 0, 1.0, -1.0).astype(F32)
    if packed:

        def put(f, start, stop, tile):
            old = main_ref[f, rest, 0, :, start:stop]
            out_ref[f, rest, 0, :, start:stop] = old + tile * sign

        unpack(back_ref, 120 + 30 * side, BACK, put, fields, width)
    else:
        out_ref[:, rest, 0] = main_ref[:, rest, 0] + back_ref[side] * sign
    cuts = [cutoff_ref[block_ref[slot] * rows + row] for slot in (mine, other)]
    for i, (slot, order) in enumerate(((mine, core), (other, 1 - core))):
        out_ref[:, slot, 0] = main_ref[:, slot, 0] + jnp.where(
            cuts[i] > 0, smooth_ref[i, side], pair_ref[order, side] * sign
        )


def final_part(main, pair, back, mine, away, inverse, turn, place, block, cutoff):
    fields, slots, rows, levels, width = main.shape
    block_spec = pl.BlockSpec(
        (fields, slots, 1, levels, width), lambda i: (0, 0, i * (rows - 1), 0, 0)
    )
    return pl.pallas_call(
        functools.partial(final_kernel, back.ndim == 2),
        grid=(2,),
        in_specs=[block_spec] + vmem(7) + smem(3),
        out_specs=block_spec,
        scratch_shapes=[pltpu.VMEM((2, 2, fields, levels, width), F32)],
        out_shape=jax.ShapeDtypeStruct(main.shape, F32),
        input_output_aliases={0: 0},
        compiler_params=pltpu.CompilerParams(vmem_limit_bytes=50 * MIB),
        cost_estimate=pl.CostEstimate(
            flops=12 * mine.shape[0] * 2 * KCUT * width,
            bytes_accessed=4 * 10**6,
            transcendentals=0,
        ),
        name="final",
    )(main, pair, back, mine, away, *inverse, turn, place, block, cutoff)


def swap(array, bit):
    size = lax.axis_size("lon")
    return lax.ppermute(array, "lon", [(i, i ^ bit) for i in range(size)])


def lon_sum(mine, other, last=None):
    total = mine + swap(other, 1)
    bit = 2
    while bit < lax.axis_size("lon"):
        total = total + swap(total, bit)
        bit *= 2
    if last is not None:
        total = total + last
    return total, swap(total, 1)


def shards(state, courant_x, courant_y, block_of_slot, face_source, cutoff):
    fields, slots, rows, levels, width = state.shape
    lat, lon = lax.axis_size("lat"), lax.axis_size("lon")
    lon_index = lax.axis_index("lon")
    place = jnp.stack([lon_index, lon_index % 2]).astype(jnp.int32)
    forward, inverse = basis_tables(width)
    turn = turn_table(lon, width)
    tables = (turn, place, block_of_slot, cutoff)

    packed = lat == levels == 8 and -(-width // LANES) * fields == 30
    if packed:
        sent = pack(state, courant_y, block_of_slot).reshape(lat, PIECE, LANES)
        got = lax.all_to_all(sent, "lat", 0, 0, tiled=True)

    west, east = edges(state, courant_x)
    west = lax.ppermute(west, "lon", [(i, (i + 1) % lon) for i in range(lon)])
    east = lax.ppermute(east, "lon", [((i + 1) % lon, i) for i in range(lon)])
    base, mine, other = local_tendency(
        state, courant_x, courant_y, west, east, forward, *tables
    )
    if packed:
        back, mine = faces_of_pieces(got, slots, cutoff, mine)
        back = lax.all_to_all(back, "lat", 0, 0, tiled=True)
        pair = rest = back.reshape(lat * BACK, LANES)
    else:
        faces = exchange_faces(state, courant_y, face_source)
        picked = pick_slots(block_of_slot, cutoff, rows)
        pair, rest = faces[jnp.stack(picked[:2])], faces[picked[2]]
    total, away = lon_sum(mine, other)
    shape = (2, 2, fields, levels, width)
    pair, rim_mine, rim_other, token = rim_spectra(pair, shape, inverse, turn, place)
    main, token = main_part(token, state, base, total, away, inverse, *tables)
    rim_total, rim_away = lon_sum(rim_mine, rim_other, token)
    return final_part(main, pair, rest, rim_total, rim_away, inverse, *tables)


def solution(mesh):
    placed = (
        P(None, "lat", None, None, "lon"),
        P("lat", None, None, "lon"),
        P("lat", None, None, "lon"),
        P("lat"),
        P("lat", None),
        P(),
    )
    return jax.shard_map(
        shards,
        mesh=mesh,
        in_specs=placed,
        out_specs=P(None, "lat", None, None, "lon"),
        check_vma=False,
    )
```

```python
import functools
import math

import jax
import jax.numpy as jnp
import numpy as np
from jax import lax
from jax.experimental import pallas as pl
from jax.experimental.pallas import tpu as pltpu
from jax.sharding import PartitionSpec as P

NLON = 2880
KCUT = 256
LANES = 128
MIB = 1024 * 1024
BF16 = jnp.bfloat16
F32 = jnp.float32


def phases(columns):
    wavenumber = np.arange(KCUT, dtype=np.int64)
    return (columns[:, None] * wavenumber[None, :] % NLON).astype(np.float64) * (
        2.0 * math.pi / NLON
    )


def basis_tables(width):
    phase = phases(np.arange(width, dtype=np.int64))
    table = np.concatenate([np.cos(phase), np.sin(phase)], axis=1).astype(np.float32)
    high = table.astype(jnp.bfloat16)
    low = (table - high.astype(np.float32)).astype(jnp.bfloat16)
    forward = (jnp.asarray(high), jnp.asarray(low))
    inverse = (
        jnp.asarray(np.ascontiguousarray(high.T)),
        jnp.asarray(np.ascontiguousarray(low.T)),
    )
    return forward, inverse


def turn_table(lon, width):
    phase = phases(np.arange(lon, dtype=np.int64) * width)
    table = np.concatenate([np.cos(phase), np.sin(phase)], axis=1).astype(np.float32)
    return jnp.asarray(table[:, None, :])


def split_dot(rows, high, low, axis=0):
    rows_high = rows.astype(BF16)
    rows_low = (rows - rows_high.astype(F32)).astype(BF16)
    dot = functools.partial(
        lax.dot_general,
        dimension_numbers=(((1,), (axis,)), ((), ())),
        preferred_element_type=F32,
    )
    return dot(rows_high, high) + (dot(rows_low, high) + dot(rows_high, low))


def turned(spec, turn, sign):
    real, imag = spec[:, :KCUT], spec[:, KCUT:]
    cos, sin = turn[:, :KCUT], turn[:, KCUT:] * sign
    return jnp.concatenate([real * cos - imag * sin, imag * cos + real * sin], axis=1)


def row_weights(cut):
    column = lax.broadcasted_iota(jnp.int32, (1, 2 * KCUT), 1)
    wavenumber = jnp.where(column >= KCUT, column - KCUT, column)
    scale = jnp.where(wavenumber == 0, 1.0 / NLON, 2.0 / NLON).astype(F32)
    return jnp.where(wavenumber < cut, scale, 0.0)


def pick_slots(block_ref, cutoff_ref, rows):
    polar1 = cutoff_ref[block_ref[1] * rows] > 0
    polar2 = cutoff_ref[block_ref[2] * rows] > 0
    rest = jnp.where(polar2, jnp.where(polar1, 0, 1), 2)
    return jnp.where(rest == 0, 1, 0), jnp.where(rest == 2, 1, 2), rest


def mine_first(pair, core):
    a, b = pair
    return jnp.where(core == 0, a, b), jnp.where(core == 0, b, a)


def vmem(count):
    return [pl.BlockSpec(memory_space=pltpu.VMEM)] * count


def smem(count):
    return [pl.BlockSpec(memory_space=pltpu.SMEM)] * count


def edge_kernel(lane_last, head_ref, tail_ref, wind_ref, west_ref, east_ref):
    fields, slots, rows = head_ref.shape[:3]
    lane = lax.broadcasted_iota(jnp.int32, (8, LANES), 1)
    for s in range(slots):
        west = jnp.zeros((8, LANES), F32)
        east = jnp.zeros((8, LANES), F32)
        for r in range(rows):
            for f in range(fields):
                here = lane == f * rows + r
                west = jnp.where(here, tail_ref[f, s, r, :, lane_last : lane_last + 1], west)
                east = jnp.where(here, head_ref[f, s, r, :, 0:1], east)
            here = lane == fields * rows + r
            west = jnp.where(here, wind_ref[s, r, :, lane_last : lane_last + 1], west)
        west_ref[s] = west
        east_ref[s] = east


def edges(state, courant_x):
    fields, slots, rows, levels, width = state.shape
    last = (width - 1) // LANES
    out = jax.ShapeDtypeStruct((slots, levels, LANES), F32)
    return pl.pallas_call(
        functools.partial(edge_kernel, (width - 1) % LANES),
        grid=(1,),
        in_specs=[
            pl.BlockSpec((fields, slots, rows, levels, LANES), lambda i: (0, 0, 0, 0, 0)),
            pl.BlockSpec((fields, slots, rows, levels, LANES), lambda i: (0, 0, 0, 0, last)),
            pl.BlockSpec((slots, rows, levels, LANES), lambda i: (0, 0, 0, last)),
        ],
        out_specs=[pl.BlockSpec((slots, levels, LANES), lambda i: (0, 0, 0))] * 2,
        out_shape=[out, out],
        cost_estimate=pl.CostEstimate(flops=10**5, bytes_accessed=1200000, transcendentals=0),
        name="edges",
    )(state, state, courant_x)


PIECE = 200
BACK = 184


def tile_of(slab, t, width):
    part = slab[:, t * LANES : min((t + 1) * LANES, width)]
    if part.shape[1] < LANES:
        part = jnp.concatenate([part, jnp.zeros((8, LANES - part.shape[1]), F32)], axis=1)
    return part


def pack_kernel(
    state_ref,
    wind_ref,
    block_ref,
    out_ref,
    first_ref,
    last_ref,
    half_ref,
    sent_ref,
    in_sem,
    out_sem,
):
    fields, slots, rows, levels, width = state_ref.shape
    tiles = -(-width // LANES)

    def incoming(j):
        return (
            pltpu.make_async_copy(state_ref.at[:, j, 0], first_ref.at[j], in_sem.at[j, 0]),
            pltpu.make_async_copy(state_ref.at[:, j, rows - 1], last_ref.at[j], in_sem.at[j, 1]),
            pltpu.make_async_copy(wind_ref.at[j, rows - 1], half_ref.at[j], in_sem.at[j, 2]),
        )

    def outgoing(j, p):
        part = pl.ds(p * PIECE + 64 * j, 64 if j < slots else PIECE - 64 * slots)
        return pltpu.make_async_copy(sent_ref.at[part], out_ref.at[part], out_sem.at[j, p])

    def put(row, tile):
        sent_ref[pl.ds(row, 8, stride=PIECE), :] = tile

    for j in range(slots):
        for copy in incoming(j):
            copy.start()
    for j in range(slots):
        for copy in incoming(j):
            copy.wait()
        half = half_ref[j] * 0.5
        for t in range(tiles):
            row = {0: 192 + 2 * j, 1: 193 + 2 * j, 2: 64 * j + 62, 3: 64 * j + 63}.get(
                t, 64 * j + 26 + t
            )
            put(row, tile_of(half, t, width))
        for f in range(fields):
            north = last_ref[j, f] * half
            south = first_ref[j, f]
            for t in range(tiles):
                put(64 * j + f * tiles + t, tile_of(north, t, width))
                put(64 * j + 32 + f * tiles + t, tile_of(south, t, width))
        for p in range(levels):
            outgoing(j, p).start()
    lane = lax.broadcasted_iota(jnp.int32, (8, LANES), 1)
    table = jnp.zeros((8, LANES), F32)
    for j in range(slots):
        table = jnp.where(lane == j, block_ref[j].astype(F32), table)
    put(198, table)
    put(199, table)
    for p in range(levels):
        outgoing(slots, p).start()
    for j in range(slots + 1):
        for p in range(levels):
            outgoing(j, p).wait()


def anywhere(count):
    return [pl.BlockSpec(memory_space=pl.ANY)] * count


def pack(state, courant_y, block):
    fields, slots, rows, levels, width = state.shape
    return pl.pallas_call(
        pack_kernel,
        in_specs=anywhere(2) + smem(1),
        out_specs=anywhere(1)[0],
        out_shape=jax.ShapeDtypeStruct((levels * PIECE, LANES), F32),
        scratch_shapes=[
            pltpu.VMEM((slots, fields, levels, width), F32),
            pltpu.VMEM((slots, fields, levels, width), F32),
            pltpu.VMEM((slots, levels, width), F32),
            pltpu.VMEM((levels * PIECE, LANES), F32),
            pltpu.SemaphoreType.DMA((slots, 3)),
            pltpu.SemaphoreType.DMA((slots + 1, levels)),
        ],
        cost_estimate=pl.CostEstimate(flops=10**5, bytes_accessed=1700000, transcendentals=0),
        name="pack",
    )(state, courant_y, block)


def face_kernel(
    from_ref,
    cutoff_ref,
    later_in_ref,
    to_ref,
    later_ref,
    got_ref,
    out_ref,
    face_ref,
    table_ref,
    slot_ref,
    sem,
    in_sem,
    out_sem,
):
    del later_in_ref, later_ref
    parts = from_ref.shape[0]
    slots = face_ref.shape[0] // parts
    count = parts * slots
    copy = pltpu.make_async_copy(from_ref.at[:, 192:200, :], table_ref, sem)
    incoming = [
        pltpu.make_async_copy(from_ref.at[d], got_ref.at[d], in_sem.at[d]) for d in range(parts)
    ]
    outgoing = [
        pltpu.make_async_copy(out_ref.at[d], to_ref.at[d], out_sem.at[d]) for d in range(parts)
    ]
    copy.start()
    for part in incoming:
        part.start()
    copy.wait()
    blocks = [table_ref[s // slots, 6, s % slots].astype(jnp.int32) for s in range(count)]
    slot_ref[0] = -1
    slot_ref[count + 1] = -1
    for s in range(count):
        slot_ref[blocks[s] + 1] = s
    for part in incoming:
        part.wait()
    for s in range(count):
        src, j = divmod(s, slots)
        south = slot_ref[blocks[s] + 2]
        safe = jnp.maximum(south, 0)
        from_src = lax.div(safe, slots)
        from_slot = safe - from_src * slots
        half = jnp.concatenate(
            [
                got_ref[src, 192 + 2 * j : 194 + 2 * j, :],
                got_ref[src, 64 * j + 62 : 64 * j + 64, :],
                got_ref[src, 64 * j + 30 : 64 * j + 32, :],
            ],
            axis=0,
        )
        half = jnp.concatenate([half] * 5 + [half[:2]], axis=0)
        other = got_ref[from_src, pl.ds(pl.multiple_of(64 * from_slot + 32, 32), 32), :]
        face = got_ref[src, 64 * j : 64 * j + 32, :] + half * other
        face_ref[s] = jnp.where(south >= 0, face, 0.0)
    for d in range(parts):
        first, second, rest = pick_slots(blocks[slots * d : slots * d + slots], cutoff_ref, 8)
        for i, slot in enumerate((first, second, rest)):
            row = 60 * i
            block = jnp.where(
                slot == 0,
                blocks[slots * d],
                jnp.where(slot == 1, blocks[slots * d + 1], blocks[slots * d + 2]),
            )
            north = slot_ref[block]
            out_ref[d, row : row + 30] = jnp.where(
                north >= 0, face_ref[jnp.maximum(north, 0), :30], 0.0
            )
            out_ref[d, row + 30 : row + 60] = face_ref[slots * d + slot, :30]
        out_ref[d, 180:184] = jnp.zeros((4, LANES), F32)
        outgoing[d].start()
    for part in outgoing:
        part.wait()


def faces_of_pieces(got, slots, cutoff, later):
    parts = got.shape[0]
    return pl.pallas_call(
        face_kernel,
        in_specs=anywhere(1) + smem(1) + anywhere(1),
        out_specs=anywhere(2),
        out_shape=[
            jax.ShapeDtypeStruct((parts, BACK, LANES), F32),
            jax.ShapeDtypeStruct(later.shape, F32),
        ],
        input_output_aliases={2: 1},
        scratch_shapes=[
            pltpu.VMEM(got.shape, F32),
            pltpu.VMEM((parts, BACK, LANES), F32),
            pltpu.VMEM((parts * slots, 32, LANES), F32),
            pltpu.SMEM((parts, 8, LANES), F32),
            pltpu.SMEM((parts * slots + 2,), jnp.int32),
            pltpu.SemaphoreType.DMA(()),
            pltpu.SemaphoreType.DMA((parts,)),
            pltpu.SemaphoreType.DMA((parts,)),
        ],
        cost_estimate=pl.CostEstimate(flops=10**5, bytes_accessed=1600000, transcendentals=0),
        name="faces",
    )(got, cutoff, later)


def to_pieces(units, parts):
    count, levels, width = units.shape
    groups = math.gcd(parts, levels)
    chunks = parts // groups
    span = -(-width // chunks)
    units = jnp.pad(units, ((0, 0), (0, 0), (0, span * chunks - width)))
    units = units.reshape(count, groups, levels // groups, chunks, span)
    return units.transpose(1, 3, 0, 2, 4).reshape(parts, count, levels // groups * span)


def from_pieces(pieces, levels, width):
    parts, count, _ = pieces.shape
    groups = math.gcd(parts, levels)
    chunks = parts // groups
    span = -(-width // chunks)
    pieces = pieces.reshape(groups, chunks, count, levels // groups, span)
    return pieces.transpose(2, 0, 3, 1, 4).reshape(count, levels, chunks * span)[:, :, :width]


def exchange_faces(state, courant_y, face_source):
    fields, slots, rows, levels, width = state.shape
    lat = lax.axis_size("lat")
    count = 2 * fields + 1
    first = state[:, :, 0].transpose(1, 0, 2, 3)
    last = state[:, :, rows - 1].transpose(1, 0, 2, 3)
    half = courant_y[:, rows - 1][:, None] * 0.5
    units = jnp.concatenate([first, last * half, half], axis=1)
    sent = to_pieces(units.reshape(slots * count, levels, width), lat)
    span = sent.shape[2]
    table = jnp.pad(
        face_source.astype(F32).reshape(1, slots * 2), ((0, 0), (0, span - slots * 2))
    )
    sent = jnp.concatenate([sent, jnp.broadcast_to(table[None], (lat, 1, span))], axis=1)
    got = lax.all_to_all(sent, "lat", 0, 0, tiled=True)
    indices = got[:, slots * count, : slots * 2].reshape(lat * slots, 2).astype(jnp.int32)
    data = got[:, : slots * count].reshape(lat * slots, count, span)
    north, south = indices[:, 0], indices[:, 1]
    face = data[:, fields : 2 * fields] + data[:, 2 * fields :] * data[
        jnp.maximum(south, 0), :fields
    ]
    face = jnp.where((south >= 0)[:, None, None], face, 0.0)
    face_north = jnp.where((north >= 0)[:, None, None], face[jnp.maximum(north, 0)], 0.0)
    back = jnp.concatenate([face_north, face], axis=1).reshape(lat, slots * 2 * fields, span)
    back = lax.all_to_all(back, "lat", 0, 0, tiled=True)
    return from_pieces(back, levels, width).reshape(slots, 2, fields, levels, width)


def tendency_kernel(
    state_ref,
    cx_ref,
    cy_ref,
    west_ref,
    east_ref,
    high_ref,
    low_ref,
    turn_ref,
    place_ref,
    block_ref,
    cutoff_ref,
    out_ref,
    mine_ref,
    other_ref,
    tend_ref,
    base_ref,
    sem,
):
    fields, slots, rows, levels, width = state_ref.shape

    def streamed(s):
        return pltpu.make_async_copy(base_ref.at[:, s], out_ref.at[:, s], sem.at[s])


    tiles = -(-width // LANES)
    lane = lax.broadcasted_iota(jnp.int32, (levels, LANES), 1)
    head, tail, last = lane == 0, lane == LANES - 1, lane == (width - 1) % LANES

    def load(ref, *index):
        out = []
        for t in range(tiles):
            part = ref[index + (slice(None), slice(t * LANES, min((t + 1) * LANES, width)))]
            if part.shape[1] < LANES:
                pad = jnp.zeros((levels, LANES - part.shape[1]), F32)
                part = jnp.concatenate([part, pad], axis=1)
            out.append(part)
        return out

    def one_slot(s, carry):
        west, east = west_ref[s], east_ref[s]
        for f in range(fields):
            above = None
            now = load(state_ref, f, s, 0)
            for r in range(rows):
                column = f * rows + r
                left = [pltpu.roll(x, LANES - 1, 1) for x in now]
                left = [
                    jnp.where(tail, left[t + 1], left[t])
                    if t + 1 < tiles
                    else jnp.where(last, east[:, column : column + 1], left[t])
                    for t in range(tiles)
                ]
                half = [x * 0.5 for x in load(cx_ref, s, r)]
                flux = [h * (x + y) for h, x, y in zip(half, now, left)]
                wind = west[:, fields * rows + r : fields * rows + r + 1] * 0.5
                first = wind * (west[:, column : column + 1] + now[0])
                right = [pltpu.roll(x, 1, 1) for x in flux]
                right = [jnp.where(head, y, x) for x, y in zip(right, [first] + right[:-1])]
                change = [x - y for x, y in zip(right, flux)]
                if above is not None:
                    change = [x + y for x, y in zip(change, above)]
                if r + 1 < rows:
                    later = load(state_ref, f, s, r + 1)
                    half = load(cy_ref, s, r)
                    above = [h * 0.5 * (x + y) for h, x, y in zip(half, now, later)]
                    change = [x - y for x, y in zip(change, above)]
                for t in range(tiles):
                    stop = min((t + 1) * LANES, width)
                    base = now[t] + change[t]
                    tend_ref[f, s, r, :, t * LANES : stop] = change[t][:, : stop - t * LANES]
                    base_ref[f, s, r, :, t * LANES : stop] = base[:, : stop - t * LANES]
                now = later
        streamed(s).start()
        return carry

    lax.fori_loop(0, slots, one_slot, 0)
    turn = turn_ref[place_ref[0]]
    first, second, _ = pick_slots(block_ref, cutoff_ref, rows)
    mine, other = mine_first((first, second), place_ref[1])
    for slot, spec_ref in ((other, other_ref), (mine, mine_ref)):
        spec = split_dot(
            tend_ref[:, slot].reshape(fields * rows * levels, width), high_ref[...], low_ref[...]
        )
        spec_ref[...] = turned(spec, turn, 1.0)
    for s in range(slots):
        streamed(s).wait()


def local_tendency(state, courant_x, courant_y, west, east, forward, turn, place, block, cutoff):
    fields, slots, rows, levels, width = state.shape
    count = fields * rows * levels
    spec = jax.ShapeDtypeStruct((count, 2 * KCUT), F32)
    return pl.pallas_call(
        tendency_kernel,
        in_specs=vmem(8) + smem(3),
        out_specs=[pl.BlockSpec(memory_space=pl.ANY)] + vmem(2),
        out_shape=[jax.ShapeDtypeStruct(state.shape, F32), spec, spec],
        scratch_shapes=[
            pltpu.VMEM(state.shape, F32),
            pltpu.VMEM(state.shape, F32),
            pltpu.SemaphoreType.DMA((slots,)),
        ],
        compiler_params=pltpu.CompilerParams(vmem_limit_bytes=50 * MIB),
        cost_estimate=pl.CostEstimate(
            flops=6 * count * 2 * KCUT * width * 2, bytes_accessed=9 * 10**6, transcendentals=0
        ),
        name="tendency",
    )(state, courant_x, courant_y, west, east, *forward, turn, place, block, cutoff)


def chosen_slot(i, place_ref, block_ref, cutoff_ref, rows):
    first, second, _ = pick_slots(block_ref, cutoff_ref, rows)
    return jnp.where(i == place_ref[1], first, second)


def main_kernel(
    place_ref,
    block_ref,
    cutoff_ref,
    state_ref,
    base_ref,
    mine_ref,
    away_ref,
    high_ref,
    low_ref,
    turn_ref,
    after_ref,
    out_ref,
    token_ref,
):
    fields, _, rows, levels, width = state_ref.shape
    del after_ref
    token_ref[...] = jnp.zeros_like(token_ref)
    i = pl.program_id(0)
    turn = turn_ref[place_ref[0]]
    slot = chosen_slot(i, place_ref, block_ref, cutoff_ref, rows)
    spec = turned(jnp.where(i == 0, mine_ref[...], away_ref[...]), turn, -1.0)
    spec = spec.reshape(fields, rows, levels, 2 * KCUT)
    cuts = [cutoff_ref[block_ref[slot] * rows + r] for r in range(rows)]
    spec = jnp.concatenate(
        [spec[:, r : r + 1] * row_weights(cuts[r]) for r in range(rows)], axis=1
    )
    smooth = split_dot(
        spec.reshape(fields * rows * levels, 2 * KCUT), high_ref[...], low_ref[...]
    ).reshape(fields, rows, levels, width)
    for r in range(rows):
        out_ref[:, 0, r] = jnp.where(
            cuts[r] > 0, state_ref[:, 0, r] + smooth[:, r], base_ref[:, 0, r]
        )


def main_part(after, state, base, mine, away, inverse, turn, place, block, cutoff):
    fields, slots, rows, levels, width = state.shape
    slot_block = pl.BlockSpec(
        (fields, 1, rows, levels, width),
        lambda i, *scalars: (0, chosen_slot(i, *scalars, rows), 0, 0, 0),
    )
    return pl.pallas_call(
        main_kernel,
        grid_spec=pltpu.PrefetchScalarGridSpec(
            num_scalar_prefetch=3,
            grid=(2,),
            in_specs=[slot_block, slot_block] + vmem(6),
            out_specs=[slot_block, pl.BlockSpec((1, 2 * KCUT), lambda i, *scalars: (0, 0))],
        ),
        out_shape=[
            jax.ShapeDtypeStruct(state.shape, F32),
            jax.ShapeDtypeStruct((1, 2 * KCUT), F32),
        ],
        input_output_aliases={4: 0},
        compiler_params=pltpu.CompilerParams(vmem_limit_bytes=50 * MIB),
        cost_estimate=pl.CostEstimate(
            flops=12 * mine.shape[0] * 2 * KCUT * width,
            bytes_accessed=6 * 10**6,
            transcendentals=0,
        ),
        name="main",
    )(place, block, cutoff, state, base, mine, away, *inverse, turn, after)


def unpack(ref, base, stride, put, fields, width):
    tiles = -(-width // LANES)
    for f in range(fields):
        for t in range(tiles):
            tile = ref[pl.ds(base + f * tiles + t, 8, stride=stride), :]
            stop = min((t + 1) * LANES, width)
            put(f, t * LANES, stop, tile[:, : stop - t * LANES])


def rim_kernel(
    packed,
    got_ref,
    high_ref,
    low_ref,
    turn_ref,
    place_ref,
    faces_ref,
    mine_ref,
    other_ref,
    token_ref,
):
    _, _, fields, levels, width = faces_ref.shape
    token_ref[...] = jnp.zeros_like(token_ref)
    if packed:
        for i in range(2):
            for side in range(2):

                def put(f, start, stop, tile, i=i, side=side):
                    faces_ref[i, side, f, :, start:stop] = tile

                unpack(got_ref, 60 * i + 30 * side, BACK, put, fields, width)
    else:
        faces_ref[...] = got_ref[...]
    turn = turn_ref[place_ref[0]]
    core = place_ref[1]
    both = jnp.concatenate(
        [part for i in (core, 1 - core) for part in (faces_ref[i, 0], -faces_ref[i, 1])], axis=0
    ).reshape(4 * fields * levels, width)
    spec = turned(split_dot(both, high_ref[...], low_ref[...], axis=1), turn, 1.0)
    mine_ref[...] = spec[: 2 * fields * levels]
    other_ref[...] = spec[2 * fields * levels :]


def rim_spectra(got, shape, inverse, turn, place):
    _, _, fields, levels, width = shape
    spec = jax.ShapeDtypeStruct((2 * fields * levels, 2 * KCUT), F32)
    return pl.pallas_call(
        functools.partial(rim_kernel, got.ndim == 2),
        in_specs=vmem(4) + smem(1),
        out_specs=vmem(4),
        out_shape=[
            jax.ShapeDtypeStruct(shape, F32),
            spec,
            spec,
            jax.ShapeDtypeStruct((8, LANES), F32),
        ],
        compiler_params=pltpu.CompilerParams(vmem_limit_bytes=50 * MIB),
        cost_estimate=pl.CostEstimate(
            flops=24 * fields * levels * 2 * KCUT * width,
            bytes_accessed=3 * 10**6,
            transcendentals=0,
        ),
        name="rim_spectra",
    )(got, *inverse, turn, place)


def final_kernel(
    packed,
    main_ref,
    pair_ref,
    back_ref,
    mine_ref,
    away_ref,
    high_ref,
    low_ref,
    turn_ref,
    place_ref,
    block_ref,
    cutoff_ref,
    out_ref,
    smooth_ref,
):
    fields, slots, _, levels, width = main_ref.shape
    rows = 8
    side = pl.program_id(0)
    row = side * (rows - 1)
    turn = turn_ref[place_ref[0]]
    core = place_ref[1]
    first, second, rest = pick_slots(block_ref, cutoff_ref, rows)
    mine, other = mine_first((first, second), core)
    count = fields * levels

    @pl.when(side == 0)
    def _():
        spec = [
            turned(ref[j * count : (j + 1) * count], turn, -1.0)
            * row_weights(cutoff_ref[block_ref[slot] * rows + j * (rows - 1)])
            for slot, ref in ((mine, mine_ref), (other, away_ref))
            for j in range(2)
        ]
        smooth = split_dot(jnp.concatenate(spec, axis=0), high_ref[...], low_ref[...])
        smooth_ref[...] = smooth.reshape(2, 2, fields, levels, width)

    sign = jnp.where(side == 0, 1.0, -1.0).astype(F32)
    if packed:

        def put(f, start, stop, tile):
            old = main_ref[f, rest, 0, :, start:stop]
            out_ref[f, rest, 0, :, start:stop] = old + tile * sign

        unpack(back_ref, 120 + 30 * side, BACK, put, fields, width)
    else:
        out_ref[:, rest, 0] = main_ref[:, rest, 0] + back_ref[side] * sign
    cuts = [cutoff_ref[block_ref[slot] * rows + row] for slot in (mine, other)]
    for i, (slot, order) in enumerate(((mine, core), (other, 1 - core))):
        out_ref[:, slot, 0] = main_ref[:, slot, 0] + jnp.where(
            cuts[i] > 0, smooth_ref[i, side], pair_ref[order, side] * sign
        )


def final_part(main, pair, back, mine, away, inverse, turn, place, block, cutoff):
    fields, slots, rows, levels, width = main.shape
    block_spec = pl.BlockSpec(
        (fields, slots, 1, levels, width), lambda i: (0, 0, i * (rows - 1), 0, 0)
    )
    return pl.pallas_call(
        functools.partial(final_kernel, back.ndim == 2),
        grid=(2,),
        in_specs=[block_spec] + vmem(7) + smem(3),
        out_specs=block_spec,
        scratch_shapes=[pltpu.VMEM((2, 2, fields, levels, width), F32)],
        out_shape=jax.ShapeDtypeStruct(main.shape, F32),
        input_output_aliases={0: 0},
        compiler_params=pltpu.CompilerParams(vmem_limit_bytes=50 * MIB),
        cost_estimate=pl.CostEstimate(
            flops=12 * mine.shape[0] * 2 * KCUT * width,
            bytes_accessed=4 * 10**6,
            transcendentals=0,
        ),
        name="final",
    )(main, pair, back, mine, away, *inverse, turn, place, block, cutoff)


def swap(array, bit):
    size = lax.axis_size("lon")
    return lax.ppermute(array, "lon", [(i, i ^ bit) for i in range(size)])


def lon_sum(mine, other, last=None):
    total = mine + swap(other, 1)
    bit = 2
    while bit < lax.axis_size("lon"):
        total = total + swap(total, bit)
        bit *= 2
    if last is not None:
        total = total + last
    return total, swap(total, 1)


def shards(state, courant_x, courant_y, block_of_slot, face_source, cutoff):
    fields, slots, rows, levels, width = state.shape
    lat, lon = lax.axis_size("lat"), lax.axis_size("lon")
    lon_index = lax.axis_index("lon")
    place = jnp.stack([lon_index, lon_index % 2]).astype(jnp.int32)
    forward, inverse = basis_tables(width)
    turn = turn_table(lon, width)
    tables = (turn, place, block_of_slot, cutoff)

    packed = lat == levels == 8 and -(-width // LANES) * fields == 30
    if packed:
        sent = pack(state, courant_y, block_of_slot).reshape(lat, PIECE, LANES)
        got = lax.all_to_all(sent, "lat", 0, 0, tiled=True)

    west, east = edges(state, courant_x)
    west = lax.ppermute(west, "lon", [(i, (i + 1) % lon) for i in range(lon)])
    east = lax.ppermute(east, "lon", [((i + 1) % lon, i) for i in range(lon)])
    base, mine, other = local_tendency(
        state, courant_x, courant_y, west, east, forward, *tables
    )
    if packed:
        back, mine = faces_of_pieces(got, slots, cutoff, mine)
        back = lax.all_to_all(back, "lat", 0, 0, tiled=True)
        pair = rest = back.reshape(lat * BACK, LANES)
    else:
        faces = exchange_faces(state, courant_y, face_source)
        picked = pick_slots(block_of_slot, cutoff, rows)
        pair, rest = faces[jnp.stack(picked[:2])], faces[picked[2]]
    total, away = lon_sum(mine, other)
    shape = (2, 2, fields, levels, width)
    pair, rim_mine, rim_other, token = rim_spectra(pair, shape, inverse, turn, place)
    main, token = main_part(token, state, base, total, away, inverse, *tables)
    rim_total, rim_away = lon_sum(rim_mine, rim_other, token)
    return final_part(main, pair, rest, rim_total, rim_away, inverse, *tables)


def solution(mesh):
    placed = (
        P(None, "lat", None, None, "lon"),
        P("lat", None, None, "lon"),
        P("lat", None, None, "lon"),
        P("lat"),
        P("lat", None),
        P(),
    )
    return jax.shard_map(
        shards,
        mesh=mesh,
        in_specs=placed,
        out_specs=P(None, "lat", None, None, "lon"),
        check_vma=False,
    )
```

```python
import functools
import math

import jax
import jax.numpy as jnp
import numpy as np
from jax import lax
from jax.experimental import pallas as pl
from jax.experimental.pallas import tpu as pltpu
from jax.sharding import PartitionSpec as P

NLON = 2880
KCUT = 256
LANES = 128
MIB = 1024 * 1024
BF16 = jnp.bfloat16
F32 = jnp.float32


def phases(columns):
    wavenumber = np.arange(KCUT, dtype=np.int64)
    return (columns[:, None] * wavenumber[None, :] % NLON).astype(np.float64) * (
        2.0 * math.pi / NLON
    )


def basis_tables(width):
    phase = phases(np.arange(width, dtype=np.int64))
    table = np.concatenate([np.cos(phase), np.sin(phase)], axis=1).astype(np.float32)
    high = table.astype(jnp.bfloat16)
    low = (table - high.astype(np.float32)).astype(jnp.bfloat16)
    forward = (jnp.asarray(high), jnp.asarray(low))
    inverse = (
        jnp.asarray(np.ascontiguousarray(high.T)),
        jnp.asarray(np.ascontiguousarray(low.T)),
    )
    return forward, inverse


def turn_table(lon, width):
    phase = phases(np.arange(lon, dtype=np.int64) * width)
    table = np.concatenate([np.cos(phase), np.sin(phase)], axis=1).astype(np.float32)
    return jnp.asarray(table[:, None, :])


def split_dot(rows, high, low, axis=0):
    rows_high = rows.astype(BF16)
    rows_low = (rows - rows_high.astype(F32)).astype(BF16)
    dot = functools.partial(
        lax.dot_general,
        dimension_numbers=(((1,), (axis,)), ((), ())),
        preferred_element_type=F32,
    )
    return dot(rows_high, high) + (dot(rows_low, high) + dot(rows_high, low))


def turned(spec, turn, sign):
    real, imag = spec[:, :KCUT], spec[:, KCUT:]
    cos, sin = turn[:, :KCUT], turn[:, KCUT:] * sign
    return jnp.concatenate([real * cos - imag * sin, imag * cos + real * sin], axis=1)


def row_weights(cut):
    column = lax.broadcasted_iota(jnp.int32, (1, 2 * KCUT), 1)
    wavenumber = jnp.where(column >= KCUT, column - KCUT, column)
    scale = jnp.where(wavenumber == 0, 1.0 / NLON, 2.0 / NLON).astype(F32)
    return jnp.where(wavenumber < cut, scale, 0.0)


def pick_slots(block_ref, cutoff_ref, rows):
    polar1 = cutoff_ref[block_ref[1] * rows] > 0
    polar2 = cutoff_ref[block_ref[2] * rows] > 0
    rest = jnp.where(polar2, jnp.where(polar1, 0, 1), 2)
    return jnp.where(rest == 0, 1, 0), jnp.where(rest == 2, 1, 2), rest


def mine_first(pair, core):
    a, b = pair
    return jnp.where(core == 0, a, b), jnp.where(core == 0, b, a)


def vmem(count):
    return [pl.BlockSpec(memory_space=pltpu.VMEM)] * count


def smem(count):
    return [pl.BlockSpec(memory_space=pltpu.SMEM)] * count


def edge_kernel(lane_last, head_ref, tail_ref, wind_ref, west_ref, east_ref):
    fields, slots, rows = head_ref.shape[:3]
    lane = lax.broadcasted_iota(jnp.int32, (8, LANES), 1)
    for s in range(slots):
        west = jnp.zeros((8, LANES), F32)
        east = jnp.zeros((8, LANES), F32)
        for r in range(rows):
            for f in range(fields):
                here = lane == f * rows + r
                west = jnp.where(here, tail_ref[f, s, r, :, lane_last : lane_last + 1], west)
                east = jnp.where(here, head_ref[f, s, r, :, 0:1], east)
            here = lane == fields * rows + r
            west = jnp.where(here, wind_ref[s, r, :, lane_last : lane_last + 1], west)
        west_ref[s] = west
        east_ref[s] = east


def edges(state, courant_x):
    fields, slots, rows, levels, width = state.shape
    last = (width - 1) // LANES
    out = jax.ShapeDtypeStruct((slots, levels, LANES), F32)
    return pl.pallas_call(
        functools.partial(edge_kernel, (width - 1) % LANES),
        grid=(1,),
        in_specs=[
            pl.BlockSpec((fields, slots, rows, levels, LANES), lambda i: (0, 0, 0, 0, 0)),
            pl.BlockSpec((fields, slots, rows, levels, LANES), lambda i: (0, 0, 0, 0, last)),
            pl.BlockSpec((slots, rows, levels, LANES), lambda i: (0, 0, 0, last)),
        ],
        out_specs=[pl.BlockSpec((slots, levels, LANES), lambda i: (0, 0, 0))] * 2,
        out_shape=[out, out],
        cost_estimate=pl.CostEstimate(flops=10**5, bytes_accessed=1200000, transcendentals=0),
        name="edges",
    )(state, state, courant_x)


PIECE = 192
BACK = 176
TAIL = 80
SPARE = LANES - TAIL


def tile_of(slab, t, width):
    part = slab[:, t * LANES : min((t + 1) * LANES, width)]
    if part.shape[1] < LANES:
        part = jnp.concatenate([part, jnp.zeros((8, LANES - part.shape[1]), F32)], axis=1)
    return part


def pack_kernel(width, first_ref, last_ref, wind_ref, block_ref, out_ref):
    fields, slots = first_ref.shape[:2]
    tiles = -(-width // LANES)

    lane = lax.broadcasted_iota(jnp.int32, (8, LANES), 1)

    def put(row, tile):
        out_ref[pl.ds(row, 8, stride=PIECE), :] = tile

    tails = []
    for j in range(slots):
        half = wind_ref[j, 0] * 0.5
        north = [last_ref[f, j, 0] * half for f in range(fields)]
        south = [first_ref[f, j, 0] for f in range(fields)]
        for t in range(tiles - 1):
            put(55 * j + 25 + t, tile_of(half, t, width))
            for f in range(fields):
                put(55 * j + t * fields + f, tile_of(north[f], t, width))
                put(55 * j + 30 + t * fields + f, tile_of(south[f], t, width))
        tails.append([tile_of(slab, tiles - 1, width) for slab in (*north, half, *south)])
    for u, (a, b, c) in enumerate(zip(*tails)):
        put(165 + u, jnp.where(lane < TAIL, a, pltpu.roll(c, TAIL, 1)))
        put(176 + u, jnp.where(lane < TAIL, b, pltpu.roll(c, LANES - 2 * SPARE, 1)))
    table = jnp.zeros((8, LANES), jnp.int32)
    for j in range(slots):
        table = jnp.where(lane == j, block_ref[j], table)
    for row in range(187, PIECE):
        put(row, table.astype(F32))


def pack(state, courant_y, block):
    fields, slots, rows, levels, width = state.shape
    return pl.pallas_call(
        functools.partial(pack_kernel, width),
        grid=(1,),
        in_specs=[
            pl.BlockSpec((fields, slots, 1, levels, width), lambda i: (0, 0, 0, 0, 0)),
            pl.BlockSpec((fields, slots, 1, levels, width), lambda i: (0, 0, rows - 1, 0, 0)),
            pl.BlockSpec((slots, 1, levels, width), lambda i: (0, rows - 1, 0, 0)),
            pl.BlockSpec(memory_space=pltpu.SMEM),
        ],
        out_specs=pl.BlockSpec((levels * PIECE, LANES), lambda i: (0, 0)),
        out_shape=jax.ShapeDtypeStruct((levels * PIECE, LANES), F32),
        cost_estimate=pl.CostEstimate(flops=10**5, bytes_accessed=1700000, transcendentals=0),
        name="pack",
    )(state, state, courant_y, block)


def face_kernel(
    got_ref,
    cutoff_ref,
    later_in_ref,
    out_ref,
    later_ref,
    face_ref,
    south_ref,
    half_ref,
    whole_ref,
    table_ref,
    slot_ref,
    sem,
):
    del later_in_ref, later_ref
    parts = got_ref.shape[0]
    slots = face_ref.shape[0] // parts
    count = parts * slots
    whole_ref[...] = got_ref[:, 184:192, :].astype(jnp.int32)
    copy = pltpu.make_async_copy(whole_ref, table_ref, sem)
    copy.start()
    lane = lax.broadcasted_iota(jnp.int32, (8, LANES), 1)
    wide = lax.broadcasted_iota(jnp.int32, (16, LANES), 1)
    tails = []
    for s in range(count):
        src, j = divmod(s, slots)
        if j < 2:
            tail = got_ref[src, 165 + 11 * j : 176 + 11 * j, :]
        else:
            one = pltpu.roll(got_ref[src, 165:181, :], SPARE, 1)
            two = pltpu.roll(got_ref[src, 176:192, :], 2 * SPARE, 1)
            tail = jnp.where(wide < SPARE, one, two)[:11]
        south_ref[s, :25] = got_ref[src, 55 * j + 30 : 55 * j + 55, :]
        south_ref[s, 25:30] = tail[6:]
        face_ref[s, :25] = got_ref[src, 55 * j : 55 * j + 25, :]
        face_ref[s, 25:30] = tail[:5]
        half_ref[s, :5] = got_ref[src, 55 * j + 25 : 55 * j + 30, :]
        half_ref[s, 5:6] = tail[5:6]
    copy.wait()
    blocks = [table_ref[s // slots, 3, s % slots] for s in range(count)]
    slot_ref[0] = -1
    slot_ref[count + 1] = -1
    for s in range(count):
        slot_ref[blocks[s] + 1] = s
    for s in range(count):
        south = slot_ref[blocks[s] + 2]
        half = jnp.concatenate(
            [jnp.broadcast_to(half_ref[s, t : t + 1], (5, LANES)) for t in range(6)], axis=0
        )
        face = face_ref[s, :30] + half * south_ref[jnp.maximum(south, 0), :30]
        face_ref[s, :30] = jnp.where(south >= 0, face, 0.0)
    for d in range(parts):
        first, second, rest = pick_slots(blocks[slots * d : slots * d + slots], cutoff_ref, 8)
        tails = []
        for i, slot in enumerate((first, second, rest)):
            block = jnp.where(
                slot == 0,
                blocks[slots * d],
                jnp.where(slot == 1, blocks[slots * d + 1], blocks[slots * d + 2]),
            )
            north = slot_ref[block]
            for q, face, there in (
                (2 * i, jnp.maximum(north, 0), north >= 0),
                (2 * i + 1, slots * d + slot, None),
            ):
                rows, tail = face_ref[face, :25], face_ref[face, 24:32]
                if there is not None:
                    rows, tail = jnp.where(there, rows, 0.0), jnp.where(there, tail, 0.0)
                out_ref[d, 25 * q : 25 * q + 25] = rows
                tails.append(tail)
        for q in range(4):
            rest_tail = pltpu.roll(tails[4 + q % 2], TAIL if q < 2 else LANES - 2 * SPARE, 1)
            tail = jnp.where(lane < TAIL, tails[q], rest_tail)
            out_ref[d, 150 + 5 * q : 155 + 5 * q] = tail[1:6]
        out_ref[d, 170:BACK] = jnp.zeros((BACK - 170, LANES), F32)


def faces_of_pieces(got, slots, cutoff, later):
    parts = got.shape[0]
    return pl.pallas_call(
        face_kernel,
        in_specs=vmem(1) + smem(1) + [pl.BlockSpec(memory_space=pl.ANY)],
        out_specs=vmem(1) + [pl.BlockSpec(memory_space=pl.ANY)],
        out_shape=[
            jax.ShapeDtypeStruct((parts, BACK, LANES), F32),
            jax.ShapeDtypeStruct(later.shape, F32),
        ],
        input_output_aliases={2: 1},
        scratch_shapes=[
            pltpu.VMEM((parts * slots, 32, LANES), F32),
            pltpu.VMEM((parts * slots, 32, LANES), F32),
            pltpu.VMEM((parts * slots, 8, LANES), F32),
            pltpu.VMEM((parts, 8, LANES), jnp.int32),
            pltpu.SMEM((parts, 8, LANES), jnp.int32),
            pltpu.SMEM((parts * slots + 2,), jnp.int32),
            pltpu.SemaphoreType.DMA(()),
        ],
        cost_estimate=pl.CostEstimate(flops=10**5, bytes_accessed=1600000, transcendentals=0),
        name="faces",
    )(got, cutoff, later)


def to_pieces(units, parts):
    count, levels, width = units.shape
    groups = math.gcd(parts, levels)
    chunks = parts // groups
    span = -(-width // chunks)
    units = jnp.pad(units, ((0, 0), (0, 0), (0, span * chunks - width)))
    units = units.reshape(count, groups, levels // groups, chunks, span)
    return units.transpose(1, 3, 0, 2, 4).reshape(parts, count, levels // groups * span)


def from_pieces(pieces, levels, width):
    parts, count, _ = pieces.shape
    groups = math.gcd(parts, levels)
    chunks = parts // groups
    span = -(-width // chunks)
    pieces = pieces.reshape(groups, chunks, count, levels // groups, span)
    return pieces.transpose(2, 0, 3, 1, 4).reshape(count, levels, chunks * span)[:, :, :width]


def exchange_faces(state, courant_y, face_source):
    fields, slots, rows, levels, width = state.shape
    lat = lax.axis_size("lat")
    count = 2 * fields + 1
    first = state[:, :, 0].transpose(1, 0, 2, 3)
    last = state[:, :, rows - 1].transpose(1, 0, 2, 3)
    half = courant_y[:, rows - 1][:, None] * 0.5
    units = jnp.concatenate([first, last * half, half], axis=1)
    sent = to_pieces(units.reshape(slots * count, levels, width), lat)
    span = sent.shape[2]
    table = jnp.pad(
        face_source.astype(F32).reshape(1, slots * 2), ((0, 0), (0, span - slots * 2))
    )
    sent = jnp.concatenate([sent, jnp.broadcast_to(table[None], (lat, 1, span))], axis=1)
    got = lax.all_to_all(sent, "lat", 0, 0, tiled=True)
    indices = got[:, slots * count, : slots * 2].reshape(lat * slots, 2).astype(jnp.int32)
    data = got[:, : slots * count].reshape(lat * slots, count, span)
    north, south = indices[:, 0], indices[:, 1]
    face = data[:, fields : 2 * fields] + data[:, 2 * fields :] * data[
        jnp.maximum(south, 0), :fields
    ]
    face = jnp.where((south >= 0)[:, None, None], face, 0.0)
    face_north = jnp.where((north >= 0)[:, None, None], face[jnp.maximum(north, 0)], 0.0)
    back = jnp.concatenate([face_north, face], axis=1).reshape(lat, slots * 2 * fields, span)
    back = lax.all_to_all(back, "lat", 0, 0, tiled=True)
    return from_pieces(back, levels, width).reshape(slots, 2, fields, levels, width)


def tendency_kernel(
    state_ref,
    cx_ref,
    cy_ref,
    west_ref,
    east_ref,
    high_ref,
    low_ref,
    turn_ref,
    place_ref,
    block_ref,
    cutoff_ref,
    out_ref,
    mine_ref,
    other_ref,
    tend_ref,
    base_ref,
    sem,
):
    fields, slots, rows, levels, width = state_ref.shape

    def streamed(s):
        return pltpu.make_async_copy(base_ref.at[:, s], out_ref.at[:, s], sem.at[s])


    tiles = -(-width // LANES)
    lane = lax.broadcasted_iota(jnp.int32, (levels, LANES), 1)
    head, tail, last = lane == 0, lane == LANES - 1, lane == (width - 1) % LANES

    def load(ref, *index):
        out = []
        for t in range(tiles):
            part = ref[index + (slice(None), slice(t * LANES, min((t + 1) * LANES, width)))]
            if part.shape[1] < LANES:
                pad = jnp.zeros((levels, LANES - part.shape[1]), F32)
                part = jnp.concatenate([part, pad], axis=1)
            out.append(part)
        return out

    def one_slot(s, carry):
        west, east = west_ref[s], east_ref[s]
        for f in range(fields):
            above = None
            now = load(state_ref, f, s, 0)
            for r in range(rows):
                column = f * rows + r
                left = [pltpu.roll(x, LANES - 1, 1) for x in now]
                left = [
                    jnp.where(tail, left[t + 1], left[t])
                    if t + 1 < tiles
                    else jnp.where(last, east[:, column : column + 1], left[t])
                    for t in range(tiles)
                ]
                half = [x * 0.5 for x in load(cx_ref, s, r)]
                flux = [h * (x + y) for h, x, y in zip(half, now, left)]
                wind = west[:, fields * rows + r : fields * rows + r + 1] * 0.5
                first = wind * (west[:, column : column + 1] + now[0])
                right = [pltpu.roll(x, 1, 1) for x in flux]
                right = [jnp.where(head, y, x) for x, y in zip(right, [first] + right[:-1])]
                change = [x - y for x, y in zip(right, flux)]
                if above is not None:
                    change = [x + y for x, y in zip(change, above)]
                if r + 1 < rows:
                    later = load(state_ref, f, s, r + 1)
                    half = load(cy_ref, s, r)
                    above = [h * 0.5 * (x + y) for h, x, y in zip(half, now, later)]
                    change = [x - y for x, y in zip(change, above)]
                for t in range(tiles):
                    stop = min((t + 1) * LANES, width)
                    base = now[t] + change[t]
                    tend_ref[f, s, r, :, t * LANES : stop] = change[t][:, : stop - t * LANES]
                    base_ref[f, s, r, :, t * LANES : stop] = base[:, : stop - t * LANES]
                now = later
        streamed(s).start()
        return carry

    lax.fori_loop(0, slots, one_slot, 0)
    turn = turn_ref[place_ref[0]]
    first, second, _ = pick_slots(block_ref, cutoff_ref, rows)
    mine, other = mine_first((first, second), place_ref[1])
    for slot, spec_ref in ((other, other_ref), (mine, mine_ref)):
        spec = split_dot(
            tend_ref[:, slot].reshape(fields * rows * levels, width), high_ref[...], low_ref[...]
        )
        spec_ref[...] = turned(spec, turn, 1.0)
    for s in range(slots):
        streamed(s).wait()


def local_tendency(state, courant_x, courant_y, west, east, forward, turn, place, block, cutoff):
    fields, slots, rows, levels, width = state.shape
    count = fields * rows * levels
    spec = jax.ShapeDtypeStruct((count, 2 * KCUT), F32)
    return pl.pallas_call(
        tendency_kernel,
        in_specs=vmem(8) + smem(3),
        out_specs=[pl.BlockSpec(memory_space=pl.ANY)] + vmem(2),
        out_shape=[jax.ShapeDtypeStruct(state.shape, F32), spec, spec],
        scratch_shapes=[
            pltpu.VMEM(state.shape, F32),
            pltpu.VMEM(state.shape, F32),
            pltpu.SemaphoreType.DMA((slots,)),
        ],
        compiler_params=pltpu.CompilerParams(vmem_limit_bytes=50 * MIB),
        cost_estimate=pl.CostEstimate(
            flops=6 * count * 2 * KCUT * width * 2, bytes_accessed=9 * 10**6, transcendentals=0
        ),
        name="tendency",
    )(state, courant_x, courant_y, west, east, *forward, turn, place, block, cutoff)


def chosen_slot(i, place_ref, block_ref, cutoff_ref, rows):
    first, second, _ = pick_slots(block_ref, cutoff_ref, rows)
    return jnp.where(i == place_ref[1], first, second)


def main_kernel(
    place_ref,
    block_ref,
    cutoff_ref,
    state_ref,
    base_ref,
    mine_ref,
    away_ref,
    high_ref,
    low_ref,
    turn_ref,
    after_ref,
    out_ref,
    token_ref,
):
    fields, _, rows, levels, width = state_ref.shape
    del after_ref
    token_ref[...] = jnp.zeros_like(token_ref)
    i = pl.program_id(0)
    turn = turn_ref[place_ref[0]]
    slot = chosen_slot(i, place_ref, block_ref, cutoff_ref, rows)
    spec = turned(jnp.where(i == 0, mine_ref[...], away_ref[...]), turn, -1.0)
    spec = spec.reshape(fields, rows, levels, 2 * KCUT)
    cuts = [cutoff_ref[block_ref[slot] * rows + r] for r in range(rows)]
    spec = jnp.concatenate(
        [spec[:, r : r + 1] * row_weights(cuts[r]) for r in range(rows)], axis=1
    )
    smooth = split_dot(
        spec.reshape(fields * rows * levels, 2 * KCUT), high_ref[...], low_ref[...]
    ).reshape(fields, rows, levels, width)
    for r in range(rows):
        out_ref[:, 0, r] = jnp.where(
            cuts[r] > 0, state_ref[:, 0, r] + smooth[:, r], base_ref[:, 0, r]
        )


def main_part(after, state, base, mine, away, inverse, turn, place, block, cutoff):
    fields, slots, rows, levels, width = state.shape
    slot_block = pl.BlockSpec(
        (fields, 1, rows, levels, width),
        lambda i, *scalars: (0, chosen_slot(i, *scalars, rows), 0, 0, 0),
    )
    return pl.pallas_call(
        main_kernel,
        grid_spec=pltpu.PrefetchScalarGridSpec(
            num_scalar_prefetch=3,
            grid=(2,),
            in_specs=[slot_block, slot_block] + vmem(6),
            out_specs=[slot_block, pl.BlockSpec((1, 2 * KCUT), lambda i, *scalars: (0, 0))],
        ),
        out_shape=[
            jax.ShapeDtypeStruct(state.shape, F32),
            jax.ShapeDtypeStruct((1, 2 * KCUT), F32),
        ],
        input_output_aliases={4: 0},
        compiler_params=pltpu.CompilerParams(vmem_limit_bytes=50 * MIB),
        cost_estimate=pl.CostEstimate(
            flops=12 * mine.shape[0] * 2 * KCUT * width,
            bytes_accessed=6 * 10**6,
            transcendentals=0,
        ),
        name="main",
    )(place, block, cutoff, state, base, mine, away, *inverse, turn, after)


def unpack(ref, full, tail, spare, put, fields, width):
    tiles = -(-width // LANES)
    lane = lax.broadcasted_iota(jnp.int32, (8, LANES), 1)

    def load(row):
        return ref[pl.ds(row, 8, stride=BACK), :]

    for f in range(fields):
        for t in range(tiles - 1):
            put(f, t * LANES, (t + 1) * LANES, load(full + t * fields + f))
        tile = load(tail + f)
        if spare is not None:
            other = pltpu.roll(load(spare + f), 2 * SPARE, 1)
            tile = jnp.where(lane < SPARE, pltpu.roll(tile, SPARE, 1), other)
        put(f, (tiles - 1) * LANES, width, tile[:, :TAIL])


def rim_kernel(
    packed,
    got_ref,
    high_ref,
    low_ref,
    turn_ref,
    place_ref,
    faces_ref,
    mine_ref,
    other_ref,
    token_ref,
):
    _, _, fields, levels, width = faces_ref.shape
    token_ref[...] = jnp.zeros_like(token_ref)
    if packed:
        for i in range(2):
            for side in range(2):

                def put(f, start, stop, tile, i=i, side=side):
                    faces_ref[i, side, f, :, start:stop] = tile

                q = 2 * i + side
                unpack(got_ref, 25 * q, 150 + 5 * q, None, put, fields, width)
    else:
        faces_ref[...] = got_ref[...]
    turn = turn_ref[place_ref[0]]
    core = place_ref[1]
    both = jnp.concatenate(
        [part for i in (core, 1 - core) for part in (faces_ref[i, 0], -faces_ref[i, 1])], axis=0
    ).reshape(4 * fields * levels, width)
    spec = turned(split_dot(both, high_ref[...], low_ref[...], axis=1), turn, 1.0)
    mine_ref[...] = spec[: 2 * fields * levels]
    other_ref[...] = spec[2 * fields * levels :]


def rim_spectra(got, shape, inverse, turn, place):
    _, _, fields, levels, width = shape
    spec = jax.ShapeDtypeStruct((2 * fields * levels, 2 * KCUT), F32)
    return pl.pallas_call(
        functools.partial(rim_kernel, got.ndim == 2),
        in_specs=vmem(4) + smem(1),
        out_specs=vmem(4),
        out_shape=[
            jax.ShapeDtypeStruct(shape, F32),
            spec,
            spec,
            jax.ShapeDtypeStruct((8, LANES), F32),
        ],
        compiler_params=pltpu.CompilerParams(vmem_limit_bytes=50 * MIB),
        cost_estimate=pl.CostEstimate(
            flops=24 * fields * levels * 2 * KCUT * width,
            bytes_accessed=3 * 10**6,
            transcendentals=0,
        ),
        name="rim_spectra",
    )(got, *inverse, turn, place)


def final_kernel(
    packed,
    main_ref,
    pair_ref,
    back_ref,
    mine_ref,
    away_ref,
    high_ref,
    low_ref,
    turn_ref,
    place_ref,
    block_ref,
    cutoff_ref,
    out_ref,
    smooth_ref,
):
    fields, slots, _, levels, width = main_ref.shape
    rows = 8
    side = pl.program_id(0)
    row = side * (rows - 1)
    turn = turn_ref[place_ref[0]]
    core = place_ref[1]
    first, second, rest = pick_slots(block_ref, cutoff_ref, rows)
    mine, other = mine_first((first, second), core)
    count = fields * levels

    @pl.when(side == 0)
    def _():
        spec = [
            turned(ref[j * count : (j + 1) * count], turn, -1.0)
            * row_weights(cutoff_ref[block_ref[slot] * rows + j * (rows - 1)])
            for slot, ref in ((mine, mine_ref), (other, away_ref))
            for j in range(2)
        ]
        smooth = split_dot(jnp.concatenate(spec, axis=0), high_ref[...], low_ref[...])
        smooth_ref[...] = smooth.reshape(2, 2, fields, levels, width)

    sign = jnp.where(side == 0, 1.0, -1.0).astype(F32)
    if packed:

        def put(f, start, stop, tile):
            old = main_ref[f, rest, 0, :, start:stop]
            out_ref[f, rest, 0, :, start:stop] = old + tile * sign

        unpack(
            back_ref, 100 + 25 * side, 150 + 5 * side, 160 + 5 * side, put, fields, width
        )
    else:
        out_ref[:, rest, 0] = main_ref[:, rest, 0] + back_ref[side] * sign
    cuts = [cutoff_ref[block_ref[slot] * rows + row] for slot in (mine, other)]
    for i, (slot, order) in enumerate(((mine, core), (other, 1 - core))):
        out_ref[:, slot, 0] = main_ref[:, slot, 0] + jnp.where(
            cuts[i] > 0, smooth_ref[i, side], pair_ref[order, side] * sign
        )


def final_part(main, pair, back, mine, away, inverse, turn, place, block, cutoff):
    fields, slots, rows, levels, width = main.shape
    block_spec = pl.BlockSpec(
        (fields, slots, 1, levels, width), lambda i: (0, 0, i * (rows - 1), 0, 0)
    )
    return pl.pallas_call(
        functools.partial(final_kernel, back.ndim == 2),
        grid=(2,),
        in_specs=[block_spec] + vmem(7) + smem(3),
        out_specs=block_spec,
        scratch_shapes=[pltpu.VMEM((2, 2, fields, levels, width), F32)],
        out_shape=jax.ShapeDtypeStruct(main.shape, F32),
        input_output_aliases={0: 0},
        compiler_params=pltpu.CompilerParams(vmem_limit_bytes=50 * MIB),
        cost_estimate=pl.CostEstimate(
            flops=12 * mine.shape[0] * 2 * KCUT * width,
            bytes_accessed=4 * 10**6,
            transcendentals=0,
        ),
        name="final",
    )(main, pair, back, mine, away, *inverse, turn, place, block, cutoff)


def swap(array, bit):
    size = lax.axis_size("lon")
    return lax.ppermute(array, "lon", [(i, i ^ bit) for i in range(size)])


def lon_sum(mine, other, last=None):
    total = mine + swap(other, 1)
    bit = 2
    while bit < lax.axis_size("lon"):
        total = total + swap(total, bit)
        bit *= 2
    if last is not None:
        total = total + last
    return total, swap(total, 1)


def shards(state, courant_x, courant_y, block_of_slot, face_source, cutoff):
    fields, slots, rows, levels, width = state.shape
    lat, lon = lax.axis_size("lat"), lax.axis_size("lon")
    lon_index = lax.axis_index("lon")
    place = jnp.stack([lon_index, lon_index % 2]).astype(jnp.int32)
    forward, inverse = basis_tables(width)
    turn = turn_table(lon, width)
    tables = (turn, place, block_of_slot, cutoff)

    packed = lat == levels == 8 and width == 5 * LANES + TAIL and fields == 5
    if packed:
        sent = pack(state, courant_y, block_of_slot).reshape(lat, PIECE, LANES)
        got = lax.all_to_all(sent, "lat", 0, 0, tiled=True)

    west, east = edges(state, courant_x)
    west = lax.ppermute(west, "lon", [(i, (i + 1) % lon) for i in range(lon)])
    east = lax.ppermute(east, "lon", [((i + 1) % lon, i) for i in range(lon)])
    base, mine, other = local_tendency(
        state, courant_x, courant_y, west, east, forward, *tables
    )
    if packed:
        back, mine = faces_of_pieces(got, slots, cutoff, mine)
        back = lax.all_to_all(back, "lat", 0, 0, tiled=True)
        pair = rest = back.reshape(lat * BACK, LANES)
    else:
        faces = exchange_faces(state, courant_y, face_source)
        picked = pick_slots(block_of_slot, cutoff, rows)
        pair, rest = faces[jnp.stack(picked[:2])], faces[picked[2]]
    total, away = lon_sum(mine, other)
    shape = (2, 2, fields, levels, width)
    pair, rim_mine, rim_other, token = rim_spectra(pair, shape, inverse, turn, place)
    main, token = main_part(token, state, base, total, away, inverse, *tables)
    rim_total, rim_away = lon_sum(rim_mine, rim_other, token)
    return final_part(main, pair, rest, rim_total, rim_away, inverse, *tables)


def solution(mesh):
    placed = (
        P(None, "lat", None, None, "lon"),
        P("lat", None, None, "lon"),
        P("lat", None, None, "lon"),
        P("lat"),
        P("lat", None),
        P(),
    )
    return jax.shard_map(
        shards,
        mesh=mesh,
        in_specs=placed,
        out_specs=P(None, "lat", None, None, "lon"),
        check_vma=False,
    )
```

```python
import functools
import math

import jax
import jax.numpy as jnp
import numpy as np
from jax import lax
from jax.experimental import pallas as pl
from jax.experimental.pallas import tpu as pltpu
from jax.sharding import PartitionSpec as P

NLON = 2880
KCUT = 256
LANES = 128
MIB = 1024 * 1024
BF16 = jnp.bfloat16
F32 = jnp.float32


def phases(columns):
    wavenumber = np.arange(KCUT, dtype=np.int64)
    return (columns[:, None] * wavenumber[None, :] % NLON).astype(np.float64) * (
        2.0 * math.pi / NLON
    )


def basis_tables(width):
    phase = phases(np.arange(width, dtype=np.int64))
    table = np.concatenate([np.cos(phase), np.sin(phase)], axis=1).astype(np.float32)
    high = table.astype(jnp.bfloat16)
    low = (table - high.astype(np.float32)).astype(jnp.bfloat16)
    forward = (jnp.asarray(high), jnp.asarray(low))
    inverse = (
        jnp.asarray(np.ascontiguousarray(high.T)),
        jnp.asarray(np.ascontiguousarray(low.T)),
    )
    return forward, inverse


def turn_table(lon, width):
    phase = phases(np.arange(lon, dtype=np.int64) * width)
    table = np.concatenate([np.cos(phase), np.sin(phase)], axis=1).astype(np.float32)
    return jnp.asarray(table[:, None, :])


def split_dot(rows, high, low, axis=0):
    rows_high = rows.astype(BF16)
    rows_low = (rows - rows_high.astype(F32)).astype(BF16)
    dot = functools.partial(
        lax.dot_general,
        dimension_numbers=(((1,), (axis,)), ((), ())),
        preferred_element_type=F32,
    )
    return dot(rows_high, high) + (dot(rows_low, high) + dot(rows_high, low))


def turned(spec, turn, sign):
    real, imag = spec[:, :KCUT], spec[:, KCUT:]
    cos, sin = turn[:, :KCUT], turn[:, KCUT:] * sign
    return jnp.concatenate([real * cos - imag * sin, imag * cos + real * sin], axis=1)


def row_weights(cut):
    column = lax.broadcasted_iota(jnp.int32, (1, 2 * KCUT), 1)
    wavenumber = jnp.where(column >= KCUT, column - KCUT, column)
    scale = jnp.where(wavenumber == 0, 1.0 / NLON, 2.0 / NLON).astype(F32)
    return jnp.where(wavenumber < cut, scale, 0.0)


def pick_slots(block_ref, cutoff_ref, rows):
    polar1 = cutoff_ref[block_ref[1] * rows] > 0
    polar2 = cutoff_ref[block_ref[2] * rows] > 0
    rest = jnp.where(polar2, jnp.where(polar1, 0, 1), 2)
    return jnp.where(rest == 0, 1, 0), jnp.where(rest == 2, 1, 2), rest


def mine_first(pair, core):
    a, b = pair
    return jnp.where(core == 0, a, b), jnp.where(core == 0, b, a)


def vmem(count):
    return [pl.BlockSpec(memory_space=pltpu.VMEM)] * count


def smem(count):
    return [pl.BlockSpec(memory_space=pltpu.SMEM)] * count


def edge_kernel(lane_last, head_ref, tail_ref, wind_ref, west_ref, east_ref):
    fields, slots, rows = head_ref.shape[:3]
    lane = lax.broadcasted_iota(jnp.int32, (8, LANES), 1)
    for s in range(slots):
        west = jnp.zeros((8, LANES), F32)
        east = jnp.zeros((8, LANES), F32)
        for r in range(rows):
            for f in range(fields):
                here = lane == f * rows + r
                west = jnp.where(here, tail_ref[f, s, r, :, lane_last : lane_last + 1], west)
                east = jnp.where(here, head_ref[f, s, r, :, 0:1], east)
            here = lane == fields * rows + r
            west = jnp.where(here, wind_ref[s, r, :, lane_last : lane_last + 1], west)
        west_ref[s] = west
        east_ref[s] = east


def edges(state, courant_x):
    fields, slots, rows, levels, width = state.shape
    last = (width - 1) // LANES
    out = jax.ShapeDtypeStruct((slots, levels, LANES), F32)
    return pl.pallas_call(
        functools.partial(edge_kernel, (width - 1) % LANES),
        grid=(1,),
        in_specs=[
            pl.BlockSpec((fields, slots, rows, levels, LANES), lambda i: (0, 0, 0, 0, 0)),
            pl.BlockSpec((fields, slots, rows, levels, LANES), lambda i: (0, 0, 0, 0, last)),
            pl.BlockSpec((slots, rows, levels, LANES), lambda i: (0, 0, 0, last)),
        ],
        out_specs=[pl.BlockSpec((slots, levels, LANES), lambda i: (0, 0, 0))] * 2,
        out_shape=[out, out],
        cost_estimate=pl.CostEstimate(flops=10**5, bytes_accessed=1200000, transcendentals=0),
        name="edges",
    )(state, state, courant_x)


PIECE = 192
BACK = 176
TAIL = 80
SPARE = LANES - TAIL


def tile_of(slab, t, width):
    part = slab[:, t * LANES : min((t + 1) * LANES, width)]
    if part.shape[1] < LANES:
        part = jnp.concatenate([part, jnp.zeros((8, LANES - part.shape[1]), F32)], axis=1)
    return part


def pack_kernel(width, first_ref, last_ref, wind_ref, block_ref, out_ref):
    fields, slots = first_ref.shape[:2]
    tiles = -(-width // LANES)

    lane = lax.broadcasted_iota(jnp.int32, (8, LANES), 1)

    def put(row, tile):
        out_ref[pl.ds(row, 8, stride=PIECE), :] = tile

    tails = []
    for j in range(slots):
        half = wind_ref[j, 0] * 0.5
        north = [last_ref[f, j, 0] * half for f in range(fields)]
        south = [first_ref[f, j, 0] for f in range(fields)]
        for t in range(tiles - 1):
            put(55 * j + 25 + t, tile_of(half, t, width))
            for f in range(fields):
                put(55 * j + t * fields + f, tile_of(north[f], t, width))
                put(55 * j + 30 + t * fields + f, tile_of(south[f], t, width))
        tails.append([tile_of(slab, tiles - 1, width) for slab in (*north, half, *south)])
    for u, (a, b, c) in enumerate(zip(*tails)):
        put(165 + u, jnp.where(lane < TAIL, a, pltpu.roll(c, TAIL, 1)))
        put(176 + u, jnp.where(lane < TAIL, b, pltpu.roll(c, LANES - 2 * SPARE, 1)))
    table = jnp.zeros((8, LANES), jnp.int32)
    for j in range(slots):
        table = jnp.where(lane == j, block_ref[j], table)
    for row in range(187, PIECE):
        put(row, table.astype(F32))


def pack(state, courant_y, block):
    fields, slots, rows, levels, width = state.shape
    return pl.pallas_call(
        functools.partial(pack_kernel, width),
        grid=(1,),
        in_specs=[
            pl.BlockSpec((fields, slots, 1, levels, width), lambda i: (0, 0, 0, 0, 0)),
            pl.BlockSpec((fields, slots, 1, levels, width), lambda i: (0, 0, rows - 1, 0, 0)),
            pl.BlockSpec((slots, 1, levels, width), lambda i: (0, rows - 1, 0, 0)),
            pl.BlockSpec(memory_space=pltpu.SMEM),
        ],
        out_specs=pl.BlockSpec((levels * PIECE, LANES), lambda i: (0, 0)),
        out_shape=jax.ShapeDtypeStruct((levels * PIECE, LANES), F32),
        cost_estimate=pl.CostEstimate(flops=10**5, bytes_accessed=1700000, transcendentals=0),
        name="pack",
    )(state, state, courant_y, block)


def face_kernel(
    got_ref,
    cutoff_ref,
    later_in_ref,
    out_ref,
    later_ref,
    face_ref,
    south_ref,
    half_ref,
    whole_ref,
    table_ref,
    slot_ref,
    sem,
):
    del later_in_ref, later_ref
    parts = got_ref.shape[0]
    slots = face_ref.shape[0] // parts
    count = parts * slots
    whole_ref[...] = got_ref[:, 184:192, :].astype(jnp.int32)
    copy = pltpu.make_async_copy(whole_ref, table_ref, sem)
    copy.start()
    lane = lax.broadcasted_iota(jnp.int32, (8, LANES), 1)
    wide = lax.broadcasted_iota(jnp.int32, (16, LANES), 1)
    tails = []
    for s in range(count):
        src, j = divmod(s, slots)
        if j < 2:
            tail = got_ref[src, 165 + 11 * j : 176 + 11 * j, :]
        else:
            one = pltpu.roll(got_ref[src, 165:181, :], SPARE, 1)
            two = pltpu.roll(got_ref[src, 176:192, :], 2 * SPARE, 1)
            tail = jnp.where(wide < SPARE, one, two)[:11]
        south_ref[s, :25] = got_ref[src, 55 * j + 30 : 55 * j + 55, :]
        south_ref[s, 25:30] = tail[6:]
        face_ref[s, :25] = got_ref[src, 55 * j : 55 * j + 25, :]
        face_ref[s, 25:30] = tail[:5]
        half_ref[s, :5] = got_ref[src, 55 * j + 25 : 55 * j + 30, :]
        half_ref[s, 5:6] = tail[5:6]
    copy.wait()
    blocks = [table_ref[s // slots, 3, s % slots] for s in range(count)]
    slot_ref[0] = -1
    slot_ref[count + 1] = -1
    for s in range(count):
        slot_ref[blocks[s] + 1] = s
    for s in range(count):
        south = slot_ref[blocks[s] + 2]
        half = jnp.concatenate(
            [jnp.broadcast_to(half_ref[s, t : t + 1], (5, LANES)) for t in range(6)], axis=0
        )
        face = face_ref[s, :30] + half * south_ref[jnp.maximum(south, 0), :30]
        face_ref[s, :30] = jnp.where(south >= 0, face, 0.0)
    for d in range(parts):
        first, second, rest = pick_slots(blocks[slots * d : slots * d + slots], cutoff_ref, 8)
        tails = []
        for i, slot in enumerate((first, second, rest)):
            block = jnp.where(
                slot == 0,
                blocks[slots * d],
                jnp.where(slot == 1, blocks[slots * d + 1], blocks[slots * d + 2]),
            )
            north = slot_ref[block]
            for q, face, there in (
                (2 * i, jnp.maximum(north, 0), north >= 0),
                (2 * i + 1, slots * d + slot, None),
            ):
                rows, tail = face_ref[face, :25], face_ref[face, 24:32]
                if there is not None:
                    rows, tail = jnp.where(there, rows, 0.0), jnp.where(there, tail, 0.0)
                out_ref[d, 25 * q : 25 * q + 25] = rows
                tails.append(tail)
        for q in range(4):
            rest_tail = pltpu.roll(tails[4 + q % 2], TAIL if q < 2 else LANES - 2 * SPARE, 1)
            tail = jnp.where(lane < TAIL, tails[q], rest_tail)
            out_ref[d, 150 + 5 * q : 155 + 5 * q] = tail[1:6]
        out_ref[d, 170:BACK] = jnp.zeros((BACK - 170, LANES), F32)


def faces_of_pieces(got, slots, cutoff, later):
    parts = got.shape[0]
    return pl.pallas_call(
        face_kernel,
        in_specs=vmem(1) + smem(1) + [pl.BlockSpec(memory_space=pl.ANY)],
        out_specs=vmem(1) + [pl.BlockSpec(memory_space=pl.ANY)],
        out_shape=[
            jax.ShapeDtypeStruct((parts, BACK, LANES), F32),
            jax.ShapeDtypeStruct(later.shape, F32),
        ],
        input_output_aliases={2: 1},
        scratch_shapes=[
            pltpu.VMEM((parts * slots, 32, LANES), F32),
            pltpu.VMEM((parts * slots, 32, LANES), F32),
            pltpu.VMEM((parts * slots, 8, LANES), F32),
            pltpu.VMEM((parts, 8, LANES), jnp.int32),
            pltpu.SMEM((parts, 8, LANES), jnp.int32),
            pltpu.SMEM((parts * slots + 2,), jnp.int32),
            pltpu.SemaphoreType.DMA(()),
        ],
        compiler_params=pltpu.CompilerParams(vmem_limit_bytes=16 * MIB),
        cost_estimate=pl.CostEstimate(flops=10**5, bytes_accessed=1600000, transcendentals=0),
        name="faces",
    )(got, cutoff, later)


def to_pieces(units, parts):
    count, levels, width = units.shape
    groups = math.gcd(parts, levels)
    chunks = parts // groups
    span = -(-width // chunks)
    units = jnp.pad(units, ((0, 0), (0, 0), (0, span * chunks - width)))
    units = units.reshape(count, groups, levels // groups, chunks, span)
    return units.transpose(1, 3, 0, 2, 4).reshape(parts, count, levels // groups * span)


def from_pieces(pieces, levels, width):
    parts, count, _ = pieces.shape
    groups = math.gcd(parts, levels)
    chunks = parts // groups
    span = -(-width // chunks)
    pieces = pieces.reshape(groups, chunks, count, levels // groups, span)
    return pieces.transpose(2, 0, 3, 1, 4).reshape(count, levels, chunks * span)[:, :, :width]


def exchange_faces(state, courant_y, face_source):
    fields, slots, rows, levels, width = state.shape
    lat = lax.axis_size("lat")
    count = 2 * fields + 1
    first = state[:, :, 0].transpose(1, 0, 2, 3)
    last = state[:, :, rows - 1].transpose(1, 0, 2, 3)
    half = courant_y[:, rows - 1][:, None] * 0.5
    units = jnp.concatenate([first, last * half, half], axis=1)
    sent = to_pieces(units.reshape(slots * count, levels, width), lat)
    span = sent.shape[2]
    table = jnp.pad(
        face_source.astype(F32).reshape(1, slots * 2), ((0, 0), (0, span - slots * 2))
    )
    sent = jnp.concatenate([sent, jnp.broadcast_to(table[None], (lat, 1, span))], axis=1)
    got = lax.all_to_all(sent, "lat", 0, 0, tiled=True)
    indices = got[:, slots * count, : slots * 2].reshape(lat * slots, 2).astype(jnp.int32)
    data = got[:, : slots * count].reshape(lat * slots, count, span)
    north, south = indices[:, 0], indices[:, 1]
    face = data[:, fields : 2 * fields] + data[:, 2 * fields :] * data[
        jnp.maximum(south, 0), :fields
    ]
    face = jnp.where((south >= 0)[:, None, None], face, 0.0)
    face_north = jnp.where((north >= 0)[:, None, None], face[jnp.maximum(north, 0)], 0.0)
    back = jnp.concatenate([face_north, face], axis=1).reshape(lat, slots * 2 * fields, span)
    back = lax.all_to_all(back, "lat", 0, 0, tiled=True)
    return from_pieces(back, levels, width).reshape(slots, 2, fields, levels, width)


def tendency_kernel(
    state_ref,
    cx_ref,
    cy_ref,
    west_ref,
    east_ref,
    high_ref,
    low_ref,
    turn_ref,
    place_ref,
    block_ref,
    cutoff_ref,
    out_ref,
    mine_ref,
    other_ref,
    tend_ref,
    base_ref,
    sem,
):
    fields, slots, rows, levels, width = state_ref.shape

    def streamed(s):
        return pltpu.make_async_copy(base_ref.at[:, s], out_ref.at[:, s], sem.at[s])


    tiles = -(-width // LANES)
    lane = lax.broadcasted_iota(jnp.int32, (levels, LANES), 1)
    head, tail, last = lane == 0, lane == LANES - 1, lane == (width - 1) % LANES

    def load(ref, *index):
        out = []
        for t in range(tiles):
            part = ref[index + (slice(None), slice(t * LANES, min((t + 1) * LANES, width)))]
            if part.shape[1] < LANES:
                pad = jnp.zeros((levels, LANES - part.shape[1]), F32)
                part = jnp.concatenate([part, pad], axis=1)
            out.append(part)
        return out

    def one_slot(s, carry):
        west, east = west_ref[s], east_ref[s]
        for f in range(fields):
            above = None
            now = load(state_ref, f, s, 0)
            for r in range(rows):
                column = f * rows + r
                left = [pltpu.roll(x, LANES - 1, 1) for x in now]
                left = [
                    jnp.where(tail, left[t + 1], left[t])
                    if t + 1 < tiles
                    else jnp.where(last, east[:, column : column + 1], left[t])
                    for t in range(tiles)
                ]
                half = [x * 0.5 for x in load(cx_ref, s, r)]
                flux = [h * (x + y) for h, x, y in zip(half, now, left)]
                wind = west[:, fields * rows + r : fields * rows + r + 1] * 0.5
                first = wind * (west[:, column : column + 1] + now[0])
                right = [pltpu.roll(x, 1, 1) for x in flux]
                right = [jnp.where(head, y, x) for x, y in zip(right, [first] + right[:-1])]
                change = [x - y for x, y in zip(right, flux)]
                if above is not None:
                    change = [x + y for x, y in zip(change, above)]
                if r + 1 < rows:
                    later = load(state_ref, f, s, r + 1)
                    half = load(cy_ref, s, r)
                    above = [h * 0.5 * (x + y) for h, x, y in zip(half, now, later)]
                    change = [x - y for x, y in zip(change, above)]
                for t in range(tiles):
                    stop = min((t + 1) * LANES, width)
                    base = now[t] + change[t]
                    tend_ref[f, s, r, :, t * LANES : stop] = change[t][:, : stop - t * LANES]
                    base_ref[f, s, r, :, t * LANES : stop] = base[:, : stop - t * LANES]
                now = later
        streamed(s).start()
        return carry

    lax.fori_loop(0, slots, one_slot, 0)
    turn = turn_ref[place_ref[0]]
    first, second, _ = pick_slots(block_ref, cutoff_ref, rows)
    mine, other = mine_first((first, second), place_ref[1])
    for slot, spec_ref in ((other, other_ref), (mine, mine_ref)):
        spec = split_dot(
            tend_ref[:, slot].reshape(fields * rows * levels, width), high_ref[...], low_ref[...]
        )
        spec_ref[...] = turned(spec, turn, 1.0)
    for s in range(slots):
        streamed(s).wait()


def local_tendency(state, courant_x, courant_y, west, east, forward, turn, place, block, cutoff):
    fields, slots, rows, levels, width = state.shape
    count = fields * rows * levels
    spec = jax.ShapeDtypeStruct((count, 2 * KCUT), F32)
    return pl.pallas_call(
        tendency_kernel,
        in_specs=vmem(8) + smem(3),
        out_specs=[pl.BlockSpec(memory_space=pl.ANY)] + vmem(2),
        out_shape=[jax.ShapeDtypeStruct(state.shape, F32), spec, spec],
        scratch_shapes=[
            pltpu.VMEM(state.shape, F32),
            pltpu.VMEM(state.shape, F32),
            pltpu.SemaphoreType.DMA((slots,)),
        ],
        compiler_params=pltpu.CompilerParams(vmem_limit_bytes=50 * MIB),
        cost_estimate=pl.CostEstimate(
            flops=6 * count * 2 * KCUT * width * 2, bytes_accessed=9 * 10**6, transcendentals=0
        ),
        name="tendency",
    )(state, courant_x, courant_y, west, east, *forward, turn, place, block, cutoff)


def chosen_slot(i, place_ref, block_ref, cutoff_ref, rows):
    first, second, _ = pick_slots(block_ref, cutoff_ref, rows)
    return jnp.where(i == place_ref[1], first, second)


def main_kernel(
    place_ref,
    block_ref,
    cutoff_ref,
    state_ref,
    base_ref,
    mine_ref,
    away_ref,
    high_ref,
    low_ref,
    turn_ref,
    after_ref,
    out_ref,
    token_ref,
):
    fields, _, rows, levels, width = state_ref.shape
    del after_ref
    token_ref[...] = jnp.zeros_like(token_ref)
    i = pl.program_id(0)
    turn = turn_ref[place_ref[0]]
    slot = chosen_slot(i, place_ref, block_ref, cutoff_ref, rows)
    spec = turned(jnp.where(i == 0, mine_ref[...], away_ref[...]), turn, -1.0)
    spec = spec.reshape(fields, rows, levels, 2 * KCUT)
    cuts = [cutoff_ref[block_ref[slot] * rows + r] for r in range(rows)]
    spec = jnp.concatenate(
        [spec[:, r : r + 1] * row_weights(cuts[r]) for r in range(rows)], axis=1
    )
    smooth = split_dot(
        spec.reshape(fields * rows * levels, 2 * KCUT), high_ref[...], low_ref[...]
    ).reshape(fields, rows, levels, width)
    for r in range(rows):
        out_ref[:, 0, r] = jnp.where(
            cuts[r] > 0, state_ref[:, 0, r] + smooth[:, r], base_ref[:, 0, r]
        )


def main_part(after, state, base, mine, away, inverse, turn, place, block, cutoff):
    fields, slots, rows, levels, width = state.shape
    slot_block = pl.BlockSpec(
        (fields, 1, rows, levels, width),
        lambda i, *scalars: (0, chosen_slot(i, *scalars, rows), 0, 0, 0),
    )
    return pl.pallas_call(
        main_kernel,
        grid_spec=pltpu.PrefetchScalarGridSpec(
            num_scalar_prefetch=3,
            grid=(2,),
            in_specs=[slot_block, slot_block] + vmem(6),
            out_specs=[slot_block, pl.BlockSpec((1, 2 * KCUT), lambda i, *scalars: (0, 0))],
        ),
        out_shape=[
            jax.ShapeDtypeStruct(state.shape, F32),
            jax.ShapeDtypeStruct((1, 2 * KCUT), F32),
        ],
        input_output_aliases={4: 0},
        compiler_params=pltpu.CompilerParams(vmem_limit_bytes=50 * MIB),
        cost_estimate=pl.CostEstimate(
            flops=12 * mine.shape[0] * 2 * KCUT * width,
            bytes_accessed=6 * 10**6,
            transcendentals=0,
        ),
        name="main",
    )(place, block, cutoff, state, base, mine, away, *inverse, turn, after)


def unpack(ref, full, tail, spare, put, fields, width):
    tiles = -(-width // LANES)
    lane = lax.broadcasted_iota(jnp.int32, (8, LANES), 1)

    def load(row):
        return ref[pl.ds(row, 8, stride=BACK), :]

    for f in range(fields):
        for t in range(tiles - 1):
            put(f, t * LANES, (t + 1) * LANES, load(full + t * fields + f))
        tile = load(tail + f)
        if spare is not None:
            other = pltpu.roll(load(spare + f), 2 * SPARE, 1)
            tile = jnp.where(lane < SPARE, pltpu.roll(tile, SPARE, 1), other)
        put(f, (tiles - 1) * LANES, width, tile[:, :TAIL])


def rim_kernel(
    packed,
    got_ref,
    high_ref,
    low_ref,
    turn_ref,
    place_ref,
    faces_ref,
    mine_ref,
    other_ref,
    token_ref,
):
    _, _, fields, levels, width = faces_ref.shape
    token_ref[...] = jnp.zeros_like(token_ref)
    if packed:
        for i in range(2):
            for side in range(2):

                def put(f, start, stop, tile, i=i, side=side):
                    faces_ref[i, side, f, :, start:stop] = tile

                q = 2 * i + side
                unpack(got_ref, 25 * q, 150 + 5 * q, None, put, fields, width)
    else:
        faces_ref[...] = got_ref[...]
    turn = turn_ref[place_ref[0]]
    core = place_ref[1]
    both = jnp.concatenate(
        [part for i in (core, 1 - core) for part in (faces_ref[i, 0], -faces_ref[i, 1])], axis=0
    ).reshape(4 * fields * levels, width)
    spec = turned(split_dot(both, high_ref[...], low_ref[...], axis=1), turn, 1.0)
    mine_ref[...] = spec[: 2 * fields * levels]
    other_ref[...] = spec[2 * fields * levels :]


def rim_spectra(got, shape, inverse, turn, place):
    _, _, fields, levels, width = shape
    spec = jax.ShapeDtypeStruct((2 * fields * levels, 2 * KCUT), F32)
    return pl.pallas_call(
        functools.partial(rim_kernel, got.ndim == 2),
        in_specs=vmem(4) + smem(1),
        out_specs=vmem(4),
        out_shape=[
            jax.ShapeDtypeStruct(shape, F32),
            spec,
            spec,
            jax.ShapeDtypeStruct((8, LANES), F32),
        ],
        compiler_params=pltpu.CompilerParams(vmem_limit_bytes=50 * MIB),
        cost_estimate=pl.CostEstimate(
            flops=24 * fields * levels * 2 * KCUT * width,
            bytes_accessed=3 * 10**6,
            transcendentals=0,
        ),
        name="rim_spectra",
    )(got, *inverse, turn, place)


def final_kernel(
    packed,
    main_ref,
    pair_ref,
    back_ref,
    mine_ref,
    away_ref,
    high_ref,
    low_ref,
    turn_ref,
    place_ref,
    block_ref,
    cutoff_ref,
    out_ref,
    smooth_ref,
):
    fields, slots, _, levels, width = main_ref.shape
    rows = 8
    side = pl.program_id(0)
    row = side * (rows - 1)
    turn = turn_ref[place_ref[0]]
    core = place_ref[1]
    first, second, rest = pick_slots(block_ref, cutoff_ref, rows)
    mine, other = mine_first((first, second), core)
    count = fields * levels

    @pl.when(side == 0)
    def _():
        spec = [
            turned(ref[j * count : (j + 1) * count], turn, -1.0)
            * row_weights(cutoff_ref[block_ref[slot] * rows + j * (rows - 1)])
            for slot, ref in ((mine, mine_ref), (other, away_ref))
            for j in range(2)
        ]
        smooth = split_dot(jnp.concatenate(spec, axis=0), high_ref[...], low_ref[...])
        smooth_ref[...] = smooth.reshape(2, 2, fields, levels, width)

    sign = jnp.where(side == 0, 1.0, -1.0).astype(F32)
    if packed:

        def put(f, start, stop, tile):
            old = main_ref[f, rest, 0, :, start:stop]
            out_ref[f, rest, 0, :, start:stop] = old + tile * sign

        unpack(
            back_ref, 100 + 25 * side, 150 + 5 * side, 160 + 5 * side, put, fields, width
        )
    else:
        out_ref[:, rest, 0] = main_ref[:, rest, 0] + back_ref[side] * sign
    cuts = [cutoff_ref[block_ref[slot] * rows + row] for slot in (mine, other)]
    for i, (slot, order) in enumerate(((mine, core), (other, 1 - core))):
        out_ref[:, slot, 0] = main_ref[:, slot, 0] + jnp.where(
            cuts[i] > 0, smooth_ref[i, side], pair_ref[order, side] * sign
        )


def final_part(main, pair, back, mine, away, inverse, turn, place, block, cutoff):
    fields, slots, rows, levels, width = main.shape
    block_spec = pl.BlockSpec(
        (fields, slots, 1, levels, width), lambda i: (0, 0, i * (rows - 1), 0, 0)
    )
    return pl.pallas_call(
        functools.partial(final_kernel, back.ndim == 2),
        grid=(2,),
        in_specs=[block_spec] + vmem(7) + smem(3),
        out_specs=block_spec,
        scratch_shapes=[pltpu.VMEM((2, 2, fields, levels, width), F32)],
        out_shape=jax.ShapeDtypeStruct(main.shape, F32),
        input_output_aliases={0: 0},
        compiler_params=pltpu.CompilerParams(vmem_limit_bytes=50 * MIB),
        cost_estimate=pl.CostEstimate(
            flops=12 * mine.shape[0] * 2 * KCUT * width,
            bytes_accessed=4 * 10**6,
            transcendentals=0,
        ),
        name="final",
    )(main, pair, back, mine, away, *inverse, turn, place, block, cutoff)


def swap(array, bit):
    size = lax.axis_size("lon")
    return lax.ppermute(array, "lon", [(i, i ^ bit) for i in range(size)])


def lon_sum(mine, other, last=None):
    total = mine + swap(other, 1)
    bit = 2
    while bit < lax.axis_size("lon"):
        total = total + swap(total, bit)
        bit *= 2
    if last is not None:
        total = total + last
    return total, swap(total, 1)


def shards(state, courant_x, courant_y, block_of_slot, face_source, cutoff):
    fields, slots, rows, levels, width = state.shape
    lat, lon = lax.axis_size("lat"), lax.axis_size("lon")
    lon_index = lax.axis_index("lon")
    place = jnp.stack([lon_index, lon_index % 2]).astype(jnp.int32)
    forward, inverse = basis_tables(width)
    turn = turn_table(lon, width)
    tables = (turn, place, block_of_slot, cutoff)

    packed = lat == levels == 8 and width == 5 * LANES + TAIL and fields == 5
    if packed:
        sent = pack(state, courant_y, block_of_slot).reshape(lat, PIECE, LANES)
        got = lax.all_to_all(sent, "lat", 0, 0, tiled=True)

    west, east = edges(state, courant_x)
    west = lax.ppermute(west, "lon", [(i, (i + 1) % lon) for i in range(lon)])
    east = lax.ppermute(east, "lon", [((i + 1) % lon, i) for i in range(lon)])
    base, mine, other = local_tendency(
        state, courant_x, courant_y, west, east, forward, *tables
    )
    if packed:
        back, mine = faces_of_pieces(got, slots, cutoff, mine)
        back = lax.all_to_all(back, "lat", 0, 0, tiled=True)
        pair = rest = back.reshape(lat * BACK, LANES)
    else:
        faces = exchange_faces(state, courant_y, face_source)
        picked = pick_slots(block_of_slot, cutoff, rows)
        pair, rest = faces[jnp.stack(picked[:2])], faces[picked[2]]
    total, away = lon_sum(mine, other)
    shape = (2, 2, fields, levels, width)
    pair, rim_mine, rim_other, token = rim_spectra(pair, shape, inverse, turn, place)
    main, token = main_part(token, state, base, total, away, inverse, *tables)
    rim_total, rim_away = lon_sum(rim_mine, rim_other, token)
    return final_part(main, pair, rest, rim_total, rim_away, inverse, *tables)


def solution(mesh):
    placed = (
        P(None, "lat", None, None, "lon"),
        P("lat", None, None, "lon"),
        P("lat", None, None, "lon"),
        P("lat"),
        P("lat", None),
        P(),
    )
    return jax.shard_map(
        shards,
        mesh=mesh,
        in_specs=placed,
        out_specs=P(None, "lat", None, None, "lon"),
        check_vma=False,
    )
```

```python
import functools
import math

import jax
import jax.numpy as jnp
import numpy as np
from jax import lax
from jax.experimental import pallas as pl
from jax.experimental.pallas import tpu as pltpu
from jax.sharding import PartitionSpec as P

NLON = 2880
KCUT = 256
LANES = 128
MIB = 1024 * 1024
BF16 = jnp.bfloat16
F32 = jnp.float32


def phases(columns):
    wavenumber = np.arange(KCUT, dtype=np.int64)
    return (columns[:, None] * wavenumber[None, :] % NLON).astype(np.float64) * (
        2.0 * math.pi / NLON
    )


def basis_tables(width):
    phase = phases(np.arange(width, dtype=np.int64))
    table = np.concatenate([np.cos(phase), np.sin(phase)], axis=1).astype(np.float32)
    high = table.astype(jnp.bfloat16)
    low = (table - high.astype(np.float32)).astype(jnp.bfloat16)
    forward = (jnp.asarray(high), jnp.asarray(low))
    inverse = (
        jnp.asarray(np.ascontiguousarray(high.T)),
        jnp.asarray(np.ascontiguousarray(low.T)),
    )
    return forward, inverse


def turn_table(lon, width):
    phase = phases(np.arange(lon, dtype=np.int64) * width)
    table = np.concatenate([np.cos(phase), np.sin(phase)], axis=1).astype(np.float32)
    return jnp.asarray(table[:, None, :])


def split_dot(rows, high, low, axis=0):
    rows_high = rows.astype(BF16)
    rows_low = (rows - rows_high.astype(F32)).astype(BF16)
    dot = functools.partial(
        lax.dot_general,
        dimension_numbers=(((1,), (axis,)), ((), ())),
        preferred_element_type=F32,
    )
    return dot(rows_high, high) + (dot(rows_low, high) + dot(rows_high, low))


def turned(spec, turn, sign):
    real, imag = spec[:, :KCUT], spec[:, KCUT:]
    cos, sin = turn[:, :KCUT], turn[:, KCUT:] * sign
    return jnp.concatenate([real * cos - imag * sin, imag * cos + real * sin], axis=1)


def row_weights(cut):
    column = lax.broadcasted_iota(jnp.int32, (1, 2 * KCUT), 1)
    wavenumber = jnp.where(column >= KCUT, column - KCUT, column)
    scale = jnp.where(wavenumber == 0, 1.0 / NLON, 2.0 / NLON).astype(F32)
    return jnp.where(wavenumber < cut, scale, 0.0)


def pick_slots(block_ref, cutoff_ref, rows):
    polar1 = cutoff_ref[block_ref[1] * rows] > 0
    polar2 = cutoff_ref[block_ref[2] * rows] > 0
    rest = jnp.where(polar2, jnp.where(polar1, 0, 1), 2)
    return jnp.where(rest == 0, 1, 0), jnp.where(rest == 2, 1, 2), rest


def mine_first(pair, core):
    a, b = pair
    return jnp.where(core == 0, a, b), jnp.where(core == 0, b, a)


def vmem(count):
    return [pl.BlockSpec(memory_space=pltpu.VMEM)] * count


def smem(count):
    return [pl.BlockSpec(memory_space=pltpu.SMEM)] * count


def hbm(count):
    return [pl.BlockSpec(memory_space=pltpu.HBM)] * count


def edge_kernel(lane_last, head_ref, tail_ref, wind_ref, west_ref, east_ref):
    fields, slots, rows = head_ref.shape[:3]
    lane = lax.broadcasted_iota(jnp.int32, (8, LANES), 1)
    for s in range(slots):
        west = jnp.zeros((8, LANES), F32)
        east = jnp.zeros((8, LANES), F32)
        for r in range(rows):
            for f in range(fields):
                here = lane == f * rows + r
                west = jnp.where(here, tail_ref[f, s, r, :, lane_last : lane_last + 1], west)
                east = jnp.where(here, head_ref[f, s, r, :, 0:1], east)
            here = lane == fields * rows + r
            west = jnp.where(here, wind_ref[s, r, :, lane_last : lane_last + 1], west)
        west_ref[s] = west
        east_ref[s] = east


def edges(state, courant_x):
    fields, slots, rows, levels, width = state.shape
    last = (width - 1) // LANES
    out = jax.ShapeDtypeStruct((slots, levels, LANES), F32)
    return pl.pallas_call(
        functools.partial(edge_kernel, (width - 1) % LANES),
        grid=(1,),
        in_specs=[
            pl.BlockSpec((fields, slots, rows, levels, LANES), lambda i: (0, 0, 0, 0, 0)),
            pl.BlockSpec((fields, slots, rows, levels, LANES), lambda i: (0, 0, 0, 0, last)),
            pl.BlockSpec((slots, rows, levels, LANES), lambda i: (0, 0, 0, last)),
        ],
        out_specs=[pl.BlockSpec((slots, levels, LANES), lambda i: (0, 0, 0))] * 2,
        out_shape=[out, out],
        cost_estimate=pl.CostEstimate(flops=10**5, bytes_accessed=1200000, transcendentals=0),
        name="edges",
    )(state, state, courant_x)


PIECE = 192
BACK = 176
TAIL = 80
SPARE = LANES - TAIL


def tile_of(slab, t, width):
    part = slab[:, t * LANES : min((t + 1) * LANES, width)]
    if part.shape[1] < LANES:
        part = jnp.concatenate([part, jnp.zeros((8, LANES - part.shape[1]), F32)], axis=1)
    return part


def pack_kernel(width, first_ref, last_ref, wind_ref, block_ref, out_ref):
    fields, slots = first_ref.shape[:2]
    tiles = -(-width // LANES)

    lane = lax.broadcasted_iota(jnp.int32, (8, LANES), 1)

    def put(row, tile):
        out_ref[pl.ds(row, 8, stride=PIECE), :] = tile

    tails = []
    for j in range(slots):
        half = wind_ref[j, 0] * 0.5
        north = [last_ref[f, j, 0] * half for f in range(fields)]
        south = [first_ref[f, j, 0] for f in range(fields)]
        for t in range(tiles - 1):
            put(55 * j + 25 + t, tile_of(half, t, width))
            for f in range(fields):
                put(55 * j + t * fields + f, tile_of(north[f], t, width))
                put(55 * j + 30 + t * fields + f, tile_of(south[f], t, width))
        tails.append([tile_of(slab, tiles - 1, width) for slab in (*north, half, *south)])
    for u, (a, b, c) in enumerate(zip(*tails)):
        put(165 + u, jnp.where(lane < TAIL, a, pltpu.roll(c, TAIL, 1)))
        put(176 + u, jnp.where(lane < TAIL, b, pltpu.roll(c, LANES - 2 * SPARE, 1)))
    table = jnp.zeros((8, LANES), jnp.int32)
    for j in range(slots):
        table = jnp.where(lane == j, block_ref[j], table)
    for row in range(187, PIECE):
        put(row, table.astype(F32))


def pack(state, courant_y, block):
    fields, slots, rows, levels, width = state.shape
    return pl.pallas_call(
        functools.partial(pack_kernel, width),
        grid=(1,),
        in_specs=[
            pl.BlockSpec((fields, slots, 1, levels, width), lambda i: (0, 0, 0, 0, 0)),
            pl.BlockSpec((fields, slots, 1, levels, width), lambda i: (0, 0, rows - 1, 0, 0)),
            pl.BlockSpec((slots, 1, levels, width), lambda i: (0, rows - 1, 0, 0)),
            pl.BlockSpec(memory_space=pltpu.SMEM),
        ],
        out_specs=pl.BlockSpec((levels * PIECE, LANES), lambda i: (0, 0)),
        out_shape=jax.ShapeDtypeStruct((levels * PIECE, LANES), F32),
        cost_estimate=pl.CostEstimate(flops=10**5, bytes_accessed=1700000, transcendentals=0),
        name="pack",
    )(state, state, courant_y, block)


def face_kernel(
    got_ref,
    cutoff_ref,
    later_in_ref,
    to_ref,
    later_ref,
    out_ref,
    face_ref,
    south_ref,
    half_ref,
    whole_ref,
    table_ref,
    slot_ref,
    sem,
    out_sem,
):
    del later_in_ref, later_ref
    parts = got_ref.shape[0]
    outgoing = [
        pltpu.make_async_copy(out_ref.at[d], to_ref.at[d], out_sem.at[d]) for d in range(parts)
    ]
    slots = face_ref.shape[0] // parts
    count = parts * slots
    whole_ref[...] = got_ref[:, 184:192, :].astype(jnp.int32)
    copy = pltpu.make_async_copy(whole_ref, table_ref, sem)
    copy.start()
    lane = lax.broadcasted_iota(jnp.int32, (8, LANES), 1)
    wide = lax.broadcasted_iota(jnp.int32, (16, LANES), 1)
    tails = []
    for s in range(count):
        src, j = divmod(s, slots)
        if j < 2:
            tail = got_ref[src, 165 + 11 * j : 176 + 11 * j, :]
        else:
            one = pltpu.roll(got_ref[src, 165:181, :], SPARE, 1)
            two = pltpu.roll(got_ref[src, 176:192, :], 2 * SPARE, 1)
            tail = jnp.where(wide < SPARE, one, two)[:11]
        south_ref[s, :25] = got_ref[src, 55 * j + 30 : 55 * j + 55, :]
        south_ref[s, 25:30] = tail[6:]
        face_ref[s, :25] = got_ref[src, 55 * j : 55 * j + 25, :]
        face_ref[s, 25:30] = tail[:5]
        half_ref[s, :5] = got_ref[src, 55 * j + 25 : 55 * j + 30, :]
        half_ref[s, 5:6] = tail[5:6]
    copy.wait()
    blocks = [table_ref[s // slots, 3, s % slots] for s in range(count)]
    slot_ref[0] = -1
    slot_ref[count + 1] = -1
    for s in range(count):
        slot_ref[blocks[s] + 1] = s
    for s in range(count):
        south = slot_ref[blocks[s] + 2]
        half = jnp.concatenate(
            [jnp.broadcast_to(half_ref[s, t : t + 1], (5, LANES)) for t in range(6)], axis=0
        )
        face = face_ref[s, :30] + half * south_ref[jnp.maximum(south, 0), :30]
        face_ref[s, :30] = jnp.where(south >= 0, face, 0.0)
    for d in range(parts):
        first, second, rest = pick_slots(blocks[slots * d : slots * d + slots], cutoff_ref, 8)
        tails = []
        for i, slot in enumerate((first, second, rest)):
            block = jnp.where(
                slot == 0,
                blocks[slots * d],
                jnp.where(slot == 1, blocks[slots * d + 1], blocks[slots * d + 2]),
            )
            north = slot_ref[block]
            for q, face, there in (
                (2 * i, jnp.maximum(north, 0), north >= 0),
                (2 * i + 1, slots * d + slot, None),
            ):
                rows, tail = face_ref[face, :25], face_ref[face, 24:32]
                if there is not None:
                    rows, tail = jnp.where(there, rows, 0.0), jnp.where(there, tail, 0.0)
                out_ref[d, 25 * q : 25 * q + 25] = rows
                tails.append(tail)
        for q in range(4):
            rest_tail = pltpu.roll(tails[4 + q % 2], TAIL if q < 2 else LANES - 2 * SPARE, 1)
            tail = jnp.where(lane < TAIL, tails[q], rest_tail)
            out_ref[d, 150 + 5 * q : 155 + 5 * q] = tail[1:6]
        out_ref[d, 170:BACK] = jnp.zeros((BACK - 170, LANES), F32)
        outgoing[d].start()
    for part in outgoing:
        part.wait()


def faces_of_pieces(got, slots, cutoff, later):
    parts = got.shape[0]
    return pl.pallas_call(
        face_kernel,
        in_specs=vmem(1) + smem(1) + [pl.BlockSpec(memory_space=pl.ANY)],
        out_specs=hbm(1) + [pl.BlockSpec(memory_space=pl.ANY)],
        out_shape=[
            jax.ShapeDtypeStruct((parts, BACK, LANES), F32),
            jax.ShapeDtypeStruct(later.shape, F32),
        ],
        input_output_aliases={2: 1},
        scratch_shapes=[
            pltpu.VMEM((parts, BACK, LANES), F32),
            pltpu.VMEM((parts * slots, 32, LANES), F32),
            pltpu.VMEM((parts * slots, 32, LANES), F32),
            pltpu.VMEM((parts * slots, 8, LANES), F32),
            pltpu.VMEM((parts, 8, LANES), jnp.int32),
            pltpu.SMEM((parts, 8, LANES), jnp.int32),
            pltpu.SMEM((parts * slots + 2,), jnp.int32),
            pltpu.SemaphoreType.DMA(()),
            pltpu.SemaphoreType.DMA((parts,)),
        ],
        compiler_params=pltpu.CompilerParams(vmem_limit_bytes=16 * MIB),
        cost_estimate=pl.CostEstimate(flops=10**5, bytes_accessed=1600000, transcendentals=0),
        name="faces",
    )(got, cutoff, later)


def to_pieces(units, parts):
    count, levels, width = units.shape
    groups = math.gcd(parts, levels)
    chunks = parts // groups
    span = -(-width // chunks)
    units = jnp.pad(units, ((0, 0), (0, 0), (0, span * chunks - width)))
    units = units.reshape(count, groups, levels // groups, chunks, span)
    return units.transpose(1, 3, 0, 2, 4).reshape(parts, count, levels // groups * span)


def from_pieces(pieces, levels, width):
    parts, count, _ = pieces.shape
    groups = math.gcd(parts, levels)
    chunks = parts // groups
    span = -(-width // chunks)
    pieces = pieces.reshape(groups, chunks, count, levels // groups, span)
    return pieces.transpose(2, 0, 3, 1, 4).reshape(count, levels, chunks * span)[:, :, :width]


def exchange_faces(state, courant_y, face_source):
    fields, slots, rows, levels, width = state.shape
    lat = lax.axis_size("lat")
    count = 2 * fields + 1
    first = state[:, :, 0].transpose(1, 0, 2, 3)
    last = state[:, :, rows - 1].transpose(1, 0, 2, 3)
    half = courant_y[:, rows - 1][:, None] * 0.5
    units = jnp.concatenate([first, last * half, half], axis=1)
    sent = to_pieces(units.reshape(slots * count, levels, width), lat)
    span = sent.shape[2]
    table = jnp.pad(
        face_source.astype(F32).reshape(1, slots * 2), ((0, 0), (0, span - slots * 2))
    )
    sent = jnp.concatenate([sent, jnp.broadcast_to(table[None], (lat, 1, span))], axis=1)
    got = lax.all_to_all(sent, "lat", 0, 0, tiled=True)
    indices = got[:, slots * count, : slots * 2].reshape(lat * slots, 2).astype(jnp.int32)
    data = got[:, : slots * count].reshape(lat * slots, count, span)
    north, south = indices[:, 0], indices[:, 1]
    face = data[:, fields : 2 * fields] + data[:, 2 * fields :] * data[
        jnp.maximum(south, 0), :fields
    ]
    face = jnp.where((south >= 0)[:, None, None], face, 0.0)
    face_north = jnp.where((north >= 0)[:, None, None], face[jnp.maximum(north, 0)], 0.0)
    back = jnp.concatenate([face_north, face], axis=1).reshape(lat, slots * 2 * fields, span)
    back = lax.all_to_all(back, "lat", 0, 0, tiled=True)
    return from_pieces(back, levels, width).reshape(slots, 2, fields, levels, width)


def tendency_kernel(
    far_state_ref,
    far_cx_ref,
    far_cy_ref,
    far_high_ref,
    far_low_ref,
    west_ref,
    east_ref,
    turn_ref,
    place_ref,
    block_ref,
    cutoff_ref,
    out_ref,
    mine_ref,
    other_ref,
    state_ref,
    cx_ref,
    cy_ref,
    high_ref,
    low_ref,
    tend_ref,
    base_ref,
    sem,
    in_sem,
    table_sem,
):
    fields, slots, rows, levels, width = state_ref.shape

    def streamed(s):
        return pltpu.make_async_copy(base_ref.at[:, s], out_ref.at[:, s], sem.at[s])

    def incoming(s):
        return (
            pltpu.make_async_copy(far_state_ref.at[:, s], state_ref.at[:, s], in_sem.at[s, 0]),
            pltpu.make_async_copy(far_cx_ref.at[s], cx_ref.at[s], in_sem.at[s, 1]),
            pltpu.make_async_copy(far_cy_ref.at[s], cy_ref.at[s], in_sem.at[s, 2]),
        )

    tables = (
        pltpu.make_async_copy(far_high_ref, high_ref, table_sem.at[0]),
        pltpu.make_async_copy(far_low_ref, low_ref, table_sem.at[1]),
    )
    for s in range(slots):
        for copy in incoming(s):
            copy.start()
    for copy in tables:
        copy.start()
    tiles = -(-width // LANES)
    lane = lax.broadcasted_iota(jnp.int32, (levels, LANES), 1)
    head, tail, last = lane == 0, lane == LANES - 1, lane == (width - 1) % LANES

    def load(ref, *index):
        out = []
        for t in range(tiles):
            part = ref[index + (slice(None), slice(t * LANES, min((t + 1) * LANES, width)))]
            if part.shape[1] < LANES:
                pad = jnp.zeros((levels, LANES - part.shape[1]), F32)
                part = jnp.concatenate([part, pad], axis=1)
            out.append(part)
        return out

    def one_slot(s, carry):
        for copy in incoming(s):
            copy.wait()
        west, east = west_ref[s], east_ref[s]
        for f in range(fields):
            above = None
            now = load(state_ref, f, s, 0)
            for r in range(rows):
                column = f * rows + r
                left = [pltpu.roll(x, LANES - 1, 1) for x in now]
                left = [
                    jnp.where(tail, left[t + 1], left[t])
                    if t + 1 < tiles
                    else jnp.where(last, east[:, column : column + 1], left[t])
                    for t in range(tiles)
                ]
                half = [x * 0.5 for x in load(cx_ref, s, r)]
                flux = [h * (x + y) for h, x, y in zip(half, now, left)]
                wind = west[:, fields * rows + r : fields * rows + r + 1] * 0.5
                first = wind * (west[:, column : column + 1] + now[0])
                right = [pltpu.roll(x, 1, 1) for x in flux]
                right = [jnp.where(head, y, x) for x, y in zip(right, [first] + right[:-1])]
                change = [x - y for x, y in zip(right, flux)]
                if above is not None:
                    change = [x + y for x, y in zip(change, above)]
                if r + 1 < rows:
                    later = load(state_ref, f, s, r + 1)
                    half = load(cy_ref, s, r)
                    above = [h * 0.5 * (x + y) for h, x, y in zip(half, now, later)]
                    change = [x - y for x, y in zip(change, above)]
                for t in range(tiles):
                    stop = min((t + 1) * LANES, width)
                    base = now[t] + change[t]
                    tend_ref[f, s, r, :, t * LANES : stop] = change[t][:, : stop - t * LANES]
                    base_ref[f, s, r, :, t * LANES : stop] = base[:, : stop - t * LANES]
                now = later
        streamed(s).start()
        return carry

    lax.fori_loop(0, slots, one_slot, 0)
    for copy in tables:
        copy.wait()
    turn = turn_ref[place_ref[0]]
    first, second, _ = pick_slots(block_ref, cutoff_ref, rows)
    mine, other = mine_first((first, second), place_ref[1])
    for slot, spec_ref in ((other, other_ref), (mine, mine_ref)):
        spec = split_dot(
            tend_ref[:, slot].reshape(fields * rows * levels, width), high_ref[...], low_ref[...]
        )
        spec_ref[...] = turned(spec, turn, 1.0)
    for s in range(slots):
        streamed(s).wait()


def local_tendency(state, courant_x, courant_y, west, east, forward, turn, place, block, cutoff):
    fields, slots, rows, levels, width = state.shape
    count = fields * rows * levels
    spec = jax.ShapeDtypeStruct((count, 2 * KCUT), F32)
    return pl.pallas_call(
        tendency_kernel,
        in_specs=hbm(5) + vmem(3) + smem(3),
        out_specs=[pl.BlockSpec(memory_space=pl.ANY)] + vmem(2),
        out_shape=[jax.ShapeDtypeStruct(state.shape, F32), spec, spec],
        scratch_shapes=[
            pltpu.VMEM(state.shape, F32),
            pltpu.VMEM(courant_x.shape, F32),
            pltpu.VMEM(courant_y.shape, F32),
            pltpu.VMEM(forward[0].shape, BF16),
            pltpu.VMEM(forward[1].shape, BF16),
            pltpu.VMEM(state.shape, F32),
            pltpu.VMEM(state.shape, F32),
            pltpu.SemaphoreType.DMA((slots,)),
            pltpu.SemaphoreType.DMA((slots, 3)),
            pltpu.SemaphoreType.DMA((2,)),
        ],
        compiler_params=pltpu.CompilerParams(vmem_limit_bytes=50 * MIB),
        cost_estimate=pl.CostEstimate(
            flops=6 * count * 2 * KCUT * width * 2, bytes_accessed=9 * 10**6, transcendentals=0
        ),
        name="tendency",
    )(state, courant_x, courant_y, *forward, west, east, turn, place, block, cutoff)


def chosen_slot(i, place_ref, block_ref, cutoff_ref, rows):
    first, second, _ = pick_slots(block_ref, cutoff_ref, rows)
    return jnp.where(i == place_ref[1], first, second)


def main_kernel(
    place_ref,
    block_ref,
    cutoff_ref,
    state_ref,
    base_ref,
    mine_ref,
    away_ref,
    high_ref,
    low_ref,
    turn_ref,
    after_ref,
    out_ref,
    token_ref,
):
    fields, _, rows, levels, width = state_ref.shape
    del after_ref
    token_ref[...] = jnp.zeros_like(token_ref)
    i = pl.program_id(0)
    turn = turn_ref[place_ref[0]]
    slot = chosen_slot(i, place_ref, block_ref, cutoff_ref, rows)
    spec = turned(jnp.where(i == 0, mine_ref[...], away_ref[...]), turn, -1.0)
    spec = spec.reshape(fields, rows, levels, 2 * KCUT)
    cuts = [cutoff_ref[block_ref[slot] * rows + r] for r in range(rows)]
    spec = jnp.concatenate(
        [spec[:, r : r + 1] * row_weights(cuts[r]) for r in range(rows)], axis=1
    )
    smooth = split_dot(
        spec.reshape(fields * rows * levels, 2 * KCUT), high_ref[...], low_ref[...]
    ).reshape(fields, rows, levels, width)
    for r in range(rows):
        out_ref[:, 0, r] = jnp.where(
            cuts[r] > 0, state_ref[:, 0, r] + smooth[:, r], base_ref[:, 0, r]
        )


def main_part(after, state, base, mine, away, inverse, turn, place, block, cutoff):
    fields, slots, rows, levels, width = state.shape
    slot_block = pl.BlockSpec(
        (fields, 1, rows, levels, width),
        lambda i, *scalars: (0, chosen_slot(i, *scalars, rows), 0, 0, 0),
    )
    return pl.pallas_call(
        main_kernel,
        grid_spec=pltpu.PrefetchScalarGridSpec(
            num_scalar_prefetch=3,
            grid=(2,),
            in_specs=[slot_block, slot_block] + vmem(6),
            out_specs=[slot_block, pl.BlockSpec((1, 2 * KCUT), lambda i, *scalars: (0, 0))],
        ),
        out_shape=[
            jax.ShapeDtypeStruct(state.shape, F32),
            jax.ShapeDtypeStruct((1, 2 * KCUT), F32),
        ],
        input_output_aliases={4: 0},
        compiler_params=pltpu.CompilerParams(vmem_limit_bytes=50 * MIB),
        cost_estimate=pl.CostEstimate(
            flops=12 * mine.shape[0] * 2 * KCUT * width,
            bytes_accessed=6 * 10**6,
            transcendentals=0,
        ),
        name="main",
    )(place, block, cutoff, state, base, mine, away, *inverse, turn, after)


def unpack(ref, full, tail, spare, put, fields, width):
    tiles = -(-width // LANES)
    lane = lax.broadcasted_iota(jnp.int32, (8, LANES), 1)

    def load(row):
        return ref[pl.ds(row, 8, stride=BACK), :]

    for f in range(fields):
        for t in range(tiles - 1):
            put(f, t * LANES, (t + 1) * LANES, load(full + t * fields + f))
        tile = load(tail + f)
        if spare is not None:
            other = pltpu.roll(load(spare + f), 2 * SPARE, 1)
            tile = jnp.where(lane < SPARE, pltpu.roll(tile, SPARE, 1), other)
        put(f, (tiles - 1) * LANES, width, tile[:, :TAIL])


def rim_kernel(
    packed,
    got_ref,
    high_ref,
    low_ref,
    turn_ref,
    place_ref,
    faces_ref,
    mine_ref,
    other_ref,
    token_ref,
):
    _, _, fields, levels, width = faces_ref.shape
    token_ref[...] = jnp.zeros_like(token_ref)
    if packed:
        for i in range(2):
            for side in range(2):

                def put(f, start, stop, tile, i=i, side=side):
                    faces_ref[i, side, f, :, start:stop] = tile

                q = 2 * i + side
                unpack(got_ref, 25 * q, 150 + 5 * q, None, put, fields, width)
    else:
        faces_ref[...] = got_ref[...]
    turn = turn_ref[place_ref[0]]
    core = place_ref[1]
    both = jnp.concatenate(
        [part for i in (core, 1 - core) for part in (faces_ref[i, 0], -faces_ref[i, 1])], axis=0
    ).reshape(4 * fields * levels, width)
    spec = turned(split_dot(both, high_ref[...], low_ref[...], axis=1), turn, 1.0)
    mine_ref[...] = spec[: 2 * fields * levels]
    other_ref[...] = spec[2 * fields * levels :]


def rim_spectra(got, shape, inverse, turn, place):
    _, _, fields, levels, width = shape
    spec = jax.ShapeDtypeStruct((2 * fields * levels, 2 * KCUT), F32)
    return pl.pallas_call(
        functools.partial(rim_kernel, got.ndim == 2),
        in_specs=vmem(4) + smem(1),
        out_specs=vmem(4),
        out_shape=[
            jax.ShapeDtypeStruct(shape, F32),
            spec,
            spec,
            jax.ShapeDtypeStruct((8, LANES), F32),
        ],
        compiler_params=pltpu.CompilerParams(vmem_limit_bytes=50 * MIB),
        cost_estimate=pl.CostEstimate(
            flops=24 * fields * levels * 2 * KCUT * width,
            bytes_accessed=3 * 10**6,
            transcendentals=0,
        ),
        name="rim_spectra",
    )(got, *inverse, turn, place)


def final_kernel(
    packed,
    main_ref,
    pair_ref,
    back_ref,
    mine_ref,
    away_ref,
    high_ref,
    low_ref,
    turn_ref,
    place_ref,
    block_ref,
    cutoff_ref,
    out_ref,
    smooth_ref,
):
    fields, slots, _, levels, width = main_ref.shape
    rows = 8
    side = pl.program_id(0)
    row = side * (rows - 1)
    turn = turn_ref[place_ref[0]]
    core = place_ref[1]
    first, second, rest = pick_slots(block_ref, cutoff_ref, rows)
    mine, other = mine_first((first, second), core)
    count = fields * levels

    @pl.when(side == 0)
    def _():
        spec = [
            turned(ref[j * count : (j + 1) * count], turn, -1.0)
            * row_weights(cutoff_ref[block_ref[slot] * rows + j * (rows - 1)])
            for slot, ref in ((mine, mine_ref), (other, away_ref))
            for j in range(2)
        ]
        smooth = split_dot(jnp.concatenate(spec, axis=0), high_ref[...], low_ref[...])
        smooth_ref[...] = smooth.reshape(2, 2, fields, levels, width)

    sign = jnp.where(side == 0, 1.0, -1.0).astype(F32)
    if packed:

        def put(f, start, stop, tile):
            old = main_ref[f, rest, 0, :, start:stop]
            out_ref[f, rest, 0, :, start:stop] = old + tile * sign

        unpack(
            back_ref, 100 + 25 * side, 150 + 5 * side, 160 + 5 * side, put, fields, width
        )
    else:
        out_ref[:, rest, 0] = main_ref[:, rest, 0] + back_ref[side] * sign
    cuts = [cutoff_ref[block_ref[slot] * rows + row] for slot in (mine, other)]
    for i, (slot, order) in enumerate(((mine, core), (other, 1 - core))):
        out_ref[:, slot, 0] = main_ref[:, slot, 0] + jnp.where(
            cuts[i] > 0, smooth_ref[i, side], pair_ref[order, side] * sign
        )


def final_part(main, pair, back, mine, away, inverse, turn, place, block, cutoff):
    fields, slots, rows, levels, width = main.shape
    block_spec = pl.BlockSpec(
        (fields, slots, 1, levels, width), lambda i: (0, 0, i * (rows - 1), 0, 0)
    )
    return pl.pallas_call(
        functools.partial(final_kernel, back.ndim == 2),
        grid=(2,),
        in_specs=[block_spec] + vmem(7) + smem(3),
        out_specs=block_spec,
        scratch_shapes=[pltpu.VMEM((2, 2, fields, levels, width), F32)],
        out_shape=jax.ShapeDtypeStruct(main.shape, F32),
        input_output_aliases={0: 0},
        compiler_params=pltpu.CompilerParams(vmem_limit_bytes=50 * MIB),
        cost_estimate=pl.CostEstimate(
            flops=12 * mine.shape[0] * 2 * KCUT * width,
            bytes_accessed=4 * 10**6,
            transcendentals=0,
        ),
        name="final",
    )(main, pair, back, mine, away, *inverse, turn, place, block, cutoff)


def swap(array, bit):
    size = lax.axis_size("lon")
    return lax.ppermute(array, "lon", [(i, i ^ bit) for i in range(size)])


def lon_sum(mine, other, last=None):
    total = mine + swap(other, 1)
    bit = 2
    while bit < lax.axis_size("lon"):
        total = total + swap(total, bit)
        bit *= 2
    if last is not None:
        total = total + last
    return total, swap(total, 1)


def shards(state, courant_x, courant_y, block_of_slot, face_source, cutoff):
    fields, slots, rows, levels, width = state.shape
    lat, lon = lax.axis_size("lat"), lax.axis_size("lon")
    lon_index = lax.axis_index("lon")
    place = jnp.stack([lon_index, lon_index % 2]).astype(jnp.int32)
    forward, inverse = basis_tables(width)
    turn = turn_table(lon, width)
    tables = (turn, place, block_of_slot, cutoff)

    packed = lat == levels == 8 and width == 5 * LANES + TAIL and fields == 5
    if packed:
        sent = pack(state, courant_y, block_of_slot).reshape(lat, PIECE, LANES)
        got = lax.all_to_all(sent, "lat", 0, 0, tiled=True)

    west, east = edges(state, courant_x)
    west = lax.ppermute(west, "lon", [(i, (i + 1) % lon) for i in range(lon)])
    east = lax.ppermute(east, "lon", [((i + 1) % lon, i) for i in range(lon)])
    base, mine, other = local_tendency(
        state, courant_x, courant_y, west, east, forward, *tables
    )
    if packed:
        back, mine = faces_of_pieces(got, slots, cutoff, mine)
        back = lax.all_to_all(back, "lat", 0, 0, tiled=True)
        pair = rest = back.reshape(lat * BACK, LANES)
    else:
        faces = exchange_faces(state, courant_y, face_source)
        picked = pick_slots(block_of_slot, cutoff, rows)
        pair, rest = faces[jnp.stack(picked[:2])], faces[picked[2]]
    total, away = lon_sum(mine, other)
    shape = (2, 2, fields, levels, width)
    pair, rim_mine, rim_other, token = rim_spectra(pair, shape, inverse, turn, place)
    main, token = main_part(token, state, base, total, away, inverse, *tables)
    rim_total, rim_away = lon_sum(rim_mine, rim_other, token)
    return final_part(main, pair, rest, rim_total, rim_away, inverse, *tables)


def solution(mesh):
    placed = (
        P(None, "lat", None, None, "lon"),
        P("lat", None, None, "lon"),
        P("lat", None, None, "lon"),
        P("lat"),
        P("lat", None),
        P(),
    )
    return jax.shard_map(
        shards,
        mesh=mesh,
        in_specs=placed,
        out_specs=P(None, "lat", None, None, "lon"),
        check_vma=False,
    )
```

```python
import functools
import math

import jax
import jax.numpy as jnp
import numpy as np
from jax import lax
from jax.experimental import pallas as pl
from jax.experimental.pallas import tpu as pltpu
from jax.sharding import PartitionSpec as P

NLON = 2880
KCUT = 256
LANES = 128
MIB = 1024 * 1024
BF16 = jnp.bfloat16
F32 = jnp.float32


def phases(columns):
    wavenumber = np.arange(KCUT, dtype=np.int64)
    return (columns[:, None] * wavenumber[None, :] % NLON).astype(np.float64) * (
        2.0 * math.pi / NLON
    )


def basis_tables(width):
    phase = phases(np.arange(width, dtype=np.int64))
    table = np.concatenate([np.cos(phase), np.sin(phase)], axis=1).astype(np.float32)
    high = table.astype(jnp.bfloat16)
    low = (table - high.astype(np.float32)).astype(jnp.bfloat16)
    forward = (jnp.asarray(high), jnp.asarray(low))
    inverse = (
        jnp.asarray(np.ascontiguousarray(high.T)),
        jnp.asarray(np.ascontiguousarray(low.T)),
    )
    return forward, inverse


def turn_table(lon, width):
    phase = phases(np.arange(lon, dtype=np.int64) * width)
    table = np.concatenate([np.cos(phase), np.sin(phase)], axis=1).astype(np.float32)
    return jnp.asarray(table[:, None, :])


def split_dot(rows, high, low, axis=0):
    rows_high = rows.astype(BF16)
    rows_low = (rows - rows_high.astype(F32)).astype(BF16)
    dot = functools.partial(
        lax.dot_general,
        dimension_numbers=(((1,), (axis,)), ((), ())),
        preferred_element_type=F32,
    )
    return dot(rows_high, high) + (dot(rows_low, high) + dot(rows_high, low))


def turned(spec, turn, sign):
    real, imag = spec[:, :KCUT], spec[:, KCUT:]
    cos, sin = turn[:, :KCUT], turn[:, KCUT:] * sign
    return jnp.concatenate([real * cos - imag * sin, imag * cos + real * sin], axis=1)


def row_weights(cut):
    column = lax.broadcasted_iota(jnp.int32, (1, 2 * KCUT), 1)
    wavenumber = jnp.where(column >= KCUT, column - KCUT, column)
    scale = jnp.where(wavenumber == 0, 1.0 / NLON, 2.0 / NLON).astype(F32)
    return jnp.where(wavenumber < cut, scale, 0.0)


def pick_slots(block_ref, cutoff_ref, rows):
    polar1 = cutoff_ref[block_ref[1] * rows] > 0
    polar2 = cutoff_ref[block_ref[2] * rows] > 0
    rest = jnp.where(polar2, jnp.where(polar1, 0, 1), 2)
    return jnp.where(rest == 0, 1, 0), jnp.where(rest == 2, 1, 2), rest


def mine_first(pair, core):
    a, b = pair
    return jnp.where(core == 0, a, b), jnp.where(core == 0, b, a)


def vmem(count):
    return [pl.BlockSpec(memory_space=pltpu.VMEM)] * count


def smem(count):
    return [pl.BlockSpec(memory_space=pltpu.SMEM)] * count


def edge_kernel(lane_last, head_ref, tail_ref, wind_ref, west_ref, east_ref):
    fields, slots, rows = head_ref.shape[:3]
    lane = lax.broadcasted_iota(jnp.int32, (8, LANES), 1)
    for s in range(slots):
        west = jnp.zeros((8, LANES), F32)
        east = jnp.zeros((8, LANES), F32)
        for r in range(rows):
            for f in range(fields):
                here = lane == f * rows + r
                west = jnp.where(here, tail_ref[f, s, r, :, lane_last : lane_last + 1], west)
                east = jnp.where(here, head_ref[f, s, r, :, 0:1], east)
            here = lane == fields * rows + r
            west = jnp.where(here, wind_ref[s, r, :, lane_last : lane_last + 1], west)
        west_ref[s] = west
        east_ref[s] = east


def edges(state, courant_x):
    fields, slots, rows, levels, width = state.shape
    last = (width - 1) // LANES
    out = jax.ShapeDtypeStruct((slots, levels, LANES), F32)
    return pl.pallas_call(
        functools.partial(edge_kernel, (width - 1) % LANES),
        grid=(1,),
        in_specs=[
            pl.BlockSpec((fields, slots, rows, levels, LANES), lambda i: (0, 0, 0, 0, 0)),
            pl.BlockSpec((fields, slots, rows, levels, LANES), lambda i: (0, 0, 0, 0, last)),
            pl.BlockSpec((slots, rows, levels, LANES), lambda i: (0, 0, 0, last)),
        ],
        out_specs=[pl.BlockSpec((slots, levels, LANES), lambda i: (0, 0, 0))] * 2,
        out_shape=[out, out],
        cost_estimate=pl.CostEstimate(flops=10**5, bytes_accessed=1200000, transcendentals=0),
        name="edges",
    )(state, state, courant_x)


PIECE = 192
BACK = 176
TAIL = 80
SPARE = LANES - TAIL


def tile_of(slab, t, width):
    part = slab[:, t * LANES : min((t + 1) * LANES, width)]
    if part.shape[1] < LANES:
        part = jnp.concatenate([part, jnp.zeros((8, LANES - part.shape[1]), F32)], axis=1)
    return part


def pack_kernel(width, first_ref, last_ref, wind_ref, block_ref, out_ref):
    fields, slots = first_ref.shape[:2]
    tiles = -(-width // LANES)

    lane = lax.broadcasted_iota(jnp.int32, (8, LANES), 1)

    def put(row, tile):
        out_ref[pl.ds(row, 8, stride=PIECE), :] = tile

    tails = []
    for j in range(slots):
        half = wind_ref[j, 0] * 0.5
        north = [last_ref[f, j, 0] * half for f in range(fields)]
        south = [first_ref[f, j, 0] for f in range(fields)]
        for t in range(tiles - 1):
            put(55 * j + 25 + t, tile_of(half, t, width))
            for f in range(fields):
                put(55 * j + t * fields + f, tile_of(north[f], t, width))
                put(55 * j + 30 + t * fields + f, tile_of(south[f], t, width))
        tails.append([tile_of(slab, tiles - 1, width) for slab in (*north, half, *south)])
    for u, (a, b, c) in enumerate(zip(*tails)):
        put(165 + u, jnp.where(lane < TAIL, a, pltpu.roll(c, TAIL, 1)))
        put(176 + u, jnp.where(lane < TAIL, b, pltpu.roll(c, LANES - 2 * SPARE, 1)))
    table = jnp.zeros((8, LANES), jnp.int32)
    for j in range(slots):
        table = jnp.where(lane == j, block_ref[j], table)
    for row in range(187, PIECE):
        put(row, table.astype(F32))


def pack(state, courant_y, block):
    fields, slots, rows, levels, width = state.shape
    return pl.pallas_call(
        functools.partial(pack_kernel, width),
        grid=(1,),
        in_specs=[
            pl.BlockSpec((fields, slots, 1, levels, width), lambda i: (0, 0, 0, 0, 0)),
            pl.BlockSpec((fields, slots, 1, levels, width), lambda i: (0, 0, rows - 1, 0, 0)),
            pl.BlockSpec((slots, 1, levels, width), lambda i: (0, rows - 1, 0, 0)),
            pl.BlockSpec(memory_space=pltpu.SMEM),
        ],
        out_specs=pl.BlockSpec((levels * PIECE, LANES), lambda i: (0, 0)),
        out_shape=jax.ShapeDtypeStruct((levels * PIECE, LANES), F32),
        cost_estimate=pl.CostEstimate(flops=10**5, bytes_accessed=1700000, transcendentals=0),
        name="pack",
    )(state, state, courant_y, block)


def face_kernel(
    got_ref,
    cutoff_ref,
    later_in_ref,
    out_ref,
    later_ref,
    face_ref,
    south_ref,
    half_ref,
    whole_ref,
    table_ref,
    slot_ref,
    sem,
):
    del later_in_ref, later_ref
    parts = got_ref.shape[0]
    slots = face_ref.shape[0] // parts
    count = parts * slots
    whole_ref[...] = got_ref[:, 184:192, :].astype(jnp.int32)
    copy = pltpu.make_async_copy(whole_ref, table_ref, sem)
    copy.start()
    lane = lax.broadcasted_iota(jnp.int32, (8, LANES), 1)
    wide = lax.broadcasted_iota(jnp.int32, (16, LANES), 1)
    tails = []
    for s in range(count):
        src, j = divmod(s, slots)
        if j < 2:
            tail = got_ref[src, 165 + 11 * j : 176 + 11 * j, :]
        else:
            one = pltpu.roll(got_ref[src, 165:181, :], SPARE, 1)
            two = pltpu.roll(got_ref[src, 176:192, :], 2 * SPARE, 1)
            tail = jnp.where(wide < SPARE, one, two)[:11]
        south_ref[s, :25] = got_ref[src, 55 * j + 30 : 55 * j + 55, :]
        south_ref[s, 25:30] = tail[6:]
        face_ref[s, :25] = got_ref[src, 55 * j : 55 * j + 25, :]
        face_ref[s, 25:30] = tail[:5]
        half_ref[s, :5] = got_ref[src, 55 * j + 25 : 55 * j + 30, :]
        half_ref[s, 5:6] = tail[5:6]
    copy.wait()
    blocks = [table_ref[s // slots, 3, s % slots] for s in range(count)]
    slot_ref[0] = -1
    slot_ref[count + 1] = -1
    for s in range(count):
        slot_ref[blocks[s] + 1] = s
    for s in range(count):
        south = slot_ref[blocks[s] + 2]
        half = jnp.concatenate(
            [jnp.broadcast_to(half_ref[s, t : t + 1], (5, LANES)) for t in range(6)], axis=0
        )
        face = face_ref[s, :30] + half * south_ref[jnp.maximum(south, 0), :30]
        face_ref[s, :30] = jnp.where(south >= 0, face, 0.0)
    for d in range(parts):
        first, second, rest = pick_slots(blocks[slots * d : slots * d + slots], cutoff_ref, 8)
        tails = []
        for i, slot in enumerate((first, second, rest)):
            block = jnp.where(
                slot == 0,
                blocks[slots * d],
                jnp.where(slot == 1, blocks[slots * d + 1], blocks[slots * d + 2]),
            )
            north = slot_ref[block]
            for q, face, there in (
                (2 * i, jnp.maximum(north, 0), north >= 0),
                (2 * i + 1, slots * d + slot, None),
            ):
                rows, tail = face_ref[face, :25], face_ref[face, 24:32]
                if there is not None:
                    rows, tail = jnp.where(there, rows, 0.0), jnp.where(there, tail, 0.0)
                out_ref[d, 25 * q : 25 * q + 25] = rows
                tails.append(tail)
        for q in range(4):
            rest_tail = pltpu.roll(tails[4 + q % 2], TAIL if q < 2 else LANES - 2 * SPARE, 1)
            tail = jnp.where(lane < TAIL, tails[q], rest_tail)
            out_ref[d, 150 + 5 * q : 155 + 5 * q] = tail[1:6]
        out_ref[d, 170:BACK] = jnp.zeros((BACK - 170, LANES), F32)


def faces_of_pieces(got, slots, cutoff, later):
    parts = got.shape[0]
    return pl.pallas_call(
        face_kernel,
        in_specs=vmem(1) + smem(1) + [pl.BlockSpec(memory_space=pl.ANY)],
        out_specs=vmem(1) + [pl.BlockSpec(memory_space=pl.ANY)],
        out_shape=[
            jax.ShapeDtypeStruct((parts, BACK, LANES), F32),
            jax.ShapeDtypeStruct(later.shape, F32),
        ],
        input_output_aliases={2: 1},
        scratch_shapes=[
            pltpu.VMEM((parts * slots, 32, LANES), F32),
            pltpu.VMEM((parts * slots, 32, LANES), F32),
            pltpu.VMEM((parts * slots, 8, LANES), F32),
            pltpu.VMEM((parts, 8, LANES), jnp.int32),
            pltpu.SMEM((parts, 8, LANES), jnp.int32),
            pltpu.SMEM((parts * slots + 2,), jnp.int32),
            pltpu.SemaphoreType.DMA(()),
        ],
        compiler_params=pltpu.CompilerParams(vmem_limit_bytes=16 * MIB),
        cost_estimate=pl.CostEstimate(flops=10**5, bytes_accessed=1600000, transcendentals=0),
        name="faces",
    )(got, cutoff, later)


def to_pieces(units, parts):
    count, levels, width = units.shape
    groups = math.gcd(parts, levels)
    chunks = parts // groups
    span = -(-width // chunks)
    units = jnp.pad(units, ((0, 0), (0, 0), (0, span * chunks - width)))
    units = units.reshape(count, groups, levels // groups, chunks, span)
    return units.transpose(1, 3, 0, 2, 4).reshape(parts, count, levels // groups * span)


def from_pieces(pieces, levels, width):
    parts, count, _ = pieces.shape
    groups = math.gcd(parts, levels)
    chunks = parts // groups
    span = -(-width // chunks)
    pieces = pieces.reshape(groups, chunks, count, levels // groups, span)
    return pieces.transpose(2, 0, 3, 1, 4).reshape(count, levels, chunks * span)[:, :, :width]


def exchange_faces(state, courant_y, face_source):
    fields, slots, rows, levels, width = state.shape
    lat = lax.axis_size("lat")
    count = 2 * fields + 1
    first = state[:, :, 0].transpose(1, 0, 2, 3)
    last = state[:, :, rows - 1].transpose(1, 0, 2, 3)
    half = courant_y[:, rows - 1][:, None] * 0.5
    units = jnp.concatenate([first, last * half, half], axis=1)
    sent = to_pieces(units.reshape(slots * count, levels, width), lat)
    span = sent.shape[2]
    table = jnp.pad(
        face_source.astype(F32).reshape(1, slots * 2), ((0, 0), (0, span - slots * 2))
    )
    sent = jnp.concatenate([sent, jnp.broadcast_to(table[None], (lat, 1, span))], axis=1)
    got = lax.all_to_all(sent, "lat", 0, 0, tiled=True)
    indices = got[:, slots * count, : slots * 2].reshape(lat * slots, 2).astype(jnp.int32)
    data = got[:, : slots * count].reshape(lat * slots, count, span)
    north, south = indices[:, 0], indices[:, 1]
    face = data[:, fields : 2 * fields] + data[:, 2 * fields :] * data[
        jnp.maximum(south, 0), :fields
    ]
    face = jnp.where((south >= 0)[:, None, None], face, 0.0)
    face_north = jnp.where((north >= 0)[:, None, None], face[jnp.maximum(north, 0)], 0.0)
    back = jnp.concatenate([face_north, face], axis=1).reshape(lat, slots * 2 * fields, span)
    back = lax.all_to_all(back, "lat", 0, 0, tiled=True)
    return from_pieces(back, levels, width).reshape(slots, 2, fields, levels, width)


def tendency_kernel(
    state_ref,
    cx_ref,
    cy_ref,
    west_ref,
    east_ref,
    high_ref,
    low_ref,
    turn_ref,
    place_ref,
    block_ref,
    cutoff_ref,
    out_ref,
    mine_ref,
    other_ref,
    tend_ref,
    base_ref,
    sem,
):
    fields, slots, rows, levels, width = state_ref.shape

    def streamed(s):
        return pltpu.make_async_copy(base_ref.at[:, s], out_ref.at[:, s], sem.at[s])


    tiles = -(-width // LANES)
    lane = lax.broadcasted_iota(jnp.int32, (levels, LANES), 1)
    head, tail, last = lane == 0, lane == LANES - 1, lane == (width - 1) % LANES

    def load(ref, *index):
        out = []
        for t in range(tiles):
            part = ref[index + (slice(None), slice(t * LANES, min((t + 1) * LANES, width)))]
            if part.shape[1] < LANES:
                pad = jnp.zeros((levels, LANES - part.shape[1]), F32)
                part = jnp.concatenate([part, pad], axis=1)
            out.append(part)
        return out

    def one_slot(s, carry):
        west, east = west_ref[s], east_ref[s]
        for f in range(fields):
            above = None
            now = load(state_ref, f, s, 0)
            for r in range(rows):
                column = f * rows + r
                left = [pltpu.roll(x, LANES - 1, 1) for x in now]
                left = [
                    jnp.where(tail, left[t + 1], left[t])
                    if t + 1 < tiles
                    else jnp.where(last, east[:, column : column + 1], left[t])
                    for t in range(tiles)
                ]
                half = [x * 0.5 for x in load(cx_ref, s, r)]
                flux = [h * (x + y) for h, x, y in zip(half, now, left)]
                wind = west[:, fields * rows + r : fields * rows + r + 1] * 0.5
                first = wind * (west[:, column : column + 1] + now[0])
                right = [pltpu.roll(x, 1, 1) for x in flux]
                right = [jnp.where(head, y, x) for x, y in zip(right, [first] + right[:-1])]
                change = [x - y for x, y in zip(right, flux)]
                if above is not None:
                    change = [x + y for x, y in zip(change, above)]
                if r + 1 < rows:
                    later = load(state_ref, f, s, r + 1)
                    half = load(cy_ref, s, r)
                    above = [h * 0.5 * (x + y) for h, x, y in zip(half, now, later)]
                    change = [x - y for x, y in zip(change, above)]
                for t in range(tiles):
                    stop = min((t + 1) * LANES, width)
                    base = now[t] + change[t]
                    tend_ref[f, s, r, :, t * LANES : stop] = change[t][:, : stop - t * LANES]
                    base_ref[f, s, r, :, t * LANES : stop] = base[:, : stop - t * LANES]
                now = later
        streamed(s).start()
        return carry

    lax.fori_loop(0, slots, one_slot, 0)
    turn = turn_ref[place_ref[0]]
    first, second, _ = pick_slots(block_ref, cutoff_ref, rows)
    mine, other = mine_first((first, second), place_ref[1])
    for slot, spec_ref in ((other, other_ref), (mine, mine_ref)):
        spec = split_dot(
            tend_ref[:, slot].reshape(fields * rows * levels, width), high_ref[...], low_ref[...]
        )
        spec_ref[...] = turned(spec, turn, 1.0)
    for s in range(slots):
        streamed(s).wait()


def local_tendency(state, courant_x, courant_y, west, east, forward, turn, place, block, cutoff):
    fields, slots, rows, levels, width = state.shape
    count = fields * rows * levels
    spec = jax.ShapeDtypeStruct((count, 2 * KCUT), F32)
    return pl.pallas_call(
        tendency_kernel,
        in_specs=vmem(8) + smem(3),
        out_specs=[pl.BlockSpec(memory_space=pl.ANY)] + vmem(2),
        out_shape=[jax.ShapeDtypeStruct(state.shape, F32), spec, spec],
        scratch_shapes=[
            pltpu.VMEM(state.shape, F32),
            pltpu.VMEM(state.shape, F32),
            pltpu.SemaphoreType.DMA((slots,)),
        ],
        compiler_params=pltpu.CompilerParams(vmem_limit_bytes=60 * MIB),
        cost_estimate=pl.CostEstimate(
            flops=6 * count * 2 * KCUT * width * 2, bytes_accessed=9 * 10**6, transcendentals=0
        ),
        name="tendency",
    )(state, courant_x, courant_y, west, east, *forward, turn, place, block, cutoff)


def chosen_slot(i, place_ref, block_ref, cutoff_ref, rows):
    first, second, _ = pick_slots(block_ref, cutoff_ref, rows)
    return jnp.where(i == place_ref[1], first, second)


def main_kernel(
    place_ref,
    block_ref,
    cutoff_ref,
    state_ref,
    base_ref,
    mine_ref,
    away_ref,
    high_ref,
    low_ref,
    turn_ref,
    after_ref,
    out_ref,
    token_ref,
):
    fields, _, rows, levels, width = state_ref.shape
    del after_ref
    token_ref[...] = jnp.zeros_like(token_ref)
    i = pl.program_id(0)
    turn = turn_ref[place_ref[0]]
    slot = chosen_slot(i, place_ref, block_ref, cutoff_ref, rows)
    spec = turned(jnp.where(i == 0, mine_ref[...], away_ref[...]), turn, -1.0)
    spec = spec.reshape(fields, rows, levels, 2 * KCUT)
    cuts = [cutoff_ref[block_ref[slot] * rows + r] for r in range(rows)]
    spec = jnp.concatenate(
        [spec[:, r : r + 1] * row_weights(cuts[r]) for r in range(rows)], axis=1
    )
    smooth = split_dot(
        spec.reshape(fields * rows * levels, 2 * KCUT), high_ref[...], low_ref[...]
    ).reshape(fields, rows, levels, width)
    for r in range(rows):
        out_ref[:, 0, r] = jnp.where(
            cuts[r] > 0, state_ref[:, 0, r] + smooth[:, r], base_ref[:, 0, r]
        )


def main_part(after, state, base, mine, away, inverse, turn, place, block, cutoff):
    fields, slots, rows, levels, width = state.shape
    slot_block = pl.BlockSpec(
        (fields, 1, rows, levels, width),
        lambda i, *scalars: (0, chosen_slot(i, *scalars, rows), 0, 0, 0),
    )
    return pl.pallas_call(
        main_kernel,
        grid_spec=pltpu.PrefetchScalarGridSpec(
            num_scalar_prefetch=3,
            grid=(2,),
            in_specs=[slot_block, slot_block] + vmem(6),
            out_specs=[slot_block, pl.BlockSpec((1, 2 * KCUT), lambda i, *scalars: (0, 0))],
        ),
        out_shape=[
            jax.ShapeDtypeStruct(state.shape, F32),
            jax.ShapeDtypeStruct((1, 2 * KCUT), F32),
        ],
        input_output_aliases={4: 0},
        compiler_params=pltpu.CompilerParams(vmem_limit_bytes=50 * MIB),
        cost_estimate=pl.CostEstimate(
            flops=12 * mine.shape[0] * 2 * KCUT * width,
            bytes_accessed=6 * 10**6,
            transcendentals=0,
        ),
        name="main",
    )(place, block, cutoff, state, base, mine, away, *inverse, turn, after)


def unpack(ref, full, tail, spare, put, fields, width):
    tiles = -(-width // LANES)
    lane = lax.broadcasted_iota(jnp.int32, (8, LANES), 1)

    def load(row):
        return ref[pl.ds(row, 8, stride=BACK), :]

    for f in range(fields):
        for t in range(tiles - 1):
            put(f, t * LANES, (t + 1) * LANES, load(full + t * fields + f))
        tile = load(tail + f)
        if spare is not None:
            other = pltpu.roll(load(spare + f), 2 * SPARE, 1)
            tile = jnp.where(lane < SPARE, pltpu.roll(tile, SPARE, 1), other)
        put(f, (tiles - 1) * LANES, width, tile[:, :TAIL])


def rim_kernel(
    packed,
    got_ref,
    high_ref,
    low_ref,
    turn_ref,
    place_ref,
    faces_ref,
    mine_ref,
    other_ref,
    token_ref,
):
    _, _, fields, levels, width = faces_ref.shape
    token_ref[...] = jnp.zeros_like(token_ref)
    if packed:
        for i in range(2):
            for side in range(2):

                def put(f, start, stop, tile, i=i, side=side):
                    faces_ref[i, side, f, :, start:stop] = tile

                q = 2 * i + side
                unpack(got_ref, 25 * q, 150 + 5 * q, None, put, fields, width)
    else:
        faces_ref[...] = got_ref[...]
    turn = turn_ref[place_ref[0]]
    core = place_ref[1]
    both = jnp.concatenate(
        [part for i in (core, 1 - core) for part in (faces_ref[i, 0], -faces_ref[i, 1])], axis=0
    ).reshape(4 * fields * levels, width)
    spec = turned(split_dot(both, high_ref[...], low_ref[...], axis=1), turn, 1.0)
    mine_ref[...] = spec[: 2 * fields * levels]
    other_ref[...] = spec[2 * fields * levels :]


def rim_spectra(got, shape, inverse, turn, place):
    _, _, fields, levels, width = shape
    spec = jax.ShapeDtypeStruct((2 * fields * levels, 2 * KCUT), F32)
    return pl.pallas_call(
        functools.partial(rim_kernel, got.ndim == 2),
        in_specs=vmem(4) + smem(1),
        out_specs=vmem(4),
        out_shape=[
            jax.ShapeDtypeStruct(shape, F32),
            spec,
            spec,
            jax.ShapeDtypeStruct((8, LANES), F32),
        ],
        compiler_params=pltpu.CompilerParams(vmem_limit_bytes=50 * MIB),
        cost_estimate=pl.CostEstimate(
            flops=24 * fields * levels * 2 * KCUT * width,
            bytes_accessed=3 * 10**6,
            transcendentals=0,
        ),
        name="rim_spectra",
    )(got, *inverse, turn, place)


def final_kernel(
    packed,
    main_ref,
    pair_ref,
    back_ref,
    mine_ref,
    away_ref,
    high_ref,
    low_ref,
    turn_ref,
    place_ref,
    block_ref,
    cutoff_ref,
    out_ref,
    smooth_ref,
):
    fields, slots, _, levels, width = main_ref.shape
    rows = 8
    side = pl.program_id(0)
    row = side * (rows - 1)
    turn = turn_ref[place_ref[0]]
    core = place_ref[1]
    first, second, rest = pick_slots(block_ref, cutoff_ref, rows)
    mine, other = mine_first((first, second), core)
    count = fields * levels

    @pl.when(side == 0)
    def _():
        spec = [
            turned(ref[j * count : (j + 1) * count], turn, -1.0)
            * row_weights(cutoff_ref[block_ref[slot] * rows + j * (rows - 1)])
            for slot, ref in ((mine, mine_ref), (other, away_ref))
            for j in range(2)
        ]
        smooth = split_dot(jnp.concatenate(spec, axis=0), high_ref[...], low_ref[...])
        smooth_ref[...] = smooth.reshape(2, 2, fields, levels, width)

    sign = jnp.where(side == 0, 1.0, -1.0).astype(F32)
    if packed:

        def put(f, start, stop, tile):
            old = main_ref[f, rest, 0, :, start:stop]
            out_ref[f, rest, 0, :, start:stop] = old + tile * sign

        unpack(
            back_ref, 100 + 25 * side, 150 + 5 * side, 160 + 5 * side, put, fields, width
        )
    else:
        out_ref[:, rest, 0] = main_ref[:, rest, 0] + back_ref[side] * sign
    cuts = [cutoff_ref[block_ref[slot] * rows + row] for slot in (mine, other)]
    for i, (slot, order) in enumerate(((mine, core), (other, 1 - core))):
        out_ref[:, slot, 0] = main_ref[:, slot, 0] + jnp.where(
            cuts[i] > 0, smooth_ref[i, side], pair_ref[order, side] * sign
        )


def final_part(main, pair, back, mine, away, inverse, turn, place, block, cutoff):
    fields, slots, rows, levels, width = main.shape
    block_spec = pl.BlockSpec(
        (fields, slots, 1, levels, width), lambda i: (0, 0, i * (rows - 1), 0, 0)
    )
    return pl.pallas_call(
        functools.partial(final_kernel, back.ndim == 2),
        grid=(2,),
        in_specs=[block_spec] + vmem(7) + smem(3),
        out_specs=block_spec,
        scratch_shapes=[pltpu.VMEM((2, 2, fields, levels, width), F32)],
        out_shape=jax.ShapeDtypeStruct(main.shape, F32),
        input_output_aliases={0: 0},
        compiler_params=pltpu.CompilerParams(vmem_limit_bytes=50 * MIB),
        cost_estimate=pl.CostEstimate(
            flops=12 * mine.shape[0] * 2 * KCUT * width,
            bytes_accessed=4 * 10**6,
            transcendentals=0,
        ),
        name="final",
    )(main, pair, back, mine, away, *inverse, turn, place, block, cutoff)


def swap(array, bit):
    size = lax.axis_size("lon")
    return lax.ppermute(array, "lon", [(i, i ^ bit) for i in range(size)])


def lon_sum(mine, other, last=None):
    total = mine + swap(other, 1)
    bit = 2
    while bit < lax.axis_size("lon"):
        total = total + swap(total, bit)
        bit *= 2
    if last is not None:
        total = total + last
    return total, swap(total, 1)


def shards(state, courant_x, courant_y, block_of_slot, face_source, cutoff):
    fields, slots, rows, levels, width = state.shape
    lat, lon = lax.axis_size("lat"), lax.axis_size("lon")
    lon_index = lax.axis_index("lon")
    place = jnp.stack([lon_index, lon_index % 2]).astype(jnp.int32)
    forward, inverse = basis_tables(width)
    turn = turn_table(lon, width)
    tables = (turn, place, block_of_slot, cutoff)

    packed = lat == levels == 8 and width == 5 * LANES + TAIL and fields == 5
    if packed:
        sent = pack(state, courant_y, block_of_slot).reshape(lat, PIECE, LANES)
        got = lax.all_to_all(sent, "lat", 0, 0, tiled=True)

    west, east = edges(state, courant_x)
    west = lax.ppermute(west, "lon", [(i, (i + 1) % lon) for i in range(lon)])
    east = lax.ppermute(east, "lon", [((i + 1) % lon, i) for i in range(lon)])
    base, mine, other = local_tendency(
        state, courant_x, courant_y, west, east, forward, *tables
    )
    if packed:
        back, mine = faces_of_pieces(got, slots, cutoff, mine)
        back = lax.all_to_all(back, "lat", 0, 0, tiled=True)
        pair = rest = back.reshape(lat * BACK, LANES)
    else:
        faces = exchange_faces(state, courant_y, face_source)
        picked = pick_slots(block_of_slot, cutoff, rows)
        pair, rest = faces[jnp.stack(picked[:2])], faces[picked[2]]
    total, away = lon_sum(mine, other)
    shape = (2, 2, fields, levels, width)
    pair, rim_mine, rim_other, token = rim_spectra(pair, shape, inverse, turn, place)
    main, token = main_part(token, state, base, total, away, inverse, *tables)
    rim_total, rim_away = lon_sum(rim_mine, rim_other, token)
    return final_part(main, pair, rest, rim_total, rim_away, inverse, *tables)


def solution(mesh):
    placed = (
        P(None, "lat", None, None, "lon"),
        P("lat", None, None, "lon"),
        P("lat", None, None, "lon"),
        P("lat"),
        P("lat", None),
        P(),
    )
    return jax.shard_map(
        shards,
        mesh=mesh,
        in_specs=placed,
        out_specs=P(None, "lat", None, None, "lon"),
        check_vma=False,
    )
```

```python
import functools
import math

import jax
import jax.numpy as jnp
import numpy as np
from jax import lax
from jax.experimental import pallas as pl
from jax.experimental.pallas import tpu as pltpu
from jax.sharding import PartitionSpec as P

NLON = 2880
KCUT = 256
LANES = 128
MIB = 1024 * 1024
BF16 = jnp.bfloat16
F32 = jnp.float32


def phases(columns):
    wavenumber = np.arange(KCUT, dtype=np.int64)
    return (columns[:, None] * wavenumber[None, :] % NLON).astype(np.float64) * (
        2.0 * math.pi / NLON
    )


def basis_tables(width):
    phase = phases(np.arange(width, dtype=np.int64))
    table = np.concatenate([np.cos(phase), np.sin(phase)], axis=1).astype(np.float32)
    high = table.astype(jnp.bfloat16)
    low = (table - high.astype(np.float32)).astype(jnp.bfloat16)
    forward = (jnp.asarray(high), jnp.asarray(low))
    inverse = (
        jnp.asarray(np.ascontiguousarray(high.T)),
        jnp.asarray(np.ascontiguousarray(low.T)),
    )
    return forward, inverse


def turn_table(lon, width):
    phase = phases(np.arange(lon, dtype=np.int64) * width)
    table = np.concatenate([np.cos(phase), np.sin(phase)], axis=1).astype(np.float32)
    return jnp.asarray(table[:, None, :])


def split_dot(rows, high, low, axis=0):
    rows_high = rows.astype(BF16)
    rows_low = (rows - rows_high.astype(F32)).astype(BF16)
    dot = functools.partial(
        lax.dot_general,
        dimension_numbers=(((1,), (axis,)), ((), ())),
        preferred_element_type=F32,
    )
    return dot(rows_high, high) + (dot(rows_low, high) + dot(rows_high, low))


def turned(spec, turn, sign):
    real, imag = spec[:, :KCUT], spec[:, KCUT:]
    cos, sin = turn[:, :KCUT], turn[:, KCUT:] * sign
    return jnp.concatenate([real * cos - imag * sin, imag * cos + real * sin], axis=1)


def row_weights(cut):
    column = lax.broadcasted_iota(jnp.int32, (1, 2 * KCUT), 1)
    wavenumber = jnp.where(column >= KCUT, column - KCUT, column)
    scale = jnp.where(wavenumber == 0, 1.0 / NLON, 2.0 / NLON).astype(F32)
    return jnp.where(wavenumber < cut, scale, 0.0)


def pick_slots(block_ref, cutoff_ref, rows):
    polar1 = cutoff_ref[block_ref[1] * rows] > 0
    polar2 = cutoff_ref[block_ref[2] * rows] > 0
    rest = jnp.where(polar2, jnp.where(polar1, 0, 1), 2)
    return jnp.where(rest == 0, 1, 0), jnp.where(rest == 2, 1, 2), rest


def mine_first(pair, core):
    a, b = pair
    return jnp.where(core == 0, a, b), jnp.where(core == 0, b, a)


def vmem(count):
    return [pl.BlockSpec(memory_space=pltpu.VMEM)] * count


def smem(count):
    return [pl.BlockSpec(memory_space=pltpu.SMEM)] * count


def edge_kernel(lane_last, head_ref, tail_ref, wind_ref, west_ref, east_ref):
    fields, slots, rows = head_ref.shape[:3]
    lane = lax.broadcasted_iota(jnp.int32, (8, LANES), 1)
    for s in range(slots):
        west = jnp.zeros((8, LANES), F32)
        east = jnp.zeros((8, LANES), F32)
        for r in range(rows):
            for f in range(fields):
                here = lane == f * rows + r
                west = jnp.where(here, tail_ref[f, s, r, :, lane_last : lane_last + 1], west)
                east = jnp.where(here, head_ref[f, s, r, :, 0:1], east)
            here = lane == fields * rows + r
            west = jnp.where(here, wind_ref[s, r, :, lane_last : lane_last + 1], west)
        west_ref[s] = west
        east_ref[s] = east


def edges(state, courant_x):
    fields, slots, rows, levels, width = state.shape
    last = (width - 1) // LANES
    out = jax.ShapeDtypeStruct((slots, levels, LANES), F32)
    return pl.pallas_call(
        functools.partial(edge_kernel, (width - 1) % LANES),
        grid=(1,),
        in_specs=[
            pl.BlockSpec((fields, slots, rows, levels, LANES), lambda i: (0, 0, 0, 0, 0)),
            pl.BlockSpec((fields, slots, rows, levels, LANES), lambda i: (0, 0, 0, 0, last)),
            pl.BlockSpec((slots, rows, levels, LANES), lambda i: (0, 0, 0, last)),
        ],
        out_specs=[pl.BlockSpec((slots, levels, LANES), lambda i: (0, 0, 0))] * 2,
        out_shape=[out, out],
        cost_estimate=pl.CostEstimate(flops=10**5, bytes_accessed=1200000, transcendentals=0),
        name="edges",
    )(state, state, courant_x)


PIECE = 200
BACK = 176
TAIL = 80
SPARE = LANES - TAIL


def tile_of(slab, t, width):
    part = slab[:, t * LANES : min((t + 1) * LANES, width)]
    if part.shape[1] < LANES:
        part = jnp.concatenate([part, jnp.zeros((8, LANES - part.shape[1]), F32)], axis=1)
    return part


def pack_kernel(width, first_ref, last_ref, wind_ref, block_ref, out_ref):
    fields, slots = first_ref.shape[:2]
    tiles = -(-width // LANES)

    lane = lax.broadcasted_iota(jnp.int32, (8, LANES), 1)

    def put(row, tile):
        out_ref[pl.ds(row, 8, stride=PIECE), :] = tile

    for j in range(slots):
        half = wind_ref[j, 0] * 0.5
        for t in range(tiles):
            row = {0: 192 + 2 * j, 1: 193 + 2 * j, 2: 64 * j + 62, 3: 64 * j + 63}.get(
                t, 64 * j + 26 + t
            )
            put(row, tile_of(half, t, width))
        for f in range(fields):
            north = last_ref[f, j, 0] * half
            south = first_ref[f, j, 0]
            for t in range(tiles):
                put(64 * j + t * fields + f, tile_of(north, t, width))
                put(64 * j + 32 + t * fields + f, tile_of(south, t, width))
    table = jnp.zeros((8, LANES), jnp.int32)
    for j in range(slots):
        table = jnp.where(lane == j, block_ref[j], table)
    put(198, table.astype(F32))
    put(199, table.astype(F32))


def pack(state, courant_y, block):
    fields, slots, rows, levels, width = state.shape
    return pl.pallas_call(
        functools.partial(pack_kernel, width),
        grid=(1,),
        in_specs=[
            pl.BlockSpec((fields, slots, 1, levels, width), lambda i: (0, 0, 0, 0, 0)),
            pl.BlockSpec((fields, slots, 1, levels, width), lambda i: (0, 0, rows - 1, 0, 0)),
            pl.BlockSpec((slots, 1, levels, width), lambda i: (0, rows - 1, 0, 0)),
            pl.BlockSpec(memory_space=pltpu.SMEM),
        ],
        out_specs=pl.BlockSpec((levels * PIECE, LANES), lambda i: (0, 0)),
        out_shape=jax.ShapeDtypeStruct((levels * PIECE, LANES), F32),
        cost_estimate=pl.CostEstimate(flops=10**5, bytes_accessed=1700000, transcendentals=0),
        name="pack",
    )(state, state, courant_y, block)


def face_kernel(
    got_ref,
    cutoff_ref,
    later_in_ref,
    out_ref,
    later_ref,
    face_ref,
    whole_ref,
    table_ref,
    slot_ref,
    sem,
):
    del later_in_ref, later_ref
    parts = got_ref.shape[0]
    slots = face_ref.shape[0] // parts
    count = parts * slots
    whole_ref[...] = got_ref[:, 192:200, :].astype(jnp.int32)
    copy = pltpu.make_async_copy(whole_ref, table_ref, sem)
    copy.start()
    lane = lax.broadcasted_iota(jnp.int32, (8, LANES), 1)
    copy.wait()
    blocks = [table_ref[s // slots, 6, s % slots] for s in range(count)]
    slot_ref[0] = -1
    slot_ref[count + 1] = -1
    for s in range(count):
        slot_ref[blocks[s] + 1] = s
    for s in range(count):
        src, j = divmod(s, slots)
        south = slot_ref[blocks[s] + 2]
        safe = jnp.maximum(south, 0)
        from_src = lax.div(safe, slots)
        from_slot = safe - from_src * slots
        half = [
            jnp.broadcast_to(got_ref[src, row : row + 1, :], (5, LANES))
            for row in (
                192 + 2 * j,
                193 + 2 * j,
                64 * j + 62,
                64 * j + 63,
                64 * j + 30,
                64 * j + 31,
            )
        ]
        other = got_ref[from_src, pl.ds(pl.multiple_of(64 * from_slot + 32, 32), 32), :]
        face = got_ref[src, 64 * j : 64 * j + 30, :] + jnp.concatenate(half, axis=0) * other[:30]
        face_ref[s, :30] = jnp.where(south >= 0, face, 0.0)
    for d in range(parts):
        first, second, rest = pick_slots(blocks[slots * d : slots * d + slots], cutoff_ref, 8)
        tails = []
        for i, slot in enumerate((first, second, rest)):
            block = jnp.where(
                slot == 0,
                blocks[slots * d],
                jnp.where(slot == 1, blocks[slots * d + 1], blocks[slots * d + 2]),
            )
            north = slot_ref[block]
            for q, face, there in (
                (2 * i, jnp.maximum(north, 0), north >= 0),
                (2 * i + 1, slots * d + slot, None),
            ):
                rows, tail = face_ref[face, :25], face_ref[face, 24:32]
                if there is not None:
                    rows, tail = jnp.where(there, rows, 0.0), jnp.where(there, tail, 0.0)
                out_ref[d, 25 * q : 25 * q + 25] = rows
                tails.append(tail)
        for q in range(4):
            rest_tail = pltpu.roll(tails[4 + q % 2], TAIL if q < 2 else LANES - 2 * SPARE, 1)
            tail = jnp.where(lane < TAIL, tails[q], rest_tail)
            out_ref[d, 150 + 5 * q : 155 + 5 * q] = tail[1:6]
        out_ref[d, 170:BACK] = jnp.zeros((BACK - 170, LANES), F32)


def faces_of_pieces(got, slots, cutoff, later):
    parts = got.shape[0]
    return pl.pallas_call(
        face_kernel,
        in_specs=vmem(1) + smem(1) + [pl.BlockSpec(memory_space=pl.ANY)],
        out_specs=vmem(1) + [pl.BlockSpec(memory_space=pl.ANY)],
        out_shape=[
            jax.ShapeDtypeStruct((parts, BACK, LANES), F32),
            jax.ShapeDtypeStruct(later.shape, F32),
        ],
        input_output_aliases={2: 1},
        scratch_shapes=[
            pltpu.VMEM((parts * slots, 32, LANES), F32),
            pltpu.VMEM((parts, 8, LANES), jnp.int32),
            pltpu.SMEM((parts, 8, LANES), jnp.int32),
            pltpu.SMEM((parts * slots + 2,), jnp.int32),
            pltpu.SemaphoreType.DMA(()),
        ],
        cost_estimate=pl.CostEstimate(flops=10**5, bytes_accessed=1600000, transcendentals=0),
        name="faces",
    )(got, cutoff, later)


def to_pieces(units, parts):
    count, levels, width = units.shape
    groups = math.gcd(parts, levels)
    chunks = parts // groups
    span = -(-width // chunks)
    units = jnp.pad(units, ((0, 0), (0, 0), (0, span * chunks - width)))
    units = units.reshape(count, groups, levels // groups, chunks, span)
    return units.transpose(1, 3, 0, 2, 4).reshape(parts, count, levels // groups * span)


def from_pieces(pieces, levels, width):
    parts, count, _ = pieces.shape
    groups = math.gcd(parts, levels)
    chunks = parts // groups
    span = -(-width // chunks)
    pieces = pieces.reshape(groups, chunks, count, levels // groups, span)
    return pieces.transpose(2, 0, 3, 1, 4).reshape(count, levels, chunks * span)[:, :, :width]


def exchange_faces(state, courant_y, face_source):
    fields, slots, rows, levels, width = state.shape
    lat = lax.axis_size("lat")
    count = 2 * fields + 1
    first = state[:, :, 0].transpose(1, 0, 2, 3)
    last = state[:, :, rows - 1].transpose(1, 0, 2, 3)
    half = courant_y[:, rows - 1][:, None] * 0.5
    units = jnp.concatenate([first, last * half, half], axis=1)
    sent = to_pieces(units.reshape(slots * count, levels, width), lat)
    span = sent.shape[2]
    table = jnp.pad(
        face_source.astype(F32).reshape(1, slots * 2), ((0, 0), (0, span - slots * 2))
    )
    sent = jnp.concatenate([sent, jnp.broadcast_to(table[None], (lat, 1, span))], axis=1)
    got = lax.all_to_all(sent, "lat", 0, 0, tiled=True)
    indices = got[:, slots * count, : slots * 2].reshape(lat * slots, 2).astype(jnp.int32)
    data = got[:, : slots * count].reshape(lat * slots, count, span)
    north, south = indices[:, 0], indices[:, 1]
    face = data[:, fields : 2 * fields] + data[:, 2 * fields :] * data[
        jnp.maximum(south, 0), :fields
    ]
    face = jnp.where((south >= 0)[:, None, None], face, 0.0)
    face_north = jnp.where((north >= 0)[:, None, None], face[jnp.maximum(north, 0)], 0.0)
    back = jnp.concatenate([face_north, face], axis=1).reshape(lat, slots * 2 * fields, span)
    back = lax.all_to_all(back, "lat", 0, 0, tiled=True)
    return from_pieces(back, levels, width).reshape(slots, 2, fields, levels, width)


def tendency_kernel(
    state_ref,
    cx_ref,
    cy_ref,
    west_ref,
    east_ref,
    high_ref,
    low_ref,
    turn_ref,
    place_ref,
    block_ref,
    cutoff_ref,
    out_ref,
    mine_ref,
    other_ref,
    tend_ref,
    base_ref,
    sem,
):
    fields, slots, rows, levels, width = state_ref.shape

    def streamed(s):
        return pltpu.make_async_copy(base_ref.at[:, s], out_ref.at[:, s], sem.at[s])


    tiles = -(-width // LANES)
    lane = lax.broadcasted_iota(jnp.int32, (levels, LANES), 1)
    head, tail, last = lane == 0, lane == LANES - 1, lane == (width - 1) % LANES

    def load(ref, *index):
        out = []
        for t in range(tiles):
            part = ref[index + (slice(None), slice(t * LANES, min((t + 1) * LANES, width)))]
            if part.shape[1] < LANES:
                pad = jnp.zeros((levels, LANES - part.shape[1]), F32)
                part = jnp.concatenate([part, pad], axis=1)
            out.append(part)
        return out

    def one_slot(s, carry):
        west, east = west_ref[s], east_ref[s]
        for f in range(fields):
            above = None
            now = load(state_ref, f, s, 0)
            for r in range(rows):
                column = f * rows + r
                left = [pltpu.roll(x, LANES - 1, 1) for x in now]
                left = [
                    jnp.where(tail, left[t + 1], left[t])
                    if t + 1 < tiles
                    else jnp.where(last, east[:, column : column + 1], left[t])
                    for t in range(tiles)
                ]
                half = [x * 0.5 for x in load(cx_ref, s, r)]
                flux = [h * (x + y) for h, x, y in zip(half, now, left)]
                wind = west[:, fields * rows + r : fields * rows + r + 1] * 0.5
                first = wind * (west[:, column : column + 1] + now[0])
                right = [pltpu.roll(x, 1, 1) for x in flux]
                right = [jnp.where(head, y, x) for x, y in zip(right, [first] + right[:-1])]
                change = [x - y for x, y in zip(right, flux)]
                if above is not None:
                    change = [x + y for x, y in zip(change, above)]
                if r + 1 < rows:
                    later = load(state_ref, f, s, r + 1)
                    half = load(cy_ref, s, r)
                    above = [h * 0.5 * (x + y) for h, x, y in zip(half, now, later)]
                    change = [x - y for x, y in zip(change, above)]
                for t in range(tiles):
                    stop = min((t + 1) * LANES, width)
                    base = now[t] + change[t]
                    tend_ref[f, s, r, :, t * LANES : stop] = change[t][:, : stop - t * LANES]
                    base_ref[f, s, r, :, t * LANES : stop] = base[:, : stop - t * LANES]
                now = later
        streamed(s).start()
        return carry

    lax.fori_loop(0, slots, one_slot, 0)
    turn = turn_ref[place_ref[0]]
    first, second, _ = pick_slots(block_ref, cutoff_ref, rows)
    mine, other = mine_first((first, second), place_ref[1])
    for slot, spec_ref in ((other, other_ref), (mine, mine_ref)):
        spec = split_dot(
            tend_ref[:, slot].reshape(fields * rows * levels, width), high_ref[...], low_ref[...]
        )
        spec_ref[...] = turned(spec, turn, 1.0)
    for s in range(slots):
        streamed(s).wait()


def local_tendency(state, courant_x, courant_y, west, east, forward, turn, place, block, cutoff):
    fields, slots, rows, levels, width = state.shape
    count = fields * rows * levels
    spec = jax.ShapeDtypeStruct((count, 2 * KCUT), F32)
    return pl.pallas_call(
        tendency_kernel,
        in_specs=vmem(8) + smem(3),
        out_specs=[pl.BlockSpec(memory_space=pl.ANY)] + vmem(2),
        out_shape=[jax.ShapeDtypeStruct(state.shape, F32), spec, spec],
        scratch_shapes=[
            pltpu.VMEM(state.shape, F32),
            pltpu.VMEM(state.shape, F32),
            pltpu.SemaphoreType.DMA((slots,)),
        ],
        compiler_params=pltpu.CompilerParams(vmem_limit_bytes=50 * MIB),
        cost_estimate=pl.CostEstimate(
            flops=6 * count * 2 * KCUT * width * 2, bytes_accessed=9 * 10**6, transcendentals=0
        ),
        name="tendency",
    )(state, courant_x, courant_y, west, east, *forward, turn, place, block, cutoff)


def chosen_slot(i, place_ref, block_ref, cutoff_ref, rows):
    first, second, _ = pick_slots(block_ref, cutoff_ref, rows)
    return jnp.where(i == place_ref[1], first, second)


def main_kernel(
    place_ref,
    block_ref,
    cutoff_ref,
    state_ref,
    base_ref,
    mine_ref,
    away_ref,
    high_ref,
    low_ref,
    turn_ref,
    after_ref,
    out_ref,
    token_ref,
):
    fields, _, rows, levels, width = state_ref.shape
    del after_ref
    token_ref[...] = jnp.zeros_like(token_ref)
    i = pl.program_id(0)
    turn = turn_ref[place_ref[0]]
    slot = chosen_slot(i, place_ref, block_ref, cutoff_ref, rows)
    spec = turned(jnp.where(i == 0, mine_ref[...], away_ref[...]), turn, -1.0)
    spec = spec.reshape(fields, rows, levels, 2 * KCUT)
    cuts = [cutoff_ref[block_ref[slot] * rows + r] for r in range(rows)]
    spec = jnp.concatenate(
        [spec[:, r : r + 1] * row_weights(cuts[r]) for r in range(rows)], axis=1
    )
    smooth = split_dot(
        spec.reshape(fields * rows * levels, 2 * KCUT), high_ref[...], low_ref[...]
    ).reshape(fields, rows, levels, width)
    for r in range(rows):
        out_ref[:, 0, r] = jnp.where(
            cuts[r] > 0, state_ref[:, 0, r] + smooth[:, r], base_ref[:, 0, r]
        )


def main_part(after, state, base, mine, away, inverse, turn, place, block, cutoff):
    fields, slots, rows, levels, width = state.shape
    slot_block = pl.BlockSpec(
        (fields, 1, rows, levels, width),
        lambda i, *scalars: (0, chosen_slot(i, *scalars, rows), 0, 0, 0),
    )
    return pl.pallas_call(
        main_kernel,
        grid_spec=pltpu.PrefetchScalarGridSpec(
            num_scalar_prefetch=3,
            grid=(2,),
            in_specs=[slot_block, slot_block] + vmem(6),
            out_specs=[slot_block, pl.BlockSpec((1, 2 * KCUT), lambda i, *scalars: (0, 0))],
        ),
        out_shape=[
            jax.ShapeDtypeStruct(state.shape, F32),
            jax.ShapeDtypeStruct((1, 2 * KCUT), F32),
        ],
        input_output_aliases={4: 0},
        compiler_params=pltpu.CompilerParams(vmem_limit_bytes=50 * MIB),
        cost_estimate=pl.CostEstimate(
            flops=12 * mine.shape[0] * 2 * KCUT * width,
            bytes_accessed=6 * 10**6,
            transcendentals=0,
        ),
        name="main",
    )(place, block, cutoff, state, base, mine, away, *inverse, turn, after)


def unpack(ref, full, tail, spare, put, fields, width):
    tiles = -(-width // LANES)
    lane = lax.broadcasted_iota(jnp.int32, (8, LANES), 1)

    def load(row):
        return ref[pl.ds(row, 8, stride=BACK), :]

    for f in range(fields):
        for t in range(tiles - 1):
            put(f, t * LANES, (t + 1) * LANES, load(full + t * fields + f))
        tile = load(tail + f)
        if spare is not None:
            other = pltpu.roll(load(spare + f), 2 * SPARE, 1)
            tile = jnp.where(lane < SPARE, pltpu.roll(tile, SPARE, 1), other)
        put(f, (tiles - 1) * LANES, width, tile[:, :TAIL])


def rim_kernel(
    packed,
    got_ref,
    high_ref,
    low_ref,
    turn_ref,
    place_ref,
    faces_ref,
    mine_ref,
    other_ref,
    token_ref,
):
    _, _, fields, levels, width = faces_ref.shape
    token_ref[...] = jnp.zeros_like(token_ref)
    if packed:
        for i in range(2):
            for side in range(2):

                def put(f, start, stop, tile, i=i, side=side):
                    faces_ref[i, side, f, :, start:stop] = tile

                q = 2 * i + side
                unpack(got_ref, 25 * q, 150 + 5 * q, None, put, fields, width)
    else:
        faces_ref[...] = got_ref[...]
    turn = turn_ref[place_ref[0]]
    core = place_ref[1]
    both = jnp.concatenate(
        [part for i in (core, 1 - core) for part in (faces_ref[i, 0], -faces_ref[i, 1])], axis=0
    ).reshape(4 * fields * levels, width)
    spec = turned(split_dot(both, high_ref[...], low_ref[...], axis=1), turn, 1.0)
    mine_ref[...] = spec[: 2 * fields * levels]
    other_ref[...] = spec[2 * fields * levels :]


def rim_spectra(got, shape, inverse, turn, place):
    _, _, fields, levels, width = shape
    spec = jax.ShapeDtypeStruct((2 * fields * levels, 2 * KCUT), F32)
    return pl.pallas_call(
        functools.partial(rim_kernel, got.ndim == 2),
        in_specs=vmem(4) + smem(1),
        out_specs=vmem(4),
        out_shape=[
            jax.ShapeDtypeStruct(shape, F32),
            spec,
            spec,
            jax.ShapeDtypeStruct((8, LANES), F32),
        ],
        compiler_params=pltpu.CompilerParams(vmem_limit_bytes=50 * MIB),
        cost_estimate=pl.CostEstimate(
            flops=24 * fields * levels * 2 * KCUT * width,
            bytes_accessed=3 * 10**6,
            transcendentals=0,
        ),
        name="rim_spectra",
    )(got, *inverse, turn, place)


def final_kernel(
    packed,
    main_ref,
    pair_ref,
    back_ref,
    mine_ref,
    away_ref,
    high_ref,
    low_ref,
    turn_ref,
    place_ref,
    block_ref,
    cutoff_ref,
    out_ref,
    smooth_ref,
):
    fields, slots, _, levels, width = main_ref.shape
    rows = 8
    side = pl.program_id(0)
    row = side * (rows - 1)
    turn = turn_ref[place_ref[0]]
    core = place_ref[1]
    first, second, rest = pick_slots(block_ref, cutoff_ref, rows)
    mine, other = mine_first((first, second), core)
    count = fields * levels

    @pl.when(side == 0)
    def _():
        spec = [
            turned(ref[j * count : (j + 1) * count], turn, -1.0)
            * row_weights(cutoff_ref[block_ref[slot] * rows + j * (rows - 1)])
            for slot, ref in ((mine, mine_ref), (other, away_ref))
            for j in range(2)
        ]
        smooth = split_dot(jnp.concatenate(spec, axis=0), high_ref[...], low_ref[...])
        smooth_ref[...] = smooth.reshape(2, 2, fields, levels, width)

    sign = jnp.where(side == 0, 1.0, -1.0).astype(F32)
    if packed:

        def put(f, start, stop, tile):
            old = main_ref[f, rest, 0, :, start:stop]
            out_ref[f, rest, 0, :, start:stop] = old + tile * sign

        unpack(
            back_ref, 100 + 25 * side, 150 + 5 * side, 160 + 5 * side, put, fields, width
        )
    else:
        out_ref[:, rest, 0] = main_ref[:, rest, 0] + back_ref[side] * sign
    cuts = [cutoff_ref[block_ref[slot] * rows + row] for slot in (mine, other)]
    for i, (slot, order) in enumerate(((mine, core), (other, 1 - core))):
        out_ref[:, slot, 0] = main_ref[:, slot, 0] + jnp.where(
            cuts[i] > 0, smooth_ref[i, side], pair_ref[order, side] * sign
        )


def final_part(main, pair, back, mine, away, inverse, turn, place, block, cutoff):
    fields, slots, rows, levels, width = main.shape
    block_spec = pl.BlockSpec(
        (fields, slots, 1, levels, width), lambda i: (0, 0, i * (rows - 1), 0, 0)
    )
    return pl.pallas_call(
        functools.partial(final_kernel, back.ndim == 2),
        grid=(2,),
        in_specs=[block_spec] + vmem(7) + smem(3),
        out_specs=block_spec,
        scratch_shapes=[pltpu.VMEM((2, 2, fields, levels, width), F32)],
        out_shape=jax.ShapeDtypeStruct(main.shape, F32),
        input_output_aliases={0: 0},
        compiler_params=pltpu.CompilerParams(vmem_limit_bytes=50 * MIB),
        cost_estimate=pl.CostEstimate(
            flops=12 * mine.shape[0] * 2 * KCUT * width,
            bytes_accessed=4 * 10**6,
            transcendentals=0,
        ),
        name="final",
    )(main, pair, back, mine, away, *inverse, turn, place, block, cutoff)


def swap(array, bit):
    size = lax.axis_size("lon")
    return lax.ppermute(array, "lon", [(i, i ^ bit) for i in range(size)])


def lon_sum(mine, other, last=None):
    total = mine + swap(other, 1)
    bit = 2
    while bit < lax.axis_size("lon"):
        total = total + swap(total, bit)
        bit *= 2
    if last is not None:
        total = total + last
    return total, swap(total, 1)


def shards(state, courant_x, courant_y, block_of_slot, face_source, cutoff):
    fields, slots, rows, levels, width = state.shape
    lat, lon = lax.axis_size("lat"), lax.axis_size("lon")
    lon_index = lax.axis_index("lon")
    place = jnp.stack([lon_index, lon_index % 2]).astype(jnp.int32)
    forward, inverse = basis_tables(width)
    turn = turn_table(lon, width)
    tables = (turn, place, block_of_slot, cutoff)

    packed = lat == levels == 8 and width == 5 * LANES + TAIL and fields == 5
    if packed:
        sent = pack(state, courant_y, block_of_slot).reshape(lat, PIECE, LANES)
        got = lax.all_to_all(sent, "lat", 0, 0, tiled=True)

    west, east = edges(state, courant_x)
    west = lax.ppermute(west, "lon", [(i, (i + 1) % lon) for i in range(lon)])
    east = lax.ppermute(east, "lon", [((i + 1) % lon, i) for i in range(lon)])
    base, mine, other = local_tendency(
        state, courant_x, courant_y, west, east, forward, *tables
    )
    if packed:
        back, mine = faces_of_pieces(got, slots, cutoff, mine)
        back = lax.all_to_all(back, "lat", 0, 0, tiled=True)
        pair = rest = back.reshape(lat * BACK, LANES)
    else:
        faces = exchange_faces(state, courant_y, face_source)
        picked = pick_slots(block_of_slot, cutoff, rows)
        pair, rest = faces[jnp.stack(picked[:2])], faces[picked[2]]
    total, away = lon_sum(mine, other)
    shape = (2, 2, fields, levels, width)
    pair, rim_mine, rim_other, token = rim_spectra(pair, shape, inverse, turn, place)
    main, token = main_part(token, state, base, total, away, inverse, *tables)
    rim_total, rim_away = lon_sum(rim_mine, rim_other, token)
    return final_part(main, pair, rest, rim_total, rim_away, inverse, *tables)


def solution(mesh):
    placed = (
        P(None, "lat", None, None, "lon"),
        P("lat", None, None, "lon"),
        P("lat", None, None, "lon"),
        P("lat"),
        P("lat", None),
        P(),
    )
    return jax.shard_map(
        shards,
        mesh=mesh,
        in_specs=placed,
        out_specs=P(None, "lat", None, None, "lon"),
        check_vma=False,
    )
```

```python
import functools
import math

import jax
import jax.numpy as jnp
import numpy as np
from jax import lax
from jax.experimental import pallas as pl
from jax.experimental.pallas import tpu as pltpu
from jax.sharding import PartitionSpec as P

NLON = 2880
KCUT = 256
LANES = 128
MIB = 1024 * 1024
BF16 = jnp.bfloat16
F32 = jnp.float32


def phases(columns):
    wavenumber = np.arange(KCUT, dtype=np.int64)
    return (columns[:, None] * wavenumber[None, :] % NLON).astype(np.float64) * (
        2.0 * math.pi / NLON
    )


def basis_tables(width):
    phase = phases(np.arange(width, dtype=np.int64))
    table = np.concatenate([np.cos(phase), np.sin(phase)], axis=1).astype(np.float32)
    high = table.astype(jnp.bfloat16)
    low = (table - high.astype(np.float32)).astype(jnp.bfloat16)
    forward = (jnp.asarray(high), jnp.asarray(low))
    inverse = (
        jnp.asarray(np.ascontiguousarray(high.T)),
        jnp.asarray(np.ascontiguousarray(low.T)),
    )
    return forward, inverse


def turn_table(lon, width):
    phase = phases(np.arange(lon, dtype=np.int64) * width)
    table = np.concatenate([np.cos(phase), np.sin(phase)], axis=1).astype(np.float32)
    return jnp.asarray(table[:, None, :])


def split_dot(rows, high, low, axis=0):
    rows_high = rows.astype(BF16)
    rows_low = (rows - rows_high.astype(F32)).astype(BF16)
    dot = functools.partial(
        lax.dot_general,
        dimension_numbers=(((1,), (axis,)), ((), ())),
        preferred_element_type=F32,
    )
    return dot(rows_high, high) + (dot(rows_low, high) + dot(rows_high, low))


def turned(spec, turn, sign):
    real, imag = spec[:, :KCUT], spec[:, KCUT:]
    cos, sin = turn[:, :KCUT], turn[:, KCUT:] * sign
    return jnp.concatenate([real * cos - imag * sin, imag * cos + real * sin], axis=1)


def row_weights(cut):
    column = lax.broadcasted_iota(jnp.int32, (1, 2 * KCUT), 1)
    wavenumber = jnp.where(column >= KCUT, column - KCUT, column)
    scale = jnp.where(wavenumber == 0, 1.0 / NLON, 2.0 / NLON).astype(F32)
    return jnp.where(wavenumber < cut, scale, 0.0)


def pick_slots(block_ref, cutoff_ref, rows):
    polar1 = cutoff_ref[block_ref[1] * rows] > 0
    polar2 = cutoff_ref[block_ref[2] * rows] > 0
    rest = jnp.where(polar2, jnp.where(polar1, 0, 1), 2)
    return jnp.where(rest == 0, 1, 0), jnp.where(rest == 2, 1, 2), rest


def mine_first(pair, core):
    a, b = pair
    return jnp.where(core == 0, a, b), jnp.where(core == 0, b, a)


def vmem(count):
    return [pl.BlockSpec(memory_space=pltpu.VMEM)] * count


def smem(count):
    return [pl.BlockSpec(memory_space=pltpu.SMEM)] * count


def edge_kernel(lane_last, head_ref, tail_ref, wind_ref, west_ref, east_ref):
    fields, slots, rows = head_ref.shape[:3]
    lane = lax.broadcasted_iota(jnp.int32, (8, LANES), 1)
    for s in range(slots):
        west = jnp.zeros((8, LANES), F32)
        east = jnp.zeros((8, LANES), F32)
        for r in range(rows):
            for f in range(fields):
                here = lane == f * rows + r
                west = jnp.where(here, tail_ref[f, s, r, :, lane_last : lane_last + 1], west)
                east = jnp.where(here, head_ref[f, s, r, :, 0:1], east)
            here = lane == fields * rows + r
            west = jnp.where(here, wind_ref[s, r, :, lane_last : lane_last + 1], west)
        west_ref[s] = west
        east_ref[s] = east


def edges(state, courant_x):
    fields, slots, rows, levels, width = state.shape
    last = (width - 1) // LANES
    out = jax.ShapeDtypeStruct((slots, levels, LANES), F32)
    return pl.pallas_call(
        functools.partial(edge_kernel, (width - 1) % LANES),
        grid=(1,),
        in_specs=[
            pl.BlockSpec((fields, slots, rows, levels, LANES), lambda i: (0, 0, 0, 0, 0)),
            pl.BlockSpec((fields, slots, rows, levels, LANES), lambda i: (0, 0, 0, 0, last)),
            pl.BlockSpec((slots, rows, levels, LANES), lambda i: (0, 0, 0, last)),
        ],
        out_specs=[pl.BlockSpec((slots, levels, LANES), lambda i: (0, 0, 0))] * 2,
        out_shape=[out, out],
        cost_estimate=pl.CostEstimate(flops=10**5, bytes_accessed=1200000, transcendentals=0),
        name="edges",
    )(state, state, courant_x)


PIECE = 200
BACK = 176
TAIL = 80
SPARE = LANES - TAIL


def tile_of(slab, t, width):
    part = slab[:, t * LANES : min((t + 1) * LANES, width)]
    if part.shape[1] < LANES:
        part = jnp.concatenate([part, jnp.zeros((8, LANES - part.shape[1]), F32)], axis=1)
    return part


def pack_kernel(width, first_ref, last_ref, wind_ref, block_ref, out_ref):
    fields, slots = first_ref.shape[:2]
    tiles = -(-width // LANES)

    lane = lax.broadcasted_iota(jnp.int32, (8, LANES), 1)

    def put(row, tile):
        out_ref[pl.ds(row, 8, stride=PIECE), :] = tile

    for j in range(slots):
        half = wind_ref[j, 0] * 0.5
        for t in range(tiles):
            row = {0: 192 + 2 * j, 1: 193 + 2 * j, 2: 64 * j + 62, 3: 64 * j + 63}.get(
                t, 64 * j + 26 + t
            )
            put(row, tile_of(half, t, width))
        for f in range(fields):
            north = last_ref[f, j, 0] * half
            south = first_ref[f, j, 0]
            for t in range(tiles):
                put(64 * j + t * fields + f, tile_of(north, t, width))
                put(64 * j + 32 + t * fields + f, tile_of(south, t, width))
    table = jnp.zeros((8, LANES), jnp.int32)
    for j in range(slots):
        table = jnp.where(lane == j, block_ref[j], table)
    put(198, table.astype(F32))
    put(199, table.astype(F32))


def pack(state, courant_y, block):
    fields, slots, rows, levels, width = state.shape
    return pl.pallas_call(
        functools.partial(pack_kernel, width),
        grid=(1,),
        in_specs=[
            pl.BlockSpec((fields, slots, 1, levels, width), lambda i: (0, 0, 0, 0, 0)),
            pl.BlockSpec((fields, slots, 1, levels, width), lambda i: (0, 0, rows - 1, 0, 0)),
            pl.BlockSpec((slots, 1, levels, width), lambda i: (0, rows - 1, 0, 0)),
            pl.BlockSpec(memory_space=pltpu.SMEM),
        ],
        out_specs=pl.BlockSpec((levels * PIECE, LANES), lambda i: (0, 0)),
        out_shape=jax.ShapeDtypeStruct((levels * PIECE, LANES), F32),
        cost_estimate=pl.CostEstimate(flops=10**5, bytes_accessed=1700000, transcendentals=0),
        name="pack",
    )(state, state, courant_y, block)


def face_kernel(
    got_ref,
    cutoff_ref,
    out_ref,
    token_ref,
    face_ref,
    whole_ref,
    table_ref,
    slot_ref,
    sem,
):
    token_ref[...] = jnp.zeros_like(token_ref)
    parts = got_ref.shape[0]
    slots = face_ref.shape[0] // parts
    count = parts * slots
    whole_ref[...] = got_ref[:, 192:200, :].astype(jnp.int32)
    copy = pltpu.make_async_copy(whole_ref, table_ref, sem)
    copy.start()
    lane = lax.broadcasted_iota(jnp.int32, (8, LANES), 1)
    copy.wait()
    blocks = [table_ref[s // slots, 6, s % slots] for s in range(count)]
    slot_ref[0] = -1
    slot_ref[count + 1] = -1
    for s in range(count):
        slot_ref[blocks[s] + 1] = s
    for s in range(count):
        src, j = divmod(s, slots)
        south = slot_ref[blocks[s] + 2]
        safe = jnp.maximum(south, 0)
        from_src = lax.div(safe, slots)
        from_slot = safe - from_src * slots
        half = [
            jnp.broadcast_to(got_ref[src, row : row + 1, :], (5, LANES))
            for row in (
                192 + 2 * j,
                193 + 2 * j,
                64 * j + 62,
                64 * j + 63,
                64 * j + 30,
                64 * j + 31,
            )
        ]
        other = got_ref[from_src, pl.ds(pl.multiple_of(64 * from_slot + 32, 32), 32), :]
        face = got_ref[src, 64 * j : 64 * j + 30, :] + jnp.concatenate(half, axis=0) * other[:30]
        face_ref[s, :30] = jnp.where(south >= 0, face, 0.0)
    for d in range(parts):
        first, second, rest = pick_slots(blocks[slots * d : slots * d + slots], cutoff_ref, 8)
        tails = []
        for i, slot in enumerate((first, second, rest)):
            block = jnp.where(
                slot == 0,
                blocks[slots * d],
                jnp.where(slot == 1, blocks[slots * d + 1], blocks[slots * d + 2]),
            )
            north = slot_ref[block]
            for q, face, there in (
                (2 * i, jnp.maximum(north, 0), north >= 0),
                (2 * i + 1, slots * d + slot, None),
            ):
                rows, tail = face_ref[face, :25], face_ref[face, 24:32]
                if there is not None:
                    rows, tail = jnp.where(there, rows, 0.0), jnp.where(there, tail, 0.0)
                out_ref[d, 25 * q : 25 * q + 25] = rows
                tails.append(tail)
        for q in range(4):
            rest_tail = pltpu.roll(tails[4 + q % 2], TAIL if q < 2 else LANES - 2 * SPARE, 1)
            tail = jnp.where(lane < TAIL, tails[q], rest_tail)
            out_ref[d, 150 + 5 * q : 155 + 5 * q] = tail[1:6]
        out_ref[d, 170:BACK] = jnp.zeros((BACK - 170, LANES), F32)


def faces_of_pieces(got, slots, cutoff):
    parts = got.shape[0]
    return pl.pallas_call(
        face_kernel,
        in_specs=vmem(1) + smem(1),
        out_specs=vmem(2),
        out_shape=[
            jax.ShapeDtypeStruct((parts, BACK, LANES), F32),
            jax.ShapeDtypeStruct((1, 2 * KCUT), F32),
        ],
        scratch_shapes=[
            pltpu.VMEM((parts * slots, 32, LANES), F32),
            pltpu.VMEM((parts, 8, LANES), jnp.int32),
            pltpu.SMEM((parts, 8, LANES), jnp.int32),
            pltpu.SMEM((parts * slots + 2,), jnp.int32),
            pltpu.SemaphoreType.DMA(()),
        ],
        cost_estimate=pl.CostEstimate(flops=10**5, bytes_accessed=1600000, transcendentals=0),
        name="faces",
    )(got, cutoff)


def to_pieces(units, parts):
    count, levels, width = units.shape
    groups = math.gcd(parts, levels)
    chunks = parts // groups
    span = -(-width // chunks)
    units = jnp.pad(units, ((0, 0), (0, 0), (0, span * chunks - width)))
    units = units.reshape(count, groups, levels // groups, chunks, span)
    return units.transpose(1, 3, 0, 2, 4).reshape(parts, count, levels // groups * span)


def from_pieces(pieces, levels, width):
    parts, count, _ = pieces.shape
    groups = math.gcd(parts, levels)
    chunks = parts // groups
    span = -(-width // chunks)
    pieces = pieces.reshape(groups, chunks, count, levels // groups, span)
    return pieces.transpose(2, 0, 3, 1, 4).reshape(count, levels, chunks * span)[:, :, :width]


def exchange_faces(state, courant_y, face_source):
    fields, slots, rows, levels, width = state.shape
    lat = lax.axis_size("lat")
    count = 2 * fields + 1
    first = state[:, :, 0].transpose(1, 0, 2, 3)
    last = state[:, :, rows - 1].transpose(1, 0, 2, 3)
    half = courant_y[:, rows - 1][:, None] * 0.5
    units = jnp.concatenate([first, last * half, half], axis=1)
    sent = to_pieces(units.reshape(slots * count, levels, width), lat)
    span = sent.shape[2]
    table = jnp.pad(
        face_source.astype(F32).reshape(1, slots * 2), ((0, 0), (0, span - slots * 2))
    )
    sent = jnp.concatenate([sent, jnp.broadcast_to(table[None], (lat, 1, span))], axis=1)
    got = lax.all_to_all(sent, "lat", 0, 0, tiled=True)
    indices = got[:, slots * count, : slots * 2].reshape(lat * slots, 2).astype(jnp.int32)
    data = got[:, : slots * count].reshape(lat * slots, count, span)
    north, south = indices[:, 0], indices[:, 1]
    face = data[:, fields : 2 * fields] + data[:, 2 * fields :] * data[
        jnp.maximum(south, 0), :fields
    ]
    face = jnp.where((south >= 0)[:, None, None], face, 0.0)
    face_north = jnp.where((north >= 0)[:, None, None], face[jnp.maximum(north, 0)], 0.0)
    back = jnp.concatenate([face_north, face], axis=1).reshape(lat, slots * 2 * fields, span)
    back = lax.all_to_all(back, "lat", 0, 0, tiled=True)
    return from_pieces(back, levels, width).reshape(slots, 2, fields, levels, width)


def tendency_kernel(
    state_ref,
    cx_ref,
    cy_ref,
    west_ref,
    east_ref,
    high_ref,
    low_ref,
    turn_ref,
    place_ref,
    block_ref,
    cutoff_ref,
    out_ref,
    mine_ref,
    other_ref,
    tend_ref,
    base_ref,
    sem,
):
    fields, slots, rows, levels, width = state_ref.shape

    def streamed(s):
        return pltpu.make_async_copy(base_ref.at[:, s], out_ref.at[:, s], sem.at[s])


    tiles = -(-width // LANES)
    lane = lax.broadcasted_iota(jnp.int32, (levels, LANES), 1)
    head, tail, last = lane == 0, lane == LANES - 1, lane == (width - 1) % LANES

    def load(ref, *index):
        out = []
        for t in range(tiles):
            part = ref[index + (slice(None), slice(t * LANES, min((t + 1) * LANES, width)))]
            if part.shape[1] < LANES:
                pad = jnp.zeros((levels, LANES - part.shape[1]), F32)
                part = jnp.concatenate([part, pad], axis=1)
            out.append(part)
        return out

    def one_slot(s, carry):
        west, east = west_ref[s], east_ref[s]
        for f in range(fields):
            above = None
            now = load(state_ref, f, s, 0)
            for r in range(rows):
                column = f * rows + r
                left = [pltpu.roll(x, LANES - 1, 1) for x in now]
                left = [
                    jnp.where(tail, left[t + 1], left[t])
                    if t + 1 < tiles
                    else jnp.where(last, east[:, column : column + 1], left[t])
                    for t in range(tiles)
                ]
                half = [x * 0.5 for x in load(cx_ref, s, r)]
                flux = [h * (x + y) for h, x, y in zip(half, now, left)]
                wind = west[:, fields * rows + r : fields * rows + r + 1] * 0.5
                first = wind * (west[:, column : column + 1] + now[0])
                right = [pltpu.roll(x, 1, 1) for x in flux]
                right = [jnp.where(head, y, x) for x, y in zip(right, [first] + right[:-1])]
                change = [x - y for x, y in zip(right, flux)]
                if above is not None:
                    change = [x + y for x, y in zip(change, above)]
                if r + 1 < rows:
                    later = load(state_ref, f, s, r + 1)
                    half = load(cy_ref, s, r)
                    above = [h * 0.5 * (x + y) for h, x, y in zip(half, now, later)]
                    change = [x - y for x, y in zip(change, above)]
                for t in range(tiles):
                    stop = min((t + 1) * LANES, width)
                    base = now[t] + change[t]
                    tend_ref[f, s, r, :, t * LANES : stop] = change[t][:, : stop - t * LANES]
                    base_ref[f, s, r, :, t * LANES : stop] = base[:, : stop - t * LANES]
                now = later
        streamed(s).start()
        return carry

    lax.fori_loop(0, slots, one_slot, 0)
    turn = turn_ref[place_ref[0]]
    first, second, _ = pick_slots(block_ref, cutoff_ref, rows)
    mine, other = mine_first((first, second), place_ref[1])
    for slot, spec_ref in ((other, other_ref), (mine, mine_ref)):
        spec = split_dot(
            tend_ref[:, slot].reshape(fields * rows * levels, width), high_ref[...], low_ref[...]
        )
        spec_ref[...] = turned(spec, turn, 1.0)
    for s in range(slots):
        streamed(s).wait()


def local_tendency(state, courant_x, courant_y, west, east, forward, turn, place, block, cutoff):
    fields, slots, rows, levels, width = state.shape
    count = fields * rows * levels
    spec = jax.ShapeDtypeStruct((count, 2 * KCUT), F32)
    return pl.pallas_call(
        tendency_kernel,
        in_specs=vmem(8) + smem(3),
        out_specs=[pl.BlockSpec(memory_space=pl.ANY)] + vmem(2),
        out_shape=[jax.ShapeDtypeStruct(state.shape, F32), spec, spec],
        scratch_shapes=[
            pltpu.VMEM(state.shape, F32),
            pltpu.VMEM(state.shape, F32),
            pltpu.SemaphoreType.DMA((slots,)),
        ],
        compiler_params=pltpu.CompilerParams(vmem_limit_bytes=50 * MIB),
        cost_estimate=pl.CostEstimate(
            flops=6 * count * 2 * KCUT * width * 2, bytes_accessed=9 * 10**6, transcendentals=0
        ),
        name="tendency",
    )(state, courant_x, courant_y, west, east, *forward, turn, place, block, cutoff)


def chosen_slot(i, place_ref, block_ref, cutoff_ref, rows):
    first, second, _ = pick_slots(block_ref, cutoff_ref, rows)
    return jnp.where(i == place_ref[1], first, second)


def main_kernel(
    place_ref,
    block_ref,
    cutoff_ref,
    state_ref,
    base_ref,
    mine_ref,
    away_ref,
    high_ref,
    low_ref,
    turn_ref,
    after_ref,
    out_ref,
    token_ref,
):
    fields, _, rows, levels, width = state_ref.shape
    del after_ref
    token_ref[...] = jnp.zeros_like(token_ref)
    i = pl.program_id(0)
    turn = turn_ref[place_ref[0]]
    slot = chosen_slot(i, place_ref, block_ref, cutoff_ref, rows)
    spec = turned(jnp.where(i == 0, mine_ref[...], away_ref[...]), turn, -1.0)
    spec = spec.reshape(fields, rows, levels, 2 * KCUT)
    cuts = [cutoff_ref[block_ref[slot] * rows + r] for r in range(rows)]
    spec = jnp.concatenate(
        [spec[:, r : r + 1] * row_weights(cuts[r]) for r in range(rows)], axis=1
    )
    smooth = split_dot(
        spec.reshape(fields * rows * levels, 2 * KCUT), high_ref[...], low_ref[...]
    ).reshape(fields, rows, levels, width)
    for r in range(rows):
        out_ref[:, 0, r] = jnp.where(
            cuts[r] > 0, state_ref[:, 0, r] + smooth[:, r], base_ref[:, 0, r]
        )


def main_part(after, state, base, mine, away, inverse, turn, place, block, cutoff):
    fields, slots, rows, levels, width = state.shape
    slot_block = pl.BlockSpec(
        (fields, 1, rows, levels, width),
        lambda i, *scalars: (0, chosen_slot(i, *scalars, rows), 0, 0, 0),
    )
    return pl.pallas_call(
        main_kernel,
        grid_spec=pltpu.PrefetchScalarGridSpec(
            num_scalar_prefetch=3,
            grid=(2,),
            in_specs=[slot_block, slot_block] + vmem(6),
            out_specs=[slot_block, pl.BlockSpec((1, 2 * KCUT), lambda i, *scalars: (0, 0))],
        ),
        out_shape=[
            jax.ShapeDtypeStruct(state.shape, F32),
            jax.ShapeDtypeStruct((1, 2 * KCUT), F32),
        ],
        input_output_aliases={4: 0},
        compiler_params=pltpu.CompilerParams(vmem_limit_bytes=50 * MIB),
        cost_estimate=pl.CostEstimate(
            flops=12 * mine.shape[0] * 2 * KCUT * width,
            bytes_accessed=6 * 10**6,
            transcendentals=0,
        ),
        name="main",
    )(place, block, cutoff, state, base, mine, away, *inverse, turn, after)


def unpack(ref, full, tail, spare, put, fields, width):
    tiles = -(-width // LANES)
    lane = lax.broadcasted_iota(jnp.int32, (8, LANES), 1)

    def load(row):
        return ref[pl.ds(row, 8, stride=BACK), :]

    for f in range(fields):
        for t in range(tiles - 1):
            put(f, t * LANES, (t + 1) * LANES, load(full + t * fields + f))
        tile = load(tail + f)
        if spare is not None:
            other = pltpu.roll(load(spare + f), 2 * SPARE, 1)
            tile = jnp.where(lane < SPARE, pltpu.roll(tile, SPARE, 1), other)
        put(f, (tiles - 1) * LANES, width, tile[:, :TAIL])


def rim_kernel(
    packed,
    got_ref,
    high_ref,
    low_ref,
    turn_ref,
    place_ref,
    faces_ref,
    mine_ref,
    other_ref,
    token_ref,
):
    _, _, fields, levels, width = faces_ref.shape
    token_ref[...] = jnp.zeros_like(token_ref)
    if packed:
        for i in range(2):
            for side in range(2):

                def put(f, start, stop, tile, i=i, side=side):
                    faces_ref[i, side, f, :, start:stop] = tile

                q = 2 * i + side
                unpack(got_ref, 25 * q, 150 + 5 * q, None, put, fields, width)
    else:
        faces_ref[...] = got_ref[...]
    turn = turn_ref[place_ref[0]]
    core = place_ref[1]
    both = jnp.concatenate(
        [part for i in (core, 1 - core) for part in (faces_ref[i, 0], -faces_ref[i, 1])], axis=0
    ).reshape(4 * fields * levels, width)
    spec = turned(split_dot(both, high_ref[...], low_ref[...], axis=1), turn, 1.0)
    mine_ref[...] = spec[: 2 * fields * levels]
    other_ref[...] = spec[2 * fields * levels :]


def rim_spectra(got, shape, inverse, turn, place):
    _, _, fields, levels, width = shape
    spec = jax.ShapeDtypeStruct((2 * fields * levels, 2 * KCUT), F32)
    return pl.pallas_call(
        functools.partial(rim_kernel, got.ndim == 2),
        in_specs=vmem(4) + smem(1),
        out_specs=vmem(4),
        out_shape=[
            jax.ShapeDtypeStruct(shape, F32),
            spec,
            spec,
            jax.ShapeDtypeStruct((8, LANES), F32),
        ],
        compiler_params=pltpu.CompilerParams(vmem_limit_bytes=50 * MIB),
        cost_estimate=pl.CostEstimate(
            flops=24 * fields * levels * 2 * KCUT * width,
            bytes_accessed=3 * 10**6,
            transcendentals=0,
        ),
        name="rim_spectra",
    )(got, *inverse, turn, place)


def final_kernel(
    packed,
    main_ref,
    pair_ref,
    back_ref,
    mine_ref,
    away_ref,
    high_ref,
    low_ref,
    turn_ref,
    place_ref,
    block_ref,
    cutoff_ref,
    out_ref,
    smooth_ref,
):
    fields, slots, _, levels, width = main_ref.shape
    rows = 8
    side = pl.program_id(0)
    row = side * (rows - 1)
    turn = turn_ref[place_ref[0]]
    core = place_ref[1]
    first, second, rest = pick_slots(block_ref, cutoff_ref, rows)
    mine, other = mine_first((first, second), core)
    count = fields * levels

    @pl.when(side == 0)
    def _():
        spec = [
            turned(ref[j * count : (j + 1) * count], turn, -1.0)
            * row_weights(cutoff_ref[block_ref[slot] * rows + j * (rows - 1)])
            for slot, ref in ((mine, mine_ref), (other, away_ref))
            for j in range(2)
        ]
        smooth = split_dot(jnp.concatenate(spec, axis=0), high_ref[...], low_ref[...])
        smooth_ref[...] = smooth.reshape(2, 2, fields, levels, width)

    sign = jnp.where(side == 0, 1.0, -1.0).astype(F32)
    if packed:

        def put(f, start, stop, tile):
            old = main_ref[f, rest, 0, :, start:stop]
            out_ref[f, rest, 0, :, start:stop] = old + tile * sign

        unpack(
            back_ref, 100 + 25 * side, 150 + 5 * side, 160 + 5 * side, put, fields, width
        )
    else:
        out_ref[:, rest, 0] = main_ref[:, rest, 0] + back_ref[side] * sign
    cuts = [cutoff_ref[block_ref[slot] * rows + row] for slot in (mine, other)]
    for i, (slot, order) in enumerate(((mine, core), (other, 1 - core))):
        out_ref[:, slot, 0] = main_ref[:, slot, 0] + jnp.where(
            cuts[i] > 0, smooth_ref[i, side], pair_ref[order, side] * sign
        )


def final_part(main, pair, back, mine, away, inverse, turn, place, block, cutoff):
    fields, slots, rows, levels, width = main.shape
    block_spec = pl.BlockSpec(
        (fields, slots, 1, levels, width), lambda i: (0, 0, i * (rows - 1), 0, 0)
    )
    return pl.pallas_call(
        functools.partial(final_kernel, back.ndim == 2),
        grid=(2,),
        in_specs=[block_spec] + vmem(7) + smem(3),
        out_specs=block_spec,
        scratch_shapes=[pltpu.VMEM((2, 2, fields, levels, width), F32)],
        out_shape=jax.ShapeDtypeStruct(main.shape, F32),
        input_output_aliases={0: 0},
        compiler_params=pltpu.CompilerParams(vmem_limit_bytes=50 * MIB),
        cost_estimate=pl.CostEstimate(
            flops=12 * mine.shape[0] * 2 * KCUT * width,
            bytes_accessed=4 * 10**6,
            transcendentals=0,
        ),
        name="final",
    )(main, pair, back, mine, away, *inverse, turn, place, block, cutoff)


def swap(array, bit):
    size = lax.axis_size("lon")
    return lax.ppermute(array, "lon", [(i, i ^ bit) for i in range(size)])


def lon_sum(mine, other, last=None):
    total = mine + swap(other, 1)
    bit = 2
    while bit < lax.axis_size("lon"):
        total = total + swap(total, bit)
        bit *= 2
    if last is not None:
        total = total + last
    return total, swap(total, 1)


def shards(state, courant_x, courant_y, block_of_slot, face_source, cutoff):
    fields, slots, rows, levels, width = state.shape
    lat, lon = lax.axis_size("lat"), lax.axis_size("lon")
    lon_index = lax.axis_index("lon")
    place = jnp.stack([lon_index, lon_index % 2]).astype(jnp.int32)
    forward, inverse = basis_tables(width)
    turn = turn_table(lon, width)
    tables = (turn, place, block_of_slot, cutoff)

    packed = lat == levels == 8 and width == 5 * LANES + TAIL and fields == 5
    if packed:
        sent = pack(state, courant_y, block_of_slot).reshape(lat, PIECE, LANES)
        got = lax.all_to_all(sent, "lat", 0, 0, tiled=True)

    west, east = edges(state, courant_x)
    west = lax.ppermute(west, "lon", [(i, (i + 1) % lon) for i in range(lon)])
    east = lax.ppermute(east, "lon", [((i + 1) % lon, i) for i in range(lon)])
    base, mine, other = local_tendency(
        state, courant_x, courant_y, west, east, forward, *tables
    )
    if packed:
        back, token = faces_of_pieces(got, slots, cutoff)
        mine = mine + token
        back = lax.all_to_all(back, "lat", 0, 0, tiled=True)
        pair = rest = back.reshape(lat * BACK, LANES)
    else:
        faces = exchange_faces(state, courant_y, face_source)
        picked = pick_slots(block_of_slot, cutoff, rows)
        pair, rest = faces[jnp.stack(picked[:2])], faces[picked[2]]
    total, away = lon_sum(mine, other)
    shape = (2, 2, fields, levels, width)
    pair, rim_mine, rim_other, token = rim_spectra(pair, shape, inverse, turn, place)
    main, token = main_part(token, state, base, total, away, inverse, *tables)
    rim_total, rim_away = lon_sum(rim_mine, rim_other, token)
    return final_part(main, pair, rest, rim_total, rim_away, inverse, *tables)


def solution(mesh):
    placed = (
        P(None, "lat", None, None, "lon"),
        P("lat", None, None, "lon"),
        P("lat", None, None, "lon"),
        P("lat"),
        P("lat", None),
        P(),
    )
    return jax.shard_map(
        shards,
        mesh=mesh,
        in_specs=placed,
        out_specs=P(None, "lat", None, None, "lon"),
        check_vma=False,
    )
```
